32 devices in a mesh: dp: 8 (over z, y), tp: 4 (over x, core).
Axes of the slice: x: 2, y: 2, z: 4, core: 2. Of those that a mesh axis runs over, the one named last changes fastest.
Arguments:
- clean_latents: float32 [128, 256, 16], P(('dp', 'tp')), may hold values from -12 to 12
- noise_field: float32 [128, 256, 16], P(('dp', 'tp')), may hold values from -6 to 6
- timesteps: int32 [128], P(('dp', 'tp')), may hold values from 0 to 999
- labels: int32 [128], P(('dp', 'tp')), may hold values from 0 to 999
- drop_flags: int32 [128], P(('dp', 'tp')), may hold values 0 or 1
- entry_weight: float32 [656, 384], P(None, 'dp'), may hold values from -0.375 to 0.375
- class_table: float32 [1001, 384], P(None, 'dp'), may hold values from -0.2 to 0.2
- attn_weight: float32 [2, 384, 1536], P(None, None, ('dp', 'tp')), may hold values from -0.3125 to 0.3125
- ffn_in_weight: float32 [2, 384, 1536], P(None, None, ('dp', 'tp')), may hold values from -0.3125 to 0.3125
- ffn_out_weight: float32 [2, 1536, 384], P(None, ('dp', 'tp')), may hold values from -0.15625 to 0.15625
- ada_weight: float32 [2, 384, 2304], P(None, None, ('dp', 'tp')), may hold values from -0.21875 to 0.21875
- final_weight: float32 [384, 800], P('dp'), may hold values from -0.3125 to 0.3125
- entry_first: float32 [656, 384], P(None, 'dp'), may hold values from -2.2888184e-05 to 2.2888184e-05
- entry_second: float32 [656, 384], P(None, 'dp'), may hold values from 1.5995127e-11 to 6.398051e-11
- class_first: float32 [1001, 384], P(None, 'dp'), may hold values from -5.722046e-06 to 5.722046e-06
- class_second: float32 [1001, 384], P(None, 'dp'), may hold values from 9.996954e-13 to 3.9987818e-12
- attn_first: float32 [2, 384, 1536], P(None, None, ('dp', 'tp')), may hold values from -2.2888184e-05 to 2.2888184e-05
- attn_second: float32 [2, 384, 1536], P(None, None, ('dp', 'tp')), may hold values from 1.5995127e-11 to 6.398051e-11
- ffn_in_first: float32 [2, 384, 1536], P(None, None, ('dp', 'tp')), may hold values from -2.2888184e-05 to 2.2888184e-05
- ffn_in_second: float32 [2, 384, 1536], P(None, None, ('dp', 'tp')), may hold values from 1.5995127e-11 to 6.398051e-11
- ffn_out_first: float32 [2, 1536, 384], P(None, ('dp', 'tp')), may hold values from -2.2888184e-05 to 2.2888184e-05
- ffn_out_second: float32 [2, 1536, 384], P(None, ('dp', 'tp')), may hold values from 1.5995127e-11 to 6.398051e-11
- ada_first: float32 [2, 384, 2304], P(None, None, ('dp', 'tp')), may hold values from -2.2888184e-05 to 2.2888184e-05
- ada_second: float32 [2, 384, 2304], P(None, None, ('dp', 'tp')), may hold values from 1.5995127e-11 to 6.398051e-11
- final_first: float32 [384, 800], P('dp'), may hold values from -2.2888184e-05 to 2.2888184e-05
- final_second: float32 [384, 800], P('dp'), may hold values from 1.5995127e-11 to 6.398051e-11
Outputs:
- entry_new: float32 [656, 384], P(None, 'dp')
- entry_first_new: float32 [656, 384], P(None, 'dp')
- entry_second_new: float32 [656, 384], P(None, 'dp')
- class_new: float32 [1001, 384], P(None, 'dp')
- class_first_new: float32 [1001, 384], P(None, 'dp')
- class_second_new: float32 [1001, 384], P(None, 'dp')
- attn_new: float32 [2, 384, 1536], P(None, None, ('dp', 'tp'))
- attn_first_new: float32 [2, 384, 1536], P(None, None, ('dp', 'tp'))
- attn_second_new: float32 [2, 384, 1536], P(None, None, ('dp', 'tp'))
- ffn_in_new: float32 [2, 384, 1536], P(None, None, ('dp', 'tp'))
- ffn_in_first_new: float32 [2, 384, 1536], P(None, None, ('dp', 'tp'))
- ffn_in_second_new: float32 [2, 384, 1536], P(None, None, ('dp', 'tp'))
- ffn_out_new: float32 [2, 1536, 384], P(None, ('dp', 'tp'))
- ffn_out_first_new: float32 [2, 1536, 384], P(None, ('dp', 'tp'))
- ffn_out_second_new: float32 [2, 1536, 384], P(None, ('dp', 'tp'))
- ada_new: float32 [2, 384, 2304], P(None, None, ('dp', 'tp'))
- ada_first_new: float32 [2, 384, 2304], P(None, None, ('dp', 'tp'))
- ada_second_new: float32 [2, 384, 2304], P(None, None, ('dp', 'tp'))
- final_new: float32 [384, 800], P('dp')
- final_first_new: float32 [384, 800], P('dp')
- final_second_new: float32 [384, 800], P('dp')
- loss_sum: float32 [], replicated
- grad_norm: float32 [], replicated
- residual_rms: float32 [2], replicated
The draws below stay inside these ranges and needn't reach their ends.
All inputs are finite; a program needn't handle non-finite values. No bound on the sum of `drop_flags` on one device may be relied on, other than what follows from the above.
Results may differ from the reference program's by a relative error of at most 0.0044.
The reference program's roundings to bfloat16 on the way count: a program that leaves them out, or rounds other values in their place, can miss the bound.
Values may be sent and summed in bfloat16 or wider, within the bound.
A program may use at most 192 MiB of HBM per device.

```python
import math
import jax
import jax.numpy as jnp
from jax import lax

D = 384
HEADS = 6
HEAD_DIM = 64
FF = 1536
CLASSES = 1000
GRID = 16
PATCH_IN = 16
OUT = 32
FREQ = 256
NOISE_STEPS = 1000
LAYERS = 2
STEP = 10
TOK = 256
LATENTS = 128
PARAMS = 6251904


def draw_clean_latents(key, part):
    key = jax.random.fold_in(key, 11)
    ramp = jnp.arange(LATENTS, dtype=jnp.float32) / (LATENTS - 1)
    base = jnp.clip(jax.random.normal(key, (LATENTS, TOK, PATCH_IN), jnp.float32), -4.0, 4.0)
    spread = 1.0 + 2.0 * ramp
    return base * spread[:, None, None]


def touch_ends(drawn, stream_key, smallest, high):
    longest = drawn.shape.index(max(drawn.shape))
    spots = []
    for shift in (0, 1):
        where = [jax.random.randint(jax.random.fold_in(stream_key, axis), (), 0, length) for axis, length in enumerate(drawn.shape)]
        where[longest] = (where[longest] + shift) % drawn.shape[longest]
        spots.append(tuple(where))
    return drawn.at[spots[0]].set(smallest).at[spots[1]].set(high)


def levels(key, extent, pieces, smallest, largest):
    gain = 1.0
    for position, parts in pieces:
        draws = jax.random.uniform(jax.random.fold_in(jax.random.fold_in(key, 6), position), (parts,), jnp.float32, smallest / len(pieces), largest / len(pieces))
        gain = gain * jnp.repeat(jnp.exp(draws), extent[position] // parts).reshape((-1,) + (1,) * (len(extent) - 1 - position))
    return gain


def centred(stream_key, extent, scale, limit, pieces=(), kind=jnp.bfloat16):
    entries = jax.random.normal(stream_key, extent, jnp.float32) * scale
    if len(pieces) > 0:
        entries = levels(stream_key, extent, pieces, -0.22, 0.18) * entries
    return jnp.clip(entries, min=-limit, max=limit).astype(kind)


def setup_inputs(seed: int = 0) -> dict:
    splits = jax.random.split(jax.random.key(seed), 27)
    return {
        "clean_latents": draw_clean_latents(jax.random.fold_in(splits[26], 71), 0),
        "noise_field": centred(splits[1], (LATENTS, TOK, PATCH_IN), 1.0, 6.0, ((0, 32),), jnp.float32),
        "timesteps": touch_ends(jax.random.randint(splits[2], (LATENTS,), 0, NOISE_STEPS), jax.random.fold_in(splits[2], 1), 0, NOISE_STEPS - 1).astype(jnp.int32),
        "labels": touch_ends(jax.random.randint(splits[3], (LATENTS,), 0, CLASSES), jax.random.fold_in(splits[3], 1), 0, CLASSES - 1).astype(jnp.int32),
        "drop_flags": touch_ends((jax.random.randint(splits[4], (LATENTS,), 0, 10) < 1).astype(jnp.int32), jax.random.fold_in(splits[4], 1), 0, 1),
        "entry_weight": centred(splits[5], (PATCH_IN + FREQ + D, D), 256 ** -0.5, 0.375, ((1, 8),), jnp.float32),
        "class_table": centred(splits[6], (CLASSES + 1, D), 0.04, 0.2, ((1, 8),), jnp.float32),
        "attn_weight": centred(splits[7], (LAYERS, D, 4 * D), D ** -0.5, 0.3125, ((2, 32),), jnp.float32),
        "ffn_in_weight": centred(splits[8], (LAYERS, D, FF), D ** -0.5, 0.3125, ((2, 32),), jnp.float32),
        "ffn_out_weight": centred(splits[9], (LAYERS, FF, D), FF ** -0.5, 0.15625, ((1, 32),), jnp.float32),
        "ada_weight": centred(splits[10], (LAYERS, D, 6 * D), (2 * D) ** -0.5, 0.21875, ((2, 32),), jnp.float32),
        "final_weight": centred(splits[11], (D, 2 * D + OUT), D ** -0.5, 0.3125, ((0, 8),), jnp.float32),
        "entry_first": centred(splits[12], (PATCH_IN + FREQ + D, D), (0.01 * PARAMS ** -0.5), 2.288818359375e-05, ((1, 8),), jnp.float32),
        "entry_second": jnp.clip(jnp.exp(math.log(6.398050839129255e-11) - 1.3862944 * jax.random.uniform(splits[13], (PATCH_IN + FREQ + D, D), jnp.float32) ** levels(splits[13], (PATCH_IN + FREQ + D, D), ((1, 8),), -0.2, 0.2)), 1.5995127097823136e-11, 6.398050839129255e-11),
        "class_first": centred(splits[14], (CLASSES + 1, D), (0.0025 * PARAMS ** -0.5), 5.7220458984375e-06, ((1, 8),), jnp.float32),
        "class_second": jnp.clip(jnp.exp(math.log(3.998781774455784e-12) - 1.3862944 * jax.random.uniform(splits[15], (CLASSES + 1, D), jnp.float32) ** levels(splits[15], (CLASSES + 1, D), ((1, 8),), -0.2, 0.2)), 9.99695443613946e-13, 3.998781774455784e-12),
        "attn_first": centred(splits[16], (LAYERS, D, 4 * D), (0.01 * PARAMS ** -0.5), 2.288818359375e-05, ((2, 32),), jnp.float32),
        "attn_second": jnp.clip(jnp.exp(math.log(6.398050839129255e-11) - 1.3862944 * jax.random.uniform(splits[17], (LAYERS, D, 4 * D), jnp.float32) ** levels(splits[17], (LAYERS, D, 4 * D), ((2, 32),), -0.2, 0.2)), 1.5995127097823136e-11, 6.398050839129255e-11),
        "ffn_in_first": centred(splits[18], (LAYERS, D, FF), (0.01 * PARAMS ** -0.5), 2.288818359375e-05, ((2, 32),), jnp.float32),
        "ffn_in_second": jnp.clip(jnp.exp(math.log(6.398050839129255e-11) - 1.3862944 * jax.random.uniform(splits[19], (LAYERS, D, FF), jnp.float32) ** levels(splits[19], (LAYERS, D, FF), ((2, 32),), -0.2, 0.2)), 1.5995127097823136e-11, 6.398050839129255e-11),
        "ffn_out_first": centred(splits[20], (LAYERS, FF, D), (0.01 * PARAMS ** -0.5), 2.288818359375e-05, ((1, 32),), jnp.float32),
        "ffn_out_second": jnp.clip(jnp.exp(math.log(6.398050839129255e-11) - 1.3862944 * jax.random.uniform(splits[21], (LAYERS, FF, D), jnp.float32) ** levels(splits[21], (LAYERS, FF, D), ((1, 32),), -0.2, 0.2)), 1.5995127097823136e-11, 6.398050839129255e-11),
        "ada_first": centred(splits[22], (LAYERS, D, 6 * D), (0.01 * PARAMS ** -0.5), 2.288818359375e-05, ((2, 32),), jnp.float32),
        "ada_second": jnp.clip(jnp.exp(math.log(6.398050839129255e-11) - 1.3862944 * jax.random.uniform(splits[23], (LAYERS, D, 6 * D), jnp.float32) ** levels(splits[23], (LAYERS, D, 6 * D), ((2, 32),), -0.2, 0.2)), 1.5995127097823136e-11, 6.398050839129255e-11),
        "final_first": centred(splits[24], (D, 2 * D + OUT), (0.01 * PARAMS ** -0.5), 2.288818359375e-05, ((0, 8),), jnp.float32),
        "final_second": jnp.clip(jnp.exp(math.log(6.398050839129255e-11) - 1.3862944 * jax.random.uniform(splits[25], (D, 2 * D + OUT), jnp.float32) ** levels(splits[25], (D, 2 * D + OUT), ((0, 8),), -0.2, 0.2)), 1.5995127097823136e-11, 6.398050839129255e-11),
    }


@jax.custom_vjp
def low(v):
    return lax.optimization_barrier(v.astype(jnp.bfloat16)).astype(jnp.float32)

@jax.custom_vjp
def low_back(v):
    return v

def low_keep(v):
    return (low(v), None)

def low_pass(kept, grad):
    return (grad,)

def back_keep(v):
    return (v, None)

def back_low(kept, grad):
    return (low(grad),)
low.defvjp(low_keep, low_pass)
low_back.defvjp(back_keep, back_low)

def matmul(former, latter):
    return jnp.dot(former, latter, precision=lax.Precision.HIGHEST, preferred_element_type=jnp.float32)

def layer_norm(stream):
    center = stream - lax.optimization_barrier(jnp.mean(stream, axis=-1, keepdims=True))
    return center * lax.rsqrt(lax.optimization_barrier(jnp.mean(center * center, axis=-1, keepdims=True)) + 1e-06)

def modulate(stream, shift_part, scale_part):
    return layer_norm(stream) * (1.0 + scale_part[:, None, :]) + shift_part[:, None, :]

def position_table(grid_side, columns):
    quarter = columns // 4
    omegas = jnp.exp(-math.log(10000.0) * jnp.arange(quarter, dtype=jnp.float32) / quarter)
    positions = jnp.arange(grid_side * grid_side, dtype=jnp.int32)
    row_pos = (positions // grid_side).astype(jnp.float32)[:, None] * omegas
    col_pos = (positions % grid_side).astype(jnp.float32)[:, None] * omegas
    return jnp.concatenate([jnp.sin(row_pos), jnp.cos(row_pos), jnp.sin(col_pos), jnp.cos(col_pos)], axis=-1)

def time_table(step_ids, columns):
    half_cols = columns // 2
    frequency = jnp.exp(-math.log(10000.0) * jnp.arange(half_cols, dtype=jnp.float32) / half_cols)
    angles = step_ids.astype(jnp.float32)[:, None] * frequency
    return jnp.concatenate([jnp.cos(angles), jnp.sin(angles)], axis=-1)

def noise_scales(step_ids):
    phases = (step_ids.astype(jnp.float32) / NOISE_STEPS + 0.008) / 1.008 * (math.pi / 2)
    return (jnp.cos(phases), jnp.sin(phases))

def softmax_rows(scores):
    shifted = jnp.exp(scores - lax.optimization_barrier(jnp.max(scores, axis=-1, keepdims=True)))
    return shifted / lax.optimization_barrier(jnp.sum(shifted, axis=-1, keepdims=True))

def forward(params, clean, noise, step_ids, label_ids, drop_ids):
    entry, table, attn, ffn_in, ffn_out, ada, final = params
    group = clean.shape[0]
    entry_low = low(entry)
    cos_part, sin_part = noise_scales(step_ids)
    noisy = low(cos_part[:, None, None] * clean + sin_part[:, None, None] * noise)
    stream = matmul(noisy.reshape(-1, PATCH_IN), entry_low[:PATCH_IN]).reshape(group, TOK, D) + position_table(GRID, D)[None]
    time_feat = low(time_table(step_ids, FREQ))
    time_act = low(jax.nn.silu(matmul(time_feat, entry_low[PATCH_IN:PATCH_IN + FREQ])))
    classes_used = jnp.where(drop_ids == 1, CLASSES, label_ids).astype(jnp.int32)
    cond = matmul(time_act, entry_low[PATCH_IN + FREQ:]) + jnp.take(low(table), classes_used, axis=0)
    cond_low = low(jax.nn.silu(cond))
    squares = []
    for layer_idx in range(LAYERS):
        attn_low = low(attn[layer_idx])
        modulation = matmul(cond_low, low(ada[layer_idx]))
        shift_one, scale_one, gate_one, shift_two, scale_two, gate_two = jnp.split(modulation, 6, axis=-1)
        attn_in = low(modulate(stream, shift_one, scale_one)).reshape(-1, D)
        qkv = low_back(low(matmul(attn_in, attn_low[:, :3 * D]))).reshape(group, TOK, 3, HEADS, HEAD_DIM)
        scores = low_back(jnp.einsum('bqhe,bkhe->bhqk', qkv[:, :, 0], qkv[:, :, 1], precision=lax.Precision.HIGHEST) * HEAD_DIM ** (-0.5))
        probs = low(softmax_rows(scores))
        mixed = low_back(low(jnp.einsum('bhqk,bkhe->bqhe', probs, qkv[:, :, 2], precision=lax.Precision.HIGHEST)))
        attn_branch = low_back(matmul(mixed.reshape(-1, D), attn_low[:, 3 * D:])).reshape(group, TOK, D)
        middle = stream + gate_one[:, None, :] * attn_branch
        mlp_input = low(modulate(middle, shift_two, scale_two)).reshape(-1, D)
        hidden = low_back(matmul(mlp_input, low(ffn_in[layer_idx])))
        act_low = low(jax.nn.gelu(hidden, approximate=True))
        mlp_branch = low_back(matmul(act_low, low(ffn_out[layer_idx]))).reshape(group, TOK, D)
        stream = middle + gate_two[:, None, :] * mlp_branch
        squares.append(jnp.sum(stream * stream))
    final_low = low(final)
    final_mod = matmul(cond_low, final_low[:, :2 * D])
    shift_fin, scale_fin = jnp.split(final_mod, 2, axis=-1)
    final_in = low(modulate(stream, shift_fin, scale_fin)).reshape(-1, D)
    predicted = low_back(matmul(final_in, final_low[:, 2 * D:]))
    target = jnp.concatenate([noise, clean], axis=-1).reshape(-1, OUT)
    errors = predicted - target
    loss_part = jnp.sum(errors * errors)
    return (loss_part / (LATENTS * TOK * OUT), (loss_part, jnp.stack(squares)))

def adam_update(weight, first, second, grad, factor):
    clipped = grad * factor
    first_new = 0.5 * first + 0.5 * clipped
    second_new = 0.5 * second + 0.5 * clipped * clipped
    correct = 1.0 - 0.5 ** STEP
    new_weight = weight - 0.02 * (first_new / correct / (jnp.sqrt(second_new / correct) + 1e-08) + 0.01 * weight)
    return (new_weight, first_new, second_new)

def reference(clean_latents, noise_field, timesteps, labels, drop_flags, entry_weight, class_table, attn_weight, ffn_in_weight, ffn_out_weight, ada_weight, final_weight, entry_first, entry_second, class_first, class_second, attn_first, attn_second, ffn_in_first, ffn_in_second, ffn_out_first, ffn_out_second, ada_first, ada_second, final_first, final_second):
    params = (entry_weight, class_table, attn_weight, ffn_in_weight, ffn_out_weight, ada_weight, final_weight)
    groups = LATENTS // 16
    data = tuple((item.reshape((groups, 16) + item.shape[1:]) for item in (clean_latents, noise_field, timesteps, labels, drop_flags)))

    def one_group(carry, piece):
        grads, loss_acc, square_acc = carry

        def group_loss(weights):
            return forward(weights, piece[0], piece[1], piece[2], piece[3], piece[4])
        value_out, back_fn, aux_out = jax.vjp(group_loss, params, has_aux=True)
        group_grads, = back_fn(jnp.ones((), jnp.float32))
        grads = jax.tree.map(jnp.add, grads, group_grads)
        return ((grads, loss_acc + aux_out[0], square_acc + aux_out[1]), None)
    init = (jax.tree.map(jnp.zeros_like, params), jnp.zeros((), jnp.float32), jnp.zeros((LAYERS,), jnp.float32))
    (grads, loss_total, square_totals), _ = lax.scan(one_group, init, data)
    grad_norm = jnp.sqrt(sum((jnp.sum(grad * grad) for grad in grads)))
    factor = jnp.minimum(1.0, 0.01 / (grad_norm + 1e-06))
    firsts = (entry_first, class_first, attn_first, ffn_in_first, ffn_out_first, ada_first, final_first)
    seconds = (entry_second, class_second, attn_second, ffn_in_second, ffn_out_second, ada_second, final_second)
    results = []
    for weight, first, second, grad in zip(params, firsts, seconds, grads):
        results.extend(adam_update(weight, first, second, grad, factor))
    residual_rms = jnp.sqrt(square_totals / (LATENTS * TOK * D))
    return (results[0], results[1], results[2], results[3], results[4], results[5], results[6], results[7], results[8], results[9], results[10], results[11], results[12], results[13], results[14], results[15], results[16], results[17], results[18], results[19], results[20], loss_total, grad_norm, residual_rms)
```

```python
import functools
import math

import jax
import jax.numpy as jnp
from jax import lax
from jax.experimental import pallas as pl
from jax.experimental.pallas import tpu as pltpu
from jax.sharding import PartitionSpec as P

D = 384
HEADS = 6
HEAD_DIM = 64
CLASSES = 1000
GRID = 16
PATCH_IN = 16
OUT = 32
FREQ = 256
NOISE_STEPS = 1000
STEP = 10
BF = jnp.bfloat16


highest = lax.Precision.HIGHEST


def dot_nn(a, b):
    return lax.dot_general(a, b, (((1,), (0,)), ((), ())), preferred_element_type=jnp.float32)


def dot_nt(a, b):
    return lax.dot_general(a, b, (((1,), (1,)), ((), ())), preferred_element_type=jnp.float32)


def dot_tn(a, b):
    return lax.dot_general(a, b, (((0,), (0,)), ((), ())), preferred_element_type=jnp.float32)


def norm_rows(rows):
    center = rows - jnp.mean(rows, axis=-1, keepdims=True)
    rstd = lax.rsqrt(jnp.mean(center * center, axis=-1, keepdims=True) + 1e-06)
    return center * rstd, rstd


def norm_back(d_out, hat, rstd, scale):
    d_shift = jnp.sum(d_out, axis=1, keepdims=True)
    d_scale = jnp.sum(d_out * hat, axis=1, keepdims=True)
    d_hat = d_out * (1.0 + scale)
    m_one = jnp.mean(d_hat, axis=-1, keepdims=True)
    m_two = jnp.mean(d_hat * hat, axis=-1, keepdims=True)
    return rstd * (d_hat - m_one - hat * m_two), d_shift, d_scale


def half_masks():
    lane = lax.broadcasted_iota(jnp.int32, (1, 2 * HEAD_DIM), 1)
    low = jnp.where(lane < HEAD_DIM, 1.0, 0.0)
    return low.astype(BF), (1.0 - low).astype(BF)


def stack_heads(pair, masks):
    return jnp.concatenate([pair * masks[0], pair * masks[1]], axis=0)


GELU_A = math.sqrt(2.0 / math.pi)
GELU_B = 0.044715


def forward_kernel(first, nb, tokens, *refs):
    if first:
        noisy_ref, patch_ref, pos_ref = refs[:3]
        refs = refs[3:]
    else:
        stream_ref = refs[0]
        refs = refs[1:]
    mod_ref, attn_ref, in_ref, out_ref = refs[:4]
    refs = refs[4:]
    if first:
        start_ref = refs[0]
        refs = refs[1:]
    (
        result_ref,
        qkv_ref,
        probs_ref,
        mixed_ref,
        branch_ref,
        middle_ref,
        mlp_ref,
        act_ref,
        slope_ref,
        square_ref,
    ) = refs
    rows = nb * tokens
    if first:
        parts = [dot_tn(noisy_ref[n], patch_ref[...]) + pos_ref[...] for n in range(nb)]
        stream = parts[0] if nb == 1 else jnp.concatenate(parts, axis=0)
        start_ref[...] = stream
    else:
        stream = stream_ref[...]
    mod = mod_ref[...]
    stream = stream.reshape(nb, tokens, D)
    hat, _ = norm_rows(stream)
    attn_in = (hat * (1.0 + mod[:, 1:2]) + mod[:, 0:1]).astype(BF).reshape(rows, D)
    qkv_ref[...] = dot_nt(attn_in, attn_ref[: 3 * D, :]).astype(BF)
    masks = half_masks()
    for n in range(nb):
        here = slice(n * tokens, (n + 1) * tokens)
        for pair in range(HEADS // 2):
            col = pair * 2 * HEAD_DIM
            queries = qkv_ref[here, col : col + 2 * HEAD_DIM] * jnp.asarray(HEAD_DIM**-0.5, BF)
            keys = stack_heads(qkv_ref[here, D + col : D + col + 2 * HEAD_DIM], masks)
            values = stack_heads(qkv_ref[here, 2 * D + col : 2 * D + col + 2 * HEAD_DIM], masks)
            scores = dot_nt(queries, keys)
            halves = []
            for side in range(2):
                part = scores[:, side * tokens : (side + 1) * tokens]
                grown = jnp.exp(part - jnp.max(part, axis=-1, keepdims=True))
                halves.append((grown * (1.0 / jnp.sum(grown, axis=-1, keepdims=True))).astype(BF))
            probs = jnp.concatenate(halves, axis=1)
            probs_ref[here, pair * 2 * tokens : (pair + 1) * 2 * tokens] = probs
            mixed_ref[here, col : col + 2 * HEAD_DIM] = dot_nn(probs, values).astype(BF)
    branch = dot_nt(mixed_ref[...], attn_ref[3 * D :, :])
    branch_ref[...] = branch.astype(BF)
    middle = stream + mod[:, 2:3] * branch.reshape(nb, tokens, D)
    middle_ref[...] = middle.reshape(rows, D)
    hat, _ = norm_rows(middle)
    mlp_in = (hat * (1.0 + mod[:, 4:5]) + mod[:, 3:4]).astype(BF).reshape(rows, D)
    hidden = dot_nt(mlp_in, in_ref[...])
    squared = hidden * hidden
    bent = jnp.tanh(hidden * (GELU_A + (GELU_A * GELU_B) * squared))
    half = 0.5 * hidden
    act = (half + half * bent).astype(BF)
    act_ref[...] = act
    slope_ref[...] = (
        0.5
        + 0.5 * bent
        + half * (1.0 - bent * bent) * (GELU_A + (3.0 * GELU_A * GELU_B) * squared)
    ).astype(BF)
    mlp = dot_nn(act, out_ref[...])
    mlp_ref[...] = mlp.astype(BF)
    result = middle + mod[:, 5:6] * mlp.reshape(nb, tokens, D)
    result_ref[...] = result.reshape(rows, D)
    square_ref[0] = jnp.sum((result * result).reshape(rows // 8, 8, D), axis=0)


def backward_kernel(first, last, nb, tokens, steps, count_all, *refs):
    if last:
        final_ref, fmod_ref, head_ref, clean_ref, noise_ref = refs[:5]
        refs = refs[5:]
    else:
        d_stream_ref = refs[0]
        refs = refs[1:]
    if first:
        noisy_ref = refs[0]
        refs = refs[1:]
    (
        mod_ref,
        attn_ref,
        in_ref,
        out_ref,
        stream_ref,
        qkv_ref,
        probs_ref,
        mixed_ref,
        branch_ref,
        middle_ref,
        mlp_ref,
        act_ref,
        slope_ref,
    ) = refs[:13]
    refs = refs[13:]
    if last:
        loss_ref, dhead_ref, dfmod_ref = refs[:3]
        refs = refs[3:]
    if first:
        dpatch_ref = refs[0]
    else:
        d_prev_ref = refs[0]
    gattn_ref, gin_ref, gout_ref, dmod_ref, acc_attn, acc_in, acc_out, d_qkv_s = refs[1:]
    rows = nb * tokens
    step = pl.program_id(0)

    @pl.when(step == 0)
    def _():
        acc_attn[...] = jnp.zeros_like(acc_attn)
        acc_in[...] = jnp.zeros_like(acc_in)
        acc_out[...] = jnp.zeros_like(acc_out)
        if last:
            dhead_ref[...] = jnp.zeros_like(dhead_ref)
        if first:
            dpatch_ref[...] = jnp.zeros_like(dpatch_ref)

    mod = mod_ref[...]
    if last:
        fmod = fmod_ref[...]
        hat, rstd = norm_rows(final_ref[...].reshape(nb, tokens, D))
        final_in = (hat * (1.0 + fmod[:, 1:2]) + fmod[:, 0:1]).astype(BF)
        d_parts = []
        loss = jnp.zeros((8, tokens), jnp.float32)
        for n in range(nb):
            predicted = lax.dot_general(
                head_ref[...], final_in[n], (((0,), (1,)), ((), ())), preferred_element_type=jnp.float32
            )
            errors = predicted - jnp.concatenate([noise_ref[n], clean_ref[n]], axis=0)
            loss = loss + jnp.sum((errors * errors).reshape(OUT // 8, 8, tokens), axis=0)
            d_pred = (errors * (2.0 / count_all)).astype(BF)
            dhead_ref[...] += dot_nn(d_pred, final_in[n])
            d_parts.append(
                lax.dot_general(
                    d_pred, head_ref[...], (((0,), (1,)), ((), ())), preferred_element_type=jnp.float32
                )
            )
        loss_ref[0] = loss
        d_final = jnp.stack(d_parts, axis=0)
        d_stream, d_shift, d_scale = norm_back(d_final, hat, rstd, fmod[:, 1:2])
        dfmod_ref[:, 0:1] = d_shift
        dfmod_ref[:, 1:2] = d_scale
    else:
        d_stream = d_stream_ref[...].reshape(nb, tokens, D)
    dmod_ref[:, 5:6] = jnp.sum(d_stream * mlp_ref[...].astype(jnp.float32).reshape(nb, tokens, D), axis=1, keepdims=True)
    d_mlp = (d_stream * mod[:, 5:6]).astype(BF).reshape(rows, D)
    d_hidden = (dot_nt(d_mlp, out_ref[...]) * slope_ref[...].astype(jnp.float32)).astype(BF)
    acc_out[...] += dot_tn(act_ref[...], d_mlp)
    hat, rstd = norm_rows(middle_ref[...].reshape(nb, tokens, D))
    mlp_in = (hat * (1.0 + mod[:, 4:5]) + mod[:, 3:4]).astype(BF).reshape(rows, D)
    acc_in[...] += dot_tn(d_hidden, mlp_in)
    d_input = dot_nn(d_hidden, in_ref[...]).reshape(nb, tokens, D)
    d_middle, d_shift, d_scale = norm_back(d_input, hat, rstd, mod[:, 4:5])
    dmod_ref[:, 3:4] = d_shift
    dmod_ref[:, 4:5] = d_scale
    d_middle = d_middle + d_stream
    dmod_ref[:, 2:3] = jnp.sum(
        d_middle * branch_ref[...].astype(jnp.float32).reshape(nb, tokens, D), axis=1, keepdims=True
    )
    d_proj = (d_middle * mod[:, 2:3]).astype(BF).reshape(rows, D)
    acc_attn[3 * D :, :] += dot_tn(d_proj, mixed_ref[...])
    d_mix = dot_nn(d_proj, attn_ref[3 * D :, :]).astype(BF)
    masks = half_masks()
    lane = lax.broadcasted_iota(jnp.int32, (tokens, 2 * HEAD_DIM), 1)
    low_side = lane < HEAD_DIM
    root = HEAD_DIM**-0.5
    for n in range(nb):
        here = slice(n * tokens, (n + 1) * tokens)
        for pair in range(HEADS // 2):
            col = pair * 2 * HEAD_DIM
            queries = qkv_ref[here, col : col + 2 * HEAD_DIM]
            keys = stack_heads(qkv_ref[here, D + col : D + col + 2 * HEAD_DIM], masks)
            values = stack_heads(qkv_ref[here, 2 * D + col : 2 * D + col + 2 * HEAD_DIM], masks)
            d_out = d_mix[here, col : col + 2 * HEAD_DIM]
            probs_bf = probs_ref[here, pair * 2 * tokens : (pair + 1) * 2 * tokens]
            d_probs = dot_nt(d_out, values)
            halves = []
            for side in range(2):
                cut = slice(side * tokens, (side + 1) * tokens)
                probs = probs_bf[:, cut].astype(jnp.float32)
                part = d_probs[:, cut]
                halves.append((probs * (part - jnp.sum(probs * part, axis=-1, keepdims=True))).astype(BF))
            d_scores = jnp.concatenate(halves, axis=1)
            d_queries = dot_nn(d_scores, keys) * root
            d_keys = dot_tn(d_scores, queries)
            d_keys = jnp.where(low_side, d_keys[:tokens], d_keys[tokens:]) * root
            d_values = dot_tn(probs_bf, d_out)
            d_values = jnp.where(low_side, d_values[:tokens], d_values[tokens:])
            d_qkv_s[here, col : col + 2 * HEAD_DIM] = d_queries.astype(BF)
            d_qkv_s[here, D + col : D + col + 2 * HEAD_DIM] = d_keys.astype(BF)
            d_qkv_s[here, 2 * D + col : 2 * D + col + 2 * HEAD_DIM] = d_values.astype(BF)
    d_qkv = d_qkv_s[...]
    hat, rstd = norm_rows(stream_ref[...].reshape(nb, tokens, D))
    attn_in = (hat * (1.0 + mod[:, 1:2]) + mod[:, 0:1]).astype(BF).reshape(rows, D)
    acc_attn[: 3 * D, :] += dot_tn(d_qkv, attn_in)
    d_attn_in = dot_nn(d_qkv, attn_ref[: 3 * D, :]).reshape(nb, tokens, D)
    d_before, d_shift, d_scale = norm_back(d_attn_in, hat, rstd, mod[:, 1:2])
    dmod_ref[:, 0:1] = d_shift
    dmod_ref[:, 1:2] = d_scale
    d_prev = d_middle + d_before
    if first:
        for n in range(nb):
            dpatch_ref[...] += lax.dot_general(
                noisy_ref[n].astype(jnp.float32), d_prev[n], (((1,), (0,)), ((), ())), precision=highest
            )
    else:
        d_prev_ref[...] = d_prev.reshape(rows, D)

    @pl.when(step == steps - 1)
    def _():
        gattn_ref[...] = acc_attn[...].astype(BF)
        gin_ref[...] = acc_in[...].astype(BF)
        gout_ref[...] = acc_out[...].astype(BF)


def whole_spec(array):
    return pl.BlockSpec(array.shape, lambda i: (0,) * array.ndim)


def lead_spec(block, ndim):
    return pl.BlockSpec(block, lambda i: (i,) + (0,) * (ndim - 1))


LIMIT = 56 * 1024 * 1024


def forward_layer(first, entry_args, mod, weights, nb, tokens):
    lat_count = mod.shape[0]
    rows = nb * tokens
    steps = lat_count // nb
    total = lat_count * tokens
    kinds = [(D, jnp.float32)] if first else []
    kinds += [
        (D, jnp.float32),
        (3 * D, BF),
        (HEADS * tokens, BF),
        (D, BF),
        (D, BF),
        (D, jnp.float32),
        (D, BF),
        (4 * D, BF),
        (4 * D, BF),
    ]
    out_shape = [jax.ShapeDtypeStruct((total, cols), kind) for cols, kind in kinds]
    out_specs = [lead_spec((rows, cols), 2) for cols, _ in kinds]
    out_shape.append(jax.ShapeDtypeStruct((steps, 8, D), jnp.float32))
    out_specs.append(lead_spec((1, 8, D), 3))
    if first:
        noisy, patch, pos = entry_args
        in_specs = [lead_spec((nb, PATCH_IN, tokens), 3), whole_spec(patch), whole_spec(pos)]
    else:
        in_specs = [lead_spec((rows, D), 2)]
    in_specs += [lead_spec((nb, 8, D), 3)] + [whole_spec(w) for w in weights]
    return pl.pallas_call(
        functools.partial(forward_kernel, first, nb, tokens),
        grid=(steps,),
        out_shape=out_shape,
        in_specs=in_specs,
        out_specs=out_specs,
        compiler_params=pltpu.CompilerParams(vmem_limit_bytes=LIMIT),
        name="block_forward",
    )(*entry_args, mod, *weights)


def backward_layer(first, last, entry_args, mod, weights, saved, nb, tokens, count_all):
    lat_count = mod.shape[0]
    rows = nb * tokens
    steps = lat_count // nb
    total = lat_count * tokens
    in_specs = []
    args = list(entry_args)
    if last:
        in_specs += [
            lead_spec((rows, D), 2),
            lead_spec((nb, 8, D), 3),
            whole_spec(args[2]),
            lead_spec((nb, PATCH_IN, tokens), 3),
            lead_spec((nb, PATCH_IN, tokens), 3),
        ]
    else:
        in_specs += [lead_spec((rows, D), 2)]
    if first:
        in_specs += [lead_spec((nb, PATCH_IN, tokens), 3)]
    in_specs += [lead_spec((nb, 8, D), 3)] + [whole_spec(w) for w in weights]
    in_specs += [lead_spec((rows, s.shape[1]), 2) for s in saved]
    out_shape = []
    out_specs = []

    def add(shape, kind, spec):
        out_shape.append(jax.ShapeDtypeStruct(shape, kind))
        out_specs.append(spec)

    def whole(shape):
        return pl.BlockSpec(shape, lambda i: (0,) * len(shape))

    if last:
        add((steps, 8, tokens), jnp.float32, lead_spec((1, 8, tokens), 3))
        add((OUT, D), jnp.float32, whole((OUT, D)))
        add((lat_count, 8, D), jnp.float32, lead_spec((nb, 8, D), 3))
    if first:
        add((PATCH_IN, D), jnp.float32, whole((PATCH_IN, D)))
    else:
        add((total, D), jnp.float32, lead_spec((rows, D), 2))
    for _ in range(3):
        add((4 * D, D), BF, whole((4 * D, D)))
    add((lat_count, 8, D), jnp.float32, lead_spec((nb, 8, D), 3))
    return pl.pallas_call(
        functools.partial(backward_kernel, first, last, nb, tokens, steps, count_all),
        grid=(steps,),
        out_shape=out_shape,
        in_specs=in_specs,
        out_specs=out_specs,
        scratch_shapes=[pltpu.VMEM((4 * D, D), jnp.float32)] * 3 + [pltpu.VMEM((rows, 3 * D), BF)],
        compiler_params=pltpu.CompilerParams(vmem_limit_bytes=LIMIT),
        name="block_backward",
    )(*args, mod, *weights, *saved)


MESH = pl.DeviceIdType.MESH


class Places:
    def __init__(self, n_dp, n_tp):
        self.digits = []
        for axis, count, top in (("dp", n_dp, 4), ("tp", n_tp, 2)):
            sizes = []
            rest = count
            while rest > 1:
                size = next((s for s in (top, 2, 3, 5, 7) if rest % s == 0), rest)
                sizes.append(size)
                rest //= size
            stride = count
            for size in sizes:
                stride //= size
                self.digits.append((axis, stride, size))
        self.dims = tuple(size for _, _, size in self.digits)
        self.count = n_dp * n_tp

    def order(self, odd):
        names = list(range(len(self.digits)))
        if odd and len(names) >= 4:
            names[-3], names[-2] = names[-2], names[-3]
        return names

    def mine(self):
        return [lax.rem(lax.axis_index(axis) // stride, size) for axis, stride, size in self.digits]

    def other(self, mine, digit, shift):
        axis, stride, size = self.digits[digit]
        value = lax.rem(mine[digit] + shift, size)
        return {axis: lax.axis_index(axis) + (value - mine[digit]) * stride}, value

    def barrier(self, mine):
        barrier = pltpu.get_barrier_semaphore()
        count = 0
        for digit, size in enumerate(self.dims):
            for shift in range(1, size):
                target, _ = self.other(mine, digit, shift)
                pl.semaphore_signal(barrier, inc=1, device_id=target, device_id_type=MESH)
                count += 1
        pl.semaphore_wait(barrier, count)


def gather_kernel(places, chunks, *refs):
    ins, outs = refs[:chunks], refs[chunks : 2 * chunks]
    send_sems, recv_sems, own_sems = refs[2 * chunks :]
    mine = places.mine()
    places.barrier(mine)
    depth = len(places.dims)
    started = {}
    own = []
    for m in range(chunks):
        copy = pltpu.make_async_copy(ins[m], outs[m].at[tuple(mine)], own_sems.at[m])
        copy.start()
        own.append(copy)

    def start(m, stage):
        order = places.order(m % 2 == 1)
        digit = order[stage]
        done = order[:stage]
        where = tuple(slice(None) if d in done else mine[d] for d in range(depth))
        source = ins[m] if stage == 0 else outs[m].at[where]
        copies = []
        for shift in range(1, places.dims[digit]):
            target, _ = places.other(mine, digit, shift)
            copy = pltpu.make_async_remote_copy(
                src_ref=source,
                dst_ref=outs[m].at[where],
                send_sem=send_sems.at[m, stage, shift - 1],
                recv_sem=recv_sems.at[m, stage, shift - 1],
                device_id=target,
                device_id_type=MESH,
            )
            copy.start()
            copies.append(copy)
        started[m, stage] = copies

    pairs = (chunks + 1) // 2
    for tick in range(pairs + depth):
        for stage in range(depth, -1, -1):
            if not 0 <= tick - stage < pairs:
                continue
            for m in range(2 * (tick - stage), min(2 * (tick - stage) + 2, chunks)):
                if stage == 1:
                    own[m].wait()
                if stage > 0:
                    for copy in started[m, stage - 1]:
                        copy.wait_recv()
                if stage < depth:
                    start(m, stage)
    for copies in started.values():
        for copy in copies:
            copy.wait_send()


def gather_all(places, parts):
    chunks = len(parts)
    depth, widest = len(places.dims), max(places.dims)
    outs = pl.pallas_call(
        functools.partial(gather_kernel, places, chunks),
        out_shape=[jax.ShapeDtypeStruct(places.dims + p.shape, p.dtype) for p in parts],
        in_specs=[pl.BlockSpec(memory_space=pl.ANY)] * chunks,
        out_specs=[pl.BlockSpec(memory_space=pl.ANY)] * chunks,
        scratch_shapes=[
            pltpu.SemaphoreType.DMA((chunks, depth, widest - 1)),
            pltpu.SemaphoreType.DMA((chunks, depth, widest - 1)),
            pltpu.SemaphoreType.DMA((chunks,)),
        ],
        compiler_params=pltpu.CompilerParams(collective_id=1, has_side_effects=True),
        name="gather_weights",
    )(*parts)
    return [o.reshape((places.count,) + o.shape[-2:]) for o in outs]


def reduce_kernel(places, chunks, *refs):
    ins, outs = refs[:chunks], refs[chunks : 2 * chunks]
    refs = refs[2 * chunks :]
    depth = len(places.dims)
    accs = refs[:chunks]
    lands = refs[chunks : chunks * (1 + depth)]
    send_sems, recv_sems, own_sems = refs[chunks * (1 + depth) :]
    mine = places.mine()
    places.barrier(mine)
    started = {}
    own = []

    def route(m):
        return places.order(m % 2 == 1)[::-1]

    for m in range(chunks):
        where = tuple(slice(None) if d < depth - 1 else mine[d] for d in range(depth))
        copy = pltpu.make_async_copy(ins[m].at[where], accs[m], own_sems.at[m])
        copy.start()
        own.append(copy)

    def start(m, stage):
        order = route(m)
        digit = order[stage]
        gone = order[:stage]
        copies = []
        for shift in range(1, places.dims[digit]):
            target, value = places.other(mine, digit, shift)
            where = tuple(
                mine[d] if d in gone else (value if d == digit else slice(None)) for d in range(depth)
            )
            source = ins[m].at[where] if stage == 0 else accs[m].at[where[: depth - 1]]
            copy = pltpu.make_async_remote_copy(
                src_ref=source,
                dst_ref=lands[m * depth + stage].at[shift - 1],
                send_sem=send_sems.at[m, stage, shift - 1],
                recv_sem=recv_sems.at[m, stage, shift - 1],
                device_id=target,
                device_id_type=MESH,
            )
            copy.start()
            copies.append(copy)
        started[m, stage] = copies

    def add(m, stage):
        order = route(m)
        gone = order[: stage + 1]
        left = [d for d in range(depth) if d not in gone]
        land = lands[m * depth + stage]
        count = math.prod(places.dims[d] for d in left)

        def one(flat, carry):
            values = {}
            rest = flat
            for d in reversed(left):
                values[d] = lax.rem(rest, places.dims[d])
                rest = rest // places.dims[d]
            here = tuple(values.get(d, mine[d]) for d in range(depth - 1))
            total = accs[m][here].astype(jnp.float32)
            for shift in range(1, places.dims[order[stage]]):
                total = total + land[(shift - 1, *(values[d] for d in left))].astype(jnp.float32)
            if left:
                accs[m][here] = total.astype(BF)
            else:
                outs[m][...] = total
            return carry

        lax.fori_loop(0, count, one, 0)

    pairs = (chunks + 1) // 2
    for tick in range(pairs + depth):
        for stage in range(depth, -1, -1):
            if not 0 <= tick - stage < pairs:
                continue
            for m in range(2 * (tick - stage), min(2 * (tick - stage) + 2, chunks)):
                if stage == 1:
                    own[m].wait()
                if stage > 0:
                    for copy in started[m, stage - 1]:
                        copy.wait_recv()
                    add(m, stage - 1)
                if stage < depth:
                    start(m, stage)
    for copies in started.values():
        for copy in copies:
            copy.wait_send()


def reduce_all(places, parts):
    chunks = len(parts)
    dims = places.dims
    depth, widest = len(dims), max(dims)
    blocks = [p.shape[1:] for p in parts]
    lands = []
    for m in range(chunks):
        order = places.order(m % 2 == 1)[::-1]
        for stage in range(depth):
            gone = order[: stage + 1]
            left = tuple(dims[d] for d in range(depth) if d not in gone)
            lands.append(pltpu.VMEM((dims[order[stage]] - 1, *left, *blocks[m]), BF))
    return pl.pallas_call(
        functools.partial(reduce_kernel, places, chunks),
        out_shape=[jax.ShapeDtypeStruct(block, jnp.float32) for block in blocks],
        in_specs=[pl.BlockSpec(memory_space=pl.ANY)] * chunks,
        out_specs=[pl.BlockSpec(memory_space=pltpu.VMEM)] * chunks,
        scratch_shapes=[pltpu.VMEM(dims[:-1] + block, BF) for block in blocks]
        + lands
        + [
            pltpu.SemaphoreType.DMA((chunks, depth, widest - 1)),
            pltpu.SemaphoreType.DMA((chunks, depth, widest - 1)),
            pltpu.SemaphoreType.DMA((chunks,)),
        ],
        compiler_params=pltpu.CompilerParams(collective_id=2, has_side_effects=True, vmem_limit_bytes=LIMIT),
        name="reduce_gradients",
    )(*[p.reshape(dims + p.shape[1:]) for p in parts])


def exact_dot(former, latter):
    return jnp.dot(former.astype(jnp.float32), latter.astype(jnp.float32), precision=highest)


def exact_cross(former, latter):
    return lax.dot_general(
        former.astype(jnp.float32), latter, (((0,), (0,)), ((), ())), precision=highest
    )


def exact_times_t(former, latter):
    return lax.dot_general(
        former, latter.astype(jnp.float32), (((1,), (1,)), ((), ())), precision=highest
    )


def position_table(grid_side, columns):
    quarter = columns // 4
    omegas = jnp.exp(-math.log(10000.0) * jnp.arange(quarter, dtype=jnp.float32) / quarter)
    positions = jnp.arange(grid_side * grid_side, dtype=jnp.int32)
    row_pos = (positions // grid_side).astype(jnp.float32)[:, None] * omegas
    col_pos = (positions % grid_side).astype(jnp.float32)[:, None] * omegas
    return jnp.concatenate(
        [jnp.sin(row_pos), jnp.cos(row_pos), jnp.sin(col_pos), jnp.cos(col_pos)], axis=-1
    )


def time_table(step_ids, columns):
    half_cols = columns // 2
    frequency = jnp.exp(-math.log(10000.0) * jnp.arange(half_cols, dtype=jnp.float32) / half_cols)
    angles = step_ids.astype(jnp.float32)[:, None] * frequency
    return jnp.concatenate([jnp.cos(angles), jnp.sin(angles)], axis=-1)


def noise_scales(step_ids):
    phases = (step_ids.astype(jnp.float32) / NOISE_STEPS + 0.008) / 1.008 * (math.pi / 2)
    return (jnp.cos(phases), jnp.sin(phases))


def adam_update(weight, first, second, grad, factor):
    clipped = grad * factor
    first_new = 0.5 * first + 0.5 * clipped
    second_new = 0.5 * second + 0.5 * clipped * clipped
    correct = 1.0 - 0.5**STEP
    new_weight = weight - 0.02 * (
        first_new / correct / (jnp.sqrt(second_new / correct) + 1e-08) + 0.01 * weight
    )
    return (new_weight, first_new, second_new)


def swap(array):
    return jnp.swapaxes(array, -1, -2)


def pad_rows(part):
    extra = -part.shape[-2] % 16
    if extra == 0:
        return part
    return jnp.pad(part, [(0, 0)] * (part.ndim - 2) + [(0, extra), (0, 0)])


def pad_cols(part, cols):
    return jnp.pad(part, [(0, 0)] * (part.ndim - 1) + [(0, cols - part.shape[-1])])


SMALL = 8


def small_chunks(entry_t, table_t, final):
    table_t = jnp.concatenate([pad_cols(table_t, 1024), final[:, 2 * D :]], axis=1)
    table_t = pad_cols(table_t, 3 * D)
    return [
        pad_cols(entry_t[:, : PATCH_IN + FREQ], D),
        entry_t[:, PATCH_IN + FREQ :],
        table_t[:, :D],
        table_t[:, D : 2 * D],
        table_t[:, 2 * D :],
        final[:, :D],
        final[:, D : 2 * D],
        jnp.zeros_like(final[:, :D]),
    ]


def from_chunks(chunks):
    table = jnp.concatenate(chunks[2:5], axis=1)
    entry_t = jnp.concatenate([chunks[0][:, : PATCH_IN + FREQ], chunks[1]], axis=1)
    final = jnp.concatenate([chunks[5], chunks[6], table[:, 1024 : 1024 + OUT]], axis=1)
    return entry_t, table[:, : CLASSES + 1], final


def body(
    clean_latents,
    noise_field,
    timesteps,
    labels,
    drop_flags,
    entry_weight,
    class_table,
    attn_weight,
    ffn_in_weight,
    ffn_out_weight,
    ada_weight,
    final_weight,
    entry_first,
    entry_second,
    class_first,
    class_second,
    attn_first,
    attn_second,
    ffn_in_first,
    ffn_in_second,
    ffn_out_first,
    ffn_out_second,
    ada_first,
    ada_second,
    final_first,
    final_second,
):
    lat_count = clean_latents.shape[0]
    tokens = clean_latents.shape[1]
    layers = attn_weight.shape[0]
    both = ("dp", "tp")
    devices = lax.axis_size("dp") * lax.axis_size("tp")
    count_all = float(lat_count * devices * tokens * OUT)
    count_rms = float(lat_count * devices * tokens * D)
    nb = 1
    clean_t, noise_t = swap(clean_latents), swap(noise_field)
    cos_part, sin_part = noise_scales(timesteps)
    noisy = (cos_part[:, None, None] * clean_t + sin_part[:, None, None] * noise_t).astype(BF)
    n_dp, n_tp = lax.axis_size("dp"), lax.axis_size("tp")
    places = Places(n_dp, n_tp)
    slots = -(-SMALL // n_tp)
    dp_rows = final_weight.shape[0]
    wide_rows = attn_weight.shape[2]
    ada_rows = ada_weight.shape[2]
    mine_tp = lax.axis_index("tp")
    small = small_chunks(*(swap(w).astype(BF) for w in (entry_weight, class_table)), final_weight.astype(BF))
    small = jnp.stack(small)
    parts = [
        pad_rows(lax.dynamic_index_in_dim(small, slots * mine_tp + s, 0, keepdims=False)) for s in range(slots)
    ]
    parts.append(pad_rows(swap(ada_weight).astype(BF).reshape(layers * ada_rows, D)))
    for l in range(layers):
        parts.append(pad_rows(swap(attn_weight[l]).astype(BF)))
        parts.append(pad_rows(swap(ffn_in_weight[l]).astype(BF)))
        parts.append(pad_rows(ffn_out_weight[l].astype(BF)))
    gathered = gather_all(places, parts)

    def whole_rows(block, rows):
        return block[:, :rows].reshape(-1, D)

    slot_full = [g[:, :dp_rows].reshape(n_dp, n_tp, dp_rows, D) for g in gathered[:slots]]
    entry_t, table_t, final_full = from_chunks(
        [slot_full[k % slots][:, k // slots].reshape(n_dp * dp_rows, D) for k in range(SMALL)]
    )
    ada_full = gathered[slots][:, : layers * ada_rows].reshape(-1, layers, ada_rows, D)
    ada_full = [ada_full[:, l].reshape(-1, D) for l in range(layers)]
    block_full = [whole_rows(g, wide_rows) for g in gathered[slots + 1 :]]
    weights = [tuple(block_full[3 * l : 3 * l + 3]) for l in range(layers)]

    time_feat = time_table(timesteps, FREQ).astype(BF)
    time_pre = dot_nt(time_feat, entry_t[:, PATCH_IN : PATCH_IN + FREQ])
    time_act = jax.nn.silu(time_pre).astype(BF)
    classes_used = jnp.where(drop_flags == 1, CLASSES, labels)
    class_hot = (classes_used[:, None] == jnp.arange(CLASSES + 1, dtype=jnp.int32)[None, :]).astype(BF)
    cond = dot_nt(time_act, entry_t[:, PATCH_IN + FREQ :]) + dot_nt(class_hot, table_t)
    cond_bf = jax.nn.silu(cond).astype(BF)

    def pad8(flat):
        parts = flat.reshape(lat_count, -1, D)
        return jnp.pad(parts, ((0, 0), (0, 8 - parts.shape[1]), (0, 0)))

    mods = [pad8(dot_nt(cond_bf, ada_full[l])) for l in range(layers)]
    fmod = pad8(dot_nn(cond_bf, final_full[:, : 2 * D]))
    head = final_full[:, 2 * D :]
    pos = position_table(GRID, D)
    saved = []
    squares = []
    stream = None
    for l in range(layers):
        if l == 0:
            outs = forward_layer(True, (noisy, entry_t[:, :PATCH_IN].T, pos), mods[l], weights[l], nb, tokens)
            stream, outs = outs[0], outs[1:]
        else:
            outs = forward_layer(False, (stream,), mods[l], weights[l], nb, tokens)
        saved.append((stream, *outs[1:9]))
        stream = outs[0]
        squares.append(jnp.sum(outs[9]))
    layer_grads = [None] * layers
    d_mods = [None] * layers
    d_stream = None
    for l in reversed(range(layers)):
        last, first = l == layers - 1, l == 0
        entry_args = (stream, fmod, head, clean_t, noise_t) if last else (d_stream,)
        if first:
            entry_args = (*entry_args, noisy)
        outs = list(backward_layer(first, last, entry_args, mods[l], weights[l], saved[l], nb, tokens, count_all))
        if last:
            loss_part, d_head_t, d_fmod = outs[:3]
            loss_part = jnp.sum(loss_part)
            outs = outs[3:]
        if first:
            d_patch = outs[0]
        else:
            d_stream = outs[0]
        layer_grads[l] = outs[1:4]
        d_mods[l] = outs[4][:, :6].reshape(lat_count, 6 * D)
    d_fmod = d_fmod[:, :2].reshape(lat_count, 2 * D)
    d_cond = exact_times_t(d_fmod, final_full[:, : 2 * D])
    for l in range(layers):
        d_cond = d_cond + exact_dot(d_mods[l], ada_full[l])
    d_ada = jnp.stack([exact_cross(d_mods[l], cond_bf.astype(jnp.float32)) for l in range(layers)])
    d_final_ada = exact_cross(cond_bf, d_fmod)
    _, silu_back = jax.vjp(jax.nn.silu, cond)
    (d_cond_pre,) = silu_back(d_cond)
    d_time_out = exact_cross(d_cond_pre, time_act.astype(jnp.float32))
    d_time_act = exact_dot(d_cond_pre, entry_t[:, PATCH_IN + FREQ :])
    _, time_back = jax.vjp(jax.nn.silu, time_pre)
    (d_time_pre,) = time_back(d_time_act)
    d_time_in = exact_cross(d_time_pre, time_feat.astype(jnp.float32))
    d_entry = jnp.concatenate([d_patch.T, d_time_in, d_time_out], axis=1)
    d_table = exact_cross(d_cond_pre, class_hot.astype(jnp.float32))
    d_final = jnp.concatenate([d_final_ada, d_head_t.T], axis=1)
    d_small = jnp.stack(small_chunks(d_entry, d_table, d_final)).astype(BF)
    d_small = d_small.reshape(n_tp, slots, n_dp, dp_rows, D).transpose(1, 2, 0, 3, 4)
    grads = [pad_rows(d_small[s].reshape(places.count, dp_rows, D)) for s in range(slots)]
    d_ada = d_ada.reshape(layers, places.count, ada_rows, D).swapaxes(0, 1).astype(BF)
    grads.append(pad_rows(d_ada.reshape(places.count, layers * ada_rows, D)))
    for l in range(layers):
        for k in range(3):
            grads.append(pad_rows(layer_grads[l][k].reshape(places.count, wide_rows, D)))
    summed = reduce_all(places, grads)
    small_grad = lax.all_gather(
        jnp.stack([g[:dp_rows] for g in summed[:slots]]), "tp", axis=0, tiled=True
    )
    entry_grad, table_grad, final_grad = from_chunks([small_grad[k] for k in range(SMALL)])
    entry_grad, table_grad = swap(entry_grad), swap(table_grad)
    ada_grad = summed[slots][: layers * ada_rows].reshape(layers, ada_rows, D)
    attn_grad, in_grad, out_grad = (
        jnp.stack([summed[slots + 1 + 3 * l + k][:wide_rows] for l in range(layers)]) for k in range(3)
    )
    layer_square = sum(jnp.sum(grad * grad) for grad in (attn_grad, ada_grad, in_grad, out_grad))
    small_square = sum(
        jnp.sum(grad * grad) for grad in (entry_grad, table_grad, final_grad)
    ) / lax.axis_size("tp")
    loss_total, square_totals, grad_square = lax.psum(
        (loss_part, jnp.stack(squares), layer_square + small_square), both
    )
    grad_norm = jnp.sqrt(grad_square)
    factor = jnp.minimum(1.0, 0.01 / (grad_norm + 1e-06))
    results = []
    for weight, first, second, grad in (
        (entry_weight, entry_first, entry_second, entry_grad),
        (class_table, class_first, class_second, table_grad),
        (attn_weight, attn_first, attn_second, swap(attn_grad)),
        (ffn_in_weight, ffn_in_first, ffn_in_second, swap(in_grad)),
        (ffn_out_weight, ffn_out_first, ffn_out_second, out_grad),
        (ada_weight, ada_first, ada_second, swap(ada_grad)),
        (final_weight, final_first, final_second, final_grad),
    ):
        results.extend(adam_update(weight, first, second, grad, factor))
    residual_rms = jnp.sqrt(square_totals / count_rms)
    return (*results, loss_total, grad_norm, residual_rms)


def solution(mesh):
    lead = P(("dp", "tp"), None, None)
    ids = P(("dp", "tp"))
    wide = P(None, "dp")
    cols = P(None, None, ("dp", "tp"))
    rows = P(None, ("dp", "tp"), None)
    top = P("dp", None)
    return jax.shard_map(
        body,
        mesh=mesh,
        in_specs=(
            lead,
            lead,
            ids,
            ids,
            ids,
            wide,
            wide,
            cols,
            cols,
            rows,
            cols,
            top,
            wide,
            wide,
            wide,
            wide,
            cols,
            cols,
            cols,
            cols,
            rows,
            rows,
            cols,
            cols,
            top,
            top,
        ),
        out_specs=(wide,) * 6 + (cols,) * 6 + (rows,) * 3 + (cols,) * 3 + (top,) * 3 + (P(), P(), P()),
        check_vma=False,
    )
```

```python
import functools
import math

import jax
import jax.numpy as jnp
from jax import lax
from jax.experimental import pallas as pl
from jax.experimental.pallas import tpu as pltpu
from jax.sharding import PartitionSpec as P

D = 384
HEADS = 6
HEAD_DIM = 64
CLASSES = 1000
GRID = 16
PATCH_IN = 16
OUT = 32
FREQ = 256
NOISE_STEPS = 1000
STEP = 10
BF = jnp.bfloat16


highest = lax.Precision.HIGHEST


def dot_nn(a, b):
    return lax.dot_general(a, b, (((1,), (0,)), ((), ())), preferred_element_type=jnp.float32)


def dot_nt(a, b):
    return lax.dot_general(a, b, (((1,), (1,)), ((), ())), preferred_element_type=jnp.float32)


def dot_tn(a, b):
    return lax.dot_general(a, b, (((0,), (0,)), ((), ())), preferred_element_type=jnp.float32)


def norm_rows(rows):
    center = rows - jnp.mean(rows, axis=-1, keepdims=True)
    rstd = lax.rsqrt(jnp.mean(center * center, axis=-1, keepdims=True) + 1e-06)
    return center * rstd, rstd


def norm_back(d_out, hat, rstd, scale):
    d_shift = jnp.sum(d_out, axis=1, keepdims=True)
    d_scale = jnp.sum(d_out * hat, axis=1, keepdims=True)
    d_hat = d_out * (1.0 + scale)
    m_one = jnp.mean(d_hat, axis=-1, keepdims=True)
    m_two = jnp.mean(d_hat * hat, axis=-1, keepdims=True)
    return rstd * (d_hat - m_one - hat * m_two), d_shift, d_scale


def half_masks():
    lane = lax.broadcasted_iota(jnp.int32, (1, 2 * HEAD_DIM), 1)
    low = jnp.where(lane < HEAD_DIM, 1.0, 0.0)
    return low.astype(BF), (1.0 - low).astype(BF)


def stack_heads(pair, masks):
    return jnp.concatenate([pair * masks[0], pair * masks[1]], axis=0)


GELU_A = math.sqrt(2.0 / math.pi)
GELU_B = 0.044715


def forward_kernel(first, nb, tokens, *refs):
    if first:
        noisy_ref, patch_ref, pos_ref = refs[:3]
        refs = refs[3:]
    else:
        stream_ref = refs[0]
        refs = refs[1:]
    mod_ref, attn_ref, in_ref, out_ref = refs[:4]
    refs = refs[4:]
    if first:
        start_ref = refs[0]
        refs = refs[1:]
    (
        result_ref,
        qkv_ref,
        probs_ref,
        mixed_ref,
        branch_ref,
        middle_ref,
        mlp_ref,
        act_ref,
        slope_ref,
        square_ref,
    ) = refs
    rows = nb * tokens
    if first:
        parts = [
            lax.dot_general(
                noisy_ref[n], patch_ref[...], (((0,), (1,)), ((), ())), preferred_element_type=jnp.float32
            )
            + pos_ref[...]
            for n in range(nb)
        ]
        stream = parts[0] if nb == 1 else jnp.concatenate(parts, axis=0)
        start_ref[...] = stream
    else:
        stream = stream_ref[...]
    mod = mod_ref[...]
    stream = stream.reshape(nb, tokens, D)
    hat, _ = norm_rows(stream)
    attn_in = (hat * (1.0 + mod[:, 1:2]) + mod[:, 0:1]).astype(BF).reshape(rows, D)
    qkv_ref[...] = dot_nt(attn_in, attn_ref[: 3 * D, :]).astype(BF)
    masks = half_masks()
    for n in range(nb):
        here = slice(n * tokens, (n + 1) * tokens)
        for pair in range(HEADS // 2):
            col = pair * 2 * HEAD_DIM
            queries = qkv_ref[here, col : col + 2 * HEAD_DIM] * jnp.asarray(HEAD_DIM**-0.5, BF)
            keys = stack_heads(qkv_ref[here, D + col : D + col + 2 * HEAD_DIM], masks)
            values = stack_heads(qkv_ref[here, 2 * D + col : 2 * D + col + 2 * HEAD_DIM], masks)
            scores = dot_nt(queries, keys)
            halves = []
            for side in range(2):
                part = scores[:, side * tokens : (side + 1) * tokens]
                grown = jnp.exp(part - jnp.max(part, axis=-1, keepdims=True))
                halves.append((grown * (1.0 / jnp.sum(grown, axis=-1, keepdims=True))).astype(BF))
            probs = jnp.concatenate(halves, axis=1)
            probs_ref[here, pair * 2 * tokens : (pair + 1) * 2 * tokens] = probs
            mixed_ref[here, col : col + 2 * HEAD_DIM] = dot_nn(probs, values).astype(BF)
    branch = dot_nt(mixed_ref[...], attn_ref[3 * D :, :])
    branch_ref[...] = branch.astype(BF)
    middle = stream + mod[:, 2:3] * branch.reshape(nb, tokens, D)
    middle_ref[...] = middle.reshape(rows, D)
    hat, _ = norm_rows(middle)
    mlp_in = (hat * (1.0 + mod[:, 4:5]) + mod[:, 3:4]).astype(BF).reshape(rows, D)
    hidden = dot_nt(mlp_in, in_ref[...])
    squared = hidden * hidden
    bent = jnp.tanh(hidden * (GELU_A + (GELU_A * GELU_B) * squared))
    half = 0.5 * hidden
    act = (half + half * bent).astype(BF)
    act_ref[...] = act
    slope_ref[...] = (
        0.5
        + 0.5 * bent
        + half * (1.0 - bent * bent) * (GELU_A + (3.0 * GELU_A * GELU_B) * squared)
    ).astype(BF)
    mlp = dot_nn(act, out_ref[...])
    mlp_ref[...] = mlp.astype(BF)
    result = middle + mod[:, 5:6] * mlp.reshape(nb, tokens, D)
    result_ref[...] = result.reshape(rows, D)
    square_ref[0] = jnp.sum((result * result).reshape(rows // 8, 8, D), axis=0)


def backward_kernel(first, last, nb, tokens, steps, count_all, *refs):
    if last:
        final_ref, fmod_ref, head_ref, clean_ref, noise_ref = refs[:5]
        refs = refs[5:]
    else:
        d_stream_ref = refs[0]
        refs = refs[1:]
    if first:
        noisy_ref = refs[0]
        refs = refs[1:]
    (
        mod_ref,
        attn_ref,
        in_ref,
        out_ref,
        stream_ref,
        qkv_ref,
        probs_ref,
        mixed_ref,
        branch_ref,
        middle_ref,
        mlp_ref,
        act_ref,
        slope_ref,
    ) = refs[:13]
    refs = refs[13:]
    if last:
        loss_ref, dhead_ref, dfmod_ref = refs[:3]
        refs = refs[3:]
    if first:
        dpatch_ref = refs[0]
    else:
        d_prev_ref = refs[0]
    gattn_ref, gin_ref, gout_ref, dmod_ref, acc_attn, acc_in, acc_out, d_qkv_s = refs[1:]
    rows = nb * tokens
    step = pl.program_id(0)

    @pl.when(step == 0)
    def _():
        acc_attn[...] = jnp.zeros_like(acc_attn)
        acc_in[...] = jnp.zeros_like(acc_in)
        acc_out[...] = jnp.zeros_like(acc_out)
        if last:
            dhead_ref[...] = jnp.zeros_like(dhead_ref)
        if first:
            dpatch_ref[...] = jnp.zeros_like(dpatch_ref)

    mod = mod_ref[...]
    if last:
        fmod = fmod_ref[...]
        hat, rstd = norm_rows(final_ref[...].reshape(nb, tokens, D))
        final_in = (hat * (1.0 + fmod[:, 1:2]) + fmod[:, 0:1]).astype(BF)
        d_parts = []
        loss = jnp.zeros((8, tokens), jnp.float32)
        for n in range(nb):
            predicted = lax.dot_general(
                head_ref[...], final_in[n], (((0,), (1,)), ((), ())), preferred_element_type=jnp.float32
            )
            errors = predicted - jnp.concatenate([noise_ref[n], clean_ref[n]], axis=0)
            loss = loss + jnp.sum((errors * errors).reshape(OUT // 8, 8, tokens), axis=0)
            d_pred = (errors * (2.0 / count_all)).astype(BF)
            dhead_ref[...] += dot_nn(d_pred, final_in[n])
            d_parts.append(
                lax.dot_general(
                    d_pred, head_ref[...], (((0,), (1,)), ((), ())), preferred_element_type=jnp.float32
                )
            )
        loss_ref[0] = loss
        d_final = jnp.stack(d_parts, axis=0)
        d_stream, d_shift, d_scale = norm_back(d_final, hat, rstd, fmod[:, 1:2])
        dfmod_ref[:, 0:1] = d_shift
        dfmod_ref[:, 1:2] = d_scale
    else:
        d_stream = d_stream_ref[...].reshape(nb, tokens, D)
    dmod_ref[:, 5:6] = jnp.sum(d_stream * mlp_ref[...].astype(jnp.float32).reshape(nb, tokens, D), axis=1, keepdims=True)
    d_mlp = (d_stream * mod[:, 5:6]).astype(BF).reshape(rows, D)
    d_hidden = (dot_nt(d_mlp, out_ref[...]) * slope_ref[...].astype(jnp.float32)).astype(BF)
    acc_out[...] += dot_tn(act_ref[...], d_mlp)
    hat, rstd = norm_rows(middle_ref[...].reshape(nb, tokens, D))
    mlp_in = (hat * (1.0 + mod[:, 4:5]) + mod[:, 3:4]).astype(BF).reshape(rows, D)
    acc_in[...] += dot_tn(d_hidden, mlp_in)
    d_input = dot_nn(d_hidden, in_ref[...]).reshape(nb, tokens, D)
    d_middle, d_shift, d_scale = norm_back(d_input, hat, rstd, mod[:, 4:5])
    dmod_ref[:, 3:4] = d_shift
    dmod_ref[:, 4:5] = d_scale
    d_middle = d_middle + d_stream
    dmod_ref[:, 2:3] = jnp.sum(
        d_middle * branch_ref[...].astype(jnp.float32).reshape(nb, tokens, D), axis=1, keepdims=True
    )
    d_proj = (d_middle * mod[:, 2:3]).astype(BF).reshape(rows, D)
    acc_attn[3 * D :, :] += dot_tn(d_proj, mixed_ref[...])
    d_mix = dot_nn(d_proj, attn_ref[3 * D :, :]).astype(BF)
    masks = half_masks()
    lane = lax.broadcasted_iota(jnp.int32, (tokens, 2 * HEAD_DIM), 1)
    low_side = lane < HEAD_DIM
    root = HEAD_DIM**-0.5
    for n in range(nb):
        here = slice(n * tokens, (n + 1) * tokens)
        for pair in range(HEADS // 2):
            col = pair * 2 * HEAD_DIM
            queries = qkv_ref[here, col : col + 2 * HEAD_DIM]
            keys = stack_heads(qkv_ref[here, D + col : D + col + 2 * HEAD_DIM], masks)
            values = stack_heads(qkv_ref[here, 2 * D + col : 2 * D + col + 2 * HEAD_DIM], masks)
            d_out = d_mix[here, col : col + 2 * HEAD_DIM]
            probs_bf = probs_ref[here, pair * 2 * tokens : (pair + 1) * 2 * tokens]
            d_probs = dot_nt(d_out, values)
            halves = []
            for side in range(2):
                cut = slice(side * tokens, (side + 1) * tokens)
                probs = probs_bf[:, cut].astype(jnp.float32)
                part = d_probs[:, cut]
                halves.append((probs * (part - jnp.sum(probs * part, axis=-1, keepdims=True))).astype(BF))
            d_scores = jnp.concatenate(halves, axis=1)
            d_queries = dot_nn(d_scores, keys) * root
            d_keys = dot_tn(d_scores, queries)
            d_keys = jnp.where(low_side, d_keys[:tokens], d_keys[tokens:]) * root
            d_values = dot_tn(probs_bf, d_out)
            d_values = jnp.where(low_side, d_values[:tokens], d_values[tokens:])
            d_qkv_s[here, col : col + 2 * HEAD_DIM] = d_queries.astype(BF)
            d_qkv_s[here, D + col : D + col + 2 * HEAD_DIM] = d_keys.astype(BF)
            d_qkv_s[here, 2 * D + col : 2 * D + col + 2 * HEAD_DIM] = d_values.astype(BF)
    d_qkv = d_qkv_s[...]
    hat, rstd = norm_rows(stream_ref[...].reshape(nb, tokens, D))
    attn_in = (hat * (1.0 + mod[:, 1:2]) + mod[:, 0:1]).astype(BF).reshape(rows, D)
    acc_attn[: 3 * D, :] += dot_tn(d_qkv, attn_in)
    d_attn_in = dot_nn(d_qkv, attn_ref[: 3 * D, :]).reshape(nb, tokens, D)
    d_before, d_shift, d_scale = norm_back(d_attn_in, hat, rstd, mod[:, 1:2])
    dmod_ref[:, 0:1] = d_shift
    dmod_ref[:, 1:2] = d_scale
    d_prev = d_middle + d_before
    if first:
        for n in range(nb):
            dpatch_ref[...] += lax.dot_general(
                noisy_ref[n].astype(jnp.float32), d_prev[n], (((1,), (0,)), ((), ())), precision=highest
            )
    else:
        d_prev_ref[...] = d_prev.reshape(rows, D)

    @pl.when(step == steps - 1)
    def _():
        gattn_ref[...] = acc_attn[...].astype(BF)
        gin_ref[...] = acc_in[...].astype(BF)
        gout_ref[...] = acc_out[...].astype(BF)


def whole_spec(array):
    return pl.BlockSpec(array.shape, lambda i: (0,) * array.ndim)


def lead_spec(block, ndim):
    return pl.BlockSpec(block, lambda i: (i,) + (0,) * (ndim - 1))


LIMIT = 56 * 1024 * 1024


def forward_layer(first, entry_args, mod, weights, nb, tokens):
    lat_count = mod.shape[0]
    rows = nb * tokens
    steps = lat_count // nb
    total = lat_count * tokens
    kinds = [(D, jnp.float32)] if first else []
    kinds += [
        (D, jnp.float32),
        (3 * D, BF),
        (HEADS * tokens, BF),
        (D, BF),
        (D, BF),
        (D, jnp.float32),
        (D, BF),
        (4 * D, BF),
        (4 * D, BF),
    ]
    out_shape = [jax.ShapeDtypeStruct((total, cols), kind) for cols, kind in kinds]
    out_specs = [lead_spec((rows, cols), 2) for cols, _ in kinds]
    out_shape.append(jax.ShapeDtypeStruct((steps, 8, D), jnp.float32))
    out_specs.append(lead_spec((1, 8, D), 3))
    if first:
        noisy, patch, pos = entry_args
        in_specs = [lead_spec((nb, PATCH_IN, tokens), 3), whole_spec(patch), whole_spec(pos)]
    else:
        in_specs = [lead_spec((rows, D), 2)]
    in_specs += [lead_spec((nb, 8, D), 3)] + [whole_spec(w) for w in weights]
    return pl.pallas_call(
        functools.partial(forward_kernel, first, nb, tokens),
        grid=(steps,),
        out_shape=out_shape,
        in_specs=in_specs,
        out_specs=out_specs,
        compiler_params=pltpu.CompilerParams(vmem_limit_bytes=LIMIT),
        name="block_forward",
    )(*entry_args, mod, *weights)


def backward_layer(first, last, entry_args, mod, weights, saved, nb, tokens, count_all):
    lat_count = mod.shape[0]
    rows = nb * tokens
    steps = lat_count // nb
    total = lat_count * tokens
    in_specs = []
    args = list(entry_args)
    if last:
        in_specs += [
            lead_spec((rows, D), 2),
            lead_spec((nb, 8, D), 3),
            whole_spec(args[2]),
            lead_spec((nb, PATCH_IN, tokens), 3),
            lead_spec((nb, PATCH_IN, tokens), 3),
        ]
    else:
        in_specs += [lead_spec((rows, D), 2)]
    if first:
        in_specs += [lead_spec((nb, PATCH_IN, tokens), 3)]
    in_specs += [lead_spec((nb, 8, D), 3)] + [whole_spec(w) for w in weights]
    in_specs += [lead_spec((rows, s.shape[1]), 2) for s in saved]
    out_shape = []
    out_specs = []

    def add(shape, kind, spec):
        out_shape.append(jax.ShapeDtypeStruct(shape, kind))
        out_specs.append(spec)

    def whole(shape):
        return pl.BlockSpec(shape, lambda i: (0,) * len(shape))

    if last:
        add((steps, 8, tokens), jnp.float32, lead_spec((1, 8, tokens), 3))
        add((OUT, D), jnp.float32, whole((OUT, D)))
        add((lat_count, 8, D), jnp.float32, lead_spec((nb, 8, D), 3))
    if first:
        add((PATCH_IN, D), jnp.float32, whole((PATCH_IN, D)))
    else:
        add((total, D), jnp.float32, lead_spec((rows, D), 2))
    for _ in range(3):
        add((4 * D, D), BF, whole((4 * D, D)))
    add((lat_count, 8, D), jnp.float32, lead_spec((nb, 8, D), 3))
    return pl.pallas_call(
        functools.partial(backward_kernel, first, last, nb, tokens, steps, count_all),
        grid=(steps,),
        out_shape=out_shape,
        in_specs=in_specs,
        out_specs=out_specs,
        scratch_shapes=[pltpu.VMEM((4 * D, D), jnp.float32)] * 3 + [pltpu.VMEM((rows, 3 * D), BF)],
        compiler_params=pltpu.CompilerParams(vmem_limit_bytes=LIMIT),
        name="block_backward",
    )(*args, mod, *weights, *saved)


MESH = pl.DeviceIdType.MESH


class Places:
    def __init__(self, n_dp, n_tp):
        self.digits = []
        for axis, count, top in (("dp", n_dp, 4), ("tp", n_tp, 2)):
            sizes = []
            rest = count
            while rest > 1:
                size = next((s for s in (top, 2, 3, 5, 7) if rest % s == 0), rest)
                sizes.append(size)
                rest //= size
            stride = count
            for size in sizes:
                stride //= size
                self.digits.append((axis, stride, size))
        self.dims = tuple(size for _, _, size in self.digits)
        self.count = n_dp * n_tp

    def order(self, odd):
        names = list(range(len(self.digits)))
        if odd and len(names) >= 4:
            names[-3], names[-2] = names[-2], names[-3]
        return names

    def mine(self):
        return [lax.rem(lax.axis_index(axis) // stride, size) for axis, stride, size in self.digits]

    def other(self, mine, digit, shift):
        axis, stride, size = self.digits[digit]
        value = lax.rem(mine[digit] + shift, size)
        return {axis: lax.axis_index(axis) + (value - mine[digit]) * stride}, value

    def barrier(self, mine):
        barrier = pltpu.get_barrier_semaphore()
        count = 0
        for digit, size in enumerate(self.dims):
            for shift in range(1, size):
                target, _ = self.other(mine, digit, shift)
                pl.semaphore_signal(barrier, inc=1, device_id=target, device_id_type=MESH)
                count += 1
        pl.semaphore_wait(barrier, count)


SMALL = 8
SPLIT = 3


def small_blocks(entry_t, table_t, final):
    early = PATCH_IN + FREQ
    return [
        (0, 0, entry_t, 0, early),
        (1, 0, entry_t, early, early + D),
        (2, 0, table_t, 0, D),
        (3, 0, table_t, D, 2 * D),
        (4, 0, table_t, 2 * D, CLASSES + 1),
        (4, 256, final, 2 * D, 2 * D + OUT),
        (5, 0, final, 0, D),
        (6, 0, final, D, 2 * D),
    ]


def gather_kernel(places, slots, layers, *refs):
    entry_ref, table_ref, final_ref, ada_ref, attn_ref, in_ref, out_ref = refs[:7]
    chunks = slots + SPLIT + 3 * layers
    outs = refs[7 : 7 + chunks]
    small, packed, send_sems, recv_sems, own_sems = refs[7 + chunks :]
    mine = places.mine()
    depth = len(places.dims)
    small[...] = jnp.zeros_like(small)
    for k, at, source, low, high in small_blocks(entry_ref, table_ref, final_ref):
        small[k, : source.shape[0], at : at + high - low] = source[:, low:high].astype(BF)
    part = -(-ada_ref.shape[0] // SPLIT)
    for p in range(SPLIT):
        packed[p, :part, :] = ada_ref[p * part : (p + 1) * part, :].astype(BF)
    for l in range(layers):
        for k, source in enumerate((attn_ref, in_ref, out_ref)):
            packed[SPLIT + 3 * l + k, : source.shape[1], :] = source[l].astype(BF)
    first = lax.axis_index("tp") * slots
    ins = [small.at[first + s] for s in range(slots)]
    ins += [packed.at[m] for m in range(SPLIT + 3 * layers)]
    places.barrier(mine)
    started = {}
    own = []
    for m in range(chunks):
        copy = pltpu.make_async_copy(ins[m], outs[m].at[tuple(mine)], own_sems.at[m])
        copy.start()
        own.append(copy)

    def start(m, stage):
        order = places.order(m % 2 == 1)
        digit = order[stage]
        done = order[:stage]
        where = tuple(slice(None) if d in done else mine[d] for d in range(depth))
        source = ins[m] if stage == 0 else outs[m].at[where]
        copies = []
        for shift in range(1, places.dims[digit]):
            target, _ = places.other(mine, digit, shift)
            copy = pltpu.make_async_remote_copy(
                src_ref=source,
                dst_ref=outs[m].at[where],
                send_sem=send_sems.at[m, stage, shift - 1],
                recv_sem=recv_sems.at[m, stage, shift - 1],
                device_id=target,
                device_id_type=MESH,
            )
            copy.start()
            copies.append(copy)
        started[m, stage] = copies

    pairs = (chunks + 1) // 2
    for tick in range(pairs + depth):
        for stage in range(depth, -1, -1):
            if not 0 <= tick - stage < pairs:
                continue
            for m in range(2 * (tick - stage), min(2 * (tick - stage) + 2, chunks)):
                if stage == 1:
                    own[m].wait()
                if stage > 0:
                    for copy in started[m, stage - 1]:
                        copy.wait_recv()
                if stage < depth:
                    start(m, stage)
    for copies in started.values():
        for copy in copies:
            copy.wait_send()


def pad16(rows):
    return rows + -rows % 16


def gather_all(places, slots, entry_t, table_t, final, ada_t, attn_t, in_t, out_w):
    layers = attn_t.shape[0]
    depth, widest = len(places.dims), max(places.dims)
    small_rows, ada_rows = pad16(final.shape[0]), pad16(-(-ada_t.shape[0] // SPLIT))
    wide_rows = pad16(attn_t.shape[1])
    sizes = [small_rows] * slots + [ada_rows] * SPLIT + [wide_rows] * (3 * layers)
    chunks = len(sizes)
    vmem = pl.BlockSpec(memory_space=pltpu.VMEM)
    packed_rows = max(ada_rows, wide_rows)
    assert packed_rows == min(ada_rows, wide_rows)
    outs = pl.pallas_call(
        functools.partial(gather_kernel, places, slots, layers),
        out_shape=[jax.ShapeDtypeStruct((*places.dims, rows, D), BF) for rows in sizes],
        in_specs=[vmem] * 7,
        out_specs=[pl.BlockSpec(memory_space=pl.ANY)] * chunks,
        scratch_shapes=[
            pltpu.VMEM((slots * lax.axis_size("tp"), small_rows, D), BF),
            pltpu.VMEM((SPLIT + 3 * layers, packed_rows, D), BF),
            pltpu.SemaphoreType.DMA((chunks, depth, widest - 1)),
            pltpu.SemaphoreType.DMA((chunks, depth, widest - 1)),
            pltpu.SemaphoreType.DMA((chunks,)),
        ],
        compiler_params=pltpu.CompilerParams(collective_id=1, has_side_effects=True, vmem_limit_bytes=LIMIT),
        name="gather_weights",
    )(entry_t, table_t, final, ada_t, attn_t, in_t, out_w)
    return [o.reshape((places.count,) + o.shape[-2:]) for o in outs]


def reduce_kernel(places, chunks, slots, layers, *refs):
    ins = refs[:chunks]
    loss_ref = refs[chunks]
    square_refs = refs[chunks + 1 : chunks + 1 + layers]
    refs = refs[chunks + 1 + layers :]
    outs, both_ref, stats_ref = refs[:chunks], refs[chunks], refs[chunks + 1]
    refs = refs[chunks + 2 :]
    stats_land, stats_send, stats_recv, both_send, both_recv = refs[-5:]
    refs = refs[:-5]
    depth = len(places.dims)
    accs = refs[:chunks]
    lands = refs[chunks : chunks * (1 + depth)]
    send_sems, recv_sems, own_sems = refs[chunks * (1 + depth) :]
    mine = places.mine()
    places.barrier(mine)
    started = {}
    own = []

    def route(m):
        return places.order(m % 2 == 1)[::-1]

    for m in range(chunks):
        where = tuple(slice(None) if d < depth - 1 else mine[d] for d in range(depth))
        copy = pltpu.make_async_copy(ins[m].at[where], accs[m], own_sems.at[m])
        copy.start()
        own.append(copy)

    def start(m, stage):
        order = route(m)
        digit = order[stage]
        gone = order[:stage]
        copies = []
        for shift in range(1, places.dims[digit]):
            target, value = places.other(mine, digit, shift)
            where = tuple(
                mine[d] if d in gone else (value if d == digit else slice(None)) for d in range(depth)
            )
            source = ins[m].at[where] if stage == 0 else accs[m].at[where[: depth - 1]]
            copy = pltpu.make_async_remote_copy(
                src_ref=source,
                dst_ref=lands[m * depth + stage].at[shift - 1],
                send_sem=send_sems.at[m, stage, shift - 1],
                recv_sem=recv_sems.at[m, stage, shift - 1],
                device_id=target,
                device_id_type=MESH,
            )
            copy.start()
            copies.append(copy)
        started[m, stage] = copies

    def add(m, stage):
        order = route(m)
        gone = order[: stage + 1]
        left = [d for d in range(depth) if d not in gone]
        land = lands[m * depth + stage]
        count = math.prod(places.dims[d] for d in left)

        def one(flat, carry):
            values = {}
            rest = flat
            for d in reversed(left):
                values[d] = lax.rem(rest, places.dims[d])
                rest = rest // places.dims[d]
            here = tuple(values.get(d, mine[d]) for d in range(depth - 1))
            total = accs[m][here].astype(jnp.float32)
            for shift in range(1, places.dims[order[stage]]):
                total = total + land[(shift - 1, *(values[d] for d in left))].astype(jnp.float32)
            if left:
                accs[m][here] = total.astype(BF)
            else:
                outs[m][...] = total
            return carry

        lax.fori_loop(0, count, one, 0)

    pairs = (chunks + 1) // 2
    for tick in range(pairs + depth):
        for stage in range(depth, -1, -1):
            if not 0 <= tick - stage < pairs:
                continue
            for m in range(2 * (tick - stage), min(2 * (tick - stage) + 2, chunks)):
                if stage == 1:
                    own[m].wait()
                if stage > 0:
                    for copy in started[m, stage - 1]:
                        copy.wait_recv()
                    add(m, stage - 1)
                if stage < depth:
                    start(m, stage)
    for copies in started.values():
        for copy in copies:
            copy.wait_send()

    def lane_sums(rows):
        total = jnp.sum(rows, axis=0, keepdims=True)
        return sum(total[:, at : at + 128] for at in range(0, total.shape[1], 128))

    grad = sum(lane_sums(out[...] * out[...]) for out in outs)
    loss = lane_sums(jnp.sum(loss_ref[...], axis=0))
    squares = [lane_sums(jnp.sum(ref[...], axis=0)) for ref in square_refs]
    stats_ref[...] = jnp.concatenate([grad, loss, *squares, jnp.zeros((6 - layers, 128), jnp.float32)], axis=0)
    for s in range(slots):
        both_ref[(lax.axis_index("tp"), s)] = outs[s][...]
    inner = [d for d in range(depth) if places.digits[d][0] == "tp"]
    for stage, digit in enumerate(reversed(range(depth))):
        size = places.dims[digit]
        axis, stride, _ = places.digits[digit]
        stats_land[stage, mine[digit]] = stats_ref[...]
        copies = []
        for shift in range(1, size):
            target, _ = places.other(mine, digit, shift)
            copies.append(
                pltpu.make_async_remote_copy(
                    src_ref=stats_ref,
                    dst_ref=stats_land.at[stage, mine[digit]],
                    send_sem=stats_send.at[stage, shift - 1],
                    recv_sem=stats_recv.at[stage, shift - 1],
                    device_id=target,
                    device_id_type=MESH,
                )
            )
            if digit in inner:
                held = stride
                start = lax.axis_index("tp") // stride * stride
                where = both_ref.at[pl.ds(start, held)]
                copies.append(
                    pltpu.make_async_remote_copy(
                        src_ref=where,
                        dst_ref=where,
                        send_sem=both_send.at[stage, shift - 1],
                        recv_sem=both_recv.at[stage, shift - 1],
                        device_id=target,
                        device_id_type=MESH,
                    )
                )
        for copy in copies:
            copy.start()
        for copy in copies:
            copy.wait()
        total = stats_land[stage, 0]
        for value in range(1, size):
            total = total + stats_land[stage, value]
        stats_ref[...] = total


def reduce_all(places, slots, parts, loss, squares):
    layers = len(squares)
    vmem = pl.BlockSpec(memory_space=pltpu.VMEM)
    chunks = len(parts)
    dims = places.dims
    depth, widest = len(dims), max(dims)
    blocks = [p.shape[1:] for p in parts]
    lands = []
    for m in range(chunks):
        order = places.order(m % 2 == 1)[::-1]
        for stage in range(depth):
            gone = order[: stage + 1]
            left = tuple(dims[d] for d in range(depth) if d not in gone)
            lands.append(pltpu.VMEM((dims[order[stage]] - 1, *left, *blocks[m]), BF))
    return pl.pallas_call(
        functools.partial(reduce_kernel, places, chunks, slots, layers),
        out_shape=[jax.ShapeDtypeStruct(block, jnp.float32) for block in blocks]
        + [
            jax.ShapeDtypeStruct((lax.axis_size("tp"), slots, *blocks[0]), jnp.float32),
            jax.ShapeDtypeStruct((8, 128), jnp.float32),
        ],
        in_specs=[pl.BlockSpec(memory_space=pl.ANY)] * chunks + [vmem] * (1 + layers),
        out_specs=[vmem] * (chunks + 2),
        scratch_shapes=[pltpu.VMEM(dims[:-1] + block, BF) for block in blocks]
        + lands
        + [
            pltpu.SemaphoreType.DMA((chunks, depth, widest - 1)),
            pltpu.SemaphoreType.DMA((chunks, depth, widest - 1)),
            pltpu.SemaphoreType.DMA((chunks,)),
            pltpu.VMEM((depth, widest, 8, 128), jnp.float32),
            pltpu.SemaphoreType.DMA((depth, widest - 1)),
            pltpu.SemaphoreType.DMA((depth, widest - 1)),
            pltpu.SemaphoreType.DMA((depth, widest - 1)),
            pltpu.SemaphoreType.DMA((depth, widest - 1)),
        ],
        compiler_params=pltpu.CompilerParams(collective_id=2, has_side_effects=True, vmem_limit_bytes=LIMIT),
        name="reduce_gradients",
    )(*[p.reshape(dims + p.shape[1:]) for p in parts], loss, *squares)


def silu(values):
    return values * (1.0 / (1.0 + jnp.exp(-values)))


def silu_slope(values):
    gate = 1.0 / (1.0 + jnp.exp(-values))
    return gate * (1.0 + values * (1.0 - gate))


def split_low(values):
    high = values.astype(BF)
    return jnp.concatenate([high, (values - high.astype(jnp.float32)).astype(BF)], axis=0)


def block_of(refs, k):
    slots = len(refs)
    part = refs[k % slots][:, k // slots]
    return part.reshape(-1, D)


def condition_kernel(slots, lat_count, *refs):
    feat_ref, hot_ref = refs[:2]
    slot_refs = refs[2 : 2 + slots]
    ada_refs = refs[2 + slots : 2 + slots + SPLIT]
    mod_ref, fmod_ref, pre_ref, cond_ref, patch_ref, head_ref = refs[2 + slots + SPLIT :]
    entry = block_of(slot_refs, 0)
    patch_ref[...] = entry[:, :PATCH_IN]
    pre = dot_nt(feat_ref[...], entry)
    pre_ref[...] = pre
    cond = dot_nt(silu(pre).astype(BF), block_of(slot_refs, 1))
    for k in range(3):
        cond = cond + dot_nt(hot_ref[:, k * D : (k + 1) * D], block_of(slot_refs, 2 + k))
    cond_ref[...] = cond
    head_ref[...] = block_of(slot_refs, 4)[:, 256 : 256 + OUT]
    act = silu(cond).astype(BF)
    for p in range(SPLIT):
        wide = ada_refs[p].shape[0]
        mod_ref[:, p * wide : (p + 1) * wide] = dot_nt(act, ada_refs[p][...])
    for k in range(2):
        part = dot_nn(act, block_of(slot_refs, 5 + k))
        for b in range(lat_count):
            fmod_ref[b, k : k + 1, :] = part[b : b + 1, :]


def condition(feat, hot, slot_full, ada_full, lat_count):
    vmem = pl.BlockSpec(memory_space=pltpu.VMEM)
    wide = ada_full[0].shape[0]
    shapes = [
        ((8, SPLIT * wide), jnp.float32),
        ((lat_count, 8, D), jnp.float32),
        ((8, D), jnp.float32),
        ((8, D), jnp.float32),
        ((D, PATCH_IN), BF),
        ((D, OUT), BF),
    ]
    return pl.pallas_call(
        functools.partial(condition_kernel, len(slot_full), lat_count),
        out_shape=[jax.ShapeDtypeStruct(*s) for s in shapes],
        in_specs=[vmem] * (2 + len(slot_full) + SPLIT),
        out_specs=[vmem] * len(shapes),
        compiler_params=pltpu.CompilerParams(vmem_limit_bytes=LIMIT),
        name="condition",
    )(feat, hot, *slot_full, *ada_full)


def condition_back_kernel(slots, lat_count, *refs):
    feat_ref, hot_ref = refs[:2]
    slot_refs = refs[2 : 2 + slots]
    ada_refs = refs[2 + slots : 2 + slots + SPLIT]
    pre_ref, cond_ref, d_mod_ref, d_fmod_ref, d_patch_ref, d_head_ref = refs[2 + slots + SPLIT :][:6]
    outs = refs[2 + slots + SPLIT + 6 :]
    g_slots, g_ada = outs[:slots], outs[slots : slots + SPLIT]
    fmod_s = outs[slots + SPLIT]
    pre, cond = pre_ref[...], cond_ref[...]
    act = silu(cond).astype(BF)
    act_two = jnp.concatenate([act, act], axis=0)
    d_cond = jnp.zeros((16, D), jnp.float32)
    for p in range(SPLIT):
        wide = ada_refs[p].shape[0]
        d_mod = split_low(d_mod_ref[:, p * wide : (p + 1) * wide])
        d_cond = d_cond + dot_nn(d_mod, ada_refs[p][...])
        g_ada[p][...] = dot_tn(d_mod, act_two).astype(BF)

    def give(k, grad):
        ref = g_slots[k % slots]
        ref[:, k // slots] = grad.astype(BF).reshape(ref.shape[0], ref.shape[2], D)

    fmod_s[...] = jnp.zeros_like(fmod_s)
    for k in range(2):
        for b in range(lat_count):
            fmod_s[k, b : b + 1, :] = d_fmod_ref[b, k : k + 1, :]
        d_fmod = split_low(fmod_s[k])
        d_cond = d_cond + dot_nt(d_fmod, block_of(slot_refs, 5 + k))
        give(5 + k, dot_tn(act_two, d_fmod))
    d_pre = split_low((d_cond[:8] + d_cond[8:]) * silu_slope(cond))
    time_act = silu(pre).astype(BF)
    give(1, dot_tn(d_pre, jnp.concatenate([time_act, time_act], axis=0)))
    d_time = dot_nn(d_pre, block_of(slot_refs, 1))
    for k in range(3):
        hot = hot_ref[:, k * D : (k + 1) * D]
        grad = dot_tn(d_pre, jnp.concatenate([hot, hot], axis=0))
        if k == 2:
            here = jnp.pad(d_head_ref[...], ((0, 128 - OUT), (0, 0))).T
            grad = jnp.concatenate([grad[:, :256], grad[:, 256:] + here], axis=1)
        give(2 + k, grad)
    d_time = split_low((d_time[:8] + d_time[8:]) * silu_slope(pre))
    grad = dot_tn(d_time, jnp.concatenate([feat_ref[...], feat_ref[...]], axis=0))
    here = jnp.pad(d_patch_ref[...], ((0, 128 - PATCH_IN), (0, 0))).T
    give(0, jnp.concatenate([grad[:, :128] + here, grad[:, 128:]], axis=1))
    for k in range(7, SMALL):
        give(k, jnp.zeros((D, D), jnp.float32))


def condition_back(feat, hot, slot_full, ada_full, pre, cond, d_mod, d_fmod, d_patch, d_head):
    vmem = pl.BlockSpec(memory_space=pltpu.VMEM)
    lat_count = d_fmod.shape[0]
    args = (feat, hot, *slot_full, *ada_full, pre, cond, d_mod, d_fmod, d_patch, d_head)
    kept = (*slot_full, *ada_full)
    return pl.pallas_call(
        functools.partial(condition_back_kernel, len(slot_full), lat_count),
        out_shape=[jax.ShapeDtypeStruct(w.shape, BF) for w in kept],
        in_specs=[vmem] * len(args),
        out_specs=[vmem] * len(kept),
        scratch_shapes=[pltpu.VMEM((2, 8, D), jnp.float32)],
        compiler_params=pltpu.CompilerParams(vmem_limit_bytes=LIMIT),
        name="condition_back",
    )(*args)


def adam_kernel(slots, layers, count_rms, *refs):
    stats_ref, both_ref = refs[:2]
    grads = refs[2 : 2 + SPLIT + 3 * layers]
    states = refs[2 + SPLIT + 3 * layers :][:21]
    outs = refs[2 + SPLIT + 3 * layers + 21 :]
    news, (loss_ref, norm_ref, rms_ref) = outs[:21], outs[21:]
    totals = jnp.sum(stats_ref[...], axis=1, keepdims=True)
    norm = jnp.sqrt(totals[0:1])
    factor = jnp.minimum(1.0, 0.01 / (norm + 1e-06))
    loss_ref[...] = totals[1:2]
    norm_ref[...] = norm
    rms_ref[...] = jnp.sqrt(totals[2 : 2 + layers] / count_rms)
    correct = 1.0 - 0.5**STEP

    def update(name, where, grad):
        weight, first, second = (ref[where] for ref in states[3 * name : 3 * name + 3])
        clipped = grad * factor
        first_new = 0.5 * first + 0.5 * clipped
        second_new = 0.5 * second + 0.5 * clipped * clipped
        root = jnp.sqrt(second_new * (1.0 / correct)) + 1e-08
        new = weight - 0.02 * (first_new * (1.0 / correct) / root + 0.01 * weight)
        news[3 * name][where] = new
        news[3 * name + 1][where] = first_new
        news[3 * name + 2][where] = second_new

    def small(k):
        return both_ref[k // slots, k % slots]

    rows = states[0].shape[0]
    early = PATCH_IN + FREQ
    every = slice(0, rows)
    update(0, (every, slice(0, early)), small(0)[:rows, :early])
    update(0, (every, slice(early, early + D)), small(1)[:rows])
    update(1, (every, slice(0, D)), small(2)[:rows])
    update(1, (every, slice(D, 2 * D)), small(3)[:rows])
    update(1, (every, slice(2 * D, CLASSES + 1)), small(4)[:rows, : CLASSES + 1 - 2 * D])
    update(6, (every, slice(0, D)), small(5)[:rows])
    update(6, (every, slice(D, 2 * D)), small(6)[:rows])
    update(6, (every, slice(2 * D, 2 * D + OUT)), small(4)[:rows, 256 : 256 + OUT])
    part = -(-states[15].shape[0] // SPLIT)
    for p in range(SPLIT):
        update(5, (slice(p * part, (p + 1) * part), slice(0, D)), grads[p][:part])
    for l in range(layers):
        for k in range(3):
            update(2 + k, (l, slice(0, states[6].shape[1]), slice(0, D)), grads[SPLIT + 3 * l + k][: states[6].shape[1]])


def adam_all(slots, layers, count_rms, stats, both, grads, states):
    vmem = pl.BlockSpec(memory_space=pltpu.VMEM)
    args = (stats, both, *grads, *states)
    return pl.pallas_call(
        functools.partial(adam_kernel, slots, layers, count_rms),
        out_shape=[jax.ShapeDtypeStruct(s.shape, jnp.float32) for s in states]
        + [jax.ShapeDtypeStruct((n, 1), jnp.float32) for n in (1, 1, layers)],
        in_specs=[vmem] * len(args),
        out_specs=[vmem] * 24,
        compiler_params=pltpu.CompilerParams(vmem_limit_bytes=LIMIT),
        name="adam",
    )(*args)


def position_table(grid_side, columns):
    quarter = columns // 4
    omegas = jnp.exp(-math.log(10000.0) * jnp.arange(quarter, dtype=jnp.float32) / quarter)
    positions = jnp.arange(grid_side * grid_side, dtype=jnp.int32)
    row_pos = (positions // grid_side).astype(jnp.float32)[:, None] * omegas
    col_pos = (positions % grid_side).astype(jnp.float32)[:, None] * omegas
    return jnp.concatenate(
        [jnp.sin(row_pos), jnp.cos(row_pos), jnp.sin(col_pos), jnp.cos(col_pos)], axis=-1
    )


def time_table(step_ids, columns):
    half_cols = columns // 2
    frequency = jnp.exp(-math.log(10000.0) * jnp.arange(half_cols, dtype=jnp.float32) / half_cols)
    angles = step_ids.astype(jnp.float32)[:, None] * frequency
    return jnp.concatenate([jnp.cos(angles), jnp.sin(angles)], axis=-1)


def noise_scales(step_ids):
    phases = (step_ids.astype(jnp.float32) / NOISE_STEPS + 0.008) / 1.008 * (math.pi / 2)
    return (jnp.cos(phases), jnp.sin(phases))


def swap(array):
    return jnp.swapaxes(array, -1, -2)


def pad_rows(part):
    extra = -part.shape[-2] % 16
    if extra == 0:
        return part
    return jnp.pad(part, [(0, 0)] * (part.ndim - 2) + [(0, extra), (0, 0)])


def body(
    clean_latents,
    noise_field,
    timesteps,
    labels,
    drop_flags,
    entry_weight,
    class_table,
    attn_weight,
    ffn_in_weight,
    ffn_out_weight,
    ada_weight,
    final_weight,
    entry_first,
    entry_second,
    class_first,
    class_second,
    attn_first,
    attn_second,
    ffn_in_first,
    ffn_in_second,
    ffn_out_first,
    ffn_out_second,
    ada_first,
    ada_second,
    final_first,
    final_second,
):
    lat_count = clean_latents.shape[0]
    tokens = clean_latents.shape[1]
    layers = attn_weight.shape[0]
    both = ("dp", "tp")
    devices = lax.axis_size("dp") * lax.axis_size("tp")
    count_all = float(lat_count * devices * tokens * OUT)
    count_rms = float(lat_count * devices * tokens * D)
    nb = 1
    clean_t, noise_t = swap(clean_latents), swap(noise_field)
    cos_part, sin_part = noise_scales(timesteps)
    noisy = (cos_part[:, None, None] * clean_t + sin_part[:, None, None] * noise_t).astype(BF)
    n_dp, n_tp = lax.axis_size("dp"), lax.axis_size("tp")
    places = Places(n_dp, n_tp)
    slots = -(-SMALL // n_tp)
    dp_rows = final_weight.shape[0]
    wide_rows = attn_weight.shape[2]
    ada_rows = ada_weight.shape[2]
    part_rows = -(-layers * ada_rows // SPLIT)

    def flat_ada(array):
        return swap(array).reshape(layers * ada_rows, D)

    gathered = gather_all(
        places,
        slots,
        swap(entry_weight),
        swap(class_table),
        final_weight,
        flat_ada(ada_weight),
        swap(attn_weight),
        swap(ffn_in_weight),
        ffn_out_weight,
    )

    def whole_rows(block, rows):
        return block[:, :rows].reshape(-1, D)

    def to_slot(block):
        if dp_rows % 16 == 0:
            return block.reshape(n_dp, n_tp, dp_rows, D)
        block = block.reshape(n_dp, n_tp, -1, D)[:, :, :dp_rows]
        return block.swapaxes(0, 1).reshape(1, n_tp, n_dp * dp_rows, D)

    def from_slot(block):
        if dp_rows % 16 == 0:
            return block.reshape(places.count, dp_rows, D)
        block = block.reshape(n_tp, n_dp, dp_rows, D).swapaxes(0, 1)
        return pad_rows(block.reshape(places.count, dp_rows, D))

    slot_full = [to_slot(g) for g in gathered[:slots]]
    ada_full = [whole_rows(g, part_rows) for g in gathered[slots : slots + SPLIT]]
    block_full = [whole_rows(g, wide_rows) for g in gathered[slots + SPLIT :]]
    weights = [tuple(block_full[3 * l : 3 * l + 3]) for l in range(layers)]

    time_feat = time_table(timesteps, FREQ).astype(BF)
    feat = jnp.pad(time_feat, ((0, 8 - lat_count), (PATCH_IN, D - PATCH_IN - FREQ)))
    classes_used = jnp.where(drop_flags == 1, CLASSES, labels)
    classes_used = jnp.pad(classes_used, (0, 8 - lat_count), constant_values=3 * D)
    class_hot = (classes_used[:, None] == jnp.arange(3 * D, dtype=jnp.int32)[None, :]).astype(BF)
    raw, fmod, pre, cond, patch_t, head = condition(feat, class_hot, slot_full, ada_full, lat_count)
    mods = raw[:lat_count].reshape(lat_count, SPLIT, places.count, part_rows).swapaxes(1, 2)
    mods = mods.reshape(lat_count, places.count, layers, ada_rows).transpose(2, 0, 1, 3)
    mods = mods.reshape(layers, lat_count, 6, D)
    mods = jnp.pad(mods, ((0, 0), (0, 0), (0, 2), (0, 0)))
    mods = [mods[l] for l in range(layers)]
    pos = position_table(GRID, D)
    saved = []
    squares = []
    stream = None
    for l in range(layers):
        if l == 0:
            outs = forward_layer(True, (noisy, patch_t, pos), mods[l], weights[l], nb, tokens)
            stream, outs = outs[0], outs[1:]
        else:
            outs = forward_layer(False, (stream,), mods[l], weights[l], nb, tokens)
        saved.append((stream, *outs[1:9]))
        stream = outs[0]
        squares.append(outs[9])
    layer_grads = [None] * layers
    d_mods = [None] * layers
    d_stream = None
    for l in reversed(range(layers)):
        last, first = l == layers - 1, l == 0
        entry_args = (stream, fmod, head, clean_t, noise_t) if last else (d_stream,)
        if first:
            entry_args = (*entry_args, noisy)
        outs = list(backward_layer(first, last, entry_args, mods[l], weights[l], saved[l], nb, tokens, count_all))
        if last:
            loss_part, d_head_t, d_fmod = outs[:3]
            outs = outs[3:]
        if first:
            d_patch = outs[0]
        else:
            d_stream = outs[0]
        layer_grads[l] = outs[1:4]
        d_mods[l] = outs[4]
    d_raw = jnp.stack([d[:, :6] for d in d_mods]).reshape(layers, lat_count, places.count, ada_rows)
    d_raw = d_raw.transpose(1, 2, 0, 3).reshape(lat_count, places.count, SPLIT, part_rows)
    d_raw = d_raw.swapaxes(1, 2).reshape(lat_count, -1)
    d_raw = jnp.pad(d_raw, ((0, 8 - lat_count), (0, 0)))
    small_grads = condition_back(
        feat, class_hot, slot_full, ada_full, pre, cond, d_raw, d_fmod, d_patch, d_head_t
    )
    grads = [from_slot(g) for g in small_grads[:slots]]
    grads += [pad_rows(g.reshape(places.count, part_rows, D)) for g in small_grads[slots:]]
    for l in reversed(range(layers)):
        for k in range(3):
            grads.append(pad_rows(layer_grads[l][k].reshape(places.count, wide_rows, D)))
    *summed, both, stats = reduce_all(places, slots, grads, loss_part, squares)
    wide = summed[slots + SPLIT :]
    wide = [wide[3 * (layers - 1 - l) + k] for l in range(layers) for k in range(3)]
    states = []
    for shape_it, triple in (
        (swap, (entry_weight, entry_first, entry_second)),
        (swap, (class_table, class_first, class_second)),
        (swap, (attn_weight, attn_first, attn_second)),
        (swap, (ffn_in_weight, ffn_in_first, ffn_in_second)),
        (lambda a: a, (ffn_out_weight, ffn_out_first, ffn_out_second)),
        (flat_ada, (ada_weight, ada_first, ada_second)),
        (lambda a: a, (final_weight, final_first, final_second)),
    ):
        states.extend(shape_it(a) for a in triple)
    out = adam_all(slots, layers, count_rms, stats, both, [*summed[slots : slots + SPLIT], *wide], states)
    news = []
    for at in range(21):
        value = out[at]
        if at // 3 == 5:
            value = value.reshape(layers, ada_rows, D)
        news.append(value if at // 3 in (4, 6) else swap(value))
    return (*news, out[21].reshape(()), out[22].reshape(()), out[23].reshape(layers))


def solution(mesh):
    lead = P(("dp", "tp"), None, None)
    ids = P(("dp", "tp"))
    wide = P(None, "dp")
    cols = P(None, None, ("dp", "tp"))
    rows = P(None, ("dp", "tp"), None)
    top = P("dp", None)
    return jax.shard_map(
        body,
        mesh=mesh,
        in_specs=(
            lead,
            lead,
            ids,
            ids,
            ids,
            wide,
            wide,
            cols,
            cols,
            rows,
            cols,
            top,
            wide,
            wide,
            wide,
            wide,
            cols,
            cols,
            cols,
            cols,
            rows,
            rows,
            cols,
            cols,
            top,
            top,
        ),
        out_specs=(wide,) * 6 + (cols,) * 6 + (rows,) * 3 + (cols,) * 3 + (top,) * 3 + (P(), P(), P()),
        check_vma=False,
    )
```

```python
import functools
import math

import jax
import jax.numpy as jnp
from jax import lax
from jax.experimental import pallas as pl
from jax.experimental.pallas import tpu as pltpu
from jax.sharding import PartitionSpec as P

D = 384
HEADS = 6
HEAD_DIM = 64
CLASSES = 1000
GRID = 16
PATCH_IN = 16
OUT = 32
FREQ = 256
NOISE_STEPS = 1000
STEP = 10
BF = jnp.bfloat16


highest = lax.Precision.HIGHEST


def dot_nn(a, b):
    return lax.dot_general(a, b, (((1,), (0,)), ((), ())), preferred_element_type=jnp.float32)


def dot_nt(a, b):
    return lax.dot_general(a, b, (((1,), (1,)), ((), ())), preferred_element_type=jnp.float32)


def dot_tn(a, b):
    return lax.dot_general(a, b, (((0,), (0,)), ((), ())), preferred_element_type=jnp.float32)


def norm_rows(rows):
    center = rows - jnp.mean(rows, axis=-1, keepdims=True)
    rstd = lax.rsqrt(jnp.mean(center * center, axis=-1, keepdims=True) + 1e-06)
    return center * rstd, rstd


def norm_back(d_out, hat, rstd, scale):
    d_shift = jnp.sum(d_out, axis=1, keepdims=True)
    d_scale = jnp.sum(d_out * hat, axis=1, keepdims=True)
    d_hat = d_out * (1.0 + scale)
    m_one = jnp.mean(d_hat, axis=-1, keepdims=True)
    m_two = jnp.mean(d_hat * hat, axis=-1, keepdims=True)
    return rstd * (d_hat - m_one - hat * m_two), d_shift, d_scale


def half_masks():
    lane = lax.broadcasted_iota(jnp.int32, (1, 2 * HEAD_DIM), 1)
    low = jnp.where(lane < HEAD_DIM, 1.0, 0.0)
    return low.astype(BF), (1.0 - low).astype(BF)


def stack_heads(pair, masks):
    return jnp.concatenate([pair * masks[0], pair * masks[1]], axis=0)


GELU_A = math.sqrt(2.0 / math.pi)
GELU_B = 0.044715


def forward_kernel(first, nb, tokens, *refs):
    if first:
        noisy_ref, patch_ref, pos_ref = refs[:3]
        refs = refs[3:]
    else:
        stream_ref = refs[0]
        refs = refs[1:]
    mod_ref, attn_ref, in_ref, out_ref = refs[:4]
    refs = refs[4:]
    if first:
        start_ref = refs[0]
        refs = refs[1:]
    (
        result_ref,
        qkv_ref,
        probs_ref,
        mixed_ref,
        branch_ref,
        middle_ref,
        mlp_ref,
        act_ref,
        slope_ref,
        square_ref,
    ) = refs
    rows = nb * tokens
    if first:
        parts = [
            lax.dot_general(
                noisy_ref[n], patch_ref[...], (((0,), (1,)), ((), ())), preferred_element_type=jnp.float32
            )
            + pos_ref[...]
            for n in range(nb)
        ]
        stream = parts[0] if nb == 1 else jnp.concatenate(parts, axis=0)
        start_ref[...] = stream
    else:
        stream = stream_ref[...]
    mod = mod_ref[...]
    stream = stream.reshape(nb, tokens, D)
    hat, _ = norm_rows(stream)
    attn_in = (hat * (1.0 + mod[:, 1:2]) + mod[:, 0:1]).astype(BF).reshape(rows, D)
    qkv_ref[...] = dot_nt(attn_in, attn_ref[: 3 * D, :]).astype(BF)
    masks = half_masks()
    for n in range(nb):
        here = slice(n * tokens, (n + 1) * tokens)
        for pair in range(HEADS // 2):
            col = pair * 2 * HEAD_DIM
            queries = qkv_ref[here, col : col + 2 * HEAD_DIM] * jnp.asarray(HEAD_DIM**-0.5, BF)
            keys = stack_heads(qkv_ref[here, D + col : D + col + 2 * HEAD_DIM], masks)
            values = stack_heads(qkv_ref[here, 2 * D + col : 2 * D + col + 2 * HEAD_DIM], masks)
            scores = dot_nt(queries, keys)
            halves = []
            for side in range(2):
                part = scores[:, side * tokens : (side + 1) * tokens]
                grown = jnp.exp(part - jnp.max(part, axis=-1, keepdims=True))
                halves.append((grown * (1.0 / jnp.sum(grown, axis=-1, keepdims=True))).astype(BF))
            probs = jnp.concatenate(halves, axis=1)
            probs_ref[here, pair * 2 * tokens : (pair + 1) * 2 * tokens] = probs
            mixed_ref[here, col : col + 2 * HEAD_DIM] = dot_nn(probs, values).astype(BF)
    branch = dot_nt(mixed_ref[...], attn_ref[3 * D :, :])
    branch_ref[...] = branch.astype(BF)
    middle = stream + mod[:, 2:3] * branch.reshape(nb, tokens, D)
    middle_ref[...] = middle.reshape(rows, D)
    hat, _ = norm_rows(middle)
    mlp_in = (hat * (1.0 + mod[:, 4:5]) + mod[:, 3:4]).astype(BF).reshape(rows, D)
    hidden = dot_nt(mlp_in, in_ref[...])
    squared = hidden * hidden
    bent = jnp.tanh(hidden * (GELU_A + (GELU_A * GELU_B) * squared))
    half = 0.5 * hidden
    act = (half + half * bent).astype(BF)
    act_ref[...] = act
    slope_ref[...] = (
        0.5
        + 0.5 * bent
        + half * (1.0 - bent * bent) * (GELU_A + (3.0 * GELU_A * GELU_B) * squared)
    ).astype(BF)
    mlp = dot_nn(act, out_ref[...])
    mlp_ref[...] = mlp.astype(BF)
    result = middle + mod[:, 5:6] * mlp.reshape(nb, tokens, D)
    result_ref[...] = result.reshape(rows, D)
    square_ref[0] = jnp.sum((result * result).reshape(rows // 8, 8, D), axis=0)


def backward_kernel(first, last, nb, tokens, steps, count_all, *refs):
    if last:
        final_ref, fmod_ref, head_ref, clean_ref, noise_ref = refs[:5]
        refs = refs[5:]
    else:
        d_stream_ref = refs[0]
        refs = refs[1:]
    if first:
        noisy_ref = refs[0]
        refs = refs[1:]
    (
        mod_ref,
        attn_ref,
        in_ref,
        out_ref,
        stream_ref,
        qkv_ref,
        probs_ref,
        mixed_ref,
        branch_ref,
        middle_ref,
        mlp_ref,
        act_ref,
        slope_ref,
    ) = refs[:13]
    refs = refs[13:]
    if last:
        loss_ref, dhead_ref, dfmod_ref = refs[:3]
        refs = refs[3:]
    if first:
        dpatch_ref = refs[0]
    else:
        d_prev_ref = refs[0]
    gattn_ref, gin_ref, gout_ref, dmod_ref, acc_attn, acc_in, acc_out, d_qkv_s = refs[1:]
    rows = nb * tokens
    step = pl.program_id(0)

    @pl.when(step == 0)
    def _():
        acc_attn[...] = jnp.zeros_like(acc_attn)
        acc_in[...] = jnp.zeros_like(acc_in)
        acc_out[...] = jnp.zeros_like(acc_out)
        if last:
            dhead_ref[...] = jnp.zeros_like(dhead_ref)
        if first:
            dpatch_ref[...] = jnp.zeros_like(dpatch_ref)

    mod = mod_ref[...]
    if last:
        fmod = fmod_ref[...]
        hat, rstd = norm_rows(final_ref[...].reshape(nb, tokens, D))
        final_in = (hat * (1.0 + fmod[:, 1:2]) + fmod[:, 0:1]).astype(BF)
        d_parts = []
        loss = jnp.zeros((8, tokens), jnp.float32)
        for n in range(nb):
            predicted = lax.dot_general(
                head_ref[...], final_in[n], (((0,), (1,)), ((), ())), preferred_element_type=jnp.float32
            )
            errors = predicted - jnp.concatenate([noise_ref[n], clean_ref[n]], axis=0)
            loss = loss + jnp.sum((errors * errors).reshape(OUT // 8, 8, tokens), axis=0)
            d_pred = (errors * (2.0 / count_all)).astype(BF)
            dhead_ref[...] += dot_nn(d_pred, final_in[n])
            d_parts.append(
                lax.dot_general(
                    d_pred, head_ref[...], (((0,), (1,)), ((), ())), preferred_element_type=jnp.float32
                )
            )
        loss_ref[0] = loss
        d_final = jnp.stack(d_parts, axis=0)
        d_stream, d_shift, d_scale = norm_back(d_final, hat, rstd, fmod[:, 1:2])
        dfmod_ref[:, 0:1] = d_shift
        dfmod_ref[:, 1:2] = d_scale
    else:
        d_stream = d_stream_ref[...].reshape(nb, tokens, D)
    dmod_ref[:, 5:6] = jnp.sum(d_stream * mlp_ref[...].astype(jnp.float32).reshape(nb, tokens, D), axis=1, keepdims=True)
    d_mlp = (d_stream * mod[:, 5:6]).astype(BF).reshape(rows, D)
    d_hidden = (dot_nt(d_mlp, out_ref[...]) * slope_ref[...].astype(jnp.float32)).astype(BF)
    acc_out[...] += dot_tn(act_ref[...], d_mlp)
    hat, rstd = norm_rows(middle_ref[...].reshape(nb, tokens, D))
    mlp_in = (hat * (1.0 + mod[:, 4:5]) + mod[:, 3:4]).astype(BF).reshape(rows, D)
    acc_in[...] += dot_tn(d_hidden, mlp_in)
    d_input = dot_nn(d_hidden, in_ref[...]).reshape(nb, tokens, D)
    d_middle, d_shift, d_scale = norm_back(d_input, hat, rstd, mod[:, 4:5])
    dmod_ref[:, 3:4] = d_shift
    dmod_ref[:, 4:5] = d_scale
    d_middle = d_middle + d_stream
    dmod_ref[:, 2:3] = jnp.sum(
        d_middle * branch_ref[...].astype(jnp.float32).reshape(nb, tokens, D), axis=1, keepdims=True
    )
    d_proj = (d_middle * mod[:, 2:3]).astype(BF).reshape(rows, D)
    acc_attn[3 * D :, :] += dot_tn(d_proj, mixed_ref[...])
    d_mix = dot_nn(d_proj, attn_ref[3 * D :, :]).astype(BF)
    masks = half_masks()
    lane = lax.broadcasted_iota(jnp.int32, (tokens, 2 * HEAD_DIM), 1)
    low_side = lane < HEAD_DIM
    root = HEAD_DIM**-0.5
    for n in range(nb):
        here = slice(n * tokens, (n + 1) * tokens)
        for pair in range(HEADS // 2):
            col = pair * 2 * HEAD_DIM
            queries = qkv_ref[here, col : col + 2 * HEAD_DIM]
            keys = stack_heads(qkv_ref[here, D + col : D + col + 2 * HEAD_DIM], masks)
            values = stack_heads(qkv_ref[here, 2 * D + col : 2 * D + col + 2 * HEAD_DIM], masks)
            d_out = d_mix[here, col : col + 2 * HEAD_DIM]
            probs_bf = probs_ref[here, pair * 2 * tokens : (pair + 1) * 2 * tokens]
            d_probs = dot_nt(d_out, values)
            halves = []
            for side in range(2):
                cut = slice(side * tokens, (side + 1) * tokens)
                probs = probs_bf[:, cut].astype(jnp.float32)
                part = d_probs[:, cut]
                halves.append((probs * (part - jnp.sum(probs * part, axis=-1, keepdims=True))).astype(BF))
            d_scores = jnp.concatenate(halves, axis=1)
            d_queries = dot_nn(d_scores, keys) * root
            d_keys = dot_tn(d_scores, queries)
            d_keys = jnp.where(low_side, d_keys[:tokens], d_keys[tokens:]) * root
            d_values = dot_tn(probs_bf, d_out)
            d_values = jnp.where(low_side, d_values[:tokens], d_values[tokens:])
            d_qkv_s[here, col : col + 2 * HEAD_DIM] = d_queries.astype(BF)
            d_qkv_s[here, D + col : D + col + 2 * HEAD_DIM] = d_keys.astype(BF)
            d_qkv_s[here, 2 * D + col : 2 * D + col + 2 * HEAD_DIM] = d_values.astype(BF)
    d_qkv = d_qkv_s[...]
    hat, rstd = norm_rows(stream_ref[...].reshape(nb, tokens, D))
    attn_in = (hat * (1.0 + mod[:, 1:2]) + mod[:, 0:1]).astype(BF).reshape(rows, D)
    acc_attn[: 3 * D, :] += dot_tn(d_qkv, attn_in)
    d_attn_in = dot_nn(d_qkv, attn_ref[: 3 * D, :]).reshape(nb, tokens, D)
    d_before, d_shift, d_scale = norm_back(d_attn_in, hat, rstd, mod[:, 1:2])
    dmod_ref[:, 0:1] = d_shift
    dmod_ref[:, 1:2] = d_scale
    d_prev = d_middle + d_before
    if first:
        for n in range(nb):
            dpatch_ref[...] += lax.dot_general(
                noisy_ref[n].astype(jnp.float32), d_prev[n], (((1,), (0,)), ((), ())), precision=highest
            )
    else:
        d_prev_ref[...] = d_prev.reshape(rows, D)

    @pl.when(step == steps - 1)
    def _():
        gattn_ref[...] = acc_attn[...].astype(BF)
        gin_ref[...] = acc_in[...].astype(BF)
        gout_ref[...] = acc_out[...].astype(BF)


def whole_spec(array):
    return pl.BlockSpec(array.shape, lambda i: (0,) * array.ndim)


def lead_spec(block, ndim):
    return pl.BlockSpec(block, lambda i: (i,) + (0,) * (ndim - 1))


LIMIT = 56 * 1024 * 1024


def forward_layer(first, entry_args, mod, weights, nb, tokens):
    lat_count = mod.shape[0]
    rows = nb * tokens
    steps = lat_count // nb
    total = lat_count * tokens
    kinds = [(D, jnp.float32)] if first else []
    kinds += [
        (D, jnp.float32),
        (3 * D, BF),
        (HEADS * tokens, BF),
        (D, BF),
        (D, BF),
        (D, jnp.float32),
        (D, BF),
        (4 * D, BF),
        (4 * D, BF),
    ]
    out_shape = [jax.ShapeDtypeStruct((total, cols), kind) for cols, kind in kinds]
    out_specs = [lead_spec((rows, cols), 2) for cols, _ in kinds]
    out_shape.append(jax.ShapeDtypeStruct((steps, 8, D), jnp.float32))
    out_specs.append(lead_spec((1, 8, D), 3))
    if first:
        noisy, patch, pos = entry_args
        in_specs = [lead_spec((nb, PATCH_IN, tokens), 3), whole_spec(patch), whole_spec(pos)]
    else:
        in_specs = [lead_spec((rows, D), 2)]
    in_specs += [lead_spec((nb, 8, D), 3)] + [whole_spec(w) for w in weights]
    return pl.pallas_call(
        functools.partial(forward_kernel, first, nb, tokens),
        grid=(steps,),
        out_shape=out_shape,
        in_specs=in_specs,
        out_specs=out_specs,
        compiler_params=pltpu.CompilerParams(vmem_limit_bytes=LIMIT),
        name="block_forward",
    )(*entry_args, mod, *weights)


def backward_layer(first, last, entry_args, mod, weights, saved, nb, tokens, count_all):
    lat_count = mod.shape[0]
    rows = nb * tokens
    steps = lat_count // nb
    total = lat_count * tokens
    in_specs = []
    args = list(entry_args)
    if last:
        if isinstance(args[0], tuple):
            layer = args[0][1]
            in_specs.append(pl.BlockSpec((None, rows, D), lambda i: (layer, i, 0)))
            args[0] = args[0][0]
        else:
            in_specs.append(lead_spec((rows, D), 2))
        in_specs += [
            lead_spec((nb, 8, D), 3),
            whole_spec(args[2]),
            lead_spec((nb, PATCH_IN, tokens), 3),
            lead_spec((nb, PATCH_IN, tokens), 3),
        ]
    else:
        in_specs += [lead_spec((rows, D), 2)]
    if first:
        in_specs += [lead_spec((nb, PATCH_IN, tokens), 3)]
    in_specs += [lead_spec((nb, 8, D), 3)] + [whole_spec(w) for w in weights]
    for kept in saved:
        if isinstance(kept, tuple):
            array, layer = kept
            in_specs.append(
                pl.BlockSpec((None, rows, array.shape[2]), lambda i, layer=layer: (layer, i, 0))
            )
        else:
            in_specs.append(lead_spec((rows, kept.shape[1]), 2))
    saved = [kept[0] if isinstance(kept, tuple) else kept for kept in saved]
    out_shape = []
    out_specs = []

    def add(shape, kind, spec):
        out_shape.append(jax.ShapeDtypeStruct(shape, kind))
        out_specs.append(spec)

    def whole(shape):
        return pl.BlockSpec(shape, lambda i: (0,) * len(shape))

    if last:
        add((steps, 8, tokens), jnp.float32, lead_spec((1, 8, tokens), 3))
        add((OUT, D), jnp.float32, whole((OUT, D)))
        add((lat_count, 8, D), jnp.float32, lead_spec((nb, 8, D), 3))
    if first:
        add((PATCH_IN, D), jnp.float32, whole((PATCH_IN, D)))
    else:
        add((total, D), jnp.float32, lead_spec((rows, D), 2))
    for _ in range(3):
        add((4 * D, D), BF, whole((4 * D, D)))
    add((lat_count, 8, D), jnp.float32, lead_spec((nb, 8, D), 3))
    return pl.pallas_call(
        functools.partial(backward_kernel, first, last, nb, tokens, steps, count_all),
        grid=(steps,),
        out_shape=out_shape,
        in_specs=in_specs,
        out_specs=out_specs,
        scratch_shapes=[pltpu.VMEM((4 * D, D), jnp.float32)] * 3 + [pltpu.VMEM((rows, 3 * D), BF)],
        compiler_params=pltpu.CompilerParams(vmem_limit_bytes=LIMIT),
        name="block_backward",
    )(*args, mod, *weights, *saved)


MESH = pl.DeviceIdType.MESH


class Places:
    def __init__(self, n_dp, n_tp):
        self.digits = []
        for axis, count, top in (("dp", n_dp, 4), ("tp", n_tp, 2)):
            sizes = []
            rest = count
            while rest > 1:
                size = next((s for s in (top, 2, 3, 5, 7) if rest % s == 0), rest)
                sizes.append(size)
                rest //= size
            stride = count
            for size in sizes:
                stride //= size
                self.digits.append((axis, stride, size))
        self.dims = tuple(size for _, _, size in self.digits)
        self.count = n_dp * n_tp

    def order(self, odd):
        names = list(range(len(self.digits)))
        if odd and len(names) >= 4:
            names[-3], names[-2] = names[-2], names[-3]
        return names

    def mine(self):
        return [lax.rem(lax.axis_index(axis) // stride, size) for axis, stride, size in self.digits]

    def other(self, mine, digit, shift):
        axis, stride, size = self.digits[digit]
        value = lax.rem(mine[digit] + shift, size)
        return {axis: lax.axis_index(axis) + (value - mine[digit]) * stride}, value

    def barrier(self, mine):
        barrier = pltpu.get_barrier_semaphore()
        count = 0
        for digit, size in enumerate(self.dims):
            for shift in range(1, size):
                target, _ = self.other(mine, digit, shift)
                pl.semaphore_signal(barrier, inc=1, device_id=target, device_id_type=MESH)
                count += 1
        pl.semaphore_wait(barrier, count)


SMALL = 8
SPLIT = 3


def small_blocks(entry_t, table_t, final):
    early = PATCH_IN + FREQ
    return [
        (0, 0, entry_t, 0, early),
        (1, 0, entry_t, early, early + D),
        (2, 0, table_t, 0, D),
        (3, 0, table_t, D, 2 * D),
        (4, 0, table_t, 2 * D, CLASSES + 1),
        (4, 256, final, 2 * D, 2 * D + OUT),
        (5, 0, final, 0, D),
        (6, 0, final, D, 2 * D),
    ]


class Traffic:
    def __init__(self, places, mine, sends, recvs, locals_):
        self.places, self.mine = places, mine
        self.sends, self.recvs, self.locals = sends, recvs, locals_
        self.used = self.used_local = 0
        self.copies = []

    def remote(self, source, target_ref, digit, shift):
        target, _ = self.places.other(self.mine, digit, shift)
        at = self.used
        self.used += 1
        copy = pltpu.make_async_remote_copy(
            src_ref=source,
            dst_ref=target_ref,
            send_sem=self.sends.at[at],
            recv_sem=self.recvs.at[at],
            device_id=target,
            device_id_type=MESH,
        )
        self.copies.append(copy)
        return copy

    def local(self, source, target_ref):
        at = self.used_local
        self.used_local += 1
        return pltpu.make_async_copy(source, target_ref, self.locals.at[at])

    def ahead(self, digit, shift):
        return lax.rem(self.mine[digit] + shift, self.places.dims[digit])

    def finish(self):
        for copy in self.copies:
            copy.wait_send()


def copies_per_part(places):
    dims = places.dims
    return sum(dims) - len(dims) + max(dims) * max(dims)


def gather_job(traffic, odd, source, out):
    places, mine = traffic.places, traffic.mine
    order = places.order(odd)
    depth = len(order)
    split = depth - 2 if depth >= 4 else -1
    own = traffic.local(source, out.at[tuple(mine)])
    waits = [[] for _ in range(depth + 1)]
    starts = [[] for _ in range(depth + 1)]

    def region(done, fixed):
        return tuple(fixed.get(d, slice(None) if d in done else mine[d]) for d in range(depth))

    for stage, digit in enumerate(order):
        done = order[:stage]
        for shift in range(1, places.dims[digit]):
            pieces = [(stage, {})]
            if stage == split:
                before = order[stage - 1]
                pieces = [(stage - 1, {before: mine[before]})]
                pieces += [(stage, {before: traffic.ahead(before, k)}) for k in range(1, places.dims[before])]
            for when, fixed in pieces:
                where = region(done, fixed)
                copy = traffic.remote(source if stage == 0 else out.at[where], out.at[where], digit, shift)
                starts[when].append(copy)
                waits[stage + 1].append(copy)

    def action(k):
        if k == 0:
            own.start()
        if k == 1:
            own.wait()
        for copy in waits[k]:
            copy.wait_recv()
        for copy in starts[k]:
            copy.start()

    return [functools.partial(action, k) for k in range(depth + 1)]


def land_shapes(places, odd, block):
    route = places.order(odd)[::-1]
    depth = len(route)
    shapes = []
    for stage, digit in enumerate(route):
        left = [d for d in range(depth) if d not in route[: stage + 1]]
        shapes.append((places.dims[digit] - 1, *(places.dims[d] for d in left), *block))
    return shapes


def reduce_job(traffic, odd, source, acc, lands, out):
    places, mine = traffic.places, traffic.mine
    route = places.order(odd)[::-1]
    depth = len(route)
    split = 1 if depth >= 4 else -1
    waits = [[] for _ in range(depth + 1)]
    starts = [[] for _ in range(depth + 1)]
    adds = [[] for _ in range(depth + 1)]
    own = traffic.local(
        source.at[tuple(mine[d] if d == route[0] else slice(None) for d in range(depth))], acc
    )

    def left_of(stage):
        return [d for d in range(depth) if d not in route[: stage + 1]]

    def in_acc(values):
        return tuple(values.get(d, mine[d]) for d in range(depth) if d != route[0])

    for stage, digit in enumerate(route):
        gone = route[:stage]
        left = left_of(stage)
        pieces = [(stage + 1, {})]
        if stage == split:
            after = route[stage + 1]
            pieces = [(stage + 1, {after: traffic.ahead(after, k)}) for k in range(1, places.dims[after])]
            pieces += [(stage + 2, {after: mine[after]})]
        for when, fixed in pieces:
            for shift in range(1, places.dims[digit]):
                values = {d: slice(None) for d in left} | fixed | {digit: traffic.ahead(digit, shift)}
                if stage == 0:
                    sent = source.at[tuple(values[d] for d in range(depth))]
                else:
                    sent = acc.at[in_acc(values)]
                target = lands[stage].at[(shift - 1, *(values[d] for d in left))]
                copy = traffic.remote(sent, target, digit, shift)
                starts[stage].append(copy)
                waits[when].append(copy)
            adds[when].append((stage, fixed))

    def add(group):
        stage, fixed = group[-1]
        free = [d for d in left_of(stage) if d not in fixed]
        count = math.prod(places.dims[d] for d in free)
        last = stage == depth - 1

        def one(flat, carry):
            values = dict(fixed)
            rest = flat
            for d in reversed(free):
                values[d] = lax.rem(rest, places.dims[d])
                rest = rest // places.dims[d]
            total = acc[in_acc(values)].astype(jnp.float32)
            for near, _ in group:
                for shift in range(places.dims[route[near]] - 1):
                    index = (shift, *(values.get(d, mine[d]) for d in left_of(near)))
                    total = total + lands[near][index].astype(jnp.float32)
            if last:
                out[...] = total
            else:
                acc[in_acc(values)] = total.astype(BF)
            return carry

        lax.fori_loop(0, count, one, 0)

    def action(k):
        if k == 0:
            own.start()
        if k == 1:
            own.wait()
        for copy in waits[k]:
            copy.wait_recv()
        if k == split + 2:
            add(adds[k])
        else:
            for entry in adds[k]:
                add([entry])
        if k < depth:
            for copy in starts[k]:
                copy.start()

    return [functools.partial(action, k) for k in range(depth + 1)]


def in_waves(jobs):
    pairs = [jobs[at : at + 2] for at in range(0, len(jobs), 2)]
    depth = len(jobs[0])
    sequence = []
    for tick in range(len(pairs) + depth - 1):
        for k in range(depth):
            if 0 <= tick - k < len(pairs):
                sequence.extend(job[k] for job in pairs[tick - k])
    return sequence


def gather_kernel(places, slots, layers, *refs):
    entry_ref, table_ref, final_ref, ada_ref, attn_ref, in_ref, out_ref = refs[:7]
    chunks = slots + SPLIT + 3 * layers
    outs = refs[7 : 7 + chunks]
    small, packed, send_sems, recv_sems, own_sems = refs[7 + chunks :]
    mine = places.mine()
    small[...] = jnp.zeros_like(small)
    for k, at, source, low, high in small_blocks(entry_ref, table_ref, final_ref):
        small[k, : source.shape[0], at : at + high - low] = source[:, low:high].astype(BF)
    part = -(-ada_ref.shape[0] // SPLIT)
    for p in range(SPLIT):
        packed[p, :part, :] = ada_ref[p * part : (p + 1) * part, :].astype(BF)
    for l in range(layers):
        for k, source in enumerate((attn_ref, in_ref, out_ref)):
            packed[SPLIT + 3 * l + k, : source.shape[1], :] = source[l].astype(BF)
    first = lax.axis_index("tp") * slots
    ins = [small.at[first + s] for s in range(slots)]
    ins += [packed.at[m] for m in range(SPLIT + 3 * layers)]
    places.barrier(mine)
    traffic = Traffic(places, mine, send_sems, recv_sems, own_sems)
    jobs = [gather_job(traffic, m % 2 == 1, ins[m], outs[m]) for m in range(chunks)]
    for action in in_waves(jobs):
        action()
    traffic.finish()


def pad16(rows):
    return rows + -rows % 16


def gather_all(places, slots, entry_t, table_t, final, ada_t, attn_t, in_t, out_w):
    layers = attn_t.shape[0]
    small_rows, ada_rows = pad16(final.shape[0]), pad16(-(-ada_t.shape[0] // SPLIT))
    wide_rows = pad16(attn_t.shape[1])
    sizes = [small_rows] * slots + [ada_rows] * SPLIT + [wide_rows] * (3 * layers)
    chunks = len(sizes)
    vmem = pl.BlockSpec(memory_space=pltpu.VMEM)
    packed_rows = max(ada_rows, wide_rows)
    assert packed_rows == min(ada_rows, wide_rows)
    outs = pl.pallas_call(
        functools.partial(gather_kernel, places, slots, layers),
        out_shape=[jax.ShapeDtypeStruct((*places.dims, rows, D), BF) for rows in sizes],
        in_specs=[vmem] * 7,
        out_specs=[pl.BlockSpec(memory_space=pl.ANY)] * chunks,
        scratch_shapes=[
            pltpu.VMEM((slots * lax.axis_size("tp"), small_rows, D), BF),
            pltpu.VMEM((SPLIT + 3 * layers, packed_rows, D), BF),
            pltpu.SemaphoreType.DMA((chunks * copies_per_part(places),)),
            pltpu.SemaphoreType.DMA((chunks * copies_per_part(places),)),
            pltpu.SemaphoreType.DMA((chunks,)),
        ],
        compiler_params=pltpu.CompilerParams(collective_id=1, has_side_effects=True, vmem_limit_bytes=LIMIT),
        name="gather_weights",
    )(entry_t, table_t, final, ada_t, attn_t, in_t, out_w)
    return [o.reshape((places.count,) + o.shape[-2:]) for o in outs]


def reduce_kernel(places, chunks, slots, layers, *refs):
    ins = refs[:chunks]
    loss_ref = refs[chunks]
    square_refs = refs[chunks + 1 : chunks + 1 + layers]
    refs = refs[chunks + 1 + layers :]
    outs, both_ref, stats_ref = refs[:chunks], refs[chunks], refs[chunks + 1]
    refs = refs[chunks + 2 :]
    stats_land, stats_send, stats_recv, both_send, both_recv = refs[-5:]
    refs = refs[:-5]
    depth = len(places.dims)
    accs = refs[:chunks]
    lands = refs[chunks : chunks * (1 + depth)]
    send_sems, recv_sems, own_sems = refs[chunks * (1 + depth) :]
    mine = places.mine()
    places.barrier(mine)
    traffic = Traffic(places, mine, send_sems, recv_sems, own_sems)
    jobs = [
        reduce_job(traffic, m % 2 == 1, ins[m], accs[m], lands[m * depth : (m + 1) * depth], outs[m])
        for m in range(chunks)
    ]
    for action in in_waves(jobs):
        action()
    traffic.finish()

    def lane_sums(rows):
        total = jnp.sum(rows, axis=0, keepdims=True)
        return sum(total[:, at : at + 128] for at in range(0, total.shape[1], 128))

    grad = sum(lane_sums(out[...] * out[...]) for out in outs)
    loss = lane_sums(jnp.sum(loss_ref[...], axis=0))
    squares = [lane_sums(jnp.sum(ref[...], axis=0)) for ref in square_refs]
    stats_ref[...] = jnp.concatenate([grad, loss, *squares, jnp.zeros((6 - layers, 128), jnp.float32)], axis=0)
    for s in range(slots):
        both_ref[(lax.axis_index("tp"), s)] = outs[s][...]
    inner = [d for d in range(depth) if places.digits[d][0] == "tp"]
    for stage, digit in enumerate(reversed(range(depth))):
        size = places.dims[digit]
        axis, stride, _ = places.digits[digit]
        stats_land[stage, mine[digit]] = stats_ref[...]
        copies = []
        for shift in range(1, size):
            target, _ = places.other(mine, digit, shift)
            copies.append(
                pltpu.make_async_remote_copy(
                    src_ref=stats_ref,
                    dst_ref=stats_land.at[stage, mine[digit]],
                    send_sem=stats_send.at[stage, shift - 1],
                    recv_sem=stats_recv.at[stage, shift - 1],
                    device_id=target,
                    device_id_type=MESH,
                )
            )
            if digit in inner:
                held = stride
                start = lax.axis_index("tp") // stride * stride
                where = both_ref.at[pl.ds(start, held)]
                copies.append(
                    pltpu.make_async_remote_copy(
                        src_ref=where,
                        dst_ref=where,
                        send_sem=both_send.at[stage, shift - 1],
                        recv_sem=both_recv.at[stage, shift - 1],
                        device_id=target,
                        device_id_type=MESH,
                    )
                )
        for copy in copies:
            copy.start()
        for copy in copies:
            copy.wait()
        total = stats_land[stage, 0]
        for value in range(1, size):
            total = total + stats_land[stage, value]
        stats_ref[...] = total


def reduce_all(places, slots, parts, loss, squares):
    layers = len(squares)
    vmem = pl.BlockSpec(memory_space=pltpu.VMEM)
    chunks = len(parts)
    dims = places.dims
    depth, widest = len(dims), max(dims)
    blocks = [p.shape[1:] for p in parts]
    lands = []
    for m in range(chunks):
        lands += [pltpu.VMEM(shape, BF) for shape in land_shapes(places, m % 2 == 1, blocks[m])]
    return pl.pallas_call(
        functools.partial(reduce_kernel, places, chunks, slots, layers),
        out_shape=[jax.ShapeDtypeStruct(block, jnp.float32) for block in blocks]
        + [
            jax.ShapeDtypeStruct((lax.axis_size("tp"), slots, *blocks[0]), jnp.float32),
            jax.ShapeDtypeStruct((8, 128), jnp.float32),
        ],
        in_specs=[pl.BlockSpec(memory_space=pl.ANY)] * chunks + [vmem] * (1 + layers),
        out_specs=[vmem] * (chunks + 2),
        scratch_shapes=[pltpu.VMEM(dims[:-1] + block, BF) for block in blocks]
        + lands
        + [
            pltpu.SemaphoreType.DMA((chunks * copies_per_part(places),)),
            pltpu.SemaphoreType.DMA((chunks * copies_per_part(places),)),
            pltpu.SemaphoreType.DMA((chunks,)),
            pltpu.VMEM((depth, widest, 8, 128), jnp.float32),
            pltpu.SemaphoreType.DMA((depth, widest - 1)),
            pltpu.SemaphoreType.DMA((depth, widest - 1)),
            pltpu.SemaphoreType.DMA((depth, widest - 1)),
            pltpu.SemaphoreType.DMA((depth, widest - 1)),
        ],
        compiler_params=pltpu.CompilerParams(collective_id=2, has_side_effects=True, vmem_limit_bytes=LIMIT),
        name="reduce_gradients",
    )(*[p.reshape(dims + p.shape[1:]) for p in parts], loss, *squares)


def silu(values):
    return values * (1.0 / (1.0 + jnp.exp(-values)))


def silu_slope(values):
    gate = 1.0 / (1.0 + jnp.exp(-values))
    return gate * (1.0 + values * (1.0 - gate))


def split_low(values):
    high = values.astype(BF)
    return jnp.concatenate([high, (values - high.astype(jnp.float32)).astype(BF)], axis=0)


def block_of(refs, k):
    slots = len(refs)
    part = refs[k % slots][:, k // slots]
    return part.reshape(-1, D)


def condition_kernel(slots, lat_count, *refs):
    feat_ref, hot_ref = refs[:2]
    slot_refs = refs[2 : 2 + slots]
    ada_refs = refs[2 + slots : 2 + slots + SPLIT]
    mod_ref, fmod_ref, pre_ref, cond_ref, patch_ref, head_ref = refs[2 + slots + SPLIT :]
    entry = block_of(slot_refs, 0)
    patch_ref[...] = entry[:, :PATCH_IN]
    pre = dot_nt(feat_ref[...], entry)
    pre_ref[...] = pre
    cond = dot_nt(silu(pre).astype(BF), block_of(slot_refs, 1))
    for k in range(3):
        cond = cond + dot_nt(hot_ref[:, k * D : (k + 1) * D], block_of(slot_refs, 2 + k))
    cond_ref[...] = cond
    head_ref[...] = block_of(slot_refs, 4)[:, 256 : 256 + OUT]
    act = silu(cond).astype(BF)
    for p in range(SPLIT):
        wide = ada_refs[p].shape[0]
        mod_ref[:, p * wide : (p + 1) * wide] = dot_nt(act, ada_refs[p][...])
    for k in range(2):
        part = dot_nn(act, block_of(slot_refs, 5 + k))
        for b in range(lat_count):
            fmod_ref[b, k : k + 1, :] = part[b : b + 1, :]


def condition(feat, hot, slot_full, ada_full, lat_count):
    vmem = pl.BlockSpec(memory_space=pltpu.VMEM)
    wide = ada_full[0].shape[0]
    shapes = [
        ((8, SPLIT * wide), jnp.float32),
        ((lat_count, 8, D), jnp.float32),
        ((8, D), jnp.float32),
        ((8, D), jnp.float32),
        ((D, PATCH_IN), BF),
        ((D, OUT), BF),
    ]
    return pl.pallas_call(
        functools.partial(condition_kernel, len(slot_full), lat_count),
        out_shape=[jax.ShapeDtypeStruct(*s) for s in shapes],
        in_specs=[vmem] * (2 + len(slot_full) + SPLIT),
        out_specs=[vmem] * len(shapes),
        compiler_params=pltpu.CompilerParams(vmem_limit_bytes=LIMIT),
        name="condition",
    )(feat, hot, *slot_full, *ada_full)


def condition_back_kernel(slots, lat_count, *refs):
    feat_ref, hot_ref = refs[:2]
    slot_refs = refs[2 : 2 + slots]
    ada_refs = refs[2 + slots : 2 + slots + SPLIT]
    pre_ref, cond_ref, d_mod_ref, d_fmod_ref, d_patch_ref, d_head_ref = refs[2 + slots + SPLIT :][:6]
    outs = refs[2 + slots + SPLIT + 6 :]
    g_slots, g_ada = outs[:slots], outs[slots : slots + SPLIT]
    fmod_s = outs[slots + SPLIT]
    pre, cond = pre_ref[...], cond_ref[...]
    act = silu(cond).astype(BF)
    act_two = jnp.concatenate([act, act], axis=0)
    d_cond = jnp.zeros((16, D), jnp.float32)
    for p in range(SPLIT):
        wide = ada_refs[p].shape[0]
        d_mod = split_low(d_mod_ref[:, p * wide : (p + 1) * wide])
        d_cond = d_cond + dot_nn(d_mod, ada_refs[p][...])
        g_ada[p][...] = dot_tn(d_mod, act_two).astype(BF)

    def give(k, grad):
        ref = g_slots[k % slots]
        ref[:, k // slots] = grad.astype(BF).reshape(ref.shape[0], ref.shape[2], D)

    fmod_s[...] = jnp.zeros_like(fmod_s)
    for k in range(2):
        for b in range(lat_count):
            fmod_s[k, b : b + 1, :] = d_fmod_ref[b, k : k + 1, :]
        d_fmod = split_low(fmod_s[k])
        d_cond = d_cond + dot_nt(d_fmod, block_of(slot_refs, 5 + k))
        give(5 + k, dot_tn(act_two, d_fmod))
    d_pre = split_low((d_cond[:8] + d_cond[8:]) * silu_slope(cond))
    time_act = silu(pre).astype(BF)
    give(1, dot_tn(d_pre, jnp.concatenate([time_act, time_act], axis=0)))
    d_time = dot_nn(d_pre, block_of(slot_refs, 1))
    for k in range(3):
        hot = hot_ref[:, k * D : (k + 1) * D]
        grad = dot_tn(d_pre, jnp.concatenate([hot, hot], axis=0))
        if k == 2:
            here = jnp.pad(d_head_ref[...], ((0, 128 - OUT), (0, 0))).T
            grad = jnp.concatenate([grad[:, :256], grad[:, 256:] + here], axis=1)
        give(2 + k, grad)
    d_time = split_low((d_time[:8] + d_time[8:]) * silu_slope(pre))
    grad = dot_tn(d_time, jnp.concatenate([feat_ref[...], feat_ref[...]], axis=0))
    here = jnp.pad(d_patch_ref[...], ((0, 128 - PATCH_IN), (0, 0))).T
    give(0, jnp.concatenate([grad[:, :128] + here, grad[:, 128:]], axis=1))
    for k in range(7, SMALL):
        give(k, jnp.zeros((D, D), jnp.float32))


def condition_back(feat, hot, slot_full, ada_full, pre, cond, d_mod, d_fmod, d_patch, d_head):
    vmem = pl.BlockSpec(memory_space=pltpu.VMEM)
    lat_count = d_fmod.shape[0]
    args = (feat, hot, *slot_full, *ada_full, pre, cond, d_mod, d_fmod, d_patch, d_head)
    kept = (*slot_full, *ada_full)
    return pl.pallas_call(
        functools.partial(condition_back_kernel, len(slot_full), lat_count),
        out_shape=[jax.ShapeDtypeStruct(w.shape, BF) for w in kept],
        in_specs=[vmem] * len(args),
        out_specs=[vmem] * len(kept),
        scratch_shapes=[pltpu.VMEM((2, 8, D), jnp.float32)],
        compiler_params=pltpu.CompilerParams(vmem_limit_bytes=LIMIT),
        name="condition_back",
    )(*args)


def adam_kernel(slots, layers, count_rms, *refs):
    stats_ref, both_ref = refs[:2]
    grads = refs[2 : 2 + SPLIT + 3 * layers]
    states = refs[2 + SPLIT + 3 * layers :][:21]
    outs = refs[2 + SPLIT + 3 * layers + 21 :]
    news, (loss_ref, norm_ref, rms_ref) = outs[:21], outs[21:]
    totals = jnp.sum(stats_ref[...], axis=1, keepdims=True)
    norm = jnp.sqrt(totals[0:1])
    factor = jnp.minimum(1.0, 0.01 / (norm + 1e-06))
    loss_ref[...] = totals[1:2]
    norm_ref[...] = norm
    rms_ref[...] = jnp.sqrt(totals[2 : 2 + layers] / count_rms)
    correct = 1.0 - 0.5**STEP

    def update(name, where, grad):
        weight, first, second = (ref[where] for ref in states[3 * name : 3 * name + 3])
        clipped = grad * factor
        first_new = 0.5 * first + 0.5 * clipped
        second_new = 0.5 * second + 0.5 * clipped * clipped
        root = jnp.sqrt(second_new * (1.0 / correct)) + 1e-08
        new = weight - 0.02 * (first_new * (1.0 / correct) / root + 0.01 * weight)
        news[3 * name][where] = new
        news[3 * name + 1][where] = first_new
        news[3 * name + 2][where] = second_new

    def small(k):
        return both_ref[k // slots, k % slots]

    rows = states[0].shape[0]
    early = PATCH_IN + FREQ
    every = slice(0, rows)
    update(0, (every, slice(0, early)), small(0)[:rows, :early])
    update(0, (every, slice(early, early + D)), small(1)[:rows])
    update(1, (every, slice(0, D)), small(2)[:rows])
    update(1, (every, slice(D, 2 * D)), small(3)[:rows])
    update(1, (every, slice(2 * D, CLASSES + 1)), small(4)[:rows, : CLASSES + 1 - 2 * D])
    update(6, (every, slice(0, D)), small(5)[:rows])
    update(6, (every, slice(D, 2 * D)), small(6)[:rows])
    update(6, (every, slice(2 * D, 2 * D + OUT)), small(4)[:rows, 256 : 256 + OUT])
    part = -(-states[15].shape[0] // SPLIT)
    for p in range(SPLIT):
        update(5, (slice(p * part, (p + 1) * part), slice(0, D)), grads[p][:part])
    for l in range(layers):
        for k in range(3):
            update(2 + k, (l, slice(0, states[6].shape[1]), slice(0, D)), grads[SPLIT + 3 * l + k][: states[6].shape[1]])


def adam_all(slots, layers, count_rms, stats, both, grads, states):
    vmem = pl.BlockSpec(memory_space=pltpu.VMEM)
    args = (stats, both, *grads, *states)
    return pl.pallas_call(
        functools.partial(adam_kernel, slots, layers, count_rms),
        out_shape=[jax.ShapeDtypeStruct(s.shape, jnp.float32) for s in states]
        + [jax.ShapeDtypeStruct((n, 1), jnp.float32) for n in (1, 1, layers)],
        in_specs=[vmem] * len(args),
        out_specs=[vmem] * 24,
        compiler_params=pltpu.CompilerParams(vmem_limit_bytes=LIMIT),
        name="adam",
    )(*args)


def modulation_pieces(layers, ada_rows, part_rows, count):
    pieces = []
    for j in range(count):
        for l in range(layers):
            low = l * ada_rows
            while low < (l + 1) * ada_rows:
                p, r = divmod(low, part_rows)
                length = min((l + 1) * ada_rows - low, part_rows - r)
                pieces.append((l, j * ada_rows + low - l * ada_rows, p, j * part_rows + r, length))
                low += length
    return pieces


def embed_condition(slots, lat_count, feat_ref, hot_ref, slot_refs, pre_ref, cond_ref, fmod_ref):
    pre = dot_nt(feat_ref[...], block_of(slot_refs, 0))
    pre_ref[...] = pre
    cond = dot_nt(silu(pre).astype(BF), block_of(slot_refs, 1))
    for k in range(3):
        cond = cond + dot_nt(hot_ref[:, k * D : (k + 1) * D], block_of(slot_refs, 2 + k))
    cond_ref[...] = cond
    act = silu(cond).astype(BF)
    for k in range(2):
        fmod_ref[:, k * D : (k + 1) * D] = dot_nn(act, block_of(slot_refs, 5 + k))


def mod_rows(mod_ref, index, n, nb, part):
    rows = [mod_ref[(*index, pl.ds(n * nb + b, 1), slice(part * D, (part + 1) * D))] for b in range(nb)]
    return jnp.stack(rows, axis=0)


def attend_forward(nb, tokens, stream, mod, attn_w, out_w, qkv_ref, probs_ref, mixed_ref, branch_ref):
    rows = nb * tokens
    hat, _ = norm_rows(stream)
    attn_in = (hat * (1.0 + mod(1)) + mod(0)).astype(BF).reshape(rows, D)
    qkv_ref[...] = dot_nt(attn_in, attn_w[...]).astype(BF)
    masks = half_masks()
    for b in range(nb):
        here = slice(b * tokens, (b + 1) * tokens)
        for pair in range(HEADS // 2):
            col = pair * 2 * HEAD_DIM
            queries = qkv_ref[here, col : col + 2 * HEAD_DIM] * jnp.asarray(HEAD_DIM**-0.5, BF)
            keys = stack_heads(qkv_ref[here, D + col : D + col + 2 * HEAD_DIM], masks)
            values = stack_heads(qkv_ref[here, 2 * D + col : 2 * D + col + 2 * HEAD_DIM], masks)
            scores = dot_nt(queries, keys)
            halves = []
            for side in range(2):
                part = scores[:, side * tokens : (side + 1) * tokens]
                grown = jnp.exp(part - jnp.max(part, axis=-1, keepdims=True))
                halves.append((grown * (1.0 / jnp.sum(grown, axis=-1, keepdims=True))).astype(BF))
            probs = jnp.concatenate(halves, axis=1)
            probs_ref[here, pair * 2 * tokens : (pair + 1) * 2 * tokens] = probs
            mixed_ref[here, col : col + 2 * HEAD_DIM] = dot_nn(probs, values).astype(BF)
    branch = dot_nt(mixed_ref[...], out_w[...])
    branch_ref[...] = branch.astype(BF)
    return stream + mod(2) * branch.reshape(nb, tokens, D)


def feed_forward(nb, tokens, middle, mod, in_w, out_w, mlp_ref, act_ref, slope_ref):
    rows = nb * tokens
    hat, _ = norm_rows(middle)
    mlp_in = (hat * (1.0 + mod(4)) + mod(3)).astype(BF).reshape(rows, D)
    hidden = dot_nt(mlp_in, in_w[...])
    squared = hidden * hidden
    bent = jnp.tanh(hidden * (GELU_A + (GELU_A * GELU_B) * squared))
    half = 0.5 * hidden
    act = (half + half * bent).astype(BF)
    act_ref[...] = act
    slope_ref[...] = (
        0.5
        + 0.5 * bent
        + half * (1.0 - bent * bent) * (GELU_A + (3.0 * GELU_A * GELU_B) * squared)
    ).astype(BF)
    mlp = dot_nn(act, out_w[...])
    mlp_ref[...] = mlp.astype(BF)
    return middle + mod(5) * mlp.reshape(nb, tokens, D)


def waves(jobs):
    pairs = [jobs[at : at + 2] for at in range(0, len(jobs), 2)]
    depth = len(jobs[0])
    ticks = []
    for tick in range(len(pairs) + depth - 1):
        ticks.append(
            [job[k] for k in range(depth) if 0 <= tick - k < len(pairs) for job in pairs[tick - k]]
        )
    return ticks


def fused_forward_kernel(places, slots, layers, nb, tokens, lat_count, sizes, *refs):
    small_rows, ada_rows, part_rows, wide_rows = sizes
    chunks = slots + SPLIT + 3 * layers
    entry_ref, table_ref, final_ref, ada_ref, attn_ref, in_ref, out_ref = refs[:7]
    feat_ref, hot_ref, noisy_ref, pos_ref = refs[7:11]
    given = refs[11 : 11 + chunks]
    (
        mods_ref,
        fmod_ref,
        pre_ref,
        cond_ref,
        start_ref,
        result_ref,
        qkv_ref,
        probs_ref,
        mixed_ref,
        branch_ref,
        middle_ref,
        mlp_ref,
        act_ref,
        slope_ref,
        square_ref,
    ) = refs[11 + chunks : 26 + chunks]
    refs = refs[26 + chunks :]
    fulls = refs[:chunks]
    small, packed, stream_s, middle_s, send_sems, recv_sems, own_sems, give_sems = refs[chunks:]
    l, h, n = (pl.program_id(axis) for axis in range(3))
    mine = places.mine()
    first = lax.axis_index("tp") * slots
    order = [*range(slots), slots, slots + 1, slots + SPLIT, slots + SPLIT + 1, slots + SPLIT + 2, slots + 2]
    order += range(slots + SPLIT + 3, chunks)
    sources = [small.at[first + s] for s in range(slots)] + [packed.at[m] for m in range(SPLIT + 3 * layers)]
    traffic = Traffic(places, mine, send_sems, recv_sems, own_sems)
    jobs = [gather_job(traffic, at % 2 == 1, sources[m], fulls[m]) for at, m in enumerate(order)]
    ticks = waves(jobs)
    handed = [
        pltpu.make_async_copy(fulls[m], given[m], give_sems.at[m]) for m in range(chunks)
    ]

    def flat(m, rows):
        return fulls[m].reshape(places.count * rows, D)

    def run(numbers):
        for tick in numbers:
            for action in ticks[tick]:
                action()

    def at_step(layer, half, step):
        return pl.when((l == layer) & (h == half) & (n == step))

    def set_mods(layer):
        act = silu(cond_ref[...]).astype(BF)
        low, high = layer * ada_rows, (layer + 1) * ada_rows
        parts = range(low // part_rows, -(-high // part_rows))
        raw = {p: dot_nt(act, flat(slots + p, part_rows)[...]) for p in parts}
        for ll, col, p, at, length in modulation_pieces(layers, ada_rows, part_rows, places.count):
            if ll == layer:
                mods_ref[layer, :, col : col + length] = raw[p][:, at : at + length]

    slot_refs = [f.reshape(-1, lax.axis_size("tp"), small_rows, D) for f in fulls[:slots]]
    last = len(ticks) - 1

    @at_step(0, 0, 0)
    def _():
        small[...] = jnp.zeros_like(small)
        for k, at, source, low, high in small_blocks(entry_ref, table_ref, final_ref):
            small[k, : source.shape[0], at : at + high - low] = source[:, low:high].astype(BF)
        for p in range(SPLIT):
            packed[p] = ada_ref[p * part_rows : (p + 1) * part_rows, :].astype(BF)
        for ll in range(layers):
            for k, source in enumerate((attn_ref, in_ref, out_ref)):
                packed[SPLIT + 3 * ll + k] = source[ll].astype(BF)
        places.barrier(mine)
        run(range(6))
        embed_condition(slots, lat_count, feat_ref, hot_ref, slot_refs, pre_ref, cond_ref, fmod_ref)
        set_mods(0)
        run([6])

    @at_step(0, 1, 0)
    def _():
        run([7])

    @at_step(1, 0, 0)
    def _():
        run([8])
        for layer in range(1, layers):
            set_mods(layer)

    @at_step(1, 1, 0)
    def _():
        run(range(9, last + 1))
        for copy in handed:
            copy.start()

    rows = nb * tokens
    here = pl.ds(pl.multiple_of(n * rows, rows), rows)

    def weight(layer, k):
        return flat(slots + SPLIT + 3 * layer + k, wide_rows)

    for layer in range(layers):
        mod = lambda part, layer=layer: mod_rows(mods_ref, (layer,), n, nb, part)

        @pl.when((l == layer) & (h == 0))
        def _(layer=layer, mod=mod):
            if layer == 0:
                patch = block_of(slot_refs, 0)[:, :PATCH_IN]
                parts = [
                    lax.dot_general(
                        noisy_ref[b], patch, (((0,), (1,)), ((), ())), preferred_element_type=jnp.float32
                    )
                    + pos_ref[...]
                    for b in range(nb)
                ]
                stream = parts[0] if nb == 1 else jnp.concatenate(parts, axis=0)
                start_ref[...] = stream
            else:
                stream = stream_s[here, :]
            stream = stream.reshape(nb, tokens, D)
            middle = attend_forward(
                nb,
                tokens,
                stream,
                mod,
                weight(layer, 0).at[: 3 * D],
                weight(layer, 0).at[3 * D :],
                qkv_ref.at[0],
                probs_ref.at[0],
                mixed_ref.at[0],
                branch_ref.at[0],
            )
            middle_ref[0] = middle.reshape(rows, D)
            middle_s[here, :] = middle.reshape(rows, D)

        @pl.when((l == layer) & (h == 1))
        def _(layer=layer, mod=mod):
            middle = middle_s[here, :].reshape(nb, tokens, D)
            result = feed_forward(
                nb,
                tokens,
                middle,
                mod,
                weight(layer, 1),
                weight(layer, 2),
                mlp_ref.at[0],
                act_ref.at[0],
                slope_ref.at[0],
            )
            result_ref[0] = result.reshape(rows, D)
            if layer < layers - 1:
                stream_s[here, :] = result.reshape(rows, D)
            square_ref[0, 0] = jnp.sum((result * result).reshape(rows // 8, 8, D), axis=0)

    @at_step(layers - 1, 1, lat_count // nb - 1)
    def _():
        for copy in handed:
            copy.wait()
        traffic.finish()


def fused_forward(places, slots, nb, weights_in, feat, hot, noisy, pos):
    entry_t, table_t, final, ada_t, attn_t, in_t, out_w = weights_in
    layers, wide_rows = attn_t.shape[:2]
    lat_count, _, tokens = noisy.shape
    small_rows, part_rows, ada_rows = final.shape[0], ada_t.shape[0] // SPLIT, ada_t.shape[0] // layers
    sizes = [small_rows] * slots + [part_rows] * SPLIT + [wide_rows] * (3 * layers)
    chunks = len(sizes)
    steps = lat_count // nb
    rows, total = nb * tokens, lat_count * tokens
    full_shapes = [(*places.dims, r, D) for r in sizes]

    def const(array):
        return pl.BlockSpec(array.shape, lambda l, h, n: (0,) * array.ndim)

    def const_shape(shape):
        return pl.BlockSpec(shape, lambda l, h, n: (0,) * len(shape))

    def early(l, h, n):
        return jnp.where(h == 0, n, steps - 1)

    def half_one(cols):
        return pl.BlockSpec((1, rows, cols), lambda l, h, n: (l, early(l, h, n), 0))

    def half_two(cols):
        def index(l, h, n):
            before = jnp.where(l == 0, 0, steps - 1)
            return (jnp.where(h == 0, jnp.maximum(l - 1, 0), l), jnp.where(h == 0, before, n), 0)

        return pl.BlockSpec((1, rows, cols), index)

    def square_index(l, h, n):
        before = jnp.where(l == 0, 0, steps - 1)
        return (jnp.where(h == 0, jnp.maximum(l - 1, 0), l), jnp.where(h == 0, before, n), 0, 0)

    out_shape = [jax.ShapeDtypeStruct(s, BF) for s in full_shapes]
    out_specs = [pl.BlockSpec(memory_space=pl.ANY)] * chunks

    def add(shape, kind, spec):
        out_shape.append(jax.ShapeDtypeStruct(shape, kind))
        out_specs.append(spec)

    for shape in ((layers, 8, 6 * D), (8, 2 * D), (8, D), (8, D)):
        add(shape, jnp.float32, const_shape(shape))
    add(
        (total, D),
        jnp.float32,
        pl.BlockSpec((rows, D), lambda l, h, n: (jnp.where((l == 0) & (h == 0), n, steps - 1), 0)),
    )
    add((layers, total, D), jnp.float32, half_two(D))
    for cols, kind in ((3 * D, BF), (HEADS * tokens, BF), (D, BF), (D, BF), (D, jnp.float32)):
        add((layers, total, cols), kind, half_one(cols))
    for cols in (D, 4 * D, 4 * D):
        add((layers, total, cols), BF, half_two(cols))
    add((layers, steps, 8, D), jnp.float32, pl.BlockSpec((1, 1, 8, D), square_index))
    args = (*weights_in, feat, hot, noisy, pos)
    in_specs = [const(a) for a in args[:-2]]
    in_specs.append(
        pl.BlockSpec(
            (nb, PATCH_IN, tokens), lambda l, h, n: (jnp.where((l == 0) & (h == 0), n, steps - 1), 0, 0)
        )
    )
    in_specs.append(const(pos))
    count = chunks * copies_per_part(places)
    return pl.pallas_call(
        functools.partial(
            fused_forward_kernel,
            places,
            slots,
            layers,
            nb,
            tokens,
            lat_count,
            (small_rows, ada_rows, part_rows, wide_rows),
        ),
        grid=(layers, 2, steps),
        out_shape=out_shape,
        in_specs=in_specs,
        out_specs=out_specs,
        scratch_shapes=[pltpu.VMEM(s, BF) for s in full_shapes]
        + [
            pltpu.VMEM((slots * lax.axis_size("tp"), small_rows, D), BF),
            pltpu.VMEM((SPLIT + 3 * layers, wide_rows, D), BF),
            pltpu.VMEM((total, D), jnp.float32),
            pltpu.VMEM((total, D), jnp.float32),
            pltpu.SemaphoreType.DMA((count,)),
            pltpu.SemaphoreType.DMA((count,)),
            pltpu.SemaphoreType.DMA((chunks,)),
            pltpu.SemaphoreType.DMA((chunks,)),
        ],
        compiler_params=pltpu.CompilerParams(
            collective_id=3, has_side_effects=True, vmem_limit_bytes=LIMIT
        ),
        name="gather_and_forward",
    )(*args)


def position_table(grid_side, columns):
    quarter = columns // 4
    omegas = jnp.exp(-math.log(10000.0) * jnp.arange(quarter, dtype=jnp.float32) / quarter)
    positions = jnp.arange(grid_side * grid_side, dtype=jnp.int32)
    row_pos = (positions // grid_side).astype(jnp.float32)[:, None] * omegas
    col_pos = (positions % grid_side).astype(jnp.float32)[:, None] * omegas
    return jnp.concatenate(
        [jnp.sin(row_pos), jnp.cos(row_pos), jnp.sin(col_pos), jnp.cos(col_pos)], axis=-1
    )


def time_table(step_ids, columns):
    half_cols = columns // 2
    frequency = jnp.exp(-math.log(10000.0) * jnp.arange(half_cols, dtype=jnp.float32) / half_cols)
    angles = step_ids.astype(jnp.float32)[:, None] * frequency
    return jnp.concatenate([jnp.cos(angles), jnp.sin(angles)], axis=-1)


def noise_scales(step_ids):
    phases = (step_ids.astype(jnp.float32) / NOISE_STEPS + 0.008) / 1.008 * (math.pi / 2)
    return (jnp.cos(phases), jnp.sin(phases))


def swap(array):
    return jnp.swapaxes(array, -1, -2)


def pad_rows(part):
    extra = -part.shape[-2] % 16
    if extra == 0:
        return part
    return jnp.pad(part, [(0, 0)] * (part.ndim - 2) + [(0, extra), (0, 0)])


def body(
    clean_latents,
    noise_field,
    timesteps,
    labels,
    drop_flags,
    entry_weight,
    class_table,
    attn_weight,
    ffn_in_weight,
    ffn_out_weight,
    ada_weight,
    final_weight,
    entry_first,
    entry_second,
    class_first,
    class_second,
    attn_first,
    attn_second,
    ffn_in_first,
    ffn_in_second,
    ffn_out_first,
    ffn_out_second,
    ada_first,
    ada_second,
    final_first,
    final_second,
):
    lat_count = clean_latents.shape[0]
    tokens = clean_latents.shape[1]
    layers = attn_weight.shape[0]
    both = ("dp", "tp")
    devices = lax.axis_size("dp") * lax.axis_size("tp")
    count_all = float(lat_count * devices * tokens * OUT)
    count_rms = float(lat_count * devices * tokens * D)
    nb = 1
    clean_t, noise_t = swap(clean_latents), swap(noise_field)
    cos_part, sin_part = noise_scales(timesteps)
    noisy = (cos_part[:, None, None] * clean_t + sin_part[:, None, None] * noise_t).astype(BF)
    n_dp, n_tp = lax.axis_size("dp"), lax.axis_size("tp")
    places = Places(n_dp, n_tp)
    slots = -(-SMALL // n_tp)
    dp_rows = final_weight.shape[0]
    wide_rows = attn_weight.shape[2]
    ada_rows = ada_weight.shape[2]
    part_rows = -(-layers * ada_rows // SPLIT)

    def flat_ada(array):
        return swap(array).reshape(layers * ada_rows, D)

    weights_in = (
        swap(entry_weight),
        swap(class_table),
        final_weight,
        flat_ada(ada_weight),
        swap(attn_weight),
        swap(ffn_in_weight),
        ffn_out_weight,
    )
    def whole_rows(block, rows):
        return block[:, :rows].reshape(-1, D)

    def to_slot(block):
        if dp_rows % 16 == 0:
            return block.reshape(n_dp, n_tp, dp_rows, D)
        block = block.reshape(n_dp, n_tp, -1, D)[:, :, :dp_rows]
        return block.swapaxes(0, 1).reshape(1, n_tp, n_dp * dp_rows, D)

    def from_slot(block):
        if dp_rows % 16 == 0:
            return block.reshape(places.count, dp_rows, D)
        block = block.reshape(n_tp, n_dp, dp_rows, D).swapaxes(0, 1)
        return pad_rows(block.reshape(places.count, dp_rows, D))

    time_feat = time_table(timesteps, FREQ).astype(BF)
    feat = jnp.pad(time_feat, ((0, 8 - lat_count), (PATCH_IN, D - PATCH_IN - FREQ)))
    classes_used = jnp.where(drop_flags == 1, CLASSES, labels)
    classes_used = jnp.pad(classes_used, (0, 8 - lat_count), constant_values=3 * D)
    class_hot = (classes_used[:, None] == jnp.arange(3 * D, dtype=jnp.int32)[None, :]).astype(BF)
    pos = position_table(GRID, D)
    fused = dp_rows == wide_rows == part_rows and dp_rows % 16 == 0 and len(places.dims) >= 4 and layers == 2
    if fused:
        outs = fused_forward(places, slots, nb, weights_in, feat, class_hot, noisy, pos)
        gathered = [o.reshape((places.count,) + o.shape[-2:]) for o in outs[: slots + SPLIT + 3 * layers]]
        mods_all, fmod_all, pre, cond, start, result, *kept, square = outs[slots + SPLIT + 3 * layers :]
    else:
        gathered = gather_all(places, slots, *weights_in)
    slot_full = [to_slot(g) for g in gathered[:slots]]
    ada_full = [whole_rows(g, part_rows) for g in gathered[slots : slots + SPLIT]]
    block_full = [whole_rows(g, wide_rows) for g in gathered[slots + SPLIT :]]
    weights = [tuple(block_full[3 * l : 3 * l + 3]) for l in range(layers)]

    if fused:
        mods = jnp.pad(mods_all[:, :lat_count].reshape(layers, lat_count, 6, D), ((0, 0), (0, 0), (0, 2), (0, 0)))
        fmod = jnp.pad(fmod_all[:lat_count].reshape(lat_count, 2, D), ((0, 0), (0, 6), (0, 0)))
        head = slot_full[4 % slots][:, 4 // slots].reshape(D, D)[:, 256 : 256 + OUT]
        saved = [(start if l == 0 else (result, l - 1), *((k, l) for k in kept)) for l in range(layers)]
        stream = (result, layers - 1)
        squares = [square[l] for l in range(layers)]
    else:
        raw, fmod, pre, cond, patch_t, head = condition(feat, class_hot, slot_full, ada_full, lat_count)
        mods = raw[:lat_count].reshape(lat_count, SPLIT, places.count, part_rows).swapaxes(1, 2)
        mods = mods.reshape(lat_count, places.count, layers, ada_rows).transpose(2, 0, 1, 3)
        mods = mods.reshape(layers, lat_count, 6, D)
        mods = jnp.pad(mods, ((0, 0), (0, 0), (0, 2), (0, 0)))
        mods = [mods[l] for l in range(layers)]
        saved = []
        squares = []
        stream = None
        for l in range(layers):
            if l == 0:
                outs = forward_layer(True, (noisy, patch_t, pos), mods[l], weights[l], nb, tokens)
                stream, outs = outs[0], outs[1:]
            else:
                outs = forward_layer(False, (stream,), mods[l], weights[l], nb, tokens)
            saved.append((stream, *outs[1:9]))
            stream = outs[0]
            squares.append(outs[9])
    layer_grads = [None] * layers
    d_mods = [None] * layers
    d_stream = None
    for l in reversed(range(layers)):
        last, first = l == layers - 1, l == 0
        entry_args = (stream, fmod, head, clean_t, noise_t) if last else (d_stream,)
        if first:
            entry_args = (*entry_args, noisy)
        outs = list(backward_layer(first, last, entry_args, mods[l], weights[l], saved[l], nb, tokens, count_all))
        if last:
            loss_part, d_head_t, d_fmod = outs[:3]
            outs = outs[3:]
        if first:
            d_patch = outs[0]
        else:
            d_stream = outs[0]
        layer_grads[l] = outs[1:4]
        d_mods[l] = outs[4]
    d_raw = jnp.stack([d[:, :6] for d in d_mods]).reshape(layers, lat_count, places.count, ada_rows)
    d_raw = d_raw.transpose(1, 2, 0, 3).reshape(lat_count, places.count, SPLIT, part_rows)
    d_raw = d_raw.swapaxes(1, 2).reshape(lat_count, -1)
    d_raw = jnp.pad(d_raw, ((0, 8 - lat_count), (0, 0)))
    small_grads = condition_back(
        feat, class_hot, slot_full, ada_full, pre, cond, d_raw, d_fmod, d_patch, d_head_t
    )
    grads = [from_slot(g) for g in small_grads[:slots]]
    grads += [pad_rows(g.reshape(places.count, part_rows, D)) for g in small_grads[slots:]]
    for l in reversed(range(layers)):
        for k in range(3):
            grads.append(pad_rows(layer_grads[l][k].reshape(places.count, wide_rows, D)))
    *summed, both, stats = reduce_all(places, slots, grads, loss_part, squares)
    wide = summed[slots + SPLIT :]
    wide = [wide[3 * (layers - 1 - l) + k] for l in range(layers) for k in range(3)]
    states = []
    for shape_it, triple in (
        (swap, (entry_weight, entry_first, entry_second)),
        (swap, (class_table, class_first, class_second)),
        (swap, (attn_weight, attn_first, attn_second)),
        (swap, (ffn_in_weight, ffn_in_first, ffn_in_second)),
        (lambda a: a, (ffn_out_weight, ffn_out_first, ffn_out_second)),
        (flat_ada, (ada_weight, ada_first, ada_second)),
        (lambda a: a, (final_weight, final_first, final_second)),
    ):
        states.extend(shape_it(a) for a in triple)
    out = adam_all(slots, layers, count_rms, stats, both, [*summed[slots : slots + SPLIT], *wide], states)
    news = []
    for at in range(21):
        value = out[at]
        if at // 3 == 5:
            value = value.reshape(layers, ada_rows, D)
        news.append(value if at // 3 in (4, 6) else swap(value))
    return (*news, out[21].reshape(()), out[22].reshape(()), out[23].reshape(layers))


def solution(mesh):
    lead = P(("dp", "tp"), None, None)
    ids = P(("dp", "tp"))
    wide = P(None, "dp")
    cols = P(None, None, ("dp", "tp"))
    rows = P(None, ("dp", "tp"), None)
    top = P("dp", None)
    return jax.shard_map(
        body,
        mesh=mesh,
        in_specs=(
            lead,
            lead,
            ids,
            ids,
            ids,
            wide,
            wide,
            cols,
            cols,
            rows,
            cols,
            top,
            wide,
            wide,
            wide,
            wide,
            cols,
            cols,
            cols,
            cols,
            rows,
            rows,
            cols,
            cols,
            top,
            top,
        ),
        out_specs=(wide,) * 6 + (cols,) * 6 + (rows,) * 3 + (cols,) * 3 + (top,) * 3 + (P(), P(), P()),
        check_vma=False,
    )
```

```python
import functools
import math

import jax
import jax.numpy as jnp
from jax import lax
from jax.experimental import pallas as pl
from jax.experimental.pallas import tpu as pltpu
from jax.sharding import PartitionSpec as P

D = 384
HEADS = 6
HEAD_DIM = 64
CLASSES = 1000
GRID = 16
PATCH_IN = 16
OUT = 32
FREQ = 256
NOISE_STEPS = 1000
STEP = 10
BF = jnp.bfloat16


highest = lax.Precision.HIGHEST


def dot_nn(a, b):
    return lax.dot_general(a, b, (((1,), (0,)), ((), ())), preferred_element_type=jnp.float32)


def dot_nt(a, b):
    return lax.dot_general(a, b, (((1,), (1,)), ((), ())), preferred_element_type=jnp.float32)


def dot_tn(a, b):
    return lax.dot_general(a, b, (((0,), (0,)), ((), ())), preferred_element_type=jnp.float32)


def norm_rows(rows):
    center = rows - jnp.mean(rows, axis=-1, keepdims=True)
    rstd = lax.rsqrt(jnp.mean(center * center, axis=-1, keepdims=True) + 1e-06)
    return center * rstd, rstd


def norm_back(d_out, hat, rstd, scale):
    d_shift = jnp.sum(d_out, axis=1, keepdims=True)
    d_scale = jnp.sum(d_out * hat, axis=1, keepdims=True)
    d_hat = d_out * (1.0 + scale)
    m_one = jnp.mean(d_hat, axis=-1, keepdims=True)
    m_two = jnp.mean(d_hat * hat, axis=-1, keepdims=True)
    return rstd * (d_hat - m_one - hat * m_two), d_shift, d_scale


def half_masks():
    lane = lax.broadcasted_iota(jnp.int32, (1, 2 * HEAD_DIM), 1)
    low = jnp.where(lane < HEAD_DIM, 1.0, 0.0)
    return low.astype(BF), (1.0 - low).astype(BF)


def stack_heads(pair, masks):
    return jnp.concatenate([pair * masks[0], pair * masks[1]], axis=0)


GELU_A = math.sqrt(2.0 / math.pi)
GELU_B = 0.044715


def forward_kernel(first, nb, tokens, *refs):
    if first:
        noisy_ref, patch_ref, pos_ref = refs[:3]
        refs = refs[3:]
    else:
        stream_ref = refs[0]
        refs = refs[1:]
    mod_ref, attn_ref, in_ref, out_ref = refs[:4]
    refs = refs[4:]
    if first:
        start_ref = refs[0]
        refs = refs[1:]
    (
        result_ref,
        qkv_ref,
        probs_ref,
        mixed_ref,
        branch_ref,
        middle_ref,
        mlp_ref,
        act_ref,
        slope_ref,
        square_ref,
    ) = refs
    rows = nb * tokens
    if first:
        parts = [
            lax.dot_general(
                noisy_ref[n], patch_ref[...], (((0,), (1,)), ((), ())), preferred_element_type=jnp.float32
            )
            + pos_ref[...]
            for n in range(nb)
        ]
        stream = parts[0] if nb == 1 else jnp.concatenate(parts, axis=0)
        start_ref[...] = stream
    else:
        stream = stream_ref[...]
    mod = mod_ref[...]
    stream = stream.reshape(nb, tokens, D)
    hat, _ = norm_rows(stream)
    attn_in = (hat * (1.0 + mod[:, 1:2]) + mod[:, 0:1]).astype(BF).reshape(rows, D)
    qkv_ref[...] = dot_nt(attn_in, attn_ref[: 3 * D, :]).astype(BF)
    masks = half_masks()
    for n in range(nb):
        here = slice(n * tokens, (n + 1) * tokens)
        for pair in range(HEADS // 2):
            col = pair * 2 * HEAD_DIM
            queries = qkv_ref[here, col : col + 2 * HEAD_DIM] * jnp.asarray(HEAD_DIM**-0.5, BF)
            keys = stack_heads(qkv_ref[here, D + col : D + col + 2 * HEAD_DIM], masks)
            values = stack_heads(qkv_ref[here, 2 * D + col : 2 * D + col + 2 * HEAD_DIM], masks)
            scores = dot_nt(queries, keys)
            halves = []
            for side in range(2):
                part = scores[:, side * tokens : (side + 1) * tokens]
                grown = jnp.exp(part - jnp.max(part, axis=-1, keepdims=True))
                halves.append((grown * (1.0 / jnp.sum(grown, axis=-1, keepdims=True))).astype(BF))
            probs = jnp.concatenate(halves, axis=1)
            probs_ref[here, pair * 2 * tokens : (pair + 1) * 2 * tokens] = probs
            mixed_ref[here, col : col + 2 * HEAD_DIM] = dot_nn(probs, values).astype(BF)
    branch = dot_nt(mixed_ref[...], attn_ref[3 * D :, :])
    branch_ref[...] = branch.astype(BF)
    middle = stream + mod[:, 2:3] * branch.reshape(nb, tokens, D)
    middle_ref[...] = middle.reshape(rows, D)
    hat, _ = norm_rows(middle)
    mlp_in = (hat * (1.0 + mod[:, 4:5]) + mod[:, 3:4]).astype(BF).reshape(rows, D)
    hidden = dot_nt(mlp_in, in_ref[...])
    squared = hidden * hidden
    bent = jnp.tanh(hidden * (GELU_A + (GELU_A * GELU_B) * squared))
    half = 0.5 * hidden
    act = (half + half * bent).astype(BF)
    act_ref[...] = act
    slope_ref[...] = (
        0.5
        + 0.5 * bent
        + half * (1.0 - bent * bent) * (GELU_A + (3.0 * GELU_A * GELU_B) * squared)
    ).astype(BF)
    mlp = dot_nn(act, out_ref[...])
    mlp_ref[...] = mlp.astype(BF)
    result = middle + mod[:, 5:6] * mlp.reshape(nb, tokens, D)
    result_ref[...] = result.reshape(rows, D)
    square_ref[0] = jnp.sum((result * result).reshape(rows // 8, 8, D), axis=0)


def backward_kernel(first, last, nb, tokens, steps, count_all, *refs):
    if last:
        final_ref, fmod_ref, head_ref, clean_ref, noise_ref = refs[:5]
        refs = refs[5:]
    else:
        d_stream_ref = refs[0]
        refs = refs[1:]
    if first:
        noisy_ref = refs[0]
        refs = refs[1:]
    (
        mod_ref,
        attn_ref,
        in_ref,
        out_ref,
        stream_ref,
        qkv_ref,
        probs_ref,
        mixed_ref,
        branch_ref,
        middle_ref,
        mlp_ref,
        act_ref,
        slope_ref,
    ) = refs[:13]
    refs = refs[13:]
    if last:
        loss_ref, dhead_ref, dfmod_ref = refs[:3]
        refs = refs[3:]
    if first:
        dpatch_ref = refs[0]
    else:
        d_prev_ref = refs[0]
    gattn_ref, gin_ref, gout_ref, dmod_ref, acc_attn, acc_in, acc_out, d_qkv_s = refs[1:]
    rows = nb * tokens
    step = pl.program_id(0)

    @pl.when(step == 0)
    def _():
        acc_attn[...] = jnp.zeros_like(acc_attn)
        acc_in[...] = jnp.zeros_like(acc_in)
        acc_out[...] = jnp.zeros_like(acc_out)
        if last:
            dhead_ref[...] = jnp.zeros_like(dhead_ref)
        if first:
            dpatch_ref[...] = jnp.zeros_like(dpatch_ref)

    mod = mod_ref[...]
    if last:
        fmod = fmod_ref[...]
        hat, rstd = norm_rows(final_ref[...].reshape(nb, tokens, D))
        final_in = (hat * (1.0 + fmod[:, 1:2]) + fmod[:, 0:1]).astype(BF)
        d_parts = []
        loss = jnp.zeros((8, tokens), jnp.float32)
        for n in range(nb):
            predicted = lax.dot_general(
                head_ref[...], final_in[n], (((0,), (1,)), ((), ())), preferred_element_type=jnp.float32
            )
            errors = predicted - jnp.concatenate([noise_ref[n], clean_ref[n]], axis=0)
            loss = loss + jnp.sum((errors * errors).reshape(OUT // 8, 8, tokens), axis=0)
            d_pred = (errors * (2.0 / count_all)).astype(BF)
            dhead_ref[...] += dot_nn(d_pred, final_in[n])
            d_parts.append(
                lax.dot_general(
                    d_pred, head_ref[...], (((0,), (1,)), ((), ())), preferred_element_type=jnp.float32
                )
            )
        loss_ref[0] = loss
        d_final = jnp.stack(d_parts, axis=0)
        d_stream, d_shift, d_scale = norm_back(d_final, hat, rstd, fmod[:, 1:2])
        dfmod_ref[:, 0:1] = d_shift
        dfmod_ref[:, 1:2] = d_scale
    else:
        d_stream = d_stream_ref[...].reshape(nb, tokens, D)
    dmod_ref[:, 5:6] = jnp.sum(d_stream * mlp_ref[...].astype(jnp.float32).reshape(nb, tokens, D), axis=1, keepdims=True)
    d_mlp = (d_stream * mod[:, 5:6]).astype(BF).reshape(rows, D)
    d_hidden = (dot_nt(d_mlp, out_ref[...]) * slope_ref[...].astype(jnp.float32)).astype(BF)
    acc_out[...] += dot_tn(act_ref[...], d_mlp)
    hat, rstd = norm_rows(middle_ref[...].reshape(nb, tokens, D))
    mlp_in = (hat * (1.0 + mod[:, 4:5]) + mod[:, 3:4]).astype(BF).reshape(rows, D)
    acc_in[...] += dot_tn(d_hidden, mlp_in)
    d_input = dot_nn(d_hidden, in_ref[...]).reshape(nb, tokens, D)
    d_middle, d_shift, d_scale = norm_back(d_input, hat, rstd, mod[:, 4:5])
    dmod_ref[:, 3:4] = d_shift
    dmod_ref[:, 4:5] = d_scale
    d_middle = d_middle + d_stream
    dmod_ref[:, 2:3] = jnp.sum(
        d_middle * branch_ref[...].astype(jnp.float32).reshape(nb, tokens, D), axis=1, keepdims=True
    )
    d_proj = (d_middle * mod[:, 2:3]).astype(BF).reshape(rows, D)
    acc_attn[3 * D :, :] += dot_tn(d_proj, mixed_ref[...])
    d_mix = dot_nn(d_proj, attn_ref[3 * D :, :]).astype(BF)
    masks = half_masks()
    lane = lax.broadcasted_iota(jnp.int32, (tokens, 2 * HEAD_DIM), 1)
    low_side = lane < HEAD_DIM
    root = HEAD_DIM**-0.5
    for n in range(nb):
        here = slice(n * tokens, (n + 1) * tokens)
        for pair in range(HEADS // 2):
            col = pair * 2 * HEAD_DIM
            queries = qkv_ref[here, col : col + 2 * HEAD_DIM]
            keys = stack_heads(qkv_ref[here, D + col : D + col + 2 * HEAD_DIM], masks)
            values = stack_heads(qkv_ref[here, 2 * D + col : 2 * D + col + 2 * HEAD_DIM], masks)
            d_out = d_mix[here, col : col + 2 * HEAD_DIM]
            probs_bf = probs_ref[here, pair * 2 * tokens : (pair + 1) * 2 * tokens]
            d_probs = dot_nt(d_out, values)
            halves = []
            for side in range(2):
                cut = slice(side * tokens, (side + 1) * tokens)
                probs = probs_bf[:, cut].astype(jnp.float32)
                part = d_probs[:, cut]
                halves.append((probs * (part - jnp.sum(probs * part, axis=-1, keepdims=True))).astype(BF))
            d_scores = jnp.concatenate(halves, axis=1)
            d_queries = dot_nn(d_scores, keys) * root
            d_keys = dot_tn(d_scores, queries)
            d_keys = jnp.where(low_side, d_keys[:tokens], d_keys[tokens:]) * root
            d_values = dot_tn(probs_bf, d_out)
            d_values = jnp.where(low_side, d_values[:tokens], d_values[tokens:])
            d_qkv_s[here, col : col + 2 * HEAD_DIM] = d_queries.astype(BF)
            d_qkv_s[here, D + col : D + col + 2 * HEAD_DIM] = d_keys.astype(BF)
            d_qkv_s[here, 2 * D + col : 2 * D + col + 2 * HEAD_DIM] = d_values.astype(BF)
    d_qkv = d_qkv_s[...]
    hat, rstd = norm_rows(stream_ref[...].reshape(nb, tokens, D))
    attn_in = (hat * (1.0 + mod[:, 1:2]) + mod[:, 0:1]).astype(BF).reshape(rows, D)
    acc_attn[: 3 * D, :] += dot_tn(d_qkv, attn_in)
    d_attn_in = dot_nn(d_qkv, attn_ref[: 3 * D, :]).reshape(nb, tokens, D)
    d_before, d_shift, d_scale = norm_back(d_attn_in, hat, rstd, mod[:, 1:2])
    dmod_ref[:, 0:1] = d_shift
    dmod_ref[:, 1:2] = d_scale
    d_prev = d_middle + d_before
    if first:
        for n in range(nb):
            dpatch_ref[...] += lax.dot_general(
                noisy_ref[n].astype(jnp.float32), d_prev[n], (((1,), (0,)), ((), ())), precision=highest
            )
    else:
        d_prev_ref[...] = d_prev.reshape(rows, D)

    @pl.when(step == steps - 1)
    def _():
        gattn_ref[...] = acc_attn[...].astype(BF)
        gin_ref[...] = acc_in[...].astype(BF)
        gout_ref[...] = acc_out[...].astype(BF)


def whole_spec(array):
    return pl.BlockSpec(array.shape, lambda i: (0,) * array.ndim)


def lead_spec(block, ndim):
    return pl.BlockSpec(block, lambda i: (i,) + (0,) * (ndim - 1))


LIMIT = 56 * 1024 * 1024


def forward_layer(first, entry_args, mod, weights, nb, tokens):
    lat_count = mod.shape[0]
    rows = nb * tokens
    steps = lat_count // nb
    total = lat_count * tokens
    kinds = [(D, jnp.float32)] if first else []
    kinds += [
        (D, jnp.float32),
        (3 * D, BF),
        (HEADS * tokens, BF),
        (D, BF),
        (D, BF),
        (D, jnp.float32),
        (D, BF),
        (4 * D, BF),
        (4 * D, BF),
    ]
    out_shape = [jax.ShapeDtypeStruct((total, cols), kind) for cols, kind in kinds]
    out_specs = [lead_spec((rows, cols), 2) for cols, _ in kinds]
    out_shape.append(jax.ShapeDtypeStruct((steps, 8, D), jnp.float32))
    out_specs.append(lead_spec((1, 8, D), 3))
    if first:
        noisy, patch, pos = entry_args
        in_specs = [lead_spec((nb, PATCH_IN, tokens), 3), whole_spec(patch), whole_spec(pos)]
    else:
        in_specs = [lead_spec((rows, D), 2)]
    in_specs += [lead_spec((nb, 8, D), 3)] + [whole_spec(w) for w in weights]
    return pl.pallas_call(
        functools.partial(forward_kernel, first, nb, tokens),
        grid=(steps,),
        out_shape=out_shape,
        in_specs=in_specs,
        out_specs=out_specs,
        compiler_params=pltpu.CompilerParams(vmem_limit_bytes=LIMIT),
        name="block_forward",
    )(*entry_args, mod, *weights)


def backward_layer(first, last, entry_args, mod, weights, saved, nb, tokens, count_all):
    lat_count = mod.shape[0]
    rows = nb * tokens
    steps = lat_count // nb
    total = lat_count * tokens
    in_specs = []
    args = list(entry_args)
    if last:
        in_specs += [
            lead_spec((rows, D), 2),
            lead_spec((nb, 8, D), 3),
            whole_spec(args[2]),
            lead_spec((nb, PATCH_IN, tokens), 3),
            lead_spec((nb, PATCH_IN, tokens), 3),
        ]
    else:
        in_specs += [lead_spec((rows, D), 2)]
    if first:
        in_specs += [lead_spec((nb, PATCH_IN, tokens), 3)]
    in_specs += [lead_spec((nb, 8, D), 3)] + [whole_spec(w) for w in weights]
    in_specs += [lead_spec((rows, s.shape[1]), 2) for s in saved]
    out_shape = []
    out_specs = []

    def add(shape, kind, spec):
        out_shape.append(jax.ShapeDtypeStruct(shape, kind))
        out_specs.append(spec)

    def whole(shape):
        return pl.BlockSpec(shape, lambda i: (0,) * len(shape))

    if last:
        add((steps, 8, tokens), jnp.float32, lead_spec((1, 8, tokens), 3))
        add((OUT, D), jnp.float32, whole((OUT, D)))
        add((lat_count, 8, D), jnp.float32, lead_spec((nb, 8, D), 3))
    if first:
        add((PATCH_IN, D), jnp.float32, whole((PATCH_IN, D)))
    else:
        add((total, D), jnp.float32, lead_spec((rows, D), 2))
    for _ in range(3):
        add((4 * D, D), BF, whole((4 * D, D)))
    add((lat_count, 8, D), jnp.float32, lead_spec((nb, 8, D), 3))
    return pl.pallas_call(
        functools.partial(backward_kernel, first, last, nb, tokens, steps, count_all),
        grid=(steps,),
        out_shape=out_shape,
        in_specs=in_specs,
        out_specs=out_specs,
        scratch_shapes=[pltpu.VMEM((4 * D, D), jnp.float32)] * 3 + [pltpu.VMEM((rows, 3 * D), BF)],
        compiler_params=pltpu.CompilerParams(vmem_limit_bytes=LIMIT),
        name="block_backward",
    )(*args, mod, *weights, *saved)


MESH = pl.DeviceIdType.MESH


class Places:
    def __init__(self, n_dp, n_tp):
        self.digits = []
        for axis, count, top in (("dp", n_dp, 4), ("tp", n_tp, 2)):
            sizes = []
            rest = count
            while rest > 1:
                size = next((s for s in (top, 2, 3, 5, 7) if rest % s == 0), rest)
                sizes.append(size)
                rest //= size
            stride = count
            for size in sizes:
                stride //= size
                self.digits.append((axis, stride, size))
        self.dims = tuple(size for _, _, size in self.digits)
        self.count = n_dp * n_tp

    def order(self, odd):
        names = list(range(len(self.digits)))
        if odd and len(names) >= 4:
            names[-3], names[-2] = names[-2], names[-3]
        return names

    def mine(self):
        return [lax.rem(lax.axis_index(axis) // stride, size) for axis, stride, size in self.digits]

    def other(self, mine, digit, shift):
        axis, stride, size = self.digits[digit]
        value = lax.rem(mine[digit] + shift, size)
        return {axis: lax.axis_index(axis) + (value - mine[digit]) * stride}, value

    def barrier(self, mine):
        barrier = pltpu.get_barrier_semaphore()
        count = 0
        for digit, size in enumerate(self.dims):
            for shift in range(1, size):
                target, _ = self.other(mine, digit, shift)
                pl.semaphore_signal(barrier, inc=1, device_id=target, device_id_type=MESH)
                count += 1
        pl.semaphore_wait(barrier, count)


SMALL = 8
SPLIT = 3


def small_blocks(entry_t, table_t, final):
    early = PATCH_IN + FREQ
    return [
        (0, 0, entry_t, 0, early),
        (1, 0, entry_t, early, early + D),
        (2, 0, table_t, 0, D),
        (3, 0, table_t, D, 2 * D),
        (4, 0, table_t, 2 * D, CLASSES + 1),
        (4, 256, final, 2 * D, 2 * D + OUT),
        (5, 0, final, 0, D),
        (6, 0, final, D, 2 * D),
    ]


class Traffic:
    def __init__(self, places, mine, sends, recvs, locals_):
        self.places, self.mine = places, mine
        self.sends, self.recvs, self.locals = sends, recvs, locals_
        self.used = self.used_local = 0
        self.copies = []

    def remote(self, source, target_ref, digit, shift):
        target, _ = self.places.other(self.mine, digit, shift)
        at = self.used
        self.used += 1
        copy = pltpu.make_async_remote_copy(
            src_ref=source,
            dst_ref=target_ref,
            send_sem=self.sends.at[at],
            recv_sem=self.recvs.at[at],
            device_id=target,
            device_id_type=MESH,
        )
        self.copies.append(copy)
        return copy

    def local(self, source, target_ref):
        at = self.used_local
        self.used_local += 1
        return pltpu.make_async_copy(source, target_ref, self.locals.at[at])

    def ahead(self, digit, shift):
        return lax.rem(self.mine[digit] + shift, self.places.dims[digit])

    def finish(self):
        for copy in self.copies:
            copy.wait_send()


def copies_per_part(places):
    dims = places.dims
    return sum(dims) - len(dims) + max(dims) * max(dims)


def gather_job(traffic, odd, source, out):
    places, mine = traffic.places, traffic.mine
    order = places.order(odd)
    depth = len(order)
    split = depth - 2 if depth >= 4 else -1
    own = traffic.local(source, out.at[tuple(mine)])
    waits = [[] for _ in range(depth + 1)]
    starts = [[] for _ in range(depth + 1)]

    def region(done, fixed):
        return tuple(fixed.get(d, slice(None) if d in done else mine[d]) for d in range(depth))

    for stage, digit in enumerate(order):
        done = order[:stage]
        for shift in range(1, places.dims[digit]):
            pieces = [(stage, {})]
            if stage == split:
                before = order[stage - 1]
                pieces = [(stage - 1, {before: mine[before]})]
                pieces += [(stage, {before: traffic.ahead(before, k)}) for k in range(1, places.dims[before])]
            for when, fixed in pieces:
                where = region(done, fixed)
                copy = traffic.remote(source if stage == 0 else out.at[where], out.at[where], digit, shift)
                starts[when].append(copy)
                waits[stage + 1].append(copy)

    def action(k):
        if k == 0:
            own.start()
        if k == 1:
            own.wait()
        for copy in waits[k]:
            copy.wait_recv()
        for copy in starts[k]:
            copy.start()

    return [functools.partial(action, k) for k in range(depth + 1)]


def land_shapes(places, odd, block):
    route = places.order(odd)[::-1]
    depth = len(route)
    shapes = []
    for stage, digit in enumerate(route):
        left = [d for d in range(depth) if d not in route[: stage + 1]]
        shapes.append((places.dims[digit] - 1, *(places.dims[d] for d in left), *block))
    return shapes


def reduce_job(traffic, odd, source, acc, lands, out):
    places, mine = traffic.places, traffic.mine
    route = places.order(odd)[::-1]
    depth = len(route)
    split = 1 if depth >= 4 else -1
    waits = [[] for _ in range(depth + 1)]
    starts = [[] for _ in range(depth + 1)]
    adds = [[] for _ in range(depth + 1)]
    own = traffic.local(
        source.at[tuple(mine[d] if d == route[0] else slice(None) for d in range(depth))], acc
    )

    def left_of(stage):
        return [d for d in range(depth) if d not in route[: stage + 1]]

    def in_acc(values):
        return tuple(values.get(d, mine[d]) for d in range(depth) if d != route[0])

    for stage, digit in enumerate(route):
        gone = route[:stage]
        left = left_of(stage)
        pieces = [(stage + 1, {})]
        if stage == split:
            after = route[stage + 1]
            pieces = [(stage + 1, {after: traffic.ahead(after, k)}) for k in range(1, places.dims[after])]
            pieces += [(stage + 2, {after: mine[after]})]
        for when, fixed in pieces:
            for shift in range(1, places.dims[digit]):
                values = {d: slice(None) for d in left} | fixed | {digit: traffic.ahead(digit, shift)}
                if stage == 0:
                    sent = source.at[tuple(values[d] for d in range(depth))]
                else:
                    sent = acc.at[in_acc(values)]
                target = lands[stage].at[(shift - 1, *(values[d] for d in left))]
                copy = traffic.remote(sent, target, digit, shift)
                starts[stage].append(copy)
                waits[when].append(copy)
            adds[when].append((stage, fixed))

    def add(group):
        stage, fixed = group[-1]
        free = [d for d in left_of(stage) if d not in fixed]
        count = math.prod(places.dims[d] for d in free)
        last = stage == depth - 1

        def one(flat, carry):
            values = dict(fixed)
            rest = flat
            for d in reversed(free):
                values[d] = lax.rem(rest, places.dims[d])
                rest = rest // places.dims[d]
            total = acc[in_acc(values)].astype(jnp.float32)
            for near, _ in group:
                for shift in range(places.dims[route[near]] - 1):
                    index = (shift, *(values.get(d, mine[d]) for d in left_of(near)))
                    total = total + lands[near][index].astype(jnp.float32)
            if last:
                out[...] = total
            else:
                acc[in_acc(values)] = total.astype(BF)
            return carry

        lax.fori_loop(0, count, one, 0)

    def action(k):
        if k == 0:
            own.start()
        if k == 1:
            own.wait()
        for copy in waits[k]:
            copy.wait_recv()
        if k == split + 2:
            add(adds[k])
        else:
            for entry in adds[k]:
                add([entry])
        if k < depth:
            for copy in starts[k]:
                copy.start()

    return [functools.partial(action, k) for k in range(depth + 1)]


def in_waves(jobs):
    pairs = [jobs[at : at + 2] for at in range(0, len(jobs), 2)]
    depth = len(jobs[0])
    sequence = []
    for tick in range(len(pairs) + depth - 1):
        for k in range(depth):
            if 0 <= tick - k < len(pairs):
                sequence.extend(job[k] for job in pairs[tick - k])
    return sequence


def gather_kernel(places, slots, layers, *refs):
    entry_ref, table_ref, final_ref, ada_ref, attn_ref, in_ref, out_ref = refs[:7]
    chunks = slots + SPLIT + 3 * layers
    outs = refs[7 : 7 + chunks]
    small, packed, send_sems, recv_sems, own_sems = refs[7 + chunks :]
    mine = places.mine()
    small[...] = jnp.zeros_like(small)
    for k, at, source, low, high in small_blocks(entry_ref, table_ref, final_ref):
        small[k, : source.shape[0], at : at + high - low] = source[:, low:high].astype(BF)
    part = -(-ada_ref.shape[0] // SPLIT)
    for p in range(SPLIT):
        packed[p, :part, :] = ada_ref[p * part : (p + 1) * part, :].astype(BF)
    for l in range(layers):
        for k, source in enumerate((attn_ref, in_ref, out_ref)):
            packed[SPLIT + 3 * l + k, : source.shape[1], :] = source[l].astype(BF)
    first = lax.axis_index("tp") * slots
    ins = [small.at[first + s] for s in range(slots)]
    ins += [packed.at[m] for m in range(SPLIT + 3 * layers)]
    places.barrier(mine)
    traffic = Traffic(places, mine, send_sems, recv_sems, own_sems)
    jobs = [gather_job(traffic, m % 2 == 1, ins[m], outs[m]) for m in range(chunks)]
    for action in in_waves(jobs):
        action()
    traffic.finish()


def pad16(rows):
    return rows + -rows % 16


def gather_all(places, slots, entry_t, table_t, final, ada_t, attn_t, in_t, out_w):
    layers = attn_t.shape[0]
    small_rows, ada_rows = pad16(final.shape[0]), pad16(-(-ada_t.shape[0] // SPLIT))
    wide_rows = pad16(attn_t.shape[1])
    sizes = [small_rows] * slots + [ada_rows] * SPLIT + [wide_rows] * (3 * layers)
    chunks = len(sizes)
    vmem = pl.BlockSpec(memory_space=pltpu.VMEM)
    packed_rows = max(ada_rows, wide_rows)
    assert packed_rows == min(ada_rows, wide_rows)
    outs = pl.pallas_call(
        functools.partial(gather_kernel, places, slots, layers),
        out_shape=[jax.ShapeDtypeStruct((*places.dims, rows, D), BF) for rows in sizes],
        in_specs=[vmem] * 7,
        out_specs=[pl.BlockSpec(memory_space=pl.ANY)] * chunks,
        scratch_shapes=[
            pltpu.VMEM((slots * lax.axis_size("tp"), small_rows, D), BF),
            pltpu.VMEM((SPLIT + 3 * layers, packed_rows, D), BF),
            pltpu.SemaphoreType.DMA((chunks * copies_per_part(places),)),
            pltpu.SemaphoreType.DMA((chunks * copies_per_part(places),)),
            pltpu.SemaphoreType.DMA((chunks,)),
        ],
        compiler_params=pltpu.CompilerParams(collective_id=1, has_side_effects=True, vmem_limit_bytes=LIMIT),
        name="gather_weights",
    )(entry_t, table_t, final, ada_t, attn_t, in_t, out_w)
    return [o.reshape((places.count,) + o.shape[-2:]) for o in outs]


def reduce_kernel(places, chunks, slots, layers, *refs):
    ins = refs[:chunks]
    loss_ref = refs[chunks]
    square_refs = refs[chunks + 1 : chunks + 1 + layers]
    refs = refs[chunks + 1 + layers :]
    outs, both_ref, stats_ref = refs[:chunks], refs[chunks], refs[chunks + 1]
    refs = refs[chunks + 2 :]
    stats_land, stats_send, stats_recv, both_send, both_recv = refs[-5:]
    refs = refs[:-5]
    depth = len(places.dims)
    accs = refs[:chunks]
    lands = refs[chunks : chunks * (1 + depth)]
    send_sems, recv_sems, own_sems = refs[chunks * (1 + depth) :]
    mine = places.mine()
    places.barrier(mine)
    traffic = Traffic(places, mine, send_sems, recv_sems, own_sems)
    jobs = [
        reduce_job(traffic, m % 2 == 1, ins[m], accs[m], lands[m * depth : (m + 1) * depth], outs[m])
        for m in range(chunks)
    ]
    for action in in_waves(jobs):
        action()
    traffic.finish()

    def lane_sums(rows):
        total = jnp.sum(rows, axis=0, keepdims=True)
        return sum(total[:, at : at + 128] for at in range(0, total.shape[1], 128))

    grad = sum(lane_sums(out[...] * out[...]) for out in outs)
    loss = lane_sums(jnp.sum(loss_ref[...], axis=0))
    squares = [lane_sums(jnp.sum(ref[...], axis=0)) for ref in square_refs]
    stats_ref[...] = jnp.concatenate([grad, loss, *squares, jnp.zeros((6 - layers, 128), jnp.float32)], axis=0)
    for s in range(slots):
        both_ref[(lax.axis_index("tp"), s)] = outs[s][...]
    inner = [d for d in range(depth) if places.digits[d][0] == "tp"]
    for stage, digit in enumerate(reversed(range(depth))):
        size = places.dims[digit]
        axis, stride, _ = places.digits[digit]
        stats_land[stage, mine[digit]] = stats_ref[...]
        copies = []
        for shift in range(1, size):
            target, _ = places.other(mine, digit, shift)
            copies.append(
                pltpu.make_async_remote_copy(
                    src_ref=stats_ref,
                    dst_ref=stats_land.at[stage, mine[digit]],
                    send_sem=stats_send.at[stage, shift - 1],
                    recv_sem=stats_recv.at[stage, shift - 1],
                    device_id=target,
                    device_id_type=MESH,
                )
            )
            if digit in inner:
                held = stride
                start = lax.axis_index("tp") // stride * stride
                where = both_ref.at[pl.ds(start, held)]
                copies.append(
                    pltpu.make_async_remote_copy(
                        src_ref=where,
                        dst_ref=where,
                        send_sem=both_send.at[stage, shift - 1],
                        recv_sem=both_recv.at[stage, shift - 1],
                        device_id=target,
                        device_id_type=MESH,
                    )
                )
        for copy in copies:
            copy.start()
        for copy in copies:
            copy.wait()
        total = stats_land[stage, 0]
        for value in range(1, size):
            total = total + stats_land[stage, value]
        stats_ref[...] = total


def reduce_all(places, slots, parts, loss, squares):
    layers = len(squares)
    vmem = pl.BlockSpec(memory_space=pltpu.VMEM)
    chunks = len(parts)
    dims = places.dims
    depth, widest = len(dims), max(dims)
    blocks = [p.shape[1:] for p in parts]
    lands = []
    for m in range(chunks):
        lands += [pltpu.VMEM(shape, BF) for shape in land_shapes(places, m % 2 == 1, blocks[m])]
    return pl.pallas_call(
        functools.partial(reduce_kernel, places, chunks, slots, layers),
        out_shape=[jax.ShapeDtypeStruct(block, jnp.float32) for block in blocks]
        + [
            jax.ShapeDtypeStruct((lax.axis_size("tp"), slots, *blocks[0]), jnp.float32),
            jax.ShapeDtypeStruct((8, 128), jnp.float32),
        ],
        in_specs=[pl.BlockSpec(memory_space=pl.ANY)] * chunks + [vmem] * (1 + layers),
        out_specs=[vmem] * (chunks + 2),
        scratch_shapes=[pltpu.VMEM(dims[:-1] + block, BF) for block in blocks]
        + lands
        + [
            pltpu.SemaphoreType.DMA((chunks * copies_per_part(places),)),
            pltpu.SemaphoreType.DMA((chunks * copies_per_part(places),)),
            pltpu.SemaphoreType.DMA((chunks,)),
            pltpu.VMEM((depth, widest, 8, 128), jnp.float32),
            pltpu.SemaphoreType.DMA((depth, widest - 1)),
            pltpu.SemaphoreType.DMA((depth, widest - 1)),
            pltpu.SemaphoreType.DMA((depth, widest - 1)),
            pltpu.SemaphoreType.DMA((depth, widest - 1)),
        ],
        compiler_params=pltpu.CompilerParams(collective_id=2, has_side_effects=True, vmem_limit_bytes=LIMIT),
        name="reduce_gradients",
    )(*[p.reshape(dims + p.shape[1:]) for p in parts], loss, *squares)


def silu(values):
    return values * (1.0 / (1.0 + jnp.exp(-values)))


def silu_slope(values):
    gate = 1.0 / (1.0 + jnp.exp(-values))
    return gate * (1.0 + values * (1.0 - gate))


def split_low(values):
    high = values.astype(BF)
    return jnp.concatenate([high, (values - high.astype(jnp.float32)).astype(BF)], axis=0)


def block_of(refs, k):
    slots = len(refs)
    part = refs[k % slots][:, k // slots]
    return part.reshape(-1, D)


def condition_kernel(slots, lat_count, *refs):
    feat_ref, hot_ref = refs[:2]
    slot_refs = refs[2 : 2 + slots]
    ada_refs = refs[2 + slots : 2 + slots + SPLIT]
    mod_ref, fmod_ref, pre_ref, cond_ref, patch_ref, head_ref = refs[2 + slots + SPLIT :]
    entry = block_of(slot_refs, 0)
    patch_ref[...] = entry[:, :PATCH_IN]
    pre = dot_nt(feat_ref[...], entry)
    pre_ref[...] = pre
    cond = dot_nt(silu(pre).astype(BF), block_of(slot_refs, 1))
    for k in range(3):
        cond = cond + dot_nt(hot_ref[:, k * D : (k + 1) * D], block_of(slot_refs, 2 + k))
    cond_ref[...] = cond
    head_ref[...] = block_of(slot_refs, 4)[:, 256 : 256 + OUT]
    act = silu(cond).astype(BF)
    for p in range(SPLIT):
        wide = ada_refs[p].shape[0]
        mod_ref[:, p * wide : (p + 1) * wide] = dot_nt(act, ada_refs[p][...])
    for k in range(2):
        part = dot_nn(act, block_of(slot_refs, 5 + k))
        for b in range(lat_count):
            fmod_ref[b, k : k + 1, :] = part[b : b + 1, :]


def condition(feat, hot, slot_full, ada_full, lat_count):
    vmem = pl.BlockSpec(memory_space=pltpu.VMEM)
    wide = ada_full[0].shape[0]
    shapes = [
        ((8, SPLIT * wide), jnp.float32),
        ((lat_count, 8, D), jnp.float32),
        ((8, D), jnp.float32),
        ((8, D), jnp.float32),
        ((D, PATCH_IN), BF),
        ((D, OUT), BF),
    ]
    return pl.pallas_call(
        functools.partial(condition_kernel, len(slot_full), lat_count),
        out_shape=[jax.ShapeDtypeStruct(*s) for s in shapes],
        in_specs=[vmem] * (2 + len(slot_full) + SPLIT),
        out_specs=[vmem] * len(shapes),
        compiler_params=pltpu.CompilerParams(vmem_limit_bytes=LIMIT),
        name="condition",
    )(feat, hot, *slot_full, *ada_full)


def condition_back_kernel(slots, lat_count, *refs):
    feat_ref, hot_ref = refs[:2]
    slot_refs = refs[2 : 2 + slots]
    ada_refs = refs[2 + slots : 2 + slots + SPLIT]
    pre_ref, cond_ref, d_mod_ref, d_fmod_ref, d_patch_ref, d_head_ref = refs[2 + slots + SPLIT :][:6]
    outs = refs[2 + slots + SPLIT + 6 :]
    g_slots, g_ada = outs[:slots], outs[slots : slots + SPLIT]
    fmod_s = outs[slots + SPLIT]
    pre, cond = pre_ref[...], cond_ref[...]
    act = silu(cond).astype(BF)
    act_two = jnp.concatenate([act, act], axis=0)
    d_cond = jnp.zeros((16, D), jnp.float32)
    for p in range(SPLIT):
        wide = ada_refs[p].shape[0]
        d_mod = split_low(d_mod_ref[:, p * wide : (p + 1) * wide])
        d_cond = d_cond + dot_nn(d_mod, ada_refs[p][...])
        g_ada[p][...] = dot_tn(d_mod, act_two).astype(BF)

    def give(k, grad):
        ref = g_slots[k % slots]
        ref[:, k // slots] = grad.astype(BF).reshape(ref.shape[0], ref.shape[2], D)

    fmod_s[...] = jnp.zeros_like(fmod_s)
    for k in range(2):
        for b in range(lat_count):
            fmod_s[k, b : b + 1, :] = d_fmod_ref[b, k : k + 1, :]
        d_fmod = split_low(fmod_s[k])
        d_cond = d_cond + dot_nt(d_fmod, block_of(slot_refs, 5 + k))
        give(5 + k, dot_tn(act_two, d_fmod))
    d_pre = split_low((d_cond[:8] + d_cond[8:]) * silu_slope(cond))
    time_act = silu(pre).astype(BF)
    give(1, dot_tn(d_pre, jnp.concatenate([time_act, time_act], axis=0)))
    d_time = dot_nn(d_pre, block_of(slot_refs, 1))
    for k in range(3):
        hot = hot_ref[:, k * D : (k + 1) * D]
        grad = dot_tn(d_pre, jnp.concatenate([hot, hot], axis=0))
        if k == 2:
            here = jnp.pad(d_head_ref[...], ((0, 128 - OUT), (0, 0))).T
            grad = jnp.concatenate([grad[:, :256], grad[:, 256:] + here], axis=1)
        give(2 + k, grad)
    d_time = split_low((d_time[:8] + d_time[8:]) * silu_slope(pre))
    grad = dot_tn(d_time, jnp.concatenate([feat_ref[...], feat_ref[...]], axis=0))
    here = jnp.pad(d_patch_ref[...], ((0, 128 - PATCH_IN), (0, 0))).T
    give(0, jnp.concatenate([grad[:, :128] + here, grad[:, 128:]], axis=1))
    for k in range(7, SMALL):
        give(k, jnp.zeros((D, D), jnp.float32))


def condition_back(feat, hot, slot_full, ada_full, pre, cond, d_mod, d_fmod, d_patch, d_head):
    vmem = pl.BlockSpec(memory_space=pltpu.VMEM)
    lat_count = d_fmod.shape[0]
    args = (feat, hot, *slot_full, *ada_full, pre, cond, d_mod, d_fmod, d_patch, d_head)
    kept = (*slot_full, *ada_full)
    return pl.pallas_call(
        functools.partial(condition_back_kernel, len(slot_full), lat_count),
        out_shape=[jax.ShapeDtypeStruct(w.shape, BF) for w in kept],
        in_specs=[vmem] * len(args),
        out_specs=[vmem] * len(kept),
        scratch_shapes=[pltpu.VMEM((2, 8, D), jnp.float32)],
        compiler_params=pltpu.CompilerParams(vmem_limit_bytes=LIMIT),
        name="condition_back",
    )(*args)


def adam_kernel(slots, layers, count_rms, *refs):
    stats_ref, both_ref = refs[:2]
    grads = refs[2 : 2 + SPLIT + 3 * layers]
    states = refs[2 + SPLIT + 3 * layers :][:21]
    outs = refs[2 + SPLIT + 3 * layers + 21 :]
    news, (loss_ref, norm_ref, rms_ref) = outs[:21], outs[21:]
    totals = jnp.sum(stats_ref[...], axis=1, keepdims=True)
    norm = jnp.sqrt(totals[0:1])
    factor = jnp.minimum(1.0, 0.01 / (norm + 1e-06))
    loss_ref[...] = totals[1:2]
    norm_ref[...] = norm
    rms_ref[...] = jnp.sqrt(totals[2 : 2 + layers] / count_rms)
    correct = 1.0 - 0.5**STEP

    def update(name, where, grad):
        weight, first, second = (ref[where] for ref in states[3 * name : 3 * name + 3])
        clipped = grad * factor
        first_new = 0.5 * first + 0.5 * clipped
        second_new = 0.5 * second + 0.5 * clipped * clipped
        root = jnp.sqrt(second_new * (1.0 / correct)) + 1e-08
        new = weight - 0.02 * (first_new * (1.0 / correct) / root + 0.01 * weight)
        news[3 * name][where] = new
        news[3 * name + 1][where] = first_new
        news[3 * name + 2][where] = second_new

    def small(k):
        return both_ref[k // slots, k % slots]

    rows = states[0].shape[0]
    early = PATCH_IN + FREQ
    every = slice(0, rows)
    update(0, (every, slice(0, early)), small(0)[:rows, :early])
    update(0, (every, slice(early, early + D)), small(1)[:rows])
    update(1, (every, slice(0, D)), small(2)[:rows])
    update(1, (every, slice(D, 2 * D)), small(3)[:rows])
    update(1, (every, slice(2 * D, CLASSES + 1)), small(4)[:rows, : CLASSES + 1 - 2 * D])
    update(6, (every, slice(0, D)), small(5)[:rows])
    update(6, (every, slice(D, 2 * D)), small(6)[:rows])
    update(6, (every, slice(2 * D, 2 * D + OUT)), small(4)[:rows, 256 : 256 + OUT])
    part = -(-states[15].shape[0] // SPLIT)
    for p in range(SPLIT):
        update(5, (slice(p * part, (p + 1) * part), slice(0, D)), grads[p][:part])
    for l in range(layers):
        for k in range(3):
            update(2 + k, (l, slice(0, states[6].shape[1]), slice(0, D)), grads[SPLIT + 3 * l + k][: states[6].shape[1]])


def adam_all(slots, layers, count_rms, stats, both, grads, states):
    vmem = pl.BlockSpec(memory_space=pltpu.VMEM)
    args = (stats, both, *grads, *states)
    return pl.pallas_call(
        functools.partial(adam_kernel, slots, layers, count_rms),
        out_shape=[jax.ShapeDtypeStruct(s.shape, jnp.float32) for s in states]
        + [jax.ShapeDtypeStruct((n, 1), jnp.float32) for n in (1, 1, layers)],
        in_specs=[vmem] * len(args),
        out_specs=[vmem] * 24,
        compiler_params=pltpu.CompilerParams(vmem_limit_bytes=LIMIT),
        name="adam",
    )(*args)


def modulation_pieces(layers, ada_rows, part_rows, count):
    pieces = []
    for j in range(count):
        for l in range(layers):
            low = l * ada_rows
            while low < (l + 1) * ada_rows:
                p, r = divmod(low, part_rows)
                length = min((l + 1) * ada_rows - low, part_rows - r)
                pieces.append((l, j * ada_rows + low - l * ada_rows, p, j * part_rows + r, length))
                low += length
    return pieces


def embed_condition(slots, lat_count, feat_ref, hot_ref, slot_refs, pre_ref, cond_ref, fmod_ref):
    pre = dot_nt(feat_ref[...], block_of(slot_refs, 0))
    pre_ref[...] = pre
    cond = dot_nt(silu(pre).astype(BF), block_of(slot_refs, 1))
    for k in range(3):
        cond = cond + dot_nt(hot_ref[:, k * D : (k + 1) * D], block_of(slot_refs, 2 + k))
    cond_ref[...] = cond
    act = silu(cond).astype(BF)
    for k in range(2):
        fmod_ref[:, k * D : (k + 1) * D] = dot_nn(act, block_of(slot_refs, 5 + k))


def mod_rows(mod_ref, index, n, nb, part):
    rows = [mod_ref[(*index, pl.ds(n * nb + b, 1), slice(part * D, (part + 1) * D))] for b in range(nb)]
    return jnp.stack(rows, axis=0)


def attend_forward(nb, tokens, stream, mod, attn_w, out_w, qkv_ref, probs_ref, mixed_ref, branch_ref):
    rows = nb * tokens
    hat, _ = norm_rows(stream)
    attn_in = (hat * (1.0 + mod(1)) + mod(0)).astype(BF).reshape(rows, D)
    qkv_ref[...] = dot_nt(attn_in, attn_w[...]).astype(BF)
    masks = half_masks()
    for b in range(nb):
        here = slice(b * tokens, (b + 1) * tokens)
        for pair in range(HEADS // 2):
            col = pair * 2 * HEAD_DIM
            queries = qkv_ref[here, col : col + 2 * HEAD_DIM] * jnp.asarray(HEAD_DIM**-0.5, BF)
            keys = stack_heads(qkv_ref[here, D + col : D + col + 2 * HEAD_DIM], masks)
            values = stack_heads(qkv_ref[here, 2 * D + col : 2 * D + col + 2 * HEAD_DIM], masks)
            scores = dot_nt(queries, keys)
            halves = []
            for side in range(2):
                part = scores[:, side * tokens : (side + 1) * tokens]
                grown = jnp.exp(part - jnp.max(part, axis=-1, keepdims=True))
                halves.append((grown * (1.0 / jnp.sum(grown, axis=-1, keepdims=True))).astype(BF))
            probs = jnp.concatenate(halves, axis=1)
            probs_ref[here, pair * 2 * tokens : (pair + 1) * 2 * tokens] = probs
            mixed_ref[here, col : col + 2 * HEAD_DIM] = dot_nn(probs, values).astype(BF)
    branch = dot_nt(mixed_ref[...], out_w[...])
    branch_ref[...] = branch.astype(BF)
    return stream + mod(2) * branch.reshape(nb, tokens, D)


def feed_forward(nb, tokens, middle, mod, in_w, out_w, mlp_ref, act_ref, slope_ref):
    rows = nb * tokens
    hat, _ = norm_rows(middle)
    mlp_in = (hat * (1.0 + mod(4)) + mod(3)).astype(BF).reshape(rows, D)
    hidden = dot_nt(mlp_in, in_w[...])
    squared = hidden * hidden
    bent = jnp.tanh(hidden * (GELU_A + (GELU_A * GELU_B) * squared))
    half = 0.5 * hidden
    act = (half + half * bent).astype(BF)
    act_ref[...] = act
    slope_ref[...] = (
        0.5
        + 0.5 * bent
        + half * (1.0 - bent * bent) * (GELU_A + (3.0 * GELU_A * GELU_B) * squared)
    ).astype(BF)
    mlp = dot_nn(act, out_w[...])
    mlp_ref[...] = mlp.astype(BF)
    return middle + mod(5) * mlp.reshape(nb, tokens, D)


def waves(jobs):
    pairs = [jobs[at : at + 2] for at in range(0, len(jobs), 2)]
    depth = len(jobs[0])
    ticks = []
    for tick in range(len(pairs) + depth - 1):
        ticks.append(
            [job[k] for k in range(depth) if 0 <= tick - k < len(pairs) for job in pairs[tick - k]]
        )
    return ticks


def fused_forward_kernel(places, slots, layers, nb, tokens, lat_count, sizes, *refs):
    small_rows, ada_rows, part_rows, wide_rows = sizes
    chunks = slots + SPLIT + 3 * layers
    entry_ref, table_ref, final_ref, ada_ref, attn_ref, in_ref, out_ref = refs[:7]
    feat_ref, hot_ref, noisy_ref, pos_ref = refs[7:11]
    given = refs[11 : 11 + chunks]
    (
        mods_ref,
        fmod_ref,
        pre_ref,
        cond_ref,
        start_ref,
        result_ref,
        qkv_ref,
        probs_ref,
        mixed_ref,
        branch_ref,
        middle_ref,
        mlp_ref,
        act_ref,
        slope_ref,
        square_ref,
    ) = refs[11 + chunks : 26 + chunks]
    refs = refs[26 + chunks :]
    fulls = refs[:chunks]
    small, packed, stream_s, middle_s, send_sems, recv_sems, own_sems, give_sems = refs[chunks:]
    l, h, n = (pl.program_id(axis) for axis in range(3))
    mine = places.mine()
    first = lax.axis_index("tp") * slots
    order = [*range(slots), slots, slots + 1, slots + SPLIT, slots + SPLIT + 1, slots + SPLIT + 2, slots + 2]
    order += range(slots + SPLIT + 3, chunks)
    sources = [small.at[first + s] for s in range(slots)] + [packed.at[m] for m in range(SPLIT + 3 * layers)]
    traffic = Traffic(places, mine, send_sems, recv_sems, own_sems)
    jobs = [gather_job(traffic, at % 2 == 1, sources[m], fulls[m]) for at, m in enumerate(order)]
    ticks = waves(jobs)
    handed = [
        pltpu.make_async_copy(fulls[m], given[m], give_sems.at[m]) for m in range(chunks)
    ]

    def flat(m, rows):
        return fulls[m].reshape(places.count * rows, D)

    def run(numbers):
        for tick in numbers:
            for action in ticks[tick]:
                action()

    def at_step(layer, half, step):
        return pl.when((l == layer) & (h == half) & (n == step))

    def set_mods(layer):
        act = silu(cond_ref[...]).astype(BF)
        low, high = layer * ada_rows, (layer + 1) * ada_rows
        parts = range(low // part_rows, -(-high // part_rows))
        raw = {p: dot_nt(act, flat(slots + p, part_rows)[...]) for p in parts}
        for ll, col, p, at, length in modulation_pieces(layers, ada_rows, part_rows, places.count):
            if ll == layer:
                mods_ref[layer, :, col : col + length] = raw[p][:, at : at + length]

    slot_refs = [f.reshape(-1, lax.axis_size("tp"), small_rows, D) for f in fulls[:slots]]
    last = len(ticks) - 1

    @at_step(0, 0, 0)
    def _():
        small[...] = jnp.zeros_like(small)
        for k, at, source, low, high in small_blocks(entry_ref, table_ref, final_ref):
            small[k, : source.shape[0], at : at + high - low] = source[:, low:high].astype(BF)
        for p in range(SPLIT):
            packed[p] = ada_ref[p * part_rows : (p + 1) * part_rows, :].astype(BF)
        for ll in range(layers):
            for k, source in enumerate((attn_ref, in_ref, out_ref)):
                packed[SPLIT + 3 * ll + k] = source[ll].astype(BF)
        places.barrier(mine)
        run(range(6))
        embed_condition(slots, lat_count, feat_ref, hot_ref, slot_refs, pre_ref, cond_ref, fmod_ref)
        set_mods(0)
        run([6])

    @at_step(0, 1, 0)
    def _():
        run([7])

    @at_step(1, 0, 0)
    def _():
        run([8])
        for layer in range(1, layers):
            set_mods(layer)

    @at_step(1, 1, 0)
    def _():
        run(range(9, last + 1))
        for copy in handed:
            copy.start()

    rows = nb * tokens
    here = pl.ds(pl.multiple_of(n * rows, rows), rows)

    def weight(layer, k):
        return flat(slots + SPLIT + 3 * layer + k, wide_rows)

    for layer in range(layers):
        mod = lambda part, layer=layer: mod_rows(mods_ref, (layer,), n, nb, part)

        @pl.when((l == layer) & (h == 0))
        def _(layer=layer, mod=mod):
            if layer == 0:
                patch = block_of(slot_refs, 0)[:, :PATCH_IN]
                parts = [
                    lax.dot_general(
                        noisy_ref[b], patch, (((0,), (1,)), ((), ())), preferred_element_type=jnp.float32
                    )
                    + pos_ref[...]
                    for b in range(nb)
                ]
                stream = parts[0] if nb == 1 else jnp.concatenate(parts, axis=0)
                start_ref[...] = stream
            else:
                stream = stream_s[here, :]
            stream = stream.reshape(nb, tokens, D)
            middle = attend_forward(
                nb,
                tokens,
                stream,
                mod,
                weight(layer, 0).at[: 3 * D],
                weight(layer, 0).at[3 * D :],
                qkv_ref.at[0],
                probs_ref.at[0],
                mixed_ref.at[0],
                branch_ref.at[0],
            )
            middle_ref[0] = middle.reshape(rows, D)
            middle_s[here, :] = middle.reshape(rows, D)

        @pl.when((l == layer) & (h == 1))
        def _(layer=layer, mod=mod):
            middle = middle_s[here, :].reshape(nb, tokens, D)
            result = feed_forward(
                nb,
                tokens,
                middle,
                mod,
                weight(layer, 1),
                weight(layer, 2),
                mlp_ref.at[0],
                act_ref.at[0],
                slope_ref.at[0],
            )
            result_ref[0] = result.reshape(rows, D)
            if layer < layers - 1:
                stream_s[here, :] = result.reshape(rows, D)
            square_ref[0, 0] = jnp.sum((result * result).reshape(rows // 8, 8, D), axis=0)

    @at_step(layers - 1, 1, lat_count // nb - 1)
    def _():
        for copy in handed:
            copy.wait()
        traffic.finish()


def fused_forward(places, slots, nb, weights_in, feat, hot, noisy, pos):
    entry_t, table_t, final, ada_t, attn_t, in_t, out_w = weights_in
    layers, wide_rows = attn_t.shape[:2]
    lat_count, _, tokens = noisy.shape
    small_rows, part_rows, ada_rows = final.shape[0], ada_t.shape[0] // SPLIT, ada_t.shape[0] // layers
    sizes = [small_rows] * slots + [part_rows] * SPLIT + [wide_rows] * (3 * layers)
    chunks = len(sizes)
    steps = lat_count // nb
    rows, total = nb * tokens, lat_count * tokens
    full_shapes = [(*places.dims, r, D) for r in sizes]

    def const(array):
        return pl.BlockSpec(array.shape, lambda l, h, n: (0,) * array.ndim)

    def const_shape(shape):
        return pl.BlockSpec(shape, lambda l, h, n: (0,) * len(shape))

    def early(l, h, n):
        return jnp.where(h == 0, n, steps - 1)

    def half_one(cols):
        return pl.BlockSpec((1, rows, cols), lambda l, h, n: (l, early(l, h, n), 0))

    def half_two(cols):
        def index(l, h, n):
            before = jnp.where(l == 0, 0, steps - 1)
            return (jnp.where(h == 0, jnp.maximum(l - 1, 0), l), jnp.where(h == 0, before, n), 0)

        return pl.BlockSpec((1, rows, cols), index)

    def square_index(l, h, n):
        before = jnp.where(l == 0, 0, steps - 1)
        return (jnp.where(h == 0, jnp.maximum(l - 1, 0), l), jnp.where(h == 0, before, n), 0, 0)

    out_shape = [jax.ShapeDtypeStruct(s, BF) for s in full_shapes]
    out_specs = [pl.BlockSpec(memory_space=pl.ANY)] * chunks

    def add(shape, kind, spec):
        out_shape.append(jax.ShapeDtypeStruct(shape, kind))
        out_specs.append(spec)

    for shape in ((layers, 8, 6 * D), (8, 2 * D), (8, D), (8, D)):
        add(shape, jnp.float32, const_shape(shape))
    add(
        (total, D),
        jnp.float32,
        pl.BlockSpec((rows, D), lambda l, h, n: (jnp.where((l == 0) & (h == 0), n, steps - 1), 0)),
    )
    add((layers, total, D), jnp.float32, half_two(D))
    for cols, kind in ((3 * D, BF), (HEADS * tokens, BF), (D, BF), (D, BF), (D, jnp.float32)):
        add((layers, total, cols), kind, half_one(cols))
    for cols in (D, 4 * D, 4 * D):
        add((layers, total, cols), BF, half_two(cols))
    add((layers, steps, 8, D), jnp.float32, pl.BlockSpec((1, 1, 8, D), square_index))
    args = (*weights_in, feat, hot, noisy, pos)
    in_specs = [const(a) for a in args[:-2]]
    in_specs.append(
        pl.BlockSpec(
            (nb, PATCH_IN, tokens), lambda l, h, n: (jnp.where((l == 0) & (h == 0), n, steps - 1), 0, 0)
        )
    )
    in_specs.append(const(pos))
    count = chunks * copies_per_part(places)
    return pl.pallas_call(
        functools.partial(
            fused_forward_kernel,
            places,
            slots,
            layers,
            nb,
            tokens,
            lat_count,
            (small_rows, ada_rows, part_rows, wide_rows),
        ),
        grid=(layers, 2, steps),
        out_shape=out_shape,
        in_specs=in_specs,
        out_specs=out_specs,
        scratch_shapes=[pltpu.VMEM(s, BF) for s in full_shapes]
        + [
            pltpu.VMEM((slots * lax.axis_size("tp"), small_rows, D), BF),
            pltpu.VMEM((SPLIT + 3 * layers, wide_rows, D), BF),
            pltpu.VMEM((total, D), jnp.float32),
            pltpu.VMEM((total, D), jnp.float32),
            pltpu.SemaphoreType.DMA((count,)),
            pltpu.SemaphoreType.DMA((count,)),
            pltpu.SemaphoreType.DMA((chunks,)),
            pltpu.SemaphoreType.DMA((chunks,)),
        ],
        compiler_params=pltpu.CompilerParams(
            collective_id=3, has_side_effects=True, vmem_limit_bytes=LIMIT
        ),
        name="gather_and_forward",
    )(*args)


LIMIT_B = 62 * 1024 * 1024


def attend_backward(nb, tokens, qkv_ref, probs_ref, d_mix, d_qkv_s):
    masks = half_masks()
    lane = lax.broadcasted_iota(jnp.int32, (tokens, 2 * HEAD_DIM), 1)
    low_side = lane < HEAD_DIM
    root = HEAD_DIM**-0.5
    for b in range(nb):
        here = slice(b * tokens, (b + 1) * tokens)
        for pair in range(HEADS // 2):
            col = pair * 2 * HEAD_DIM
            queries = qkv_ref[here, col : col + 2 * HEAD_DIM]
            keys = stack_heads(qkv_ref[here, D + col : D + col + 2 * HEAD_DIM], masks)
            values = stack_heads(qkv_ref[here, 2 * D + col : 2 * D + col + 2 * HEAD_DIM], masks)
            d_out = d_mix[here, col : col + 2 * HEAD_DIM]
            probs_bf = probs_ref[here, pair * 2 * tokens : (pair + 1) * 2 * tokens]
            d_probs = dot_nt(d_out, values)
            halves = []
            for side in range(2):
                cut = slice(side * tokens, (side + 1) * tokens)
                probs = probs_bf[:, cut].astype(jnp.float32)
                part = d_probs[:, cut]
                halves.append((probs * (part - jnp.sum(probs * part, axis=-1, keepdims=True))).astype(BF))
            d_scores = jnp.concatenate(halves, axis=1)
            d_queries = dot_nn(d_scores, keys) * root
            d_keys = dot_tn(d_scores, queries)
            d_keys = jnp.where(low_side, d_keys[:tokens], d_keys[tokens:]) * root
            d_values = dot_tn(probs_bf, d_out)
            d_values = jnp.where(low_side, d_values[:tokens], d_values[tokens:])
            d_qkv_s[here, col : col + 2 * HEAD_DIM] = d_queries.astype(BF)
            d_qkv_s[here, D + col : D + col + 2 * HEAD_DIM] = d_keys.astype(BF)
            d_qkv_s[here, 2 * D + col : 2 * D + col + 2 * HEAD_DIM] = d_values.astype(BF)


def lane_sums(rows):
    total = jnp.sum(rows, axis=0, keepdims=True)
    return sum(total[:, at : at + 128] for at in range(0, total.shape[1], 128))


def fused_backward_kernel(places, slots, layers, nb, tokens, lat_count, count_all, sizes, *refs):
    small_rows, ada_rows, part_rows, wide_rows = sizes
    chunks = slots + SPLIT + 3 * layers
    steps = lat_count // nb
    depth = len(places.dims)
    rows = nb * tokens
    given = refs[:chunks]
    feat_ref, hot_ref, mods_ref, fmod_ref, pre_ref, cond_ref, square_ref = refs[chunks : chunks + 7]
    (
        clean_ref,
        noise_ref,
        noisy_ref,
        start_ref,
        result_ref,
        qkv_ref,
        probs_ref,
        mixed_ref,
        branch_ref,
        middle_ref,
        mlp_ref,
        act_ref,
        slope_ref,
    ) = refs[chunks + 7 : chunks + 20]
    refs = refs[chunks + 20 :]
    outs, both_ref, stats_ref = refs[:chunks], refs[chunks], refs[chunks + 1]
    refs = refs[chunks + 2 :]
    fulls, accs = refs[:chunks], refs[chunks : 2 * chunks]
    lands = refs[2 * chunks : (2 + depth) * chunks]
    (
        stage_attn,
        stage_in,
        stage_out,
        acc_one,
        acc_two,
        d_stream_s,
        d_qkv_s,
        d_mods_s,
        d_raw_s,
        d_fmod_s,
        d_patch_s,
        d_head_s,
        loss_s,
        sum_s,
        stats_s,
        both_s,
        stats_land,
        send_sems,
        recv_sems,
        own_sems,
        take_sems,
        stats_send,
        stats_recv,
        both_send,
        both_recv,
    ) = refs[(2 + depth) * chunks :]
    turn, h, n = (pl.program_id(axis) for axis in range(3))
    mine = places.mine()
    lead = slots + SPLIT

    def flat(ref, count):
        return ref.reshape(places.count * count, D)

    takes = [pltpu.make_async_copy(given[m], fulls[m], take_sems.at[m]) for m in range(chunks)]
    slot_refs = [f.reshape(-1, lax.axis_size("tp"), small_rows, D) for f in fulls[:slots]]
    ada_refs = [flat(f, part_rows) for f in fulls[slots:lead]]
    staged = {0: stage_attn, 1: stage_in, 2: stage_out}
    order = [lead + 4, lead + 5, lead + 3, slots + 2, lead + 1, lead + 2, lead, 0, 1, slots, slots + 1]
    traffic = Traffic(places, mine, send_sems, recv_sems, own_sems)
    jobs = []
    first_copies = []
    for at, m in enumerate(order):
        source = fulls[m] if m < lead else staged[(m - lead) % 3]
        used = traffic.used
        jobs.append(
            reduce_job(
                traffic, at % 2 == 1, source, accs[at], lands[at * depth : (at + 1) * depth], outs[m]
            )
        )
        digit = places.order(at % 2 == 1)[-1]
        first_copies.append(traffic.copies[used : used + places.dims[digit] - 1])

    def run(*names):
        for job, k in names:
            jobs[job][k]()

    def at_step(number):
        layer_turn, rest = divmod(number, 2 * steps)
        half, step = divmod(rest, steps)
        return pl.when((turn == layer_turn) & (h == half) & (n == step))

    def both(pair, k):
        return [(job, k) for job in (2 * pair, 2 * pair + 1) if job < len(jobs)]

    here = pl.ds(pl.multiple_of(n * rows, rows), rows)

    def mod_of(layer):
        return lambda part: mod_rows(mods_ref, (layer,), n, nb, part)

    def put_mod(layer, part, value):
        for b in range(nb):
            d_mods_s[layer, pl.ds(n * nb + b, 1), part * D : (part + 1) * D] = value[b]

    @at_step(0)
    def _():
        for m in [*range(slots), lead + 5, lead + 4, lead + 3, lead + 2, lead + 1, lead, *range(slots, lead)]:
            takes[m].start()
        d_mods_s[...] = jnp.zeros_like(d_mods_s)
        d_fmod_s[...] = jnp.zeros_like(d_fmod_s)
        d_patch_s[...] = jnp.zeros_like(d_patch_s)
        d_head_s[...] = jnp.zeros_like(d_head_s)
        loss_s[...] = jnp.zeros_like(loss_s)
        sum_s[...] = jnp.zeros_like(sum_s)
        places.barrier(mine)
        for m in (*range(slots), lead + 5, lead + 4):
            takes[m].wait()

    hooks = {
        steps: [],
        steps + 1: both(0, 1),
        2 * steps - 1: both(0, 2),
        2 * steps + 1: both(0, 3) + both(1, 1),
        3 * steps - 1: both(1, 2) + both(0, 4),
        3 * steps + 1: both(1, 3) + both(2, 1),
        4 * steps - 1: both(2, 2) + both(1, 4),
    }
    early_ada = [slots + p for p in range(SPLIT) if p * part_rows < (layers - 1) * ada_rows]
    loads = {steps: [lead + 3], 2 * steps: [lead + 2, lead + 1], 3 * steps: [lead, *early_ada]}
    for number in sorted(set(hooks) | set(loads)):

        @at_step(number)
        def _(number=number):
            for m in loads.get(number, []):
                takes[m].wait()
            run(*hooks.get(number, []))

    def spread(layer):
        wide = places.count * part_rows
        for l, col, p, at, length in modulation_pieces(layers, ada_rows, part_rows, places.count):
            if l == layer:
                d_raw_s[:, p * wide + at : p * wide + at + length] = d_mods_s[layer, :, col : col + length]

    def finish_all():
        run((6, 0))
        cond = cond_ref[...]
        pre = pre_ref[...]
        cond_act = silu(cond).astype(BF)
        cond_two = jnp.concatenate([cond_act, cond_act], axis=0)
        spread(0)
        wide = places.count * part_rows
        d_cond = sum_s[...]
        d_mods = {}
        for p in range(SPLIT):
            if p * part_rows < (layers - 1) * ada_rows:
                d_mods[p] = split_low(d_raw_s[:, p * wide : (p + 1) * wide])
                d_cond = d_cond + dot_nn(d_mods[p], ada_refs[p][...])
        d_fmods = [split_low(d_fmod_s[:, k * D : (k + 1) * D]) for k in range(2)]
        for k in range(2):
            d_cond = d_cond + dot_nt(d_fmods[k], block_of(slot_refs, 5 + k))
        run(*both(2, 3))
        d_pre = split_low((d_cond[:8] + d_cond[8:]) * silu_slope(cond))
        d_time = dot_nn(d_pre, block_of(slot_refs, 1))
        d_time = split_low((d_time[:8] + d_time[8:]) * silu_slope(pre))
        time_act = silu(pre).astype(BF)

        def give(k, grad):
            ref = slot_refs[k % slots]
            ref[:, k // slots] = grad.astype(BF).reshape(ref.shape[0], ref.shape[2], D)

        def twice(values):
            return jnp.concatenate([values, values], axis=0)

        def k_time():
            grad = dot_tn(d_time, twice(feat_ref[...]))
            corner = jnp.pad(d_patch_s[...], ((0, 128 - PATCH_IN), (0, 0))).T
            return jnp.concatenate([grad[:, :128] + corner, grad[:, 128:]], axis=1)

        def k_class(k):
            grad = dot_tn(d_pre, twice(hot_ref[:, k * D : (k + 1) * D]))
            if k == 2:
                corner = jnp.pad(d_head_s[...], ((0, 128 - OUT), (0, 0))).T
                grad = jnp.concatenate([grad[:, :256], grad[:, 256:] + corner], axis=1)
            return grad

        makers = {
            0: k_time,
            1: lambda: dot_tn(d_pre, twice(time_act)),
            2: lambda: k_class(0),
            3: lambda: k_class(1),
            4: lambda: k_class(2),
            5: lambda: dot_tn(cond_two, d_fmods[0]),
            6: lambda: dot_tn(cond_two, d_fmods[1]),
        }
        for slot in range(slots):
            for k in range(slot, SMALL, slots):
                give(k, makers[k]() if k in makers else jnp.zeros((D, D), jnp.float32))
            if slot == 0:
                run((7, 0), (6, 1))
        run((8, 0))
        for p, d_mod in d_mods.items():
            ada_refs[p][...] = dot_tn(d_mod, cond_two).astype(BF)
        run((9, 0), (10, 0), (7, 1), (8, 1), (9, 1))
        run(*both(2, 4), *both(3, 2), (10, 1), (8, 2), *both(3, 3), (9, 2), (10, 2), (8, 3))
        run((9, 3), *both(3, 4), (8, 4))
        inner = [d for d in reversed(range(depth)) if places.digits[d][0] == "tp"]
        for s in range(slots):
            both_s[(lax.axis_index("tp"), s)] = outs[s][...]

        def both_stage(stage):
            digit = inner[stage]
            _, stride, size = places.digits[digit]
            start = lax.axis_index("tp") // stride * stride
            copies = []
            for shift in range(1, size):
                target, _ = places.other(mine, digit, shift)
                where = both_s.at[pl.ds(start, stride)]
                copies.append(
                    pltpu.make_async_remote_copy(
                        src_ref=where,
                        dst_ref=where,
                        send_sem=both_send.at[stage, shift - 1],
                        recv_sem=both_recv.at[stage, shift - 1],
                        device_id=target,
                        device_id_type=MESH,
                    )
                )
                copies[-1].start()
            return copies

        pending = both_stage(0)
        run((10, 3), (9, 4))
        for stage in range(1, len(inner)):
            for copy in pending:
                copy.wait()
            pending = both_stage(stage)
        run((10, 4))
        grad = sum(lane_sums(out[...] * out[...]) for out in outs)
        squares = [lane_sums(jnp.sum(square_ref[l], axis=0)) for l in range(layers)]
        stats_s[...] = jnp.concatenate(
            [grad, lane_sums(loss_s[...]), *squares, jnp.zeros((6 - layers, 128), jnp.float32)], axis=0
        )
        for stage, digit in enumerate(reversed(range(depth))):
            size = places.dims[digit]
            stats_land[stage, mine[digit]] = stats_s[...]
            copies = []
            for shift in range(1, size):
                target, _ = places.other(mine, digit, shift)
                copies.append(
                    pltpu.make_async_remote_copy(
                        src_ref=stats_s,
                        dst_ref=stats_land.at[stage, mine[digit]],
                        send_sem=stats_send.at[stage, shift - 1],
                        recv_sem=stats_recv.at[stage, shift - 1],
                        device_id=target,
                        device_id_type=MESH,
                    )
                )
                copies[-1].start()
            for copy in copies:
                copy.wait()
            total = stats_land[stage, 0]
            for value in range(1, size):
                total = total + stats_land[stage, value]
            stats_s[...] = total
        stats_ref[...] = stats_s[...]
        for copy in pending:
            copy.wait()
        both_ref[...] = both_s[...]
        waited = {id(copy) for group in first_copies[:3] for copy in group}
        for copy in traffic.copies:
            if id(copy) not in waited:
                copy.wait_send()

    for layer in range(layers):
        mod = mod_of(layer)
        is_turn = turn == layers - 1 - layer
        attn_w, in_w, out_w = (flat(fulls[lead + 3 * layer + k], wide_rows) for k in range(3))

        @pl.when(is_turn & (h == 0))
        def _(layer=layer, mod=mod, in_w=in_w, out_w=out_w):
            @pl.when(n == 0)
            def _():
                acc_one[...] = jnp.zeros_like(acc_one)
                acc_two[...] = jnp.zeros_like(acc_two)

            if layer == layers - 1:
                head = block_of(slot_refs, 4)[:, 256 : 256 + OUT]
                fmod = lambda part: mod_rows(fmod_ref, (), n, nb, part)
                hat, rstd = norm_rows(result_ref[0].reshape(nb, tokens, D))
                final_in = (hat * (1.0 + fmod(1)) + fmod(0)).astype(BF)
                d_parts = []
                for b in range(nb):
                    predicted = lax.dot_general(
                        head, final_in[b], (((0,), (1,)), ((), ())), preferred_element_type=jnp.float32
                    )
                    errors = predicted - jnp.concatenate([noise_ref[b], clean_ref[b]], axis=0)
                    loss_s[...] += jnp.sum((errors * errors).reshape(OUT // 8, 8, tokens), axis=0)
                    d_pred = (errors * (2.0 / count_all)).astype(BF)
                    d_head_s[...] += dot_nn(d_pred, final_in[b])
                    d_parts.append(
                        lax.dot_general(
                            d_pred, head, (((0,), (1,)), ((), ())), preferred_element_type=jnp.float32
                        )
                    )
                d_stream, d_shift, d_scale = norm_back(jnp.stack(d_parts, axis=0), hat, rstd, fmod(1))
                for b in range(nb):
                    d_fmod_s[pl.ds(n * nb + b, 1), :D] = d_shift[b]
                    d_fmod_s[pl.ds(n * nb + b, 1), D:] = d_scale[b]
            else:
                d_stream = d_stream_s[here, :].reshape(nb, tokens, D)
            mlp = mlp_ref[0].astype(jnp.float32).reshape(nb, tokens, D)
            put_mod(layer, 5, jnp.sum(d_stream * mlp, axis=1, keepdims=True))
            d_mlp = (d_stream * mod(5)).astype(BF).reshape(rows, D)
            d_hidden = (dot_nt(d_mlp, out_w[...]) * slope_ref[0].astype(jnp.float32)).astype(BF)
            acc_two[...] += dot_tn(act_ref[0], d_mlp)
            hat, rstd = norm_rows(middle_ref[0].reshape(nb, tokens, D))
            mlp_in = (hat * (1.0 + mod(4)) + mod(3)).astype(BF).reshape(rows, D)
            acc_one[...] += dot_tn(d_hidden, mlp_in)
            d_input = dot_nn(d_hidden, in_w[...]).reshape(nb, tokens, D)
            d_middle, d_shift, d_scale = norm_back(d_input, hat, rstd, mod(4))
            put_mod(layer, 3, d_shift)
            put_mod(layer, 4, d_scale)
            d_stream_s[here, :] = (d_middle + d_stream).reshape(rows, D)

            @pl.when(n == steps - 1)
            def _():
                pair = 0 if layer == layers - 1 else 2
                if pair:
                    for copy in first_copies[0] + first_copies[1]:
                        copy.wait_send()
                flat(stage_in, wide_rows)[...] = acc_one[...].astype(BF)
                flat(stage_out, wide_rows)[...] = acc_two[...].astype(BF)
                run(*both(pair, 0))

        @pl.when(is_turn & (h == 1))
        def _(layer=layer, mod=mod, attn_w=attn_w):
            @pl.when(n == 0)
            def _():
                acc_one[...] = jnp.zeros_like(acc_one)

            d_middle = d_stream_s[here, :].reshape(nb, tokens, D)
            branch = branch_ref[0].astype(jnp.float32).reshape(nb, tokens, D)
            put_mod(layer, 2, jnp.sum(d_middle * branch, axis=1, keepdims=True))
            d_proj = (d_middle * mod(2)).astype(BF).reshape(rows, D)
            acc_one[3 * D :, :] += dot_tn(d_proj, mixed_ref[0])
            d_mix = dot_nn(d_proj, attn_w[3 * D :, :]).astype(BF)
            attend_backward(nb, tokens, qkv_ref.at[0], probs_ref.at[0], d_mix, d_qkv_s)
            d_qkv = d_qkv_s[...]
            stream = start_ref[...] if layer == 0 else result_ref[0]
            hat, rstd = norm_rows(stream.reshape(nb, tokens, D))
            attn_in = (hat * (1.0 + mod(1)) + mod(0)).astype(BF).reshape(rows, D)
            acc_one[: 3 * D, :] += dot_tn(d_qkv, attn_in)
            d_attn_in = dot_nn(d_qkv, attn_w[: 3 * D, :]).reshape(nb, tokens, D)
            d_before, d_shift, d_scale = norm_back(d_attn_in, hat, rstd, mod(1))
            put_mod(layer, 0, d_shift)
            put_mod(layer, 1, d_scale)
            d_prev = d_middle + d_before
            if layer == 0:
                for b in range(nb):
                    d_patch_s[...] += lax.dot_general(
                        noisy_ref[b].astype(jnp.float32),
                        d_prev[b],
                        (((1,), (0,)), ((), ())),
                        precision=highest,
                    )
            else:
                d_stream_s[here, :] = d_prev.reshape(rows, D)

            @pl.when(n == steps - 1)
            def _():
                if layer == 0:
                    for copy in first_copies[2]:
                        copy.wait_send()
                flat(stage_attn, wide_rows)[...] = acc_one[...].astype(BF)
                if layer > 0:
                    cond_act = silu(cond_ref[...]).astype(BF)
                    cond_two = jnp.concatenate([cond_act, cond_act], axis=0)
                    spread(layer)
                    wide = places.count * part_rows
                    for p in range(SPLIT):
                        if p * part_rows >= layer * ada_rows:
                            d_mod = split_low(d_raw_s[:, p * wide : (p + 1) * wide])
                            takes[slots + p].wait()
                            sum_s[...] += dot_nn(d_mod, ada_refs[p][...])
                            ada_refs[p][...] = dot_tn(d_mod, cond_two).astype(BF)
                    run(*both(1, 0))
                else:
                    finish_all()


def fused_backward(places, slots, nb, count_all, given, feat, hot, mods, fmod, pre, cond, square, streams):
    clean_t, noise_t, noisy, start, result, *kept = streams
    layers = mods.shape[0]
    lat_count, _, tokens = noisy.shape
    total, rows, steps = lat_count * tokens, nb * tokens, lat_count // nb
    chunks = len(given)
    dims = places.dims
    depth, widest = len(dims), max(dims)
    block = given[0].shape[-2:]
    last = steps - 1

    def const_shape(shape):
        return pl.BlockSpec(shape, lambda t, h, n: (0,) * len(shape))

    def only(turn, half, before, after):
        def pick(t, h, n):
            at, phase = 2 * t + h, 2 * turn + half
            return jnp.where(at == phase, n, jnp.where(at < phase, before, after))

        return pick

    def spec(block_shape, pick):
        return pl.BlockSpec(block_shape, lambda t, h, n: (pick(t, h, n),) + (0,) * (len(block_shape) - 1))

    def result_index(t, h, n):
        head = (t == 0) & (h == 0)
        body_step = (t == 0) & (h == 1)
        return (jnp.where(head, 1, 0), jnp.where(head | body_step, n, last), 0)

    def mlp_spec(cols):
        return pl.BlockSpec(
            (1, rows, cols), lambda t, h, n: (layers - 1 - t, jnp.where(h == 0, n, last), 0)
        )

    def attn_spec(cols):
        return pl.BlockSpec((1, rows, cols), lambda t, h, n: (layers - 1 - t, jnp.where(h == 1, n, 0), 0))

    consts = (feat, hot, mods, fmod, pre, cond, square)
    in_specs = [pl.BlockSpec(memory_space=pl.ANY)] * chunks + [const_shape(a.shape) for a in consts]
    in_specs += [spec((nb, PATCH_IN, tokens), only(0, 0, 0, last))] * 2
    in_specs += [
        spec((nb, PATCH_IN, tokens), only(1, 1, 0, last)),
        spec((rows, D), only(1, 1, 0, last)),
        pl.BlockSpec((1, rows, D), result_index),
    ]
    in_specs += [attn_spec(a.shape[2]) for a in kept[:4]] + [mlp_spec(a.shape[2]) for a in kept[4:]]
    shared = (lax.axis_size("tp"), slots, *block)
    out_shape = [jax.ShapeDtypeStruct(block, jnp.float32)] * chunks
    out_shape += [jax.ShapeDtypeStruct(s, jnp.float32) for s in (shared, (8, 128))]
    full = (*dims, *block)
    lands = []
    for at in range(chunks):
        lands += [pltpu.VMEM(shape, BF) for shape in land_shapes(places, at % 2 == 1, block)]
    f32 = jnp.float32
    scratch = [pltpu.VMEM(full, BF)] * chunks + [pltpu.VMEM(dims[:-1] + block, BF)] * chunks + lands
    scratch += [pltpu.VMEM(full, BF)] * 3
    scratch += [
        pltpu.VMEM(shape, kind)
        for shape, kind in (
            ((4 * D, D), f32),
            ((4 * D, D), f32),
            ((total, D), f32),
            ((rows, 3 * D), BF),
            (mods.shape, f32),
            ((8, SPLIT * places.count * block[0]), f32),
            ((8, 2 * D), f32),
            ((PATCH_IN, D), f32),
            ((OUT, D), f32),
            ((8, tokens), f32),
            ((16, D), f32),
            ((8, 128), f32),
            (shared, f32),
            ((depth, widest, 8, 128), f32),
        )
    ]
    dma = pltpu.SemaphoreType.DMA
    count = chunks * copies_per_part(places)
    scratch += [dma((count,)), dma((count,)), dma((chunks,)), dma((chunks,))]
    scratch += [dma((depth, widest - 1))] * 4
    sizes = (block[0], 6 * D // places.count, block[0], block[0])
    return pl.pallas_call(
        functools.partial(
            fused_backward_kernel, places, slots, layers, nb, tokens, lat_count, count_all, sizes
        ),
        grid=(layers, 2, steps),
        out_shape=out_shape,
        in_specs=in_specs,
        out_specs=[const_shape(s.shape) for s in out_shape],
        scratch_shapes=scratch,
        compiler_params=pltpu.CompilerParams(
            collective_id=4, has_side_effects=True, vmem_limit_bytes=LIMIT_B
        ),
        name="backward_and_reduce",
    )(*given, *consts, *streams)


def position_table(grid_side, columns):
    quarter = columns // 4
    omegas = jnp.exp(-math.log(10000.0) * jnp.arange(quarter, dtype=jnp.float32) / quarter)
    positions = jnp.arange(grid_side * grid_side, dtype=jnp.int32)
    row_pos = (positions // grid_side).astype(jnp.float32)[:, None] * omegas
    col_pos = (positions % grid_side).astype(jnp.float32)[:, None] * omegas
    return jnp.concatenate(
        [jnp.sin(row_pos), jnp.cos(row_pos), jnp.sin(col_pos), jnp.cos(col_pos)], axis=-1
    )


def time_table(step_ids, columns):
    half_cols = columns // 2
    frequency = jnp.exp(-math.log(10000.0) * jnp.arange(half_cols, dtype=jnp.float32) / half_cols)
    angles = step_ids.astype(jnp.float32)[:, None] * frequency
    return jnp.concatenate([jnp.cos(angles), jnp.sin(angles)], axis=-1)


def noise_scales(step_ids):
    phases = (step_ids.astype(jnp.float32) / NOISE_STEPS + 0.008) / 1.008 * (math.pi / 2)
    return (jnp.cos(phases), jnp.sin(phases))


def swap(array):
    return jnp.swapaxes(array, -1, -2)


def pad_rows(part):
    extra = -part.shape[-2] % 16
    if extra == 0:
        return part
    return jnp.pad(part, [(0, 0)] * (part.ndim - 2) + [(0, extra), (0, 0)])


def body(
    clean_latents,
    noise_field,
    timesteps,
    labels,
    drop_flags,
    entry_weight,
    class_table,
    attn_weight,
    ffn_in_weight,
    ffn_out_weight,
    ada_weight,
    final_weight,
    entry_first,
    entry_second,
    class_first,
    class_second,
    attn_first,
    attn_second,
    ffn_in_first,
    ffn_in_second,
    ffn_out_first,
    ffn_out_second,
    ada_first,
    ada_second,
    final_first,
    final_second,
):
    lat_count = clean_latents.shape[0]
    tokens = clean_latents.shape[1]
    layers = attn_weight.shape[0]
    both = ("dp", "tp")
    devices = lax.axis_size("dp") * lax.axis_size("tp")
    count_all = float(lat_count * devices * tokens * OUT)
    count_rms = float(lat_count * devices * tokens * D)
    nb = 1
    clean_t, noise_t = swap(clean_latents), swap(noise_field)
    cos_part, sin_part = noise_scales(timesteps)
    noisy = (cos_part[:, None, None] * clean_t + sin_part[:, None, None] * noise_t).astype(BF)
    n_dp, n_tp = lax.axis_size("dp"), lax.axis_size("tp")
    places = Places(n_dp, n_tp)
    slots = -(-SMALL // n_tp)
    dp_rows = final_weight.shape[0]
    wide_rows = attn_weight.shape[2]
    ada_rows = ada_weight.shape[2]
    part_rows = -(-layers * ada_rows // SPLIT)

    def flat_ada(array):
        return swap(array).reshape(layers * ada_rows, D)

    weights_in = (
        swap(entry_weight),
        swap(class_table),
        final_weight,
        flat_ada(ada_weight),
        swap(attn_weight),
        swap(ffn_in_weight),
        ffn_out_weight,
    )
    def whole_rows(block, rows):
        return block[:, :rows].reshape(-1, D)

    def to_slot(block):
        if dp_rows % 16 == 0:
            return block.reshape(n_dp, n_tp, dp_rows, D)
        block = block.reshape(n_dp, n_tp, -1, D)[:, :, :dp_rows]
        return block.swapaxes(0, 1).reshape(1, n_tp, n_dp * dp_rows, D)

    def from_slot(block):
        if dp_rows % 16 == 0:
            return block.reshape(places.count, dp_rows, D)
        block = block.reshape(n_tp, n_dp, dp_rows, D).swapaxes(0, 1)
        return pad_rows(block.reshape(places.count, dp_rows, D))

    time_feat = time_table(timesteps, FREQ).astype(BF)
    feat = jnp.pad(time_feat, ((0, 8 - lat_count), (PATCH_IN, D - PATCH_IN - FREQ)))
    classes_used = jnp.where(drop_flags == 1, CLASSES, labels)
    classes_used = jnp.pad(classes_used, (0, 8 - lat_count), constant_values=3 * D)
    class_hot = (classes_used[:, None] == jnp.arange(3 * D, dtype=jnp.int32)[None, :]).astype(BF)
    pos = position_table(GRID, D)
    fused = dp_rows == wide_rows == part_rows and dp_rows % 16 == 0 and len(places.dims) >= 4 and layers == 2
    if fused:
        outs = fused_forward(places, slots, nb, weights_in, feat, class_hot, noisy, pos)
        chunks = slots + SPLIT + 3 * layers
        mods, fmod, pre, cond, start, result, *kept, square = outs[chunks:]
        streams = (clean_t, noise_t, noisy, start, result, *kept)
        *summed, both, stats = fused_backward(
            places, slots, nb, count_all, outs[:chunks], feat, class_hot, mods, fmod, pre, cond, square, streams
        )
        wide = summed[slots + SPLIT :]
    else:
        gathered = gather_all(places, slots, *weights_in)
        slot_full = [to_slot(g) for g in gathered[:slots]]
        ada_full = [whole_rows(g, part_rows) for g in gathered[slots : slots + SPLIT]]
        block_full = [whole_rows(g, wide_rows) for g in gathered[slots + SPLIT :]]
        weights = [tuple(block_full[3 * l : 3 * l + 3]) for l in range(layers)]

        raw, fmod, pre, cond, patch_t, head = condition(feat, class_hot, slot_full, ada_full, lat_count)
        mods = raw[:lat_count].reshape(lat_count, SPLIT, places.count, part_rows).swapaxes(1, 2)
        mods = mods.reshape(lat_count, places.count, layers, ada_rows).transpose(2, 0, 1, 3)
        mods = mods.reshape(layers, lat_count, 6, D)
        mods = jnp.pad(mods, ((0, 0), (0, 0), (0, 2), (0, 0)))
        mods = [mods[l] for l in range(layers)]
        saved = []
        squares = []
        stream = None
        for l in range(layers):
            if l == 0:
                outs = forward_layer(True, (noisy, patch_t, pos), mods[l], weights[l], nb, tokens)
                stream, outs = outs[0], outs[1:]
            else:
                outs = forward_layer(False, (stream,), mods[l], weights[l], nb, tokens)
            saved.append((stream, *outs[1:9]))
            stream = outs[0]
            squares.append(outs[9])
        layer_grads = [None] * layers
        d_mods = [None] * layers
        d_stream = None
        for l in reversed(range(layers)):
            last, first = l == layers - 1, l == 0
            entry_args = (stream, fmod, head, clean_t, noise_t) if last else (d_stream,)
            if first:
                entry_args = (*entry_args, noisy)
            outs = list(backward_layer(first, last, entry_args, mods[l], weights[l], saved[l], nb, tokens, count_all))
            if last:
                loss_part, d_head_t, d_fmod = outs[:3]
                outs = outs[3:]
            if first:
                d_patch = outs[0]
            else:
                d_stream = outs[0]
            layer_grads[l] = outs[1:4]
            d_mods[l] = outs[4]
        d_raw = jnp.stack([d[:, :6] for d in d_mods]).reshape(layers, lat_count, places.count, ada_rows)
        d_raw = d_raw.transpose(1, 2, 0, 3).reshape(lat_count, places.count, SPLIT, part_rows)
        d_raw = d_raw.swapaxes(1, 2).reshape(lat_count, -1)
        d_raw = jnp.pad(d_raw, ((0, 8 - lat_count), (0, 0)))
        small_grads = condition_back(
            feat, class_hot, slot_full, ada_full, pre, cond, d_raw, d_fmod, d_patch, d_head_t
        )
        grads = [from_slot(g) for g in small_grads[:slots]]
        grads += [pad_rows(g.reshape(places.count, part_rows, D)) for g in small_grads[slots:]]
        for l in reversed(range(layers)):
            for k in range(3):
                grads.append(pad_rows(layer_grads[l][k].reshape(places.count, wide_rows, D)))
        *summed, both, stats = reduce_all(places, slots, grads, loss_part, squares)
        wide = summed[slots + SPLIT :]
        wide = [wide[3 * (layers - 1 - l) + k] for l in range(layers) for k in range(3)]
    states = []
    for shape_it, triple in (
        (swap, (entry_weight, entry_first, entry_second)),
        (swap, (class_table, class_first, class_second)),
        (swap, (attn_weight, attn_first, attn_second)),
        (swap, (ffn_in_weight, ffn_in_first, ffn_in_second)),
        (lambda a: a, (ffn_out_weight, ffn_out_first, ffn_out_second)),
        (flat_ada, (ada_weight, ada_first, ada_second)),
        (lambda a: a, (final_weight, final_first, final_second)),
    ):
        states.extend(shape_it(a) for a in triple)
    out = adam_all(slots, layers, count_rms, stats, both, [*summed[slots : slots + SPLIT], *wide], states)
    news = []
    for at in range(21):
        value = out[at]
        if at // 3 == 5:
            value = value.reshape(layers, ada_rows, D)
        news.append(value if at // 3 in (4, 6) else swap(value))
    return (*news, out[21].reshape(()), out[22].reshape(()), out[23].reshape(layers))


def solution(mesh):
    lead = P(("dp", "tp"), None, None)
    ids = P(("dp", "tp"))
    wide = P(None, "dp")
    cols = P(None, None, ("dp", "tp"))
    rows = P(None, ("dp", "tp"), None)
    top = P("dp", None)
    return jax.shard_map(
        body,
        mesh=mesh,
        in_specs=(
            lead,
            lead,
            ids,
            ids,
            ids,
            wide,
            wide,
            cols,
            cols,
            rows,
            cols,
            top,
            wide,
            wide,
            wide,
            wide,
            cols,
            cols,
            cols,
            cols,
            rows,
            rows,
            cols,
            cols,
            top,
            top,
        ),
        out_specs=(wide,) * 6 + (cols,) * 6 + (rows,) * 3 + (cols,) * 3 + (top,) * 3 + (P(), P(), P()),
        check_vma=False,
    )
```

```python
import functools
import math

import jax
import jax.numpy as jnp
import numpy as np
from jax import lax
from jax.experimental import pallas as pl
from jax.experimental.pallas import tpu as pltpu
from jax.sharding import PartitionSpec as P

D = 384
HEADS = 6
HEAD_DIM = 64
CLASSES = 1000
GRID = 16
PATCH_IN = 16
OUT = 32
FREQ = 256
NOISE_STEPS = 1000
STEP = 10
BF = jnp.bfloat16


highest = lax.Precision.HIGHEST


def dot_nn(a, b):
    return lax.dot_general(a, b, (((1,), (0,)), ((), ())), preferred_element_type=jnp.float32)


def dot_nt(a, b):
    return lax.dot_general(a, b, (((1,), (1,)), ((), ())), preferred_element_type=jnp.float32)


def dot_tn(a, b):
    return lax.dot_general(a, b, (((0,), (0,)), ((), ())), preferred_element_type=jnp.float32)


def norm_rows(rows):
    center = rows - jnp.mean(rows, axis=-1, keepdims=True)
    rstd = lax.rsqrt(jnp.mean(center * center, axis=-1, keepdims=True) + 1e-06)
    return center * rstd, rstd


def norm_back(d_out, hat, rstd, scale):
    d_shift = jnp.sum(d_out, axis=1, keepdims=True)
    d_scale = jnp.sum(d_out * hat, axis=1, keepdims=True)
    d_hat = d_out * (1.0 + scale)
    m_one = jnp.mean(d_hat, axis=-1, keepdims=True)
    m_two = jnp.mean(d_hat * hat, axis=-1, keepdims=True)
    return rstd * (d_hat - m_one - hat * m_two), d_shift, d_scale


def half_masks():
    lane = lax.broadcasted_iota(jnp.int32, (1, 2 * HEAD_DIM), 1)
    low = jnp.where(lane < HEAD_DIM, 1.0, 0.0)
    return low.astype(BF), (1.0 - low).astype(BF)


def stack_heads(pair, masks):
    return jnp.concatenate([pair * masks[0], pair * masks[1]], axis=0)


GELU_A = math.sqrt(2.0 / math.pi)
GELU_B = 0.044715


def forward_kernel(first, nb, tokens, *refs):
    if first:
        noisy_ref, patch_ref, pos_ref = refs[:3]
        refs = refs[3:]
    else:
        stream_ref = refs[0]
        refs = refs[1:]
    mod_ref, attn_ref, in_ref, out_ref = refs[:4]
    refs = refs[4:]
    if first:
        start_ref = refs[0]
        refs = refs[1:]
    (
        result_ref,
        qkv_ref,
        probs_ref,
        mixed_ref,
        branch_ref,
        middle_ref,
        mlp_ref,
        act_ref,
        slope_ref,
        square_ref,
    ) = refs
    rows = nb * tokens
    if first:
        parts = [
            lax.dot_general(
                noisy_ref[n], patch_ref[...], (((0,), (1,)), ((), ())), preferred_element_type=jnp.float32
            )
            + pos_ref[...]
            for n in range(nb)
        ]
        stream = parts[0] if nb == 1 else jnp.concatenate(parts, axis=0)
        start_ref[...] = stream
    else:
        stream = stream_ref[...]
    mod = mod_ref[...]
    stream = stream.reshape(nb, tokens, D)
    hat, _ = norm_rows(stream)
    attn_in = (hat * (1.0 + mod[:, 1:2]) + mod[:, 0:1]).astype(BF).reshape(rows, D)
    qkv_ref[...] = dot_nt(attn_in, attn_ref[: 3 * D, :]).astype(BF)
    masks = half_masks()
    for n in range(nb):
        here = slice(n * tokens, (n + 1) * tokens)
        for pair in range(HEADS // 2):
            col = pair * 2 * HEAD_DIM
            queries = qkv_ref[here, col : col + 2 * HEAD_DIM] * jnp.asarray(HEAD_DIM**-0.5, BF)
            keys = stack_heads(qkv_ref[here, D + col : D + col + 2 * HEAD_DIM], masks)
            values = stack_heads(qkv_ref[here, 2 * D + col : 2 * D + col + 2 * HEAD_DIM], masks)
            scores = dot_nt(queries, keys)
            halves = []
            for side in range(2):
                part = scores[:, side * tokens : (side + 1) * tokens]
                grown = jnp.exp(part - jnp.max(part, axis=-1, keepdims=True))
                halves.append((grown * (1.0 / jnp.sum(grown, axis=-1, keepdims=True))).astype(BF))
            probs = jnp.concatenate(halves, axis=1)
            probs_ref[here, pair * 2 * tokens : (pair + 1) * 2 * tokens] = probs
            mixed_ref[here, col : col + 2 * HEAD_DIM] = dot_nn(probs, values).astype(BF)
    branch = dot_nt(mixed_ref[...], attn_ref[3 * D :, :])
    branch_ref[...] = branch.astype(BF)
    middle = stream + mod[:, 2:3] * branch.reshape(nb, tokens, D)
    middle_ref[...] = middle.reshape(rows, D)
    hat, _ = norm_rows(middle)
    mlp_in = (hat * (1.0 + mod[:, 4:5]) + mod[:, 3:4]).astype(BF).reshape(rows, D)
    hidden = dot_nt(mlp_in, in_ref[...])
    squared = hidden * hidden
    bent = jnp.tanh(hidden * (GELU_A + (GELU_A * GELU_B) * squared))
    half = 0.5 * hidden
    act = (half + half * bent).astype(BF)
    act_ref[...] = act
    slope_ref[...] = (
        0.5
        + 0.5 * bent
        + half * (1.0 - bent * bent) * (GELU_A + (3.0 * GELU_A * GELU_B) * squared)
    ).astype(BF)
    mlp = dot_nn(act, out_ref[...])
    mlp_ref[...] = mlp.astype(BF)
    result = middle + mod[:, 5:6] * mlp.reshape(nb, tokens, D)
    result_ref[...] = result.reshape(rows, D)
    square_ref[0] = jnp.sum((result * result).reshape(rows // 8, 8, D), axis=0)


def backward_kernel(first, last, nb, tokens, steps, count_all, *refs):
    if last:
        final_ref, fmod_ref, head_ref, clean_ref, noise_ref = refs[:5]
        refs = refs[5:]
    else:
        d_stream_ref = refs[0]
        refs = refs[1:]
    if first:
        noisy_ref = refs[0]
        refs = refs[1:]
    (
        mod_ref,
        attn_ref,
        in_ref,
        out_ref,
        stream_ref,
        qkv_ref,
        probs_ref,
        mixed_ref,
        branch_ref,
        middle_ref,
        mlp_ref,
        act_ref,
        slope_ref,
    ) = refs[:13]
    refs = refs[13:]
    if last:
        loss_ref, dhead_ref, dfmod_ref = refs[:3]
        refs = refs[3:]
    if first:
        dpatch_ref = refs[0]
    else:
        d_prev_ref = refs[0]
    gattn_ref, gin_ref, gout_ref, dmod_ref, acc_attn, acc_in, acc_out, d_qkv_s = refs[1:]
    rows = nb * tokens
    step = pl.program_id(0)

    @pl.when(step == 0)
    def _():
        acc_attn[...] = jnp.zeros_like(acc_attn)
        acc_in[...] = jnp.zeros_like(acc_in)
        acc_out[...] = jnp.zeros_like(acc_out)
        if last:
            dhead_ref[...] = jnp.zeros_like(dhead_ref)
        if first:
            dpatch_ref[...] = jnp.zeros_like(dpatch_ref)

    mod = mod_ref[...]
    if last:
        fmod = fmod_ref[...]
        hat, rstd = norm_rows(final_ref[...].reshape(nb, tokens, D))
        final_in = (hat * (1.0 + fmod[:, 1:2]) + fmod[:, 0:1]).astype(BF)
        d_parts = []
        loss = jnp.zeros((8, tokens), jnp.float32)
        for n in range(nb):
            predicted = lax.dot_general(
                head_ref[...], final_in[n], (((0,), (1,)), ((), ())), preferred_element_type=jnp.float32
            )
            errors = predicted - jnp.concatenate([noise_ref[n], clean_ref[n]], axis=0)
            loss = loss + jnp.sum((errors * errors).reshape(OUT // 8, 8, tokens), axis=0)
            d_pred = (errors * (2.0 / count_all)).astype(BF)
            dhead_ref[...] += dot_nn(d_pred, final_in[n])
            d_parts.append(
                lax.dot_general(
                    d_pred, head_ref[...], (((0,), (1,)), ((), ())), preferred_element_type=jnp.float32
                )
            )
        loss_ref[0] = loss
        d_final = jnp.stack(d_parts, axis=0)
        d_stream, d_shift, d_scale = norm_back(d_final, hat, rstd, fmod[:, 1:2])
        dfmod_ref[:, 0:1] = d_shift
        dfmod_ref[:, 1:2] = d_scale
    else:
        d_stream = d_stream_ref[...].reshape(nb, tokens, D)
    dmod_ref[:, 5:6] = jnp.sum(d_stream * mlp_ref[...].astype(jnp.float32).reshape(nb, tokens, D), axis=1, keepdims=True)
    d_mlp = (d_stream * mod[:, 5:6]).astype(BF).reshape(rows, D)
    d_hidden = (dot_nt(d_mlp, out_ref[...]) * slope_ref[...].astype(jnp.float32)).astype(BF)
    acc_out[...] += dot_tn(act_ref[...], d_mlp)
    hat, rstd = norm_rows(middle_ref[...].reshape(nb, tokens, D))
    mlp_in = (hat * (1.0 + mod[:, 4:5]) + mod[:, 3:4]).astype(BF).reshape(rows, D)
    acc_in[...] += dot_tn(d_hidden, mlp_in)
    d_input = dot_nn(d_hidden, in_ref[...]).reshape(nb, tokens, D)
    d_middle, d_shift, d_scale = norm_back(d_input, hat, rstd, mod[:, 4:5])
    dmod_ref[:, 3:4] = d_shift
    dmod_ref[:, 4:5] = d_scale
    d_middle = d_middle + d_stream
    dmod_ref[:, 2:3] = jnp.sum(
        d_middle * branch_ref[...].astype(jnp.float32).reshape(nb, tokens, D), axis=1, keepdims=True
    )
    d_proj = (d_middle * mod[:, 2:3]).astype(BF).reshape(rows, D)
    acc_attn[3 * D :, :] += dot_tn(d_proj, mixed_ref[...])
    d_mix = dot_nn(d_proj, attn_ref[3 * D :, :]).astype(BF)
    masks = half_masks()
    lane = lax.broadcasted_iota(jnp.int32, (tokens, 2 * HEAD_DIM), 1)
    low_side = lane < HEAD_DIM
    root = HEAD_DIM**-0.5
    for n in range(nb):
        here = slice(n * tokens, (n + 1) * tokens)
        for pair in range(HEADS // 2):
            col = pair * 2 * HEAD_DIM
            queries = qkv_ref[here, col : col + 2 * HEAD_DIM]
            keys = stack_heads(qkv_ref[here, D + col : D + col + 2 * HEAD_DIM], masks)
            values = stack_heads(qkv_ref[here, 2 * D + col : 2 * D + col + 2 * HEAD_DIM], masks)
            d_out = d_mix[here, col : col + 2 * HEAD_DIM]
            probs_bf = probs_ref[here, pair * 2 * tokens : (pair + 1) * 2 * tokens]
            d_probs = dot_nt(d_out, values)
            halves = []
            for side in range(2):
                cut = slice(side * tokens, (side + 1) * tokens)
                probs = probs_bf[:, cut].astype(jnp.float32)
                part = d_probs[:, cut]
                halves.append((probs * (part - jnp.sum(probs * part, axis=-1, keepdims=True))).astype(BF))
            d_scores = jnp.concatenate(halves, axis=1)
            d_queries = dot_nn(d_scores, keys) * root
            d_keys = dot_tn(d_scores, queries)
            d_keys = jnp.where(low_side, d_keys[:tokens], d_keys[tokens:]) * root
            d_values = dot_tn(probs_bf, d_out)
            d_values = jnp.where(low_side, d_values[:tokens], d_values[tokens:])
            d_qkv_s[here, col : col + 2 * HEAD_DIM] = d_queries.astype(BF)
            d_qkv_s[here, D + col : D + col + 2 * HEAD_DIM] = d_keys.astype(BF)
            d_qkv_s[here, 2 * D + col : 2 * D + col + 2 * HEAD_DIM] = d_values.astype(BF)
    d_qkv = d_qkv_s[...]
    hat, rstd = norm_rows(stream_ref[...].reshape(nb, tokens, D))
    attn_in = (hat * (1.0 + mod[:, 1:2]) + mod[:, 0:1]).astype(BF).reshape(rows, D)
    acc_attn[: 3 * D, :] += dot_tn(d_qkv, attn_in)
    d_attn_in = dot_nn(d_qkv, attn_ref[: 3 * D, :]).reshape(nb, tokens, D)
    d_before, d_shift, d_scale = norm_back(d_attn_in, hat, rstd, mod[:, 1:2])
    dmod_ref[:, 0:1] = d_shift
    dmod_ref[:, 1:2] = d_scale
    d_prev = d_middle + d_before
    if first:
        for n in range(nb):
            dpatch_ref[...] += lax.dot_general(
                noisy_ref[n].astype(jnp.float32), d_prev[n], (((1,), (0,)), ((), ())), precision=highest
            )
    else:
        d_prev_ref[...] = d_prev.reshape(rows, D)

    @pl.when(step == steps - 1)
    def _():
        gattn_ref[...] = acc_attn[...].astype(BF)
        gin_ref[...] = acc_in[...].astype(BF)
        gout_ref[...] = acc_out[...].astype(BF)


def whole_spec(array):
    return pl.BlockSpec(array.shape, lambda i: (0,) * array.ndim)


def lead_spec(block, ndim):
    return pl.BlockSpec(block, lambda i: (i,) + (0,) * (ndim - 1))


LIMIT = 56 * 1024 * 1024


def forward_layer(first, entry_args, mod, weights, nb, tokens):
    lat_count = mod.shape[0]
    rows = nb * tokens
    steps = lat_count // nb
    total = lat_count * tokens
    kinds = [(D, jnp.float32)] if first else []
    kinds += [
        (D, jnp.float32),
        (3 * D, BF),
        (HEADS * tokens, BF),
        (D, BF),
        (D, BF),
        (D, jnp.float32),
        (D, BF),
        (4 * D, BF),
        (4 * D, BF),
    ]
    out_shape = [jax.ShapeDtypeStruct((total, cols), kind) for cols, kind in kinds]
    out_specs = [lead_spec((rows, cols), 2) for cols, _ in kinds]
    out_shape.append(jax.ShapeDtypeStruct((steps, 8, D), jnp.float32))
    out_specs.append(lead_spec((1, 8, D), 3))
    if first:
        noisy, patch, pos = entry_args
        in_specs = [lead_spec((nb, PATCH_IN, tokens), 3), whole_spec(patch), whole_spec(pos)]
    else:
        in_specs = [lead_spec((rows, D), 2)]
    in_specs += [lead_spec((nb, 8, D), 3)] + [whole_spec(w) for w in weights]
    return pl.pallas_call(
        functools.partial(forward_kernel, first, nb, tokens),
        grid=(steps,),
        out_shape=out_shape,
        in_specs=in_specs,
        out_specs=out_specs,
        compiler_params=pltpu.CompilerParams(vmem_limit_bytes=LIMIT),
        name="block_forward",
    )(*entry_args, mod, *weights)


def backward_layer(first, last, entry_args, mod, weights, saved, nb, tokens, count_all):
    lat_count = mod.shape[0]
    rows = nb * tokens
    steps = lat_count // nb
    total = lat_count * tokens
    in_specs = []
    args = list(entry_args)
    if last:
        in_specs += [
            lead_spec((rows, D), 2),
            lead_spec((nb, 8, D), 3),
            whole_spec(args[2]),
            lead_spec((nb, PATCH_IN, tokens), 3),
            lead_spec((nb, PATCH_IN, tokens), 3),
        ]
    else:
        in_specs += [lead_spec((rows, D), 2)]
    if first:
        in_specs += [lead_spec((nb, PATCH_IN, tokens), 3)]
    in_specs += [lead_spec((nb, 8, D), 3)] + [whole_spec(w) for w in weights]
    in_specs += [lead_spec((rows, s.shape[1]), 2) for s in saved]
    out_shape = []
    out_specs = []

    def add(shape, kind, spec):
        out_shape.append(jax.ShapeDtypeStruct(shape, kind))
        out_specs.append(spec)

    def whole(shape):
        return pl.BlockSpec(shape, lambda i: (0,) * len(shape))

    if last:
        add((steps, 8, tokens), jnp.float32, lead_spec((1, 8, tokens), 3))
        add((OUT, D), jnp.float32, whole((OUT, D)))
        add((lat_count, 8, D), jnp.float32, lead_spec((nb, 8, D), 3))
    if first:
        add((PATCH_IN, D), jnp.float32, whole((PATCH_IN, D)))
    else:
        add((total, D), jnp.float32, lead_spec((rows, D), 2))
    for _ in range(3):
        add((4 * D, D), BF, whole((4 * D, D)))
    add((lat_count, 8, D), jnp.float32, lead_spec((nb, 8, D), 3))
    return pl.pallas_call(
        functools.partial(backward_kernel, first, last, nb, tokens, steps, count_all),
        grid=(steps,),
        out_shape=out_shape,
        in_specs=in_specs,
        out_specs=out_specs,
        scratch_shapes=[pltpu.VMEM((4 * D, D), jnp.float32)] * 3 + [pltpu.VMEM((rows, 3 * D), BF)],
        compiler_params=pltpu.CompilerParams(vmem_limit_bytes=LIMIT),
        name="block_backward",
    )(*args, mod, *weights, *saved)


MESH = pl.DeviceIdType.MESH


class Places:
    def __init__(self, n_dp, n_tp):
        self.digits = []
        for axis, count, top in (("dp", n_dp, 4), ("tp", n_tp, 2)):
            sizes = []
            rest = count
            while rest > 1:
                size = next((s for s in (top, 2, 3, 5, 7) if rest % s == 0), rest)
                sizes.append(size)
                rest //= size
            stride = count
            for size in sizes:
                stride //= size
                self.digits.append((axis, stride, size))
        self.dims = tuple(size for _, _, size in self.digits)
        self.count = n_dp * n_tp

    def order(self, odd):
        names = list(range(len(self.digits)))
        if odd and len(names) >= 4:
            names[-3], names[-2] = names[-2], names[-3]
        return names

    def mine(self):
        return [lax.rem(lax.axis_index(axis) // stride, size) for axis, stride, size in self.digits]

    def other(self, mine, digit, shift):
        axis, stride, size = self.digits[digit]
        value = lax.rem(mine[digit] + shift, size)
        return {axis: lax.axis_index(axis) + (value - mine[digit]) * stride}, value

    def barrier(self, mine):
        barrier = pltpu.get_barrier_semaphore()
        count = 0
        for digit, size in enumerate(self.dims):
            for shift in range(1, size):
                target, _ = self.other(mine, digit, shift)
                pl.semaphore_signal(barrier, inc=1, device_id=target, device_id_type=MESH)
                count += 1
        pl.semaphore_wait(barrier, count)


SMALL = 8
SPLIT = 3


def small_blocks(entry_t, table_t, final):
    early = PATCH_IN + FREQ
    return [
        (0, 0, entry_t, 0, early),
        (1, 0, entry_t, early, early + D),
        (2, 0, table_t, 0, D),
        (3, 0, table_t, D, 2 * D),
        (4, 0, table_t, 2 * D, CLASSES + 1),
        (4, 256, final, 2 * D, 2 * D + OUT),
        (5, 0, final, 0, D),
        (6, 0, final, D, 2 * D),
    ]


class Traffic:
    def __init__(self, places, mine, sends, recvs, locals_):
        self.places, self.mine = places, mine
        self.sends, self.recvs, self.locals = sends, recvs, locals_
        self.used = self.used_local = 0
        self.copies = []

    def remote(self, source, target_ref, digit, shift):
        target, _ = self.places.other(self.mine, digit, shift)
        at = self.used
        self.used += 1
        copy = pltpu.make_async_remote_copy(
            src_ref=source,
            dst_ref=target_ref,
            send_sem=self.sends.at[at],
            recv_sem=self.recvs.at[at],
            device_id=target,
            device_id_type=MESH,
        )
        self.copies.append(copy)
        return copy

    def local(self, source, target_ref):
        at = self.used_local
        self.used_local += 1
        return pltpu.make_async_copy(source, target_ref, self.locals.at[at])

    def ahead(self, digit, shift):
        return lax.rem(self.mine[digit] + shift, self.places.dims[digit])

    def finish(self):
        for copy in self.copies:
            copy.wait_send()


def copies_per_part(places):
    dims = places.dims
    return sum(dims) - len(dims) + max(dims) * max(dims)


def gather_job(traffic, odd, source, out):
    places, mine = traffic.places, traffic.mine
    order = places.order(odd)
    depth = len(order)
    split = depth - 2 if depth >= 4 else -1
    own = traffic.local(source, out.at[tuple(mine)])
    waits = [[] for _ in range(depth + 1)]
    starts = [[] for _ in range(depth + 1)]

    def region(done, fixed):
        return tuple(fixed.get(d, slice(None) if d in done else mine[d]) for d in range(depth))

    for stage, digit in enumerate(order):
        done = order[:stage]
        for shift in range(1, places.dims[digit]):
            pieces = [(stage, {})]
            if stage == split:
                before = order[stage - 1]
                pieces = [(stage - 1, {before: mine[before]})]
                pieces += [(stage, {before: traffic.ahead(before, k)}) for k in range(1, places.dims[before])]
            for when, fixed in pieces:
                where = region(done, fixed)
                copy = traffic.remote(source if stage == 0 else out.at[where], out.at[where], digit, shift)
                starts[when].append(copy)
                waits[stage + 1].append(copy)

    def action(k):
        if k == 0:
            own.start()
        if k == 1:
            own.wait()
        for copy in waits[k]:
            copy.wait_recv()
        for copy in starts[k]:
            copy.start()

    return [functools.partial(action, k) for k in range(depth + 1)]


def land_shapes(places, odd, block):
    route = places.order(odd)[::-1]
    depth = len(route)
    shapes = []
    for stage, digit in enumerate(route):
        left = [d for d in range(depth) if d not in route[: stage + 1]]
        shapes.append((places.dims[digit] - 1, *(places.dims[d] for d in left), *block))
    return shapes


def reduce_job(traffic, odd, source, acc, lands, out):
    places, mine = traffic.places, traffic.mine
    route = places.order(odd)[::-1]
    depth = len(route)
    split = 1 if depth >= 4 else -1
    waits = [[] for _ in range(depth + 1)]
    starts = [[] for _ in range(depth + 1)]
    adds = [[] for _ in range(depth + 1)]
    own = traffic.local(
        source.at[tuple(mine[d] if d == route[0] else slice(None) for d in range(depth))], acc
    )

    def left_of(stage):
        return [d for d in range(depth) if d not in route[: stage + 1]]

    def in_acc(values):
        return tuple(values.get(d, mine[d]) for d in range(depth) if d != route[0])

    for stage, digit in enumerate(route):
        gone = route[:stage]
        left = left_of(stage)
        pieces = [(stage + 1, {})]
        if stage == split:
            after = route[stage + 1]
            pieces = [(stage + 1, {after: traffic.ahead(after, k)}) for k in range(1, places.dims[after])]
            pieces += [(stage + 2, {after: mine[after]})]
        for when, fixed in pieces:
            for shift in range(1, places.dims[digit]):
                values = {d: slice(None) for d in left} | fixed | {digit: traffic.ahead(digit, shift)}
                if stage == 0:
                    sent = source.at[tuple(values[d] for d in range(depth))]
                else:
                    sent = acc.at[in_acc(values)]
                target = lands[stage].at[(shift - 1, *(values[d] for d in left))]
                copy = traffic.remote(sent, target, digit, shift)
                starts[stage].append(copy)
                waits[when].append(copy)
            adds[when].append((stage, fixed))

    def add(group):
        stage, fixed = group[-1]
        free = [d for d in left_of(stage) if d not in fixed]
        count = math.prod(places.dims[d] for d in free)
        last = stage == depth - 1

        def one(flat, carry):
            values = dict(fixed)
            rest = flat
            for d in reversed(free):
                values[d] = lax.rem(rest, places.dims[d])
                rest = rest // places.dims[d]
            total = acc[in_acc(values)].astype(jnp.float32)
            for near, _ in group:
                for shift in range(places.dims[route[near]] - 1):
                    index = (shift, *(values.get(d, mine[d]) for d in left_of(near)))
                    total = total + lands[near][index].astype(jnp.float32)
            if last:
                out[...] = total
            else:
                acc[in_acc(values)] = total.astype(BF)
            return carry

        lax.fori_loop(0, count, one, 0)

    def action(k):
        if k == 0:
            own.start()
        if k == 1:
            own.wait()
        for copy in waits[k]:
            copy.wait_recv()
        if k == split + 2:
            add(adds[k])
        else:
            for entry in adds[k]:
                add([entry])
        if k < depth:
            for copy in starts[k]:
                copy.start()

    return [functools.partial(action, k) for k in range(depth + 1)]


def in_waves(jobs):
    pairs = [jobs[at : at + 2] for at in range(0, len(jobs), 2)]
    depth = len(jobs[0])
    sequence = []
    for tick in range(len(pairs) + depth - 1):
        for k in range(depth):
            if 0 <= tick - k < len(pairs):
                sequence.extend(job[k] for job in pairs[tick - k])
    return sequence


def gather_kernel(places, slots, layers, *refs):
    entry_ref, table_ref, final_ref, ada_ref, attn_ref, in_ref, out_ref = refs[:7]
    chunks = slots + SPLIT + 3 * layers
    outs = refs[7 : 7 + chunks]
    small, packed, send_sems, recv_sems, own_sems = refs[7 + chunks :]
    mine = places.mine()
    small[...] = jnp.zeros_like(small)
    for k, at, source, low, high in small_blocks(entry_ref, table_ref, final_ref):
        small[k, : source.shape[0], at : at + high - low] = source[:, low:high].astype(BF)
    part = -(-ada_ref.shape[0] // SPLIT)
    for p in range(SPLIT):
        packed[p, :part, :] = ada_ref[p * part : (p + 1) * part, :].astype(BF)
    for l in range(layers):
        for k, source in enumerate((attn_ref, in_ref, out_ref)):
            packed[SPLIT + 3 * l + k, : source.shape[1], :] = source[l].astype(BF)
    first = lax.axis_index("tp") * slots
    ins = [small.at[first + s] for s in range(slots)]
    ins += [packed.at[m] for m in range(SPLIT + 3 * layers)]
    places.barrier(mine)
    traffic = Traffic(places, mine, send_sems, recv_sems, own_sems)
    jobs = [gather_job(traffic, m % 2 == 1, ins[m], outs[m]) for m in range(chunks)]
    for action in in_waves(jobs):
        action()
    traffic.finish()


def pad16(rows):
    return rows + -rows % 16


def gather_all(places, slots, entry_t, table_t, final, ada_t, attn_t, in_t, out_w):
    layers = attn_t.shape[0]
    small_rows, ada_rows = pad16(final.shape[0]), pad16(-(-ada_t.shape[0] // SPLIT))
    wide_rows = pad16(attn_t.shape[1])
    sizes = [small_rows] * slots + [ada_rows] * SPLIT + [wide_rows] * (3 * layers)
    chunks = len(sizes)
    vmem = pl.BlockSpec(memory_space=pltpu.VMEM)
    packed_rows = max(ada_rows, wide_rows)
    assert packed_rows == min(ada_rows, wide_rows)
    outs = pl.pallas_call(
        functools.partial(gather_kernel, places, slots, layers),
        out_shape=[jax.ShapeDtypeStruct((*places.dims, rows, D), BF) for rows in sizes],
        in_specs=[vmem] * 7,
        out_specs=[pl.BlockSpec(memory_space=pl.ANY)] * chunks,
        scratch_shapes=[
            pltpu.VMEM((slots * lax.axis_size("tp"), small_rows, D), BF),
            pltpu.VMEM((SPLIT + 3 * layers, packed_rows, D), BF),
            pltpu.SemaphoreType.DMA((chunks * copies_per_part(places),)),
            pltpu.SemaphoreType.DMA((chunks * copies_per_part(places),)),
            pltpu.SemaphoreType.DMA((chunks,)),
        ],
        compiler_params=pltpu.CompilerParams(collective_id=1, has_side_effects=True, vmem_limit_bytes=LIMIT),
        name="gather_weights",
    )(entry_t, table_t, final, ada_t, attn_t, in_t, out_w)
    return [o.reshape((places.count,) + o.shape[-2:]) for o in outs]


def reduce_kernel(places, chunks, slots, layers, *refs):
    ins = refs[:chunks]
    loss_ref = refs[chunks]
    square_refs = refs[chunks + 1 : chunks + 1 + layers]
    refs = refs[chunks + 1 + layers :]
    outs, both_ref, stats_ref = refs[:chunks], refs[chunks], refs[chunks + 1]
    refs = refs[chunks + 2 :]
    stats_land, stats_send, stats_recv, both_send, both_recv = refs[-5:]
    refs = refs[:-5]
    depth = len(places.dims)
    accs = refs[:chunks]
    lands = refs[chunks : chunks * (1 + depth)]
    send_sems, recv_sems, own_sems = refs[chunks * (1 + depth) :]
    mine = places.mine()
    places.barrier(mine)
    traffic = Traffic(places, mine, send_sems, recv_sems, own_sems)
    jobs = [
        reduce_job(traffic, m % 2 == 1, ins[m], accs[m], lands[m * depth : (m + 1) * depth], outs[m])
        for m in range(chunks)
    ]
    for action in in_waves(jobs):
        action()
    traffic.finish()

    def lane_sums(rows):
        total = jnp.sum(rows, axis=0, keepdims=True)
        return sum(total[:, at : at + 128] for at in range(0, total.shape[1], 128))

    grad = sum(lane_sums(out[...] * out[...]) for out in outs)
    loss = lane_sums(jnp.sum(loss_ref[...], axis=0))
    squares = [lane_sums(jnp.sum(ref[...], axis=0)) for ref in square_refs]
    stats_ref[...] = jnp.concatenate([grad, loss, *squares, jnp.zeros((6 - layers, 128), jnp.float32)], axis=0)
    for s in range(slots):
        both_ref[(lax.axis_index("tp"), s)] = outs[s][...]
    inner = [d for d in range(depth) if places.digits[d][0] == "tp"]
    for stage, digit in enumerate(reversed(range(depth))):
        size = places.dims[digit]
        axis, stride, _ = places.digits[digit]
        stats_land[stage, mine[digit]] = stats_ref[...]
        copies = []
        for shift in range(1, size):
            target, _ = places.other(mine, digit, shift)
            copies.append(
                pltpu.make_async_remote_copy(
                    src_ref=stats_ref,
                    dst_ref=stats_land.at[stage, mine[digit]],
                    send_sem=stats_send.at[stage, shift - 1],
                    recv_sem=stats_recv.at[stage, shift - 1],
                    device_id=target,
                    device_id_type=MESH,
                )
            )
            if digit in inner:
                held = stride
                start = lax.axis_index("tp") // stride * stride
                where = both_ref.at[pl.ds(start, held)]
                copies.append(
                    pltpu.make_async_remote_copy(
                        src_ref=where,
                        dst_ref=where,
                        send_sem=both_send.at[stage, shift - 1],
                        recv_sem=both_recv.at[stage, shift - 1],
                        device_id=target,
                        device_id_type=MESH,
                    )
                )
        for copy in copies:
            copy.start()
        for copy in copies:
            copy.wait()
        total = stats_land[stage, 0]
        for value in range(1, size):
            total = total + stats_land[stage, value]
        stats_ref[...] = total


def reduce_all(places, slots, parts, loss, squares):
    layers = len(squares)
    vmem = pl.BlockSpec(memory_space=pltpu.VMEM)
    chunks = len(parts)
    dims = places.dims
    depth, widest = len(dims), max(dims)
    blocks = [p.shape[1:] for p in parts]
    lands = []
    for m in range(chunks):
        lands += [pltpu.VMEM(shape, BF) for shape in land_shapes(places, m % 2 == 1, blocks[m])]
    return pl.pallas_call(
        functools.partial(reduce_kernel, places, chunks, slots, layers),
        out_shape=[jax.ShapeDtypeStruct(block, jnp.float32) for block in blocks]
        + [
            jax.ShapeDtypeStruct((lax.axis_size("tp"), slots, *blocks[0]), jnp.float32),
            jax.ShapeDtypeStruct((8, 128), jnp.float32),
        ],
        in_specs=[pl.BlockSpec(memory_space=pl.ANY)] * chunks + [vmem] * (1 + layers),
        out_specs=[vmem] * (chunks + 2),
        scratch_shapes=[pltpu.VMEM(dims[:-1] + block, BF) for block in blocks]
        + lands
        + [
            pltpu.SemaphoreType.DMA((chunks * copies_per_part(places),)),
            pltpu.SemaphoreType.DMA((chunks * copies_per_part(places),)),
            pltpu.SemaphoreType.DMA((chunks,)),
            pltpu.VMEM((depth, widest, 8, 128), jnp.float32),
            pltpu.SemaphoreType.DMA((depth, widest - 1)),
            pltpu.SemaphoreType.DMA((depth, widest - 1)),
            pltpu.SemaphoreType.DMA((depth, widest - 1)),
            pltpu.SemaphoreType.DMA((depth, widest - 1)),
        ],
        compiler_params=pltpu.CompilerParams(collective_id=2, has_side_effects=True, vmem_limit_bytes=LIMIT),
        name="reduce_gradients",
    )(*[p.reshape(dims + p.shape[1:]) for p in parts], loss, *squares)


def silu(values):
    return values * (1.0 / (1.0 + jnp.exp(-values)))


def silu_slope(values):
    gate = 1.0 / (1.0 + jnp.exp(-values))
    return gate * (1.0 + values * (1.0 - gate))


def split_low(values):
    high = values.astype(BF)
    return jnp.concatenate([high, (values - high.astype(jnp.float32)).astype(BF)], axis=0)


def block_of(refs, k):
    slots = len(refs)
    part = refs[k % slots][:, k // slots]
    return part.reshape(-1, D)


def condition_kernel(slots, lat_count, *refs):
    feat_ref, hot_ref = refs[:2]
    slot_refs = refs[2 : 2 + slots]
    ada_refs = refs[2 + slots : 2 + slots + SPLIT]
    mod_ref, fmod_ref, pre_ref, cond_ref, patch_ref, head_ref = refs[2 + slots + SPLIT :]
    entry = block_of(slot_refs, 0)
    patch_ref[...] = entry[:, :PATCH_IN]
    pre = dot_nt(feat_ref[...], entry)
    pre_ref[...] = pre
    cond = dot_nt(silu(pre).astype(BF), block_of(slot_refs, 1))
    for k in range(3):
        cond = cond + dot_nt(hot_ref[:, k * D : (k + 1) * D], block_of(slot_refs, 2 + k))
    cond_ref[...] = cond
    head_ref[...] = block_of(slot_refs, 4)[:, 256 : 256 + OUT]
    act = silu(cond).astype(BF)
    for p in range(SPLIT):
        wide = ada_refs[p].shape[0]
        mod_ref[:, p * wide : (p + 1) * wide] = dot_nt(act, ada_refs[p][...])
    for k in range(2):
        part = dot_nn(act, block_of(slot_refs, 5 + k))
        for b in range(lat_count):
            fmod_ref[b, k : k + 1, :] = part[b : b + 1, :]


def condition(feat, hot, slot_full, ada_full, lat_count):
    vmem = pl.BlockSpec(memory_space=pltpu.VMEM)
    wide = ada_full[0].shape[0]
    shapes = [
        ((8, SPLIT * wide), jnp.float32),
        ((lat_count, 8, D), jnp.float32),
        ((8, D), jnp.float32),
        ((8, D), jnp.float32),
        ((D, PATCH_IN), BF),
        ((D, OUT), BF),
    ]
    return pl.pallas_call(
        functools.partial(condition_kernel, len(slot_full), lat_count),
        out_shape=[jax.ShapeDtypeStruct(*s) for s in shapes],
        in_specs=[vmem] * (2 + len(slot_full) + SPLIT),
        out_specs=[vmem] * len(shapes),
        compiler_params=pltpu.CompilerParams(vmem_limit_bytes=LIMIT),
        name="condition",
    )(feat, hot, *slot_full, *ada_full)


def condition_back_kernel(slots, lat_count, *refs):
    feat_ref, hot_ref = refs[:2]
    slot_refs = refs[2 : 2 + slots]
    ada_refs = refs[2 + slots : 2 + slots + SPLIT]
    pre_ref, cond_ref, d_mod_ref, d_fmod_ref, d_patch_ref, d_head_ref = refs[2 + slots + SPLIT :][:6]
    outs = refs[2 + slots + SPLIT + 6 :]
    g_slots, g_ada = outs[:slots], outs[slots : slots + SPLIT]
    fmod_s = outs[slots + SPLIT]
    pre, cond = pre_ref[...], cond_ref[...]
    act = silu(cond).astype(BF)
    act_two = jnp.concatenate([act, act], axis=0)
    d_cond = jnp.zeros((16, D), jnp.float32)
    for p in range(SPLIT):
        wide = ada_refs[p].shape[0]
        d_mod = split_low(d_mod_ref[:, p * wide : (p + 1) * wide])
        d_cond = d_cond + dot_nn(d_mod, ada_refs[p][...])
        g_ada[p][...] = dot_tn(d_mod, act_two).astype(BF)

    def give(k, grad):
        ref = g_slots[k % slots]
        ref[:, k // slots] = grad.astype(BF).reshape(ref.shape[0], ref.shape[2], D)

    fmod_s[...] = jnp.zeros_like(fmod_s)
    for k in range(2):
        for b in range(lat_count):
            fmod_s[k, b : b + 1, :] = d_fmod_ref[b, k : k + 1, :]
        d_fmod = split_low(fmod_s[k])
        d_cond = d_cond + dot_nt(d_fmod, block_of(slot_refs, 5 + k))
        give(5 + k, dot_tn(act_two, d_fmod))
    d_pre = split_low((d_cond[:8] + d_cond[8:]) * silu_slope(cond))
    time_act = silu(pre).astype(BF)
    give(1, dot_tn(d_pre, jnp.concatenate([time_act, time_act], axis=0)))
    d_time = dot_nn(d_pre, block_of(slot_refs, 1))
    for k in range(3):
        hot = hot_ref[:, k * D : (k + 1) * D]
        grad = dot_tn(d_pre, jnp.concatenate([hot, hot], axis=0))
        if k == 2:
            here = jnp.pad(d_head_ref[...], ((0, 128 - OUT), (0, 0))).T
            grad = jnp.concatenate([grad[:, :256], grad[:, 256:] + here], axis=1)
        give(2 + k, grad)
    d_time = split_low((d_time[:8] + d_time[8:]) * silu_slope(pre))
    grad = dot_tn(d_time, jnp.concatenate([feat_ref[...], feat_ref[...]], axis=0))
    here = jnp.pad(d_patch_ref[...], ((0, 128 - PATCH_IN), (0, 0))).T
    give(0, jnp.concatenate([grad[:, :128] + here, grad[:, 128:]], axis=1))
    for k in range(7, SMALL):
        give(k, jnp.zeros((D, D), jnp.float32))


def condition_back(feat, hot, slot_full, ada_full, pre, cond, d_mod, d_fmod, d_patch, d_head):
    vmem = pl.BlockSpec(memory_space=pltpu.VMEM)
    lat_count = d_fmod.shape[0]
    args = (feat, hot, *slot_full, *ada_full, pre, cond, d_mod, d_fmod, d_patch, d_head)
    kept = (*slot_full, *ada_full)
    return pl.pallas_call(
        functools.partial(condition_back_kernel, len(slot_full), lat_count),
        out_shape=[jax.ShapeDtypeStruct(w.shape, BF) for w in kept],
        in_specs=[vmem] * len(args),
        out_specs=[vmem] * len(kept),
        scratch_shapes=[pltpu.VMEM((2, 8, D), jnp.float32)],
        compiler_params=pltpu.CompilerParams(vmem_limit_bytes=LIMIT),
        name="condition_back",
    )(*args)


def adam_kernel(slots, layers, count_rms, *refs):
    stats_ref, both_ref = refs[:2]
    grads = refs[2 : 2 + SPLIT + 3 * layers]
    states = refs[2 + SPLIT + 3 * layers :][:21]
    outs = refs[2 + SPLIT + 3 * layers + 21 :]
    news, (loss_ref, norm_ref, rms_ref) = outs[:21], outs[21:]
    totals = jnp.sum(stats_ref[...], axis=1, keepdims=True)
    norm = jnp.sqrt(totals[0:1])
    factor = jnp.minimum(1.0, 0.01 / (norm + 1e-06))
    loss_ref[...] = totals[1:2]
    norm_ref[...] = norm
    rms_ref[...] = jnp.sqrt(totals[2 : 2 + layers] / count_rms)
    correct = 1.0 - 0.5**STEP

    def update(name, where, grad):
        weight, first, second = (ref[where] for ref in states[3 * name : 3 * name + 3])
        clipped = grad * factor
        first_new = 0.5 * first + 0.5 * clipped
        second_new = 0.5 * second + 0.5 * clipped * clipped
        root = jnp.sqrt(second_new * (1.0 / correct)) + 1e-08
        new = weight - 0.02 * (first_new * (1.0 / correct) / root + 0.01 * weight)
        news[3 * name][where] = new
        news[3 * name + 1][where] = first_new
        news[3 * name + 2][where] = second_new

    def small(k):
        return both_ref[k // slots, k % slots]

    rows = states[0].shape[0]
    early = PATCH_IN + FREQ
    every = slice(0, rows)
    update(0, (every, slice(0, early)), small(0)[:rows, :early])
    update(0, (every, slice(early, early + D)), small(1)[:rows])
    update(1, (every, slice(0, D)), small(2)[:rows])
    update(1, (every, slice(D, 2 * D)), small(3)[:rows])
    update(1, (every, slice(2 * D, CLASSES + 1)), small(4)[:rows, : CLASSES + 1 - 2 * D])
    update(6, (every, slice(0, D)), small(5)[:rows])
    update(6, (every, slice(D, 2 * D)), small(6)[:rows])
    update(6, (every, slice(2 * D, 2 * D + OUT)), small(4)[:rows, 256 : 256 + OUT])
    part = -(-states[15].shape[0] // SPLIT)
    for p in range(SPLIT):
        update(5, (slice(p * part, (p + 1) * part), slice(0, D)), grads[p][:part])
    for l in range(layers):
        for k in range(3):
            update(2 + k, (l, slice(0, states[6].shape[1]), slice(0, D)), grads[SPLIT + 3 * l + k][: states[6].shape[1]])


def adam_all(slots, layers, count_rms, stats, both, grads, states):
    vmem = pl.BlockSpec(memory_space=pltpu.VMEM)
    args = (stats, both, *grads, *states)
    return pl.pallas_call(
        functools.partial(adam_kernel, slots, layers, count_rms),
        out_shape=[jax.ShapeDtypeStruct(s.shape, jnp.float32) for s in states]
        + [jax.ShapeDtypeStruct((n, 1), jnp.float32) for n in (1, 1, layers)],
        in_specs=[vmem] * len(args),
        out_specs=[vmem] * 24,
        compiler_params=pltpu.CompilerParams(vmem_limit_bytes=LIMIT),
        name="adam",
    )(*args)


def fused_adam_kernel(layers, count_rms, *refs):
    stats_ref, both_ref, early_ref, late_ref, class_ref, ada_ref, patch_ref = refs[:7]
    grads = refs[7 : 7 + 3 * layers]
    states = refs[7 + 3 * layers :][:21]
    outs = refs[7 + 3 * layers + 21 :]
    news, (loss_ref, norm_ref, rms_ref) = outs[:21], outs[21:]
    totals = jnp.sum(stats_ref[...], axis=1, keepdims=True)
    norm = jnp.sqrt(totals[0:1])
    factor = jnp.minimum(1.0, 0.01 / (norm + 1e-06))
    loss_ref[...] = totals[1:2]
    norm_ref[...] = norm
    rms = jnp.sqrt(totals / count_rms)
    rms_ref[...] = jnp.concatenate([rms[2 + l : 3 + l] for l in range(layers)], axis=1)
    correct = 1.0 - 0.5**STEP

    def update(name, where, grad):
        weight, first, second = (ref[where] for ref in states[3 * name : 3 * name + 3])
        clipped = grad * factor
        first_new = 0.5 * first + 0.5 * clipped
        second_new = 0.5 * second + 0.5 * clipped * clipped
        root = jnp.sqrt(second_new * (1.0 / correct)) + 1e-08
        new = weight - 0.02 * (first_new * (1.0 / correct) / root + 0.01 * weight)
        news[3 * name][where] = new
        news[3 * name + 1][where] = first_new
        news[3 * name + 2][where] = second_new

    rows = states[0].shape[0]
    early = PATCH_IN + FREQ
    every = slice(0, rows)
    patch = patch_ref[...].T[:rows, :PATCH_IN]
    update(0, (every, slice(0, PATCH_IN)), patch)
    update(0, (every, slice(PATCH_IN, early)), early_ref[:, PATCH_IN:early])
    update(0, (every, slice(early, early + D)), late_ref[...])
    update(1, (every, slice(0, CLASSES + 1)), class_ref[:, : CLASSES + 1])
    update(6, (every, slice(0, D)), both_ref[1])
    update(6, (every, slice(D, 2 * D)), both_ref[2])
    update(6, (every, slice(2 * D, 2 * D + OUT)), both_ref[0][:, :OUT])
    update(5, (slice(0, states[15].shape[0]), slice(0, D)), ada_ref[...])
    for l in range(layers):
        for k in range(3):
            update(2 + k, (l, slice(0, states[6].shape[1]), slice(0, D)), grads[3 * l + k][: states[6].shape[1]])


def fused_adam(layers, count_rms, small, grads, states):
    vmem = pl.BlockSpec(memory_space=pltpu.VMEM)
    args = (*small, *grads, *states)
    return pl.pallas_call(
        functools.partial(fused_adam_kernel, layers, count_rms),
        out_shape=[jax.ShapeDtypeStruct(s.shape, jnp.float32) for s in states]
        + [jax.ShapeDtypeStruct((1, n), jnp.float32) for n in (1, 1, layers)],
        in_specs=[vmem] * len(args),
        out_specs=[vmem] * 24,
        compiler_params=pltpu.CompilerParams(vmem_limit_bytes=LIMIT),
        name="adam_update",
    )(*args)


def modulation_pieces(layers, ada_rows, part_rows, count):
    pieces = []
    for j in range(count):
        for l in range(layers):
            low = l * ada_rows
            while low < (l + 1) * ada_rows:
                p, r = divmod(low, part_rows)
                length = min((l + 1) * ada_rows - low, part_rows - r)
                pieces.append((l, j * ada_rows + low - l * ada_rows, p, j * part_rows + r, length))
                low += length
    return pieces


def class_of(labels_ref, drops_ref, b):
    return jnp.where(drops_ref[b] == 1, CLASSES, labels_ref[b])


def embed_inputs(lat_count, times_ref, labels_ref, drops_ref, freq_ref, feat_s, hot_s, fact_s):
    feat_s[...] = jnp.zeros_like(feat_s)
    hot_s[...] = jnp.zeros_like(hot_s)
    fact_s[...] = jnp.zeros_like(fact_s)
    column = lax.broadcasted_iota(jnp.int32, (1, 3 * D), 1)
    half = FREQ // 2
    for b in range(lat_count):
        angles = times_ref[b].astype(jnp.float32) * freq_ref[...]
        feat_s[b : b + 1, PATCH_IN : PATCH_IN + half] = jnp.cos(angles)
        feat_s[b : b + 1, PATCH_IN + half : PATCH_IN + FREQ] = jnp.sin(angles)
        label = class_of(labels_ref, drops_ref, b)
        hot_s[b : b + 1, :] = jnp.where(column == label, 1.0, 0.0)
        low = lax.rem(label, 32)
        high = (label - low) // 32
        fact_s[12 + b : 13 + b, :128] = jnp.full((1, 128), low, jnp.int32).astype(jnp.float32)
        fact_s[12 + b : 13 + b, 128:256] = jnp.full((1, 128), high, jnp.int32).astype(jnp.float32)
    fact_s[8 : 8 + lat_count, :] = feat_s[:lat_count, :]


def embed_condition(lat_count, feat_s, hot_s, fact_s, slot_refs, pre_ref, cond_ref, fmod_ref):
    pre = dot_nt(feat_s[...].astype(BF), block_of(slot_refs, 0))
    pre_ref[...] = pre
    time_act = silu(pre).astype(BF)
    cond = dot_nt(time_act, block_of(slot_refs, 1))
    for k in range(3):
        cond = cond + dot_nt(hot_s[:, k * D : (k + 1) * D].astype(BF), block_of(slot_refs, 2 + k))
    cond_ref[...] = cond
    act = silu(cond).astype(BF)
    fact_s[:lat_count, :] = act.astype(jnp.float32)[:lat_count]
    fact_s[4 : 4 + lat_count, :] = time_act.astype(jnp.float32)[:lat_count]
    for k in range(2):
        fmod_ref[:, k * D : (k + 1) * D] = dot_nn(act, block_of(slot_refs, 5 + k))


def mod_rows(mod_ref, index, n, nb, part):
    rows = [mod_ref[(*index, pl.ds(n * nb + b, 1), slice(part * D, (part + 1) * D))] for b in range(nb)]
    return jnp.stack(rows, axis=0)


def attend_forward(nb, tokens, stream, mod, attn_w, out_w, qkv_ref, probs_ref, mixed_ref, branch_ref):
    rows = nb * tokens
    hat, _ = norm_rows(stream)
    attn_in = (hat * (1.0 + mod(1)) + mod(0)).astype(BF).reshape(rows, D)
    qkv_ref[...] = dot_nt(attn_in, attn_w[...]).astype(BF)
    masks = half_masks()
    for b in range(nb):
        here = slice(b * tokens, (b + 1) * tokens)
        for pair in range(HEADS // 2):
            col = pair * 2 * HEAD_DIM
            queries = qkv_ref[here, col : col + 2 * HEAD_DIM] * jnp.asarray(HEAD_DIM**-0.5, BF)
            keys = stack_heads(qkv_ref[here, D + col : D + col + 2 * HEAD_DIM], masks)
            values = stack_heads(qkv_ref[here, 2 * D + col : 2 * D + col + 2 * HEAD_DIM], masks)
            scores = dot_nt(queries, keys)
            halves = []
            for side in range(2):
                part = scores[:, side * tokens : (side + 1) * tokens]
                grown = jnp.exp(part - jnp.max(part, axis=-1, keepdims=True))
                halves.append((grown * (1.0 / jnp.sum(grown, axis=-1, keepdims=True))).astype(BF))
            probs = jnp.concatenate(halves, axis=1)
            probs_ref[here, pair * 2 * tokens : (pair + 1) * 2 * tokens] = probs
            mixed_ref[here, col : col + 2 * HEAD_DIM] = dot_nn(probs, values).astype(BF)
    branch = dot_nt(mixed_ref[...], out_w[...])
    branch_ref[...] = branch.astype(BF)
    return stream + mod(2) * branch.reshape(nb, tokens, D)


def feed_forward(nb, tokens, middle, mod, in_w, out_w, mlp_ref, act_ref, slope_ref):
    rows = nb * tokens
    hat, _ = norm_rows(middle)
    mlp_in = (hat * (1.0 + mod(4)) + mod(3)).astype(BF).reshape(rows, D)
    hidden = dot_nt(mlp_in, in_w[...])
    squared = hidden * hidden
    bent = jnp.tanh(hidden * (GELU_A + (GELU_A * GELU_B) * squared))
    half = 0.5 * hidden
    act = (half + half * bent).astype(BF)
    act_ref[...] = act
    slope_ref[...] = (
        0.5
        + 0.5 * bent
        + half * (1.0 - bent * bent) * (GELU_A + (3.0 * GELU_A * GELU_B) * squared)
    ).astype(BF)
    mlp = dot_nn(act, out_w[...])
    mlp_ref[...] = mlp.astype(BF)
    return middle + mod(5) * mlp.reshape(nb, tokens, D)


def fixed_tables(tokens):
    half, quarter = FREQ // 2, D // 4
    freq = np.exp(np.float32(-math.log(10000.0)) * np.arange(half, dtype=np.float32) / np.float32(half))
    omegas = np.exp(np.float32(-math.log(10000.0)) * np.arange(quarter, dtype=np.float32) / np.float32(quarter))
    token = np.arange(tokens)
    row = (token // GRID).astype(np.float32)[:, None] * omegas
    col = (token % GRID).astype(np.float32)[:, None] * omegas
    table = np.concatenate([np.sin(row), np.cos(row), np.sin(col), np.cos(col)], axis=-1)
    return jnp.asarray(freq[None], jnp.float32), jnp.asarray(table, jnp.float32)


PROLOGUE = [
    (0, 1),
    (2, 0),
    (1, 1),
    (0, 2),
    (3, 0),
    (2, 1),
    (1, 2),
    (0, 3),
    (4, 0),
    (3, 1),
    (2, 2),
    (1, 3),
    (0, 4),
    "cond",
    (5, 0),
    (4, 1),
    (3, 2),
    (2, 3),
    (1, 4),
    "mods",
    (5, 1),
    (4, 2),
    (3, 3),
    (2, 4),
]
LATER = {
    1: [(6, 0)],
    3: [(6, 1)],
    4: [(5, 2), (4, 3), (3, 4)],
    6: [(6, 2)],
    8: [(5, 3), (4, 4), "mods", (6, 3)],
    12: [(5, 4), (6, 4), "hand"],
}


def fused_forward_kernel(places, slots, layers, nb, tokens, lat_count, sizes, *refs):
    small_rows, ada_rows, part_rows, wide_rows = sizes
    chunks = slots + SPLIT + 3 * layers
    entry_ref, table_ref, final_ref, ada_ref, attn_ref, in_ref, out_ref = refs[:7]
    times_ref, labels_ref, drops_ref, freq_ref, clean_ref, noise_ref, pos_ref = refs[7:14]
    refs = refs[14:]
    given = refs[: chunks + 1]
    (
        mods_ref,
        fmod_ref,
        pre_ref,
        cond_ref,
        noisy_ref,
        start_ref,
        result_ref,
        qkv_ref,
        probs_ref,
        mixed_ref,
        branch_ref,
        middle_ref,
        mlp_ref,
        act_ref,
        slope_ref,
        square_ref,
    ) = refs[chunks + 1 : chunks + 17]
    refs = refs[chunks + 17 :]
    fulls = refs[: chunks + 1]
    (
        small,
        packed,
        stream_s,
        middle_s,
        feat_s,
        hot_s,
        fact_s,
        fact_bf,
        send_sems,
        recv_sems,
        own_sems,
        give_sems,
    ) = refs[chunks + 1 :]
    l, h, n = (pl.program_id(axis) for axis in range(3))
    mine = places.mine()
    first = lax.axis_index("tp") * slots
    order = [*range(slots), slots, slots + 1, slots + SPLIT, slots + SPLIT + 1, slots + SPLIT + 2, slots + 2]
    order += range(slots + SPLIT + 3, chunks)
    sources = [small.at[first + s] for s in range(slots)] + [packed.at[m] for m in range(SPLIT + 3 * layers)]
    traffic = Traffic(places, mine, send_sems, recv_sems, own_sems)
    jobs = [gather_job(traffic, at % 2 == 1, sources[m], fulls[m]) for at, m in enumerate(order)]
    pairs = [jobs[at : at + 2] for at in range(0, chunks, 2)]
    pairs.append([gather_job(traffic, False, fact_bf, fulls[chunks])])
    handed = [pltpu.make_async_copy(fulls[m], given[m], give_sems.at[m]) for m in range(chunks + 1)]

    def flat(m, rows):
        return fulls[m].reshape(places.count * rows, D)

    def run(*names):
        for pair, k in names:
            for job in pairs[pair]:
                job[k]()

    def at_step(layer, half, step):
        return pl.when((l == layer) & (h == half) & (n == step))

    def set_mods(layer):
        act = silu(cond_ref[...]).astype(BF)
        low, high = layer * ada_rows, (layer + 1) * ada_rows
        parts = range(low // part_rows, -(-high // part_rows))
        raw = {p: dot_nt(act, flat(slots + p, part_rows)[...]) for p in parts}
        for ll, col, p, at, length in modulation_pieces(layers, ada_rows, part_rows, places.count):
            if ll == layer:
                mods_ref[layer, :, col : col + length] = raw[p][:, at : at + length]

    slot_refs = [f.reshape(-1, lax.axis_size("tp"), small_rows, D) for f in fulls[:slots]]

    def pack_blocks():
        for ll in range(layers):
            for k, source in enumerate((attn_ref, in_ref, out_ref)):
                packed[SPLIT + 3 * ll + k] = source[ll].astype(BF)

    @at_step(0, 0, 0)
    def _():
        small[...] = jnp.zeros_like(small)
        for k, at, source, low, high in small_blocks(entry_ref, table_ref, final_ref):
            small[k, : source.shape[0], at : at + high - low] = source[:, low:high].astype(BF)
        places.barrier(mine)
        run((0, 0))
        for p in range(SPLIT):
            packed[p] = ada_ref[p * part_rows : (p + 1) * part_rows, :].astype(BF)
        run((1, 0))
        pack_blocks()
        embed_inputs(lat_count, times_ref, labels_ref, drops_ref, freq_ref, feat_s, hot_s, fact_s)
        for entry in PROLOGUE:
            if entry == "cond":
                embed_condition(lat_count, feat_s, hot_s, fact_s, slot_refs, pre_ref, cond_ref, fmod_ref)
                fact_bf[...] = fact_s[...].astype(BF)
            elif entry == "mods":
                set_mods(0)
            else:
                run(entry)

    steps = lat_count // nb
    for number, names in sorted(LATER.items()):
        number = number * steps // 4
        layer_at, rest = divmod(number, 2 * steps)

        @at_step(layer_at, rest // steps, rest % steps)
        def _(names=names):
            for entry in names:
                if entry == "mods":
                    for layer in range(1, layers):
                        set_mods(layer)
                elif entry == "hand":
                    for copy in handed:
                        copy.start()
                else:
                    run(entry)

    rows = nb * tokens
    here = pl.ds(pl.multiple_of(n * rows, rows), rows)

    def weight(layer, k):
        return flat(slots + SPLIT + 3 * layer + k, wide_rows)

    for layer in range(layers):
        mod = lambda part, layer=layer: mod_rows(mods_ref, (layer,), n, nb, part)

        @pl.when((l == layer) & (h == 0))
        def _(layer=layer, mod=mod):
            if layer == 0:
                patch = block_of(slot_refs, 0)[:, :PATCH_IN]
                for b in range(nb):
                    when = jnp.full((1, tokens), times_ref[n * nb + b], jnp.int32).astype(jnp.float32)
                    phase = (when / NOISE_STEPS + 0.008) / 1.008 * (math.pi / 2)
                    noisy_ref[b] = (jnp.cos(phase) * clean_ref[b] + jnp.sin(phase) * noise_ref[b]).astype(BF)
                parts = [
                    lax.dot_general(
                        noisy_ref[b], patch, (((0,), (1,)), ((), ())), preferred_element_type=jnp.float32
                    )
                    + pos_ref[...]
                    for b in range(nb)
                ]
                stream = parts[0] if nb == 1 else jnp.concatenate(parts, axis=0)
                start_ref[...] = stream
            else:
                stream = stream_s[here, :]
            stream = stream.reshape(nb, tokens, D)
            middle = attend_forward(
                nb,
                tokens,
                stream,
                mod,
                weight(layer, 0).at[: 3 * D],
                weight(layer, 0).at[3 * D :],
                qkv_ref.at[0],
                probs_ref.at[0],
                mixed_ref.at[0],
                branch_ref.at[0],
            )
            middle_ref[0] = middle.reshape(rows, D)
            middle_s[here, :] = middle.reshape(rows, D)

        @pl.when((l == layer) & (h == 1))
        def _(layer=layer, mod=mod):
            middle = middle_s[here, :].reshape(nb, tokens, D)
            result = feed_forward(
                nb,
                tokens,
                middle,
                mod,
                weight(layer, 1),
                weight(layer, 2),
                mlp_ref.at[0],
                act_ref.at[0],
                slope_ref.at[0],
            )
            result_ref[0] = result.reshape(rows, D)
            if layer < layers - 1:
                stream_s[here, :] = result.reshape(rows, D)
            square_ref[0, 0] = jnp.sum((result * result).reshape(rows // 8, 8, D), axis=0)

    @at_step(layers - 1, 1, lat_count // nb - 1)
    def _():
        for copy in handed:
            copy.wait()
        traffic.finish()


def fused_forward(places, slots, nb, weights_in, ids, clean_t, noise_t):
    entry_t, table_t, final, ada_t, attn_t, in_t, out_w = weights_in
    layers, wide_rows = attn_t.shape[:2]
    lat_count, _, tokens = clean_t.shape
    small_rows, part_rows, ada_rows = final.shape[0], ada_t.shape[0] // SPLIT, ada_t.shape[0] // layers
    sizes = [small_rows] * slots + [part_rows] * SPLIT + [wide_rows] * (3 * layers)
    chunks = len(sizes)
    steps = lat_count // nb
    rows, total = nb * tokens, lat_count * tokens
    full_shapes = [(*places.dims, r, D) for r in (*sizes, 16)]

    def const(array):
        return pl.BlockSpec(array.shape, lambda l, h, n: (0,) * array.ndim)

    def const_shape(shape):
        return pl.BlockSpec(shape, lambda l, h, n: (0,) * len(shape))

    def early(l, h, n):
        return jnp.where(h == 0, n, steps - 1)

    def half_one(cols):
        return pl.BlockSpec((1, rows, cols), lambda l, h, n: (l, early(l, h, n), 0))

    def half_two(cols):
        def index(l, h, n):
            before = jnp.where(l == 0, 0, steps - 1)
            return (jnp.where(h == 0, jnp.maximum(l - 1, 0), l), jnp.where(h == 0, before, n), 0)

        return pl.BlockSpec((1, rows, cols), index)

    def square_index(l, h, n):
        before = jnp.where(l == 0, 0, steps - 1)
        return (jnp.where(h == 0, jnp.maximum(l - 1, 0), l), jnp.where(h == 0, before, n), 0, 0)

    out_shape = [jax.ShapeDtypeStruct(s, BF) for s in full_shapes]
    out_specs = [pl.BlockSpec(memory_space=pl.ANY)] * (chunks + 1)

    def add(shape, kind, spec):
        out_shape.append(jax.ShapeDtypeStruct(shape, kind))
        out_specs.append(spec)

    for shape in ((layers, 8, 6 * D), (8, 2 * D), (8, D), (8, D)):
        add(shape, jnp.float32, const_shape(shape))
    def opening(l, h, n):
        return jnp.where((l == 0) & (h == 0), n, steps - 1)

    latents = pl.BlockSpec((nb, PATCH_IN, tokens), lambda l, h, n: (opening(l, h, n), 0, 0))
    add((lat_count, PATCH_IN, tokens), BF, latents)
    add((total, D), jnp.float32, pl.BlockSpec((rows, D), lambda l, h, n: (opening(l, h, n), 0)))
    add((layers, total, D), jnp.float32, half_two(D))
    for cols, kind in ((3 * D, BF), (HEADS * tokens, BF), (D, BF), (D, BF), (D, jnp.float32)):
        add((layers, total, cols), kind, half_one(cols))
    for cols in (D, 4 * D, 4 * D):
        add((layers, total, cols), BF, half_two(cols))
    add((layers, steps, 8, D), jnp.float32, pl.BlockSpec((1, 1, 8, D), square_index))
    freq, pos = fixed_tables(tokens)
    args = (*weights_in, *ids, freq, clean_t, noise_t, pos)
    in_specs = [const(a) for a in weights_in]
    in_specs += [pl.BlockSpec(memory_space=pltpu.SMEM)] * 3 + [const(freq), latents, latents, const(pos)]
    count = (chunks + 1) * copies_per_part(places)
    return pl.pallas_call(
        functools.partial(
            fused_forward_kernel,
            places,
            slots,
            layers,
            nb,
            tokens,
            lat_count,
            (small_rows, ada_rows, part_rows, wide_rows),
        ),
        grid=(layers, 2, steps),
        out_shape=out_shape,
        in_specs=in_specs,
        out_specs=out_specs,
        scratch_shapes=[pltpu.VMEM(s, BF) for s in full_shapes]
        + [
            pltpu.VMEM((slots * lax.axis_size("tp"), small_rows, D), BF),
            pltpu.VMEM((SPLIT + 3 * layers, wide_rows, D), BF),
            pltpu.VMEM((total, D), jnp.float32),
            pltpu.VMEM((total, D), jnp.float32),
            pltpu.VMEM((8, D), jnp.float32),
            pltpu.VMEM((8, 3 * D), jnp.float32),
            pltpu.VMEM((16, D), jnp.float32),
            pltpu.VMEM((16, D), BF),
            pltpu.SemaphoreType.DMA((count,)),
            pltpu.SemaphoreType.DMA((count,)),
            pltpu.SemaphoreType.DMA((chunks + 1,)),
            pltpu.SemaphoreType.DMA((chunks + 1,)),
        ],
        compiler_params=pltpu.CompilerParams(
            collective_id=3, has_side_effects=True, vmem_limit_bytes=LIMIT
        ),
        name="gather_and_forward",
    )(*args)


LIMIT_B = 62 * 1024 * 1024

LATER_BACK = {
    5: [(0, 1)],
    7: [(0, 2)],
    9: [(0, 3), (1, 1), (7, 1)],
    11: [(1, 2), (0, 4), (7, 2)],
    13: [(1, 3), (2, 1), (7, 3)],
    14: [(1, 4), (7, 4)],
    15: [(2, 2)],
}
SHARES = {14: 0, 15: 1}
TAIL_ONE = [(3, 1), (6, 1), (4, 1)]
TAIL_TWO = [
    (5, 0),
    (2, 3),
    (3, 2),
    (6, 2),
    (5, 1),
    (4, 2),
    (3, 3),
    (6, 3),
    (5, 2),
    (4, 3),
    (2, 4),
    (5, 3),
    (6, 4),
    "ada",
    (5, 4),
    "small",
    "share",
    (4, 4),
    (3, 4),
]


def exchange_job(traffic, bufs):
    places, mine = traffic.places, traffic.mine
    depth = len(places.dims)
    stages = []
    for k, digit in enumerate(reversed(range(depth))):
        copies = []
        for shift in range(1, places.dims[digit]):
            there = tuple(traffic.ahead(digit, shift) if d == digit else slice(None) for d in range(depth))
            here = tuple(mine[d] if d == digit else slice(None) for d in range(depth))
            copies.append(traffic.remote(bufs[k].at[there], bufs[k + 1].at[here], digit, shift))
        stages.append((copies, here))

    def action(k):
        if k > 0:
            for copy in stages[k - 1][0]:
                copy.wait_recv()
        if k < depth:
            copies, here = stages[k]
            for copy in copies:
                copy.start()
            bufs[k + 1][here] = bufs[k][here]

    return [functools.partial(action, k) for k in range(depth + 1)]


def attend_backward(nb, tokens, qkv_ref, probs_ref, d_mix, d_qkv_s):
    masks = half_masks()
    lane = lax.broadcasted_iota(jnp.int32, (tokens, 2 * HEAD_DIM), 1)
    low_side = lane < HEAD_DIM
    root = HEAD_DIM**-0.5
    for b in range(nb):
        here = slice(b * tokens, (b + 1) * tokens)
        for pair in range(HEADS // 2):
            col = pair * 2 * HEAD_DIM
            queries = qkv_ref[here, col : col + 2 * HEAD_DIM]
            keys = stack_heads(qkv_ref[here, D + col : D + col + 2 * HEAD_DIM], masks)
            values = stack_heads(qkv_ref[here, 2 * D + col : 2 * D + col + 2 * HEAD_DIM], masks)
            d_out = d_mix[here, col : col + 2 * HEAD_DIM]
            probs_bf = probs_ref[here, pair * 2 * tokens : (pair + 1) * 2 * tokens]
            d_probs = dot_nt(d_out, values)
            halves = []
            for side in range(2):
                cut = slice(side * tokens, (side + 1) * tokens)
                probs = probs_bf[:, cut].astype(jnp.float32)
                part = d_probs[:, cut]
                halves.append((probs * (part - jnp.sum(probs * part, axis=-1, keepdims=True))).astype(BF))
            d_scores = jnp.concatenate(halves, axis=1)
            d_queries = dot_nn(d_scores, keys) * root
            d_keys = dot_tn(d_scores, queries)
            d_keys = jnp.where(low_side, d_keys[:tokens], d_keys[tokens:]) * root
            d_values = dot_tn(probs_bf, d_out)
            d_values = jnp.where(low_side, d_values[:tokens], d_values[tokens:])
            d_qkv_s[here, col : col + 2 * HEAD_DIM] = d_queries.astype(BF)
            d_qkv_s[here, D + col : D + col + 2 * HEAD_DIM] = d_keys.astype(BF)
            d_qkv_s[here, 2 * D + col : 2 * D + col + 2 * HEAD_DIM] = d_values.astype(BF)


def lane_sums(rows):
    total = jnp.sum(rows, axis=0, keepdims=True)
    return sum(total[:, at : at + 128] for at in range(0, total.shape[1], 128))


def fused_backward_kernel(places, slots, layers, nb, tokens, lat_count, count_all, sizes, *refs):
    small_rows, ada_rows, part_rows, wide_rows = sizes
    chunks = slots + SPLIT + 3 * layers
    steps = lat_count // nb
    depth = len(places.dims)
    rows = nb * tokens
    given = refs[: chunks + 1]
    refs = refs[1:]
    mods_ref, fmod_ref, pre_ref, cond_ref, square_ref = refs[chunks : chunks + 5]
    (
        clean_ref,
        noise_ref,
        noisy_ref,
        start_ref,
        result_ref,
        qkv_ref,
        probs_ref,
        mixed_ref,
        branch_ref,
        middle_ref,
        mlp_ref,
        act_ref,
        slope_ref,
    ) = refs[chunks + 5 : chunks + 18]
    refs = refs[chunks + 18 :]
    count = 3 * layers + 2
    outs = refs[: count - 1]
    both_ref, early_ref, late_ref, class_ref, ada_grad_ref, stats_ref = refs[count - 1 : count + 5]
    refs = refs[count + 5 :]
    fulls = refs[: chunks + 1]
    refs = refs[chunks + 1 :]
    accs = refs[:count]
    lands = refs[count : (1 + depth) * count]
    (
        *swaps,
        wide_s,
        small_s,
        patch_s,
        small_out,
        mine_s,
        all_s,
        stage_attn,
        stage_in,
        stage_out,
        acc_one,
        acc_two,
        d_stream_s,
        d_qkv_s,
        d_mods_s,
        d_raw_s,
        d_fmod_s,
        d_patch_s,
        d_head_s,
        loss_s,
        sum_s,
        stats_s,
        both_s,
        stats_land,
        send_sems,
        recv_sems,
        own_sems,
        take_sems,
        stats_send,
        stats_recv,
        both_send,
        both_recv,
    ) = refs[(1 + depth) * count :]
    turn, h, n = (pl.program_id(axis) for axis in range(3))
    mine = places.mine()
    lead = slots + SPLIT

    def flat(ref, count):
        return ref.reshape(places.count * count, D)

    takes = [pltpu.make_async_copy(given[m], fulls[m], take_sems.at[m]) for m in range(chunks + 1)]
    slot_refs = [f.reshape(-1, lax.axis_size("tp"), small_rows, D) for f in fulls[:slots]]
    ada_refs = [flat(f, part_rows) for f in fulls[slots:lead]]
    staged = {0: stage_attn, 1: stage_in, 2: stage_out}
    order = [lead + 4, lead + 5, lead + 3, lead + 1, lead + 2, lead]
    sources = [staged[(m - lead) % 3] for m in order] + [patch_s]
    targets = [outs[m - lead] for m in order] + [outs[count - 2]]
    sources.insert(3, small_s)
    targets.insert(3, small_out)
    traffic = Traffic(places, mine, send_sems, recv_sems, own_sems)
    jobs = []
    first_copies = []
    for at in range(count):
        used = traffic.used
        jobs.append(
            reduce_job(
                traffic, at % 2 == 1, sources[at], accs[at], lands[at * depth : (at + 1) * depth], targets[at]
            )
        )
        digit = places.order(at % 2 == 1)[-1]
        first_copies.append(traffic.copies[used : used + places.dims[digit] - 1])
    factors = len(jobs)
    jobs.append(gather_job(traffic, False, mine_s, all_s))
    for l in range(layers):
        jobs.append(exchange_job(traffic, swaps[l * (depth + 1) : (l + 1) * (depth + 1)]))
    inner = [d for d in reversed(range(depth)) if places.digits[d][0] == "tp"]

    def both_copies(stage):
        digit = inner[stage]
        _, stride, size = places.digits[digit]
        where = both_s.at[pl.ds(lax.axis_index("tp") // stride * stride, stride)]
        return [
            pltpu.make_async_remote_copy(
                src_ref=where,
                dst_ref=where,
                send_sem=both_send.at[stage, shift - 1],
                recv_sem=both_recv.at[stage, shift - 1],
                device_id=places.other(mine, digit, shift)[0],
                device_id_type=MESH,
            )
            for shift in range(1, size)
        ]

    exchange = [both_copies(stage) for stage in range(len(inner))]

    def share(stage):
        if stage == 0:
            both_s[lax.axis_index("tp")] = small_out[...]
        else:
            for copy in exchange[stage - 1]:
                copy.wait()
        if stage < len(exchange):
            for copy in exchange[stage]:
                copy.start()

    def run(*names):
        for job, k in names:
            jobs[job][k]()

    def at_step(number):
        layer_turn, rest = divmod(number, 2 * steps)
        half, step = divmod(rest, steps)
        return pl.when((turn == layer_turn) & (h == half) & (n == step))

    def both(pair, k):
        return [(job, k) for job in (2 * pair, 2 * pair + 1)]

    def extra(name, k):
        return [({3: 6, 4: 7}.get(name, name + 3), k)]

    def swap_job(layer):
        return factors + 1 + layer

    here = pl.ds(pl.multiple_of(n * rows, rows), rows)

    def mod_of(layer):
        return lambda part: mod_rows(mods_ref, (layer,), n, nb, part)

    def put_mod(layer, part, value):
        for b in range(nb):
            d_mods_s[layer, pl.ds(n * nb + b, 1), part * D : (part + 1) * D] = value[b]

    @at_step(0)
    def _():
        for m in [*range(slots), *range(chunks - 1, slots - 1, -1), chunks]:
            takes[m].start()
        d_mods_s[...] = jnp.zeros_like(d_mods_s)
        d_fmod_s[...] = jnp.zeros_like(d_fmod_s)
        d_patch_s[...] = jnp.zeros_like(d_patch_s)
        d_head_s[...] = jnp.zeros_like(d_head_s)
        loss_s[...] = jnp.zeros_like(loss_s)
        sum_s[...] = jnp.zeros_like(sum_s)
        mine_s[...] = jnp.zeros_like(mine_s)
        wide_s[...] = jnp.zeros_like(wide_s)
        small_s[...] = jnp.zeros_like(small_s)
        patch_s[...] = jnp.zeros_like(patch_s)
        places.barrier(mine)
        for m in (*range(slots), lead + 5, lead + 4):
            takes[m].wait()

    hooks = {
        at * steps // 4: [job for name, k in names for job in (both(name, k) if name < 3 else extra(name, k))]
        for at, names in LATER_BACK.items()
    }
    shares = {at * steps // 4: stage for at, stage in SHARES.items()}
    early_ada = [slots + p for p in range(SPLIT) if p * part_rows < (layers - 1) * ada_rows]
    loads = {steps: [lead + 3], 2 * steps: [lead + 2, lead + 1], 3 * steps: [lead, chunks, *early_ada]}
    for number in sorted(set(hooks) | set(loads)):

        @at_step(number)
        def _(number=number):
            for m in loads.get(number, []):
                takes[m].wait()
            run(*hooks.get(number, []))
            if number in shares:
                share(shares[number])

    def raw_part(p):
        wide = places.count * part_rows
        return split_low(d_raw_s[:, p * wide : (p + 1) * wide])

    def send_mods(layer):
        first = swaps[layer * (depth + 1)].reshape(places.count, 8, 128)
        for j in range(places.count):
            first[j] = d_mods_s[layer, :, j * ada_rows : j * ada_rows + 128]
        run((swap_job(layer), 0))

    def ada_grads(layer):
        arrived = swaps[layer * (depth + 1) + depth].reshape(places.count, 8, 128)
        wide_s[:, :8, :] = arrived[...]
        signal = wide_s.reshape(places.count * 16, 128)[...]
        high = signal.astype(BF)
        low = (signal - high.astype(jnp.float32)).astype(BF)
        fact = fulls[chunks].reshape(places.count * 16, D)[...]
        grad = dot_tn(high, fact) + dot_tn(low, fact)
        ada_grad_ref[layer * ada_rows : (layer + 1) * ada_rows, :] = grad[:ada_rows]

    def spread(layer):
        wide = places.count * part_rows
        for l, col, p, at, length in modulation_pieces(layers, ada_rows, part_rows, places.count):
            if l == layer:
                d_raw_s[:, p * wide + at : p * wide + at + length] = d_mods_s[layer, :, col : col + length]

    def send_small():
        cond_act = silu(cond_ref[...]).astype(BF)
        cond_two = jnp.concatenate([cond_act, cond_act], axis=0)
        view = small_s.reshape(-1, lax.axis_size("tp"), small_rows, D)

        def give(k, grad):
            view[:, k] = grad.astype(BF).reshape(view.shape[0], small_rows, D)

        head = jnp.pad(d_head_s[...], ((0, 128 - OUT), (0, 0))).T
        give(0, jnp.pad(head, ((0, 0), (0, D - 128))))
        for k in range(2):
            give(1 + k, dot_tn(cond_two, split_low(d_fmod_s[:, k * D : (k + 1) * D])))

    def expand(entry):
        name, k = entry
        return both(name, k) if name < 3 else extra(name, k)

    def finish_all():
        run((6, 0))
        send_mods(0)
        patch = jnp.pad(d_patch_s[...], ((0, 0), (0, 128)))
        view = patch_s.reshape(-1, lax.axis_size("tp"), PATCH_IN, 128)
        for i in range(view.shape[0]):
            here_cols = patch[:, i * small_rows : i * small_rows + 128].astype(BF)
            for t in range(view.shape[1]):
                view[i, t] = here_cols
        run((7, 0))
        for entry in TAIL_ONE:
            run(*expand(entry))
        cond = cond_ref[...]
        pre = pre_ref[...]
        spread(0)
        d_cond = sum_s[...]
        for p in range(SPLIT):
            if p * part_rows < (layers - 1) * ada_rows:
                d_cond = d_cond + dot_nn(raw_part(p), ada_refs[p][...])
        for k in range(2):
            d_fmod = split_low(d_fmod_s[:, k * D : (k + 1) * D])
            d_cond = d_cond + dot_nt(d_fmod, block_of(slot_refs, 5 + k))
        d_pre = (d_cond[:8] + d_cond[8:]) * silu_slope(cond)
        d_time = dot_nn(split_low(d_pre), block_of(slot_refs, 1))
        d_time = (d_time[:8] + d_time[8:]) * silu_slope(pre)
        mine_s[4 : 4 + lat_count, :] = d_pre[:lat_count]
        mine_s[8 : 8 + lat_count, :] = d_time[:lat_count]
        mine_s[12 : 12 + lat_count, :] = d_pre[:lat_count]
        for entry in TAIL_TWO:
            if entry == "small":
                small_grads()
            elif entry == "ada":
                for layer in range(layers):
                    ada_grads(layer)
            elif entry == "share":
                share(len(exchange))
            else:
                run(*expand(entry))
        copies_of_tp = 1.0 / lax.axis_size("tp")
        grad = sum(lane_sums(out[...] * out[...]) for out in (*outs[:-1], small_out, ada_grad_ref))
        lane = lax.broadcasted_iota(jnp.int32, (PATCH_IN, 128), 1)
        patch = jnp.where(lane < small_rows, outs[-1][...], 0.0)
        alike = sum(lane_sums(g * g) for g in (patch, early_ref[...], late_ref[...], class_ref[...]))
        grad = grad + alike * copies_of_tp
        squares = [lane_sums(jnp.sum(square_ref[l], axis=0)) for l in range(layers)]
        stats_s[...] = jnp.concatenate(
            [grad, lane_sums(loss_s[...]), *squares, jnp.zeros((6 - layers, 128), jnp.float32)], axis=0
        )
        for stage, digit in enumerate(reversed(range(depth))):
            size = places.dims[digit]
            stats_land[stage, mine[digit]] = stats_s[...]
            copies = []
            for shift in range(1, size):
                target, _ = places.other(mine, digit, shift)
                copies.append(
                    pltpu.make_async_remote_copy(
                        src_ref=stats_s,
                        dst_ref=stats_land.at[stage, mine[digit]],
                        send_sem=stats_send.at[stage, shift - 1],
                        recv_sem=stats_recv.at[stage, shift - 1],
                        device_id=target,
                        device_id_type=MESH,
                    )
                )
                copies[-1].start()
            for copy in copies:
                copy.wait()
            total = stats_land[stage, 0]
            for value in range(1, size):
                total = total + stats_land[stage, value]
            stats_s[...] = total
        stats_ref[...] = stats_s[...]
        both_ref[...] = both_s[...]
        waited = {id(copy) for group in first_copies[:3] for copy in group}
        for copy in traffic.copies:
            if id(copy) not in waited:
                copy.wait_send()

    def small_grads():
        total = places.count * 16
        fact = fulls[chunks].reshape(total, D)[...]
        signal = all_s.reshape(total, D)[...]
        row = lax.broadcasted_iota(jnp.int32, (D, small_rows), 0)
        column = lax.broadcasted_iota(jnp.int32, (D, small_rows), 1)
        pick = jnp.where(row == column + lax.axis_index("dp") * small_rows, 1.0, 0.0).astype(BF)
        high = signal.astype(BF)
        low = (signal - high.astype(jnp.float32)).astype(BF)
        picked = [dot_nn(part, pick).astype(BF) for part in (high, low)]
        kind = lax.rem(lax.broadcasted_iota(jnp.int32, (total, 1), 0), 16) // 4

        def rows_of(which):
            mask = jnp.where(kind == which, 1.0, 0.0).astype(BF)
            return [part * mask for part in picked]

        late_ref[...] = sum(dot_tn(part, fact) for part in rows_of(1))
        early_ref[...] = sum(dot_tn(part, fact) for part in rows_of(2))
        label = fact[:, 0:1].astype(jnp.float32) + 32.0 * fact[:, 128:129].astype(jnp.float32)
        wide = lax.broadcasted_iota(jnp.int32, (total, 3 * D), 1).astype(jnp.float32)
        hot = jnp.where(wide == label, 1.0, 0.0).astype(BF)
        class_ref[...] = sum(dot_tn(part, hot) for part in rows_of(3))

    for layer in range(layers):
        mod = mod_of(layer)
        is_turn = turn == layers - 1 - layer
        attn_w, in_w, out_w = (flat(fulls[lead + 3 * layer + k], wide_rows) for k in range(3))

        @pl.when(is_turn & (h == 0))
        def _(layer=layer, mod=mod, in_w=in_w, out_w=out_w):
            @pl.when(n == 0)
            def _():
                acc_one[...] = jnp.zeros_like(acc_one)
                acc_two[...] = jnp.zeros_like(acc_two)

            if layer == layers - 1:
                head = block_of(slot_refs, 4)[:, 256 : 256 + OUT]
                fmod = lambda part: mod_rows(fmod_ref, (), n, nb, part)
                hat, rstd = norm_rows(result_ref[0].reshape(nb, tokens, D))
                final_in = (hat * (1.0 + fmod(1)) + fmod(0)).astype(BF)
                d_parts = []
                for b in range(nb):
                    predicted = lax.dot_general(
                        head, final_in[b], (((0,), (1,)), ((), ())), preferred_element_type=jnp.float32
                    )
                    errors = predicted - jnp.concatenate([noise_ref[b], clean_ref[b]], axis=0)
                    loss_s[...] += jnp.sum((errors * errors).reshape(OUT // 8, 8, tokens), axis=0)
                    d_pred = (errors * (2.0 / count_all)).astype(BF)
                    d_head_s[...] += dot_nn(d_pred, final_in[b])
                    d_parts.append(
                        lax.dot_general(
                            d_pred, head, (((0,), (1,)), ((), ())), preferred_element_type=jnp.float32
                        )
                    )
                d_stream, d_shift, d_scale = norm_back(jnp.stack(d_parts, axis=0), hat, rstd, fmod(1))
                for b in range(nb):
                    d_fmod_s[pl.ds(n * nb + b, 1), :D] = d_shift[b]
                    d_fmod_s[pl.ds(n * nb + b, 1), D:] = d_scale[b]
            else:
                d_stream = d_stream_s[here, :].reshape(nb, tokens, D)
            mlp = mlp_ref[0].astype(jnp.float32).reshape(nb, tokens, D)
            put_mod(layer, 5, jnp.sum(d_stream * mlp, axis=1, keepdims=True))
            d_mlp = (d_stream * mod(5)).astype(BF).reshape(rows, D)
            d_hidden = (dot_nt(d_mlp, out_w[...]) * slope_ref[0].astype(jnp.float32)).astype(BF)
            acc_two[...] += dot_tn(act_ref[0], d_mlp)
            hat, rstd = norm_rows(middle_ref[0].reshape(nb, tokens, D))
            mlp_in = (hat * (1.0 + mod(4)) + mod(3)).astype(BF).reshape(rows, D)
            acc_one[...] += dot_tn(d_hidden, mlp_in)
            d_input = dot_nn(d_hidden, in_w[...]).reshape(nb, tokens, D)
            d_middle, d_shift, d_scale = norm_back(d_input, hat, rstd, mod(4))
            put_mod(layer, 3, d_shift)
            put_mod(layer, 4, d_scale)
            d_stream_s[here, :] = (d_middle + d_stream).reshape(rows, D)

            @pl.when(n == steps - 1)
            def _():
                pair = 0 if layer == layers - 1 else 2
                if pair:
                    for copy in first_copies[0] + first_copies[1]:
                        copy.wait_send()
                flat(stage_in, wide_rows)[...] = acc_one[...].astype(BF)
                flat(stage_out, wide_rows)[...] = acc_two[...].astype(BF)
                run(*both(pair, 0))
                if layer == layers - 1:
                    send_small()

        @pl.when(is_turn & (h == 1))
        def _(layer=layer, mod=mod, attn_w=attn_w):
            @pl.when(n == 0)
            def _():
                acc_one[...] = jnp.zeros_like(acc_one)

            d_middle = d_stream_s[here, :].reshape(nb, tokens, D)
            branch = branch_ref[0].astype(jnp.float32).reshape(nb, tokens, D)
            put_mod(layer, 2, jnp.sum(d_middle * branch, axis=1, keepdims=True))
            d_proj = (d_middle * mod(2)).astype(BF).reshape(rows, D)
            acc_one[3 * D :, :] += dot_tn(d_proj, mixed_ref[0])
            d_mix = dot_nn(d_proj, attn_w[3 * D :, :]).astype(BF)
            attend_backward(nb, tokens, qkv_ref.at[0], probs_ref.at[0], d_mix, d_qkv_s)
            d_qkv = d_qkv_s[...]
            stream = start_ref[...] if layer == 0 else result_ref[0]
            hat, rstd = norm_rows(stream.reshape(nb, tokens, D))
            attn_in = (hat * (1.0 + mod(1)) + mod(0)).astype(BF).reshape(rows, D)
            acc_one[: 3 * D, :] += dot_tn(d_qkv, attn_in)
            d_attn_in = dot_nn(d_qkv, attn_w[: 3 * D, :]).reshape(nb, tokens, D)
            d_before, d_shift, d_scale = norm_back(d_attn_in, hat, rstd, mod(1))
            put_mod(layer, 0, d_shift)
            put_mod(layer, 1, d_scale)
            d_prev = d_middle + d_before
            if layer == 0:
                for b in range(nb):
                    d_patch_s[...] += lax.dot_general(
                        noisy_ref[b].astype(jnp.float32),
                        d_prev[b],
                        (((1,), (0,)), ((), ())),
                        precision=highest,
                    )
            else:
                d_stream_s[here, :] = d_prev.reshape(rows, D)

            @pl.when(n == steps - 1)
            def _():
                if layer == 0:
                    for copy in first_copies[2]:
                        copy.wait_send()
                flat(stage_attn, wide_rows)[...] = acc_one[...].astype(BF)
                if layer > 0:
                    run(*both(1, 0))
                    spread(layer)
                    for p in range(SPLIT):
                        if p * part_rows >= layer * ada_rows:
                            takes[slots + p].wait()
                            sum_s[...] += dot_nn(raw_part(p), ada_refs[p][...])
                    send_mods(layer)
                else:
                    finish_all()


def fused_backward(places, slots, nb, count_all, given, mods, fmod, pre, cond, square, streams):
    clean_t, noise_t, noisy, start, result, *kept = streams
    layers = mods.shape[0]
    lat_count, _, tokens = noisy.shape
    total, rows, steps = lat_count * tokens, nb * tokens, lat_count // nb
    chunks = len(given) - 1
    jobs = chunks - slots - SPLIT + 2
    dims = places.dims
    depth, widest = len(dims), max(dims)
    block = given[0].shape[-2:]
    last = steps - 1

    def const_shape(shape):
        return pl.BlockSpec(shape, lambda t, h, n: (0,) * len(shape))

    def only(turn, half, before, after):
        def pick(t, h, n):
            at, phase = 2 * t + h, 2 * turn + half
            return jnp.where(at == phase, n, jnp.where(at < phase, before, after))

        return pick

    def spec(block_shape, pick):
        return pl.BlockSpec(block_shape, lambda t, h, n: (pick(t, h, n),) + (0,) * (len(block_shape) - 1))

    def result_index(t, h, n):
        head = (t == 0) & (h == 0)
        body_step = (t == 0) & (h == 1)
        return (jnp.where(head, 1, 0), jnp.where(head | body_step, n, last), 0)

    def mlp_spec(cols):
        return pl.BlockSpec(
            (1, rows, cols), lambda t, h, n: (layers - 1 - t, jnp.where(h == 0, n, last), 0)
        )

    def attn_spec(cols):
        return pl.BlockSpec((1, rows, cols), lambda t, h, n: (layers - 1 - t, jnp.where(h == 1, n, 0), 0))

    consts = (mods, fmod, pre, cond, square)
    in_specs = [pl.BlockSpec(memory_space=pl.ANY)] * (chunks + 1) + [const_shape(a.shape) for a in consts]
    in_specs += [spec((nb, PATCH_IN, tokens), only(0, 0, 0, last))] * 2
    in_specs += [
        spec((nb, PATCH_IN, tokens), only(1, 1, 0, last)),
        spec((rows, D), only(1, 1, 0, last)),
        pl.BlockSpec((1, rows, D), result_index),
    ]
    in_specs += [attn_spec(a.shape[2]) for a in kept[:4]] + [mlp_spec(a.shape[2]) for a in kept[4:]]
    patch_block = (PATCH_IN, 128)
    shared = (lax.axis_size("tp"), *block)
    out_shape = [jax.ShapeDtypeStruct(block, jnp.float32)] * (jobs - 2)
    out_shape += [
        jax.ShapeDtypeStruct(s, jnp.float32)
        for s in (patch_block, shared, block, block, (block[0], 3 * D), (layers * mods.shape[2] // places.count, D), (8, 128))
    ]
    full = (*dims, *block)
    blocks = [block] * (jobs - 1) + [patch_block]
    accs, lands = [], []
    for at in range(jobs):
        accs.append(pltpu.VMEM(dims[:-1] + blocks[at], BF))
        lands += [pltpu.VMEM(shape, BF) for shape in land_shapes(places, at % 2 == 1, blocks[at])]
    f32 = jnp.float32
    scratch = [pltpu.VMEM(full, BF)] * chunks + [pltpu.VMEM((*dims, 16, D), BF)] + accs + lands
    scratch += [pltpu.VMEM((*dims, 8, 128), f32)] * (layers * (depth + 1))
    scratch += [
        pltpu.VMEM((places.count, 16, 128), f32),
        pltpu.VMEM(full, BF),
        pltpu.VMEM((*dims, *patch_block), BF),
        pltpu.VMEM(block, f32),
        pltpu.VMEM((16, D), f32),
        pltpu.VMEM((*dims, 16, D), f32),
    ]
    scratch += [pltpu.VMEM(full, BF)] * 3
    scratch += [
        pltpu.VMEM(shape, kind)
        for shape, kind in (
            ((4 * D, D), f32),
            ((4 * D, D), f32),
            ((total, D), f32),
            ((rows, 3 * D), BF),
            ((*mods.shape[:2], mods.shape[2] + 128), f32),
            ((8, SPLIT * places.count * block[0]), f32),
            ((8, 2 * D), f32),
            ((PATCH_IN, D), f32),
            ((OUT, D), f32),
            ((8, tokens), f32),
            ((16, D), f32),
            ((8, 128), f32),
            (shared, f32),
            ((depth, widest, 8, 128), f32),
        )
    ]
    dma = pltpu.SemaphoreType.DMA
    count = (jobs + 1 + layers) * copies_per_part(places)
    scratch += [dma((count,)), dma((count,)), dma((jobs + 1,)), dma((chunks + 1,))]
    scratch += [dma((depth, widest - 1))] * 4
    sizes = (block[0], 6 * D // places.count, block[0], block[0])
    return pl.pallas_call(
        functools.partial(
            fused_backward_kernel, places, slots, layers, nb, tokens, lat_count, count_all, sizes
        ),
        grid=(layers, 2, steps),
        out_shape=out_shape,
        in_specs=in_specs,
        out_specs=[const_shape(s.shape) for s in out_shape],
        scratch_shapes=scratch,
        compiler_params=pltpu.CompilerParams(
            collective_id=4, has_side_effects=True, vmem_limit_bytes=LIMIT_B
        ),
        name="backward_and_reduce",
    )(*given, *consts, *streams)


def position_table(grid_side, columns):
    quarter = columns // 4
    omegas = jnp.exp(-math.log(10000.0) * jnp.arange(quarter, dtype=jnp.float32) / quarter)
    positions = jnp.arange(grid_side * grid_side, dtype=jnp.int32)
    row_pos = (positions // grid_side).astype(jnp.float32)[:, None] * omegas
    col_pos = (positions % grid_side).astype(jnp.float32)[:, None] * omegas
    return jnp.concatenate(
        [jnp.sin(row_pos), jnp.cos(row_pos), jnp.sin(col_pos), jnp.cos(col_pos)], axis=-1
    )


def time_table(step_ids, columns):
    half_cols = columns // 2
    frequency = jnp.exp(-math.log(10000.0) * jnp.arange(half_cols, dtype=jnp.float32) / half_cols)
    angles = step_ids.astype(jnp.float32)[:, None] * frequency
    return jnp.concatenate([jnp.cos(angles), jnp.sin(angles)], axis=-1)


def noise_scales(step_ids):
    phases = (step_ids.astype(jnp.float32) / NOISE_STEPS + 0.008) / 1.008 * (math.pi / 2)
    return (jnp.cos(phases), jnp.sin(phases))


def swap(array):
    return jnp.swapaxes(array, -1, -2)


def pad_rows(part):
    extra = -part.shape[-2] % 16
    if extra == 0:
        return part
    return jnp.pad(part, [(0, 0)] * (part.ndim - 2) + [(0, extra), (0, 0)])


def body(
    clean_latents,
    noise_field,
    timesteps,
    labels,
    drop_flags,
    entry_weight,
    class_table,
    attn_weight,
    ffn_in_weight,
    ffn_out_weight,
    ada_weight,
    final_weight,
    entry_first,
    entry_second,
    class_first,
    class_second,
    attn_first,
    attn_second,
    ffn_in_first,
    ffn_in_second,
    ffn_out_first,
    ffn_out_second,
    ada_first,
    ada_second,
    final_first,
    final_second,
):
    lat_count = clean_latents.shape[0]
    tokens = clean_latents.shape[1]
    layers = attn_weight.shape[0]
    both = ("dp", "tp")
    devices = lax.axis_size("dp") * lax.axis_size("tp")
    count_all = float(lat_count * devices * tokens * OUT)
    count_rms = float(lat_count * devices * tokens * D)
    nb = 1
    clean_t, noise_t = swap(clean_latents), swap(noise_field)
    n_dp, n_tp = lax.axis_size("dp"), lax.axis_size("tp")
    places = Places(n_dp, n_tp)
    slots = -(-SMALL // n_tp)
    dp_rows = final_weight.shape[0]
    wide_rows = attn_weight.shape[2]
    ada_rows = ada_weight.shape[2]
    part_rows = -(-layers * ada_rows // SPLIT)

    def flat_ada(array):
        return swap(array).reshape(layers * ada_rows, D)

    weights_in = (
        swap(entry_weight),
        swap(class_table),
        final_weight,
        flat_ada(ada_weight),
        swap(attn_weight),
        swap(ffn_in_weight),
        ffn_out_weight,
    )
    def whole_rows(block, rows):
        return block[:, :rows].reshape(-1, D)

    def to_slot(block):
        if dp_rows % 16 == 0:
            return block.reshape(n_dp, n_tp, dp_rows, D)
        block = block.reshape(n_dp, n_tp, -1, D)[:, :, :dp_rows]
        return block.swapaxes(0, 1).reshape(1, n_tp, n_dp * dp_rows, D)

    def from_slot(block):
        if dp_rows % 16 == 0:
            return block.reshape(places.count, dp_rows, D)
        block = block.reshape(n_tp, n_dp, dp_rows, D).swapaxes(0, 1)
        return pad_rows(block.reshape(places.count, dp_rows, D))

    fused = dp_rows == wide_rows == part_rows and dp_rows % 16 == 0 and len(places.dims) >= 4 and layers == 2
    fused = fused and n_tp >= 3 and lat_count == 4
    if fused:
        outs = fused_forward(
            places, slots, nb, weights_in, (timesteps, labels, drop_flags), clean_t, noise_t
        )
        chunks = slots + SPLIT + 3 * layers
        mods, fmod, pre, cond, noisy, start, result, *kept, square = outs[chunks + 1 :]
        streams = (clean_t, noise_t, noisy, start, result, *kept)
        *summed, patch, both, early, late, classes, ada_grad, stats = fused_backward(
            places, slots, nb, count_all, outs[: chunks + 1], mods, fmod, pre, cond, square, streams
        )
    else:
        cos_part, sin_part = noise_scales(timesteps)
        noisy = (cos_part[:, None, None] * clean_t + sin_part[:, None, None] * noise_t).astype(BF)
        time_feat = time_table(timesteps, FREQ).astype(BF)
        feat = jnp.pad(time_feat, ((0, 8 - lat_count), (PATCH_IN, D - PATCH_IN - FREQ)))
        classes_used = jnp.where(drop_flags == 1, CLASSES, labels)
        classes_used = jnp.pad(classes_used, (0, 8 - lat_count), constant_values=3 * D)
        class_hot = (classes_used[:, None] == jnp.arange(3 * D, dtype=jnp.int32)[None, :]).astype(BF)
        pos = position_table(GRID, D)
        gathered = gather_all(places, slots, *weights_in)
        slot_full = [to_slot(g) for g in gathered[:slots]]
        ada_full = [whole_rows(g, part_rows) for g in gathered[slots : slots + SPLIT]]
        block_full = [whole_rows(g, wide_rows) for g in gathered[slots + SPLIT :]]
        weights = [tuple(block_full[3 * l : 3 * l + 3]) for l in range(layers)]

        raw, fmod, pre, cond, patch_t, head = condition(feat, class_hot, slot_full, ada_full, lat_count)
        mods = raw[:lat_count].reshape(lat_count, SPLIT, places.count, part_rows).swapaxes(1, 2)
        mods = mods.reshape(lat_count, places.count, layers, ada_rows).transpose(2, 0, 1, 3)
        mods = mods.reshape(layers, lat_count, 6, D)
        mods = jnp.pad(mods, ((0, 0), (0, 0), (0, 2), (0, 0)))
        mods = [mods[l] for l in range(layers)]
        saved = []
        squares = []
        stream = None
        for l in range(layers):
            if l == 0:
                outs = forward_layer(True, (noisy, patch_t, pos), mods[l], weights[l], nb, tokens)
                stream, outs = outs[0], outs[1:]
            else:
                outs = forward_layer(False, (stream,), mods[l], weights[l], nb, tokens)
            saved.append((stream, *outs[1:9]))
            stream = outs[0]
            squares.append(outs[9])
        layer_grads = [None] * layers
        d_mods = [None] * layers
        d_stream = None
        for l in reversed(range(layers)):
            last, first = l == layers - 1, l == 0
            entry_args = (stream, fmod, head, clean_t, noise_t) if last else (d_stream,)
            if first:
                entry_args = (*entry_args, noisy)
            outs = list(backward_layer(first, last, entry_args, mods[l], weights[l], saved[l], nb, tokens, count_all))
            if last:
                loss_part, d_head_t, d_fmod = outs[:3]
                outs = outs[3:]
            if first:
                d_patch = outs[0]
            else:
                d_stream = outs[0]
            layer_grads[l] = outs[1:4]
            d_mods[l] = outs[4]
        d_raw = jnp.stack([d[:, :6] for d in d_mods]).reshape(layers, lat_count, places.count, ada_rows)
        d_raw = d_raw.transpose(1, 2, 0, 3).reshape(lat_count, places.count, SPLIT, part_rows)
        d_raw = d_raw.swapaxes(1, 2).reshape(lat_count, -1)
        d_raw = jnp.pad(d_raw, ((0, 8 - lat_count), (0, 0)))
        small_grads = condition_back(
            feat, class_hot, slot_full, ada_full, pre, cond, d_raw, d_fmod, d_patch, d_head_t
        )
        grads = [from_slot(g) for g in small_grads[:slots]]
        grads += [pad_rows(g.reshape(places.count, part_rows, D)) for g in small_grads[slots:]]
        for l in reversed(range(layers)):
            for k in range(3):
                grads.append(pad_rows(layer_grads[l][k].reshape(places.count, wide_rows, D)))
        *summed, both, stats = reduce_all(places, slots, grads, loss_part, squares)
        wide = summed[slots + SPLIT :]
        wide = [wide[3 * (layers - 1 - l) + k] for l in range(layers) for k in range(3)]
    states = []
    for shape_it, triple in (
        (swap, (entry_weight, entry_first, entry_second)),
        (swap, (class_table, class_first, class_second)),
        (swap, (attn_weight, attn_first, attn_second)),
        (swap, (ffn_in_weight, ffn_in_first, ffn_in_second)),
        (lambda a: a, (ffn_out_weight, ffn_out_first, ffn_out_second)),
        (flat_ada, (ada_weight, ada_first, ada_second)),
        (lambda a: a, (final_weight, final_first, final_second)),
    ):
        states.extend(shape_it(a) for a in triple)
    if fused:
        out = fused_adam(layers, count_rms, (stats, both, early, late, classes, ada_grad, patch), summed, states)
    else:
        out = adam_all(slots, layers, count_rms, stats, both, [*summed[slots : slots + SPLIT], *wide], states)
    news = []
    for at in range(21):
        value = out[at]
        if at // 3 == 5:
            value = value.reshape(layers, ada_rows, D)
        news.append(value if at // 3 in (4, 6) else swap(value))
    return (*news, out[21].reshape(()), out[22].reshape(()), out[23].reshape(layers))


def solution(mesh):
    lead = P(("dp", "tp"), None, None)
    ids = P(("dp", "tp"))
    wide = P(None, "dp")
    cols = P(None, None, ("dp", "tp"))
    rows = P(None, ("dp", "tp"), None)
    top = P("dp", None)
    return jax.shard_map(
        body,
        mesh=mesh,
        in_specs=(
            lead,
            lead,
            ids,
            ids,
            ids,
            wide,
            wide,
            cols,
            cols,
            rows,
            cols,
            top,
            wide,
            wide,
            wide,
            wide,
            cols,
            cols,
            cols,
            cols,
            rows,
            rows,
            cols,
            cols,
            top,
            top,
        ),
        out_specs=(wide,) * 6 + (cols,) * 6 + (rows,) * 3 + (cols,) * 3 + (top,) * 3 + (P(), P(), P()),
        check_vma=False,
    )
```

```python
import functools
import math

import jax
import jax.numpy as jnp
import numpy as np
from jax import lax
from jax.experimental import pallas as pl
from jax.experimental.pallas import tpu as pltpu
from jax.sharding import PartitionSpec as P

D = 384
HEADS = 6
HEAD_DIM = 64
CLASSES = 1000
GRID = 16
PATCH_IN = 16
OUT = 32
FREQ = 256
NOISE_STEPS = 1000
STEP = 10
BF = jnp.bfloat16
NB_FORWARD = 1


highest = lax.Precision.HIGHEST


def dot_nn(a, b):
    return lax.dot_general(a, b, (((1,), (0,)), ((), ())), preferred_element_type=jnp.float32)


def dot_nt(a, b):
    return lax.dot_general(a, b, (((1,), (1,)), ((), ())), preferred_element_type=jnp.float32)


def dot_tn(a, b):
    return lax.dot_general(a, b, (((0,), (0,)), ((), ())), preferred_element_type=jnp.float32)


def norm_rows(rows):
    center = rows - jnp.mean(rows, axis=-1, keepdims=True)
    rstd = lax.rsqrt(jnp.mean(center * center, axis=-1, keepdims=True) + 1e-06)
    return center * rstd, rstd


def norm_back(d_out, hat, rstd, scale):
    d_shift = jnp.sum(d_out, axis=1, keepdims=True)
    d_scale = jnp.sum(d_out * hat, axis=1, keepdims=True)
    d_hat = d_out * (1.0 + scale)
    m_one = jnp.mean(d_hat, axis=-1, keepdims=True)
    m_two = jnp.mean(d_hat * hat, axis=-1, keepdims=True)
    return rstd * (d_hat - m_one - hat * m_two), d_shift, d_scale


def half_masks():
    lane = lax.broadcasted_iota(jnp.int32, (1, 2 * HEAD_DIM), 1)
    low = jnp.where(lane < HEAD_DIM, 1.0, 0.0)
    return low.astype(BF), (1.0 - low).astype(BF)


def stack_heads(pair, masks):
    return jnp.concatenate([pair * masks[0], pair * masks[1]], axis=0)


GELU_A = math.sqrt(2.0 / math.pi)
GELU_B = 0.044715


def forward_kernel(first, nb, tokens, *refs):
    if first:
        noisy_ref, patch_ref, pos_ref = refs[:3]
        refs = refs[3:]
    else:
        stream_ref = refs[0]
        refs = refs[1:]
    mod_ref, attn_ref, in_ref, out_ref = refs[:4]
    refs = refs[4:]
    if first:
        start_ref = refs[0]
        refs = refs[1:]
    (
        result_ref,
        qkv_ref,
        probs_ref,
        mixed_ref,
        branch_ref,
        middle_ref,
        mlp_ref,
        act_ref,
        slope_ref,
        square_ref,
    ) = refs
    rows = nb * tokens
    if first:
        parts = [
            lax.dot_general(
                noisy_ref[n], patch_ref[...], (((0,), (1,)), ((), ())), preferred_element_type=jnp.float32
            )
            + pos_ref[...]
            for n in range(nb)
        ]
        stream = parts[0] if nb == 1 else jnp.concatenate(parts, axis=0)
        start_ref[...] = stream
    else:
        stream = stream_ref[...]
    mod = mod_ref[...]
    stream = stream.reshape(nb, tokens, D)
    hat, _ = norm_rows(stream)
    attn_in = (hat * (1.0 + mod[:, 1:2]) + mod[:, 0:1]).astype(BF).reshape(rows, D)
    qkv_ref[...] = dot_nt(attn_in, attn_ref[: 3 * D, :]).astype(BF)
    masks = half_masks()
    for n in range(nb):
        here = slice(n * tokens, (n + 1) * tokens)
        for pair in range(HEADS // 2):
            col = pair * 2 * HEAD_DIM
            queries = qkv_ref[here, col : col + 2 * HEAD_DIM] * jnp.asarray(HEAD_DIM**-0.5, BF)
            keys = stack_heads(qkv_ref[here, D + col : D + col + 2 * HEAD_DIM], masks)
            values = stack_heads(qkv_ref[here, 2 * D + col : 2 * D + col + 2 * HEAD_DIM], masks)
            scores = dot_nt(queries, keys)
            halves = []
            for side in range(2):
                part = scores[:, side * tokens : (side + 1) * tokens]
                grown = jnp.exp(part - jnp.max(part, axis=-1, keepdims=True))
                halves.append((grown * (1.0 / jnp.sum(grown, axis=-1, keepdims=True))).astype(BF))
            probs = jnp.concatenate(halves, axis=1)
            probs_ref[here, pair * 2 * tokens : (pair + 1) * 2 * tokens] = probs
            mixed_ref[here, col : col + 2 * HEAD_DIM] = dot_nn(probs, values).astype(BF)
    branch = dot_nt(mixed_ref[...], attn_ref[3 * D :, :])
    branch_ref[...] = branch.astype(BF)
    middle = stream + mod[:, 2:3] * branch.reshape(nb, tokens, D)
    middle_ref[...] = middle.reshape(rows, D)
    hat, _ = norm_rows(middle)
    mlp_in = (hat * (1.0 + mod[:, 4:5]) + mod[:, 3:4]).astype(BF).reshape(rows, D)
    hidden = dot_nt(mlp_in, in_ref[...])
    squared = hidden * hidden
    bent = jnp.tanh(hidden * (GELU_A + (GELU_A * GELU_B) * squared))
    half = 0.5 * hidden
    act = (half + half * bent).astype(BF)
    act_ref[...] = act
    slope_ref[...] = (
        0.5
        + 0.5 * bent
        + half * (1.0 - bent * bent) * (GELU_A + (3.0 * GELU_A * GELU_B) * squared)
    ).astype(BF)
    mlp = dot_nn(act, out_ref[...])
    mlp_ref[...] = mlp.astype(BF)
    result = middle + mod[:, 5:6] * mlp.reshape(nb, tokens, D)
    result_ref[...] = result.reshape(rows, D)
    square_ref[0] = jnp.sum((result * result).reshape(rows // 8, 8, D), axis=0)


def backward_kernel(first, last, nb, tokens, steps, count_all, *refs):
    if last:
        final_ref, fmod_ref, head_ref, clean_ref, noise_ref = refs[:5]
        refs = refs[5:]
    else:
        d_stream_ref = refs[0]
        refs = refs[1:]
    if first:
        noisy_ref = refs[0]
        refs = refs[1:]
    (
        mod_ref,
        attn_ref,
        in_ref,
        out_ref,
        stream_ref,
        qkv_ref,
        probs_ref,
        mixed_ref,
        branch_ref,
        middle_ref,
        mlp_ref,
        act_ref,
        slope_ref,
    ) = refs[:13]
    refs = refs[13:]
    if last:
        loss_ref, dhead_ref, dfmod_ref = refs[:3]
        refs = refs[3:]
    if first:
        dpatch_ref = refs[0]
    else:
        d_prev_ref = refs[0]
    gattn_ref, gin_ref, gout_ref, dmod_ref, acc_attn, acc_in, acc_out, d_qkv_s = refs[1:]
    rows = nb * tokens
    step = pl.program_id(0)

    @pl.when(step == 0)
    def _():
        acc_attn[...] = jnp.zeros_like(acc_attn)
        acc_in[...] = jnp.zeros_like(acc_in)
        acc_out[...] = jnp.zeros_like(acc_out)
        if last:
            dhead_ref[...] = jnp.zeros_like(dhead_ref)
        if first:
            dpatch_ref[...] = jnp.zeros_like(dpatch_ref)

    mod = mod_ref[...]
    if last:
        fmod = fmod_ref[...]
        hat, rstd = norm_rows(final_ref[...].reshape(nb, tokens, D))
        final_in = (hat * (1.0 + fmod[:, 1:2]) + fmod[:, 0:1]).astype(BF)
        d_parts = []
        loss = jnp.zeros((8, tokens), jnp.float32)
        for n in range(nb):
            predicted = lax.dot_general(
                head_ref[...], final_in[n], (((0,), (1,)), ((), ())), preferred_element_type=jnp.float32
            )
            errors = predicted - jnp.concatenate([noise_ref[n], clean_ref[n]], axis=0)
            loss = loss + jnp.sum((errors * errors).reshape(OUT // 8, 8, tokens), axis=0)
            d_pred = (errors * (2.0 / count_all)).astype(BF)
            dhead_ref[...] += dot_nn(d_pred, final_in[n])
            d_parts.append(
                lax.dot_general(
                    d_pred, head_ref[...], (((0,), (1,)), ((), ())), preferred_element_type=jnp.float32
                )
            )
        loss_ref[0] = loss
        d_final = jnp.stack(d_parts, axis=0)
        d_stream, d_shift, d_scale = norm_back(d_final, hat, rstd, fmod[:, 1:2])
        dfmod_ref[:, 0:1] = d_shift
        dfmod_ref[:, 1:2] = d_scale
    else:
        d_stream = d_stream_ref[...].reshape(nb, tokens, D)
    dmod_ref[:, 5:6] = jnp.sum(d_stream * mlp_ref[...].astype(jnp.float32).reshape(nb, tokens, D), axis=1, keepdims=True)
    d_mlp = (d_stream * mod[:, 5:6]).astype(BF).reshape(rows, D)
    d_hidden = (dot_nt(d_mlp, out_ref[...]) * slope_ref[...].astype(jnp.float32)).astype(BF)
    acc_out[...] += dot_tn(act_ref[...], d_mlp)
    hat, rstd = norm_rows(middle_ref[...].reshape(nb, tokens, D))
    mlp_in = (hat * (1.0 + mod[:, 4:5]) + mod[:, 3:4]).astype(BF).reshape(rows, D)
    acc_in[...] += dot_tn(d_hidden, mlp_in)
    d_input = dot_nn(d_hidden, in_ref[...]).reshape(nb, tokens, D)
    d_middle, d_shift, d_scale = norm_back(d_input, hat, rstd, mod[:, 4:5])
    dmod_ref[:, 3:4] = d_shift
    dmod_ref[:, 4:5] = d_scale
    d_middle = d_middle + d_stream
    dmod_ref[:, 2:3] = jnp.sum(
        d_middle * branch_ref[...].astype(jnp.float32).reshape(nb, tokens, D), axis=1, keepdims=True
    )
    d_proj = (d_middle * mod[:, 2:3]).astype(BF).reshape(rows, D)
    acc_attn[3 * D :, :] += dot_tn(d_proj, mixed_ref[...])
    d_mix = dot_nn(d_proj, attn_ref[3 * D :, :]).astype(BF)
    masks = half_masks()
    lane = lax.broadcasted_iota(jnp.int32, (tokens, 2 * HEAD_DIM), 1)
    low_side = lane < HEAD_DIM
    root = HEAD_DIM**-0.5
    for n in range(nb):
        here = slice(n * tokens, (n + 1) * tokens)
        for pair in range(HEADS // 2):
            col = pair * 2 * HEAD_DIM
            queries = qkv_ref[here, col : col + 2 * HEAD_DIM]
            keys = stack_heads(qkv_ref[here, D + col : D + col + 2 * HEAD_DIM], masks)
            values = stack_heads(qkv_ref[here, 2 * D + col : 2 * D + col + 2 * HEAD_DIM], masks)
            d_out = d_mix[here, col : col + 2 * HEAD_DIM]
            probs_bf = probs_ref[here, pair * 2 * tokens : (pair + 1) * 2 * tokens]
            d_probs = dot_nt(d_out, values)
            halves = []
            for side in range(2):
                cut = slice(side * tokens, (side + 1) * tokens)
                probs = probs_bf[:, cut].astype(jnp.float32)
                part = d_probs[:, cut]
                halves.append((probs * (part - jnp.sum(probs * part, axis=-1, keepdims=True))).astype(BF))
            d_scores = jnp.concatenate(halves, axis=1)
            d_queries = dot_nn(d_scores, keys) * root
            d_keys = dot_tn(d_scores, queries)
            d_keys = jnp.where(low_side, d_keys[:tokens], d_keys[tokens:]) * root
            d_values = dot_tn(probs_bf, d_out)
            d_values = jnp.where(low_side, d_values[:tokens], d_values[tokens:])
            d_qkv_s[here, col : col + 2 * HEAD_DIM] = d_queries.astype(BF)
            d_qkv_s[here, D + col : D + col + 2 * HEAD_DIM] = d_keys.astype(BF)
            d_qkv_s[here, 2 * D + col : 2 * D + col + 2 * HEAD_DIM] = d_values.astype(BF)
    d_qkv = d_qkv_s[...]
    hat, rstd = norm_rows(stream_ref[...].reshape(nb, tokens, D))
    attn_in = (hat * (1.0 + mod[:, 1:2]) + mod[:, 0:1]).astype(BF).reshape(rows, D)
    acc_attn[: 3 * D, :] += dot_tn(d_qkv, attn_in)
    d_attn_in = dot_nn(d_qkv, attn_ref[: 3 * D, :]).reshape(nb, tokens, D)
    d_before, d_shift, d_scale = norm_back(d_attn_in, hat, rstd, mod[:, 1:2])
    dmod_ref[:, 0:1] = d_shift
    dmod_ref[:, 1:2] = d_scale
    d_prev = d_middle + d_before
    if first:
        for n in range(nb):
            dpatch_ref[...] += lax.dot_general(
                noisy_ref[n].astype(jnp.float32), d_prev[n], (((1,), (0,)), ((), ())), precision=highest
            )
    else:
        d_prev_ref[...] = d_prev.reshape(rows, D)

    @pl.when(step == steps - 1)
    def _():
        gattn_ref[...] = acc_attn[...].astype(BF)
        gin_ref[...] = acc_in[...].astype(BF)
        gout_ref[...] = acc_out[...].astype(BF)


def whole_spec(array):
    return pl.BlockSpec(array.shape, lambda i: (0,) * array.ndim)


def lead_spec(block, ndim):
    return pl.BlockSpec(block, lambda i: (i,) + (0,) * (ndim - 1))


LIMIT = 56 * 1024 * 1024


def forward_layer(first, entry_args, mod, weights, nb, tokens):
    lat_count = mod.shape[0]
    rows = nb * tokens
    steps = lat_count // nb
    total = lat_count * tokens
    kinds = [(D, jnp.float32)] if first else []
    kinds += [
        (D, jnp.float32),
        (3 * D, BF),
        (HEADS * tokens, BF),
        (D, BF),
        (D, BF),
        (D, jnp.float32),
        (D, BF),
        (4 * D, BF),
        (4 * D, BF),
    ]
    out_shape = [jax.ShapeDtypeStruct((total, cols), kind) for cols, kind in kinds]
    out_specs = [lead_spec((rows, cols), 2) for cols, _ in kinds]
    out_shape.append(jax.ShapeDtypeStruct((steps, 8, D), jnp.float32))
    out_specs.append(lead_spec((1, 8, D), 3))
    if first:
        noisy, patch, pos = entry_args
        in_specs = [lead_spec((nb, PATCH_IN, tokens), 3), whole_spec(patch), whole_spec(pos)]
    else:
        in_specs = [lead_spec((rows, D), 2)]
    in_specs += [lead_spec((nb, 8, D), 3)] + [whole_spec(w) for w in weights]
    return pl.pallas_call(
        functools.partial(forward_kernel, first, nb, tokens),
        grid=(steps,),
        out_shape=out_shape,
        in_specs=in_specs,
        out_specs=out_specs,
        compiler_params=pltpu.CompilerParams(vmem_limit_bytes=LIMIT),
        name="block_forward",
    )(*entry_args, mod, *weights)


def backward_layer(first, last, entry_args, mod, weights, saved, nb, tokens, count_all):
    lat_count = mod.shape[0]
    rows = nb * tokens
    steps = lat_count // nb
    total = lat_count * tokens
    in_specs = []
    args = list(entry_args)
    if last:
        in_specs += [
            lead_spec((rows, D), 2),
            lead_spec((nb, 8, D), 3),
            whole_spec(args[2]),
            lead_spec((nb, PATCH_IN, tokens), 3),
            lead_spec((nb, PATCH_IN, tokens), 3),
        ]
    else:
        in_specs += [lead_spec((rows, D), 2)]
    if first:
        in_specs += [lead_spec((nb, PATCH_IN, tokens), 3)]
    in_specs += [lead_spec((nb, 8, D), 3)] + [whole_spec(w) for w in weights]
    in_specs += [lead_spec((rows, s.shape[1]), 2) for s in saved]
    out_shape = []
    out_specs = []

    def add(shape, kind, spec):
        out_shape.append(jax.ShapeDtypeStruct(shape, kind))
        out_specs.append(spec)

    def whole(shape):
        return pl.BlockSpec(shape, lambda i: (0,) * len(shape))

    if last:
        add((steps, 8, tokens), jnp.float32, lead_spec((1, 8, tokens), 3))
        add((OUT, D), jnp.float32, whole((OUT, D)))
        add((lat_count, 8, D), jnp.float32, lead_spec((nb, 8, D), 3))
    if first:
        add((PATCH_IN, D), jnp.float32, whole((PATCH_IN, D)))
    else:
        add((total, D), jnp.float32, lead_spec((rows, D), 2))
    for _ in range(3):
        add((4 * D, D), BF, whole((4 * D, D)))
    add((lat_count, 8, D), jnp.float32, lead_spec((nb, 8, D), 3))
    return pl.pallas_call(
        functools.partial(backward_kernel, first, last, nb, tokens, steps, count_all),
        grid=(steps,),
        out_shape=out_shape,
        in_specs=in_specs,
        out_specs=out_specs,
        scratch_shapes=[pltpu.VMEM((4 * D, D), jnp.float32)] * 3 + [pltpu.VMEM((rows, 3 * D), BF)],
        compiler_params=pltpu.CompilerParams(vmem_limit_bytes=LIMIT),
        name="block_backward",
    )(*args, mod, *weights, *saved)


MESH = pl.DeviceIdType.MESH


class Places:
    def __init__(self, n_dp, n_tp):
        self.digits = []
        for axis, count, top in (("dp", n_dp, 4), ("tp", n_tp, 2)):
            sizes = []
            rest = count
            while rest > 1:
                size = next((s for s in (top, 2, 3, 5, 7) if rest % s == 0), rest)
                sizes.append(size)
                rest //= size
            stride = count
            for size in sizes:
                stride //= size
                self.digits.append((axis, stride, size))
        self.dims = tuple(size for _, _, size in self.digits)
        self.count = n_dp * n_tp
        self.n_tp = n_tp

    def order(self, odd):
        names = list(range(len(self.digits)))
        if odd and len(names) >= 4:
            names[-3], names[-2] = names[-2], names[-3]
        return names

    def mine(self):
        return [lax.rem(lax.axis_index(axis) // stride, size) for axis, stride, size in self.digits]

    def other(self, mine, digit, shift):
        axis, stride, size = self.digits[digit]
        value = lax.rem(mine[digit] + shift, size)
        return {axis: lax.axis_index(axis) + (value - mine[digit]) * stride}, value

    def index(self):
        return lax.axis_index("dp") * self.n_tp + lax.axis_index("tp")

    def device(self, index):
        return (index // self.n_tp, lax.rem(index, self.n_tp))

    def barrier_all(self):
        barrier = pltpu.get_barrier_semaphore()
        me = self.index()
        for shift in range(1, self.count):
            target = self.device(lax.rem(me + shift, self.count))
            pl.semaphore_signal(barrier, inc=1, device_id=target, device_id_type=MESH)
        pl.semaphore_wait(barrier, self.count - 1)

    def barrier(self, mine):
        barrier = pltpu.get_barrier_semaphore()
        count = 0
        for digit, size in enumerate(self.dims):
            for shift in range(1, size):
                target, _ = self.other(mine, digit, shift)
                pl.semaphore_signal(barrier, inc=1, device_id=target, device_id_type=MESH)
                count += 1
        pl.semaphore_wait(barrier, count)


SMALL = 8
SPLIT = 2


def small_blocks(entry_t, table_t, final):
    early = PATCH_IN + FREQ
    return [
        (0, 0, entry_t, 0, early),
        (1, 0, entry_t, early, early + D),
        (2, 0, table_t, 0, D),
        (3, 0, table_t, D, 2 * D),
        (4, 0, table_t, 2 * D, CLASSES + 1),
        (4, 256, final, 2 * D, 2 * D + OUT),
        (5, 0, final, 0, D),
        (6, 0, final, D, 2 * D),
    ]


class Traffic:
    def __init__(self, places, mine, sends, recvs, locals_):
        self.places, self.mine = places, mine
        self.sends, self.recvs, self.locals = sends, recvs, locals_
        self.used = self.used_local = 0
        self.copies = []

    def remote(self, source, target_ref, digit, shift):
        target, _ = self.places.other(self.mine, digit, shift)
        at = self.used
        self.used += 1
        copy = pltpu.make_async_remote_copy(
            src_ref=source,
            dst_ref=target_ref,
            send_sem=self.sends.at[at],
            recv_sem=self.recvs.at[at],
            device_id=target,
            device_id_type=MESH,
        )
        self.copies.append(copy)
        return copy

    def local(self, source, target_ref):
        at = self.used_local
        self.used_local += 1
        return pltpu.make_async_copy(source, target_ref, self.locals.at[at])

    def ahead(self, digit, shift):
        return lax.rem(self.mine[digit] + shift, self.places.dims[digit])

    def finish(self):
        for copy in self.copies:
            copy.wait_send()


def copies_per_part(places):
    dims = places.dims
    return sum(dims) - len(dims) + max(dims) * max(dims)


def gather_job(traffic, odd, source, out):
    places, mine = traffic.places, traffic.mine
    order = places.order(odd)
    depth = len(order)
    split = depth - 2 if depth >= 4 else -1
    own = traffic.local(source, out.at[tuple(mine)])
    waits = [[] for _ in range(depth + 1)]
    starts = [[] for _ in range(depth + 1)]

    def region(done, fixed):
        return tuple(fixed.get(d, slice(None) if d in done else mine[d]) for d in range(depth))

    for stage, digit in enumerate(order):
        done = order[:stage]
        for shift in range(1, places.dims[digit]):
            pieces = [(stage, {})]
            if stage == split:
                before = order[stage - 1]
                pieces = [(stage - 1, {before: mine[before]})]
                pieces += [(stage, {before: traffic.ahead(before, k)}) for k in range(1, places.dims[before])]
            for when, fixed in pieces:
                where = region(done, fixed)
                copy = traffic.remote(source if stage == 0 else out.at[where], out.at[where], digit, shift)
                starts[when].append(copy)
                waits[stage + 1].append(copy)

    def action(k):
        if k == 0:
            own.start()
        if k == 1:
            own.wait()
        for copy in waits[k]:
            copy.wait_recv()
        for copy in starts[k]:
            copy.start()

    return [functools.partial(action, k) for k in range(depth + 1)]


def land_shapes(places, odd, block):
    route = places.order(odd)[::-1]
    depth = len(route)
    shapes = []
    for stage, digit in enumerate(route):
        left = [d for d in range(depth) if d not in route[: stage + 1]]
        shapes.append((places.dims[digit] - 1, *(places.dims[d] for d in left), *block))
    return shapes


def reduce_job(traffic, odd, source, acc, lands, out):
    places, mine = traffic.places, traffic.mine
    route = places.order(odd)[::-1]
    depth = len(route)
    split = 1 if depth >= 4 else -1
    waits = [[] for _ in range(depth + 1)]
    starts = [[] for _ in range(depth + 1)]
    adds = [[] for _ in range(depth + 1)]
    own = traffic.local(
        source.at[tuple(mine[d] if d == route[0] else slice(None) for d in range(depth))], acc
    )

    def left_of(stage):
        return [d for d in range(depth) if d not in route[: stage + 1]]

    def in_acc(values):
        return tuple(values.get(d, mine[d]) for d in range(depth) if d != route[0])

    for stage, digit in enumerate(route):
        gone = route[:stage]
        left = left_of(stage)
        pieces = [(stage + 1, {})]
        if stage == split:
            after = route[stage + 1]
            pieces = [(stage + 1, {after: traffic.ahead(after, k)}) for k in range(1, places.dims[after])]
            pieces += [(stage + 2, {after: mine[after]})]
        for when, fixed in pieces:
            for shift in range(1, places.dims[digit]):
                values = {d: slice(None) for d in left} | fixed | {digit: traffic.ahead(digit, shift)}
                if stage == 0:
                    sent = source.at[tuple(values[d] for d in range(depth))]
                else:
                    sent = acc.at[in_acc(values)]
                target = lands[stage].at[(shift - 1, *(values[d] for d in left))]
                copy = traffic.remote(sent, target, digit, shift)
                starts[stage].append(copy)
                waits[when].append(copy)
            adds[when].append((stage, fixed))

    def add(group):
        stage, fixed = group[-1]
        free = [d for d in left_of(stage) if d not in fixed]
        count = math.prod(places.dims[d] for d in free)
        last = stage == depth - 1

        def one(flat, carry):
            values = dict(fixed)
            rest = flat
            for d in reversed(free):
                values[d] = lax.rem(rest, places.dims[d])
                rest = rest // places.dims[d]
            total = acc[in_acc(values)].astype(jnp.float32)
            for near, _ in group:
                for shift in range(places.dims[route[near]] - 1):
                    index = (shift, *(values.get(d, mine[d]) for d in left_of(near)))
                    total = total + lands[near][index].astype(jnp.float32)
            if last:
                out[...] = total
            else:
                acc[in_acc(values)] = total.astype(BF)
            return carry

        lax.fori_loop(0, count, one, 0)

    def action(k):
        if k == 0:
            own.start()
        if k == 1:
            own.wait()
        for copy in waits[k]:
            copy.wait_recv()
        if k == split + 2:
            add(adds[k])
        else:
            for entry in adds[k]:
                add([entry])
        if k < depth:
            for copy in starts[k]:
                copy.start()

    return [functools.partial(action, k) for k in range(depth + 1)]


def in_waves(jobs):
    pairs = [jobs[at : at + 2] for at in range(0, len(jobs), 2)]
    depth = len(jobs[0])
    sequence = []
    for tick in range(len(pairs) + depth - 1):
        for k in range(depth):
            if 0 <= tick - k < len(pairs):
                sequence.extend(job[k] for job in pairs[tick - k])
    return sequence


def gather_kernel(places, slots, layers, *refs):
    entry_ref, table_ref, final_ref, ada_ref, attn_ref, in_ref, out_ref = refs[:7]
    chunks = slots + SPLIT + 3 * layers
    outs = refs[7 : 7 + chunks]
    small, packed, send_sems, recv_sems, own_sems = refs[7 + chunks :]
    mine = places.mine()
    small[...] = jnp.zeros_like(small)
    for k, at, source, low, high in small_blocks(entry_ref, table_ref, final_ref):
        small[k, : source.shape[0], at : at + high - low] = source[:, low:high].astype(BF)
    part = -(-ada_ref.shape[0] // SPLIT)
    for p in range(SPLIT):
        packed[p, :part, :] = ada_ref[p * part : (p + 1) * part, :].astype(BF)
    for l in range(layers):
        for k, source in enumerate((attn_ref, in_ref, out_ref)):
            packed[SPLIT + 3 * l + k, : source.shape[1], :] = source[l].astype(BF)
    first = lax.axis_index("tp") * slots
    ins = [small.at[first + s] for s in range(slots)]
    ins += [packed.at[m, : outs[slots + m].shape[-2]] for m in range(SPLIT + 3 * layers)]
    places.barrier(mine)
    traffic = Traffic(places, mine, send_sems, recv_sems, own_sems)
    jobs = [gather_job(traffic, m % 2 == 1, ins[m], outs[m]) for m in range(chunks)]
    for action in in_waves(jobs):
        action()
    traffic.finish()


def pad16(rows):
    return rows + -rows % 16


def gather_all(places, slots, entry_t, table_t, final, ada_t, attn_t, in_t, out_w):
    layers = attn_t.shape[0]
    small_rows, ada_rows = pad16(final.shape[0]), pad16(-(-ada_t.shape[0] // SPLIT))
    wide_rows = pad16(attn_t.shape[1])
    sizes = [small_rows] * slots + [ada_rows] * SPLIT + [wide_rows] * (3 * layers)
    chunks = len(sizes)
    vmem = pl.BlockSpec(memory_space=pltpu.VMEM)
    packed_rows = max(ada_rows, wide_rows)
    outs = pl.pallas_call(
        functools.partial(gather_kernel, places, slots, layers),
        out_shape=[jax.ShapeDtypeStruct((*places.dims, rows, D), BF) for rows in sizes],
        in_specs=[vmem] * 7,
        out_specs=[pl.BlockSpec(memory_space=pl.ANY)] * chunks,
        scratch_shapes=[
            pltpu.VMEM((slots * lax.axis_size("tp"), small_rows, D), BF),
            pltpu.VMEM((SPLIT + 3 * layers, packed_rows, D), BF),
            pltpu.SemaphoreType.DMA((chunks * copies_per_part(places),)),
            pltpu.SemaphoreType.DMA((chunks * copies_per_part(places),)),
            pltpu.SemaphoreType.DMA((chunks,)),
        ],
        compiler_params=pltpu.CompilerParams(collective_id=1, has_side_effects=True, vmem_limit_bytes=LIMIT),
        name="gather_weights",
    )(entry_t, table_t, final, ada_t, attn_t, in_t, out_w)
    return [o.reshape((places.count,) + o.shape[-2:]) for o in outs]


def reduce_kernel(places, chunks, slots, layers, *refs):
    ins = refs[:chunks]
    loss_ref = refs[chunks]
    square_refs = refs[chunks + 1 : chunks + 1 + layers]
    refs = refs[chunks + 1 + layers :]
    outs, both_ref, stats_ref = refs[:chunks], refs[chunks], refs[chunks + 1]
    refs = refs[chunks + 2 :]
    stats_land, stats_send, stats_recv, both_send, both_recv = refs[-5:]
    refs = refs[:-5]
    depth = len(places.dims)
    accs = refs[:chunks]
    lands = refs[chunks : chunks * (1 + depth)]
    send_sems, recv_sems, own_sems = refs[chunks * (1 + depth) :]
    mine = places.mine()
    places.barrier(mine)
    traffic = Traffic(places, mine, send_sems, recv_sems, own_sems)
    jobs = [
        reduce_job(traffic, m % 2 == 1, ins[m], accs[m], lands[m * depth : (m + 1) * depth], outs[m])
        for m in range(chunks)
    ]
    for action in in_waves(jobs):
        action()
    traffic.finish()

    def lane_sums(rows):
        total = jnp.sum(rows, axis=0, keepdims=True)
        return sum(total[:, at : at + 128] for at in range(0, total.shape[1], 128))

    grad = sum(lane_sums(out[...] * out[...]) for out in outs)
    loss = lane_sums(jnp.sum(loss_ref[...], axis=0))
    squares = [lane_sums(jnp.sum(ref[...], axis=0)) for ref in square_refs]
    stats_ref[...] = jnp.concatenate([grad, loss, *squares, jnp.zeros((6 - layers, 128), jnp.float32)], axis=0)
    for s in range(slots):
        both_ref[(lax.axis_index("tp"), s)] = outs[s][...]
    inner = [d for d in range(depth) if places.digits[d][0] == "tp"]
    for stage, digit in enumerate(reversed(range(depth))):
        size = places.dims[digit]
        axis, stride, _ = places.digits[digit]
        stats_land[stage, mine[digit]] = stats_ref[...]
        copies = []
        for shift in range(1, size):
            target, _ = places.other(mine, digit, shift)
            copies.append(
                pltpu.make_async_remote_copy(
                    src_ref=stats_ref,
                    dst_ref=stats_land.at[stage, mine[digit]],
                    send_sem=stats_send.at[stage, shift - 1],
                    recv_sem=stats_recv.at[stage, shift - 1],
                    device_id=target,
                    device_id_type=MESH,
                )
            )
            if digit in inner:
                held = stride
                start = lax.axis_index("tp") // stride * stride
                where = both_ref.at[pl.ds(start, held)]
                copies.append(
                    pltpu.make_async_remote_copy(
                        src_ref=where,
                        dst_ref=where,
                        send_sem=both_send.at[stage, shift - 1],
                        recv_sem=both_recv.at[stage, shift - 1],
                        device_id=target,
                        device_id_type=MESH,
                    )
                )
        for copy in copies:
            copy.start()
        for copy in copies:
            copy.wait()
        total = stats_land[stage, 0]
        for value in range(1, size):
            total = total + stats_land[stage, value]
        stats_ref[...] = total


def reduce_all(places, slots, parts, loss, squares):
    layers = len(squares)
    vmem = pl.BlockSpec(memory_space=pltpu.VMEM)
    chunks = len(parts)
    dims = places.dims
    depth, widest = len(dims), max(dims)
    blocks = [p.shape[1:] for p in parts]
    lands = []
    for m in range(chunks):
        lands += [pltpu.VMEM(shape, BF) for shape in land_shapes(places, m % 2 == 1, blocks[m])]
    return pl.pallas_call(
        functools.partial(reduce_kernel, places, chunks, slots, layers),
        out_shape=[jax.ShapeDtypeStruct(block, jnp.float32) for block in blocks]
        + [
            jax.ShapeDtypeStruct((lax.axis_size("tp"), slots, *blocks[0]), jnp.float32),
            jax.ShapeDtypeStruct((8, 128), jnp.float32),
        ],
        in_specs=[pl.BlockSpec(memory_space=pl.ANY)] * chunks + [vmem] * (1 + layers),
        out_specs=[vmem] * (chunks + 2),
        scratch_shapes=[pltpu.VMEM(dims[:-1] + block, BF) for block in blocks]
        + lands
        + [
            pltpu.SemaphoreType.DMA((chunks * copies_per_part(places),)),
            pltpu.SemaphoreType.DMA((chunks * copies_per_part(places),)),
            pltpu.SemaphoreType.DMA((chunks,)),
            pltpu.VMEM((depth, widest, 8, 128), jnp.float32),
            pltpu.SemaphoreType.DMA((depth, widest - 1)),
            pltpu.SemaphoreType.DMA((depth, widest - 1)),
            pltpu.SemaphoreType.DMA((depth, widest - 1)),
            pltpu.SemaphoreType.DMA((depth, widest - 1)),
        ],
        compiler_params=pltpu.CompilerParams(collective_id=2, has_side_effects=True, vmem_limit_bytes=LIMIT),
        name="reduce_gradients",
    )(*[p.reshape(dims + p.shape[1:]) for p in parts], loss, *squares)


def silu(values):
    return values * (1.0 / (1.0 + jnp.exp(-values)))


def silu_slope(values):
    gate = 1.0 / (1.0 + jnp.exp(-values))
    return gate * (1.0 + values * (1.0 - gate))


def split_low(values):
    high = values.astype(BF)
    return jnp.concatenate([high, (values - high.astype(jnp.float32)).astype(BF)], axis=0)


def block_of(refs, k):
    slots = len(refs)
    part = refs[k % slots][:, k // slots]
    return part.reshape(-1, D)


def condition_kernel(slots, lat_count, *refs):
    feat_ref, hot_ref = refs[:2]
    slot_refs = refs[2 : 2 + slots]
    ada_refs = refs[2 + slots : 2 + slots + SPLIT]
    mod_ref, fmod_ref, pre_ref, cond_ref, patch_ref, head_ref = refs[2 + slots + SPLIT :]
    entry = block_of(slot_refs, 0)
    patch_ref[...] = entry[:, :PATCH_IN]
    pre = dot_nt(feat_ref[...], entry)
    pre_ref[...] = pre
    cond = dot_nt(silu(pre).astype(BF), block_of(slot_refs, 1))
    for k in range(3):
        cond = cond + dot_nt(hot_ref[:, k * D : (k + 1) * D], block_of(slot_refs, 2 + k))
    cond_ref[...] = cond
    head_ref[...] = block_of(slot_refs, 4)[:, 256 : 256 + OUT]
    act = silu(cond).astype(BF)
    for p in range(SPLIT):
        wide = ada_refs[p].shape[0]
        mod_ref[:, p * wide : (p + 1) * wide] = dot_nt(act, ada_refs[p][...])
    for k in range(2):
        part = dot_nn(act, block_of(slot_refs, 5 + k))
        for b in range(lat_count):
            fmod_ref[b, k : k + 1, :] = part[b : b + 1, :]


def condition(feat, hot, slot_full, ada_full, lat_count):
    vmem = pl.BlockSpec(memory_space=pltpu.VMEM)
    wide = ada_full[0].shape[0]
    shapes = [
        ((8, SPLIT * wide), jnp.float32),
        ((lat_count, 8, D), jnp.float32),
        ((8, D), jnp.float32),
        ((8, D), jnp.float32),
        ((D, PATCH_IN), BF),
        ((D, OUT), BF),
    ]
    return pl.pallas_call(
        functools.partial(condition_kernel, len(slot_full), lat_count),
        out_shape=[jax.ShapeDtypeStruct(*s) for s in shapes],
        in_specs=[vmem] * (2 + len(slot_full) + SPLIT),
        out_specs=[vmem] * len(shapes),
        compiler_params=pltpu.CompilerParams(vmem_limit_bytes=LIMIT),
        name="condition",
    )(feat, hot, *slot_full, *ada_full)


def condition_back_kernel(slots, lat_count, *refs):
    feat_ref, hot_ref = refs[:2]
    slot_refs = refs[2 : 2 + slots]
    ada_refs = refs[2 + slots : 2 + slots + SPLIT]
    pre_ref, cond_ref, d_mod_ref, d_fmod_ref, d_patch_ref, d_head_ref = refs[2 + slots + SPLIT :][:6]
    outs = refs[2 + slots + SPLIT + 6 :]
    g_slots, g_ada = outs[:slots], outs[slots : slots + SPLIT]
    fmod_s = outs[slots + SPLIT]
    pre, cond = pre_ref[...], cond_ref[...]
    act = silu(cond).astype(BF)
    act_two = jnp.concatenate([act, act], axis=0)
    d_cond = jnp.zeros((16, D), jnp.float32)
    for p in range(SPLIT):
        wide = ada_refs[p].shape[0]
        d_mod = split_low(d_mod_ref[:, p * wide : (p + 1) * wide])
        d_cond = d_cond + dot_nn(d_mod, ada_refs[p][...])
        g_ada[p][...] = dot_tn(d_mod, act_two).astype(BF)

    def give(k, grad):
        ref = g_slots[k % slots]
        ref[:, k // slots] = grad.astype(BF).reshape(ref.shape[0], ref.shape[2], D)

    fmod_s[...] = jnp.zeros_like(fmod_s)
    for k in range(2):
        for b in range(lat_count):
            fmod_s[k, b : b + 1, :] = d_fmod_ref[b, k : k + 1, :]
        d_fmod = split_low(fmod_s[k])
        d_cond = d_cond + dot_nt(d_fmod, block_of(slot_refs, 5 + k))
        give(5 + k, dot_tn(act_two, d_fmod))
    d_pre = split_low((d_cond[:8] + d_cond[8:]) * silu_slope(cond))
    time_act = silu(pre).astype(BF)
    give(1, dot_tn(d_pre, jnp.concatenate([time_act, time_act], axis=0)))
    d_time = dot_nn(d_pre, block_of(slot_refs, 1))
    for k in range(3):
        hot = hot_ref[:, k * D : (k + 1) * D]
        grad = dot_tn(d_pre, jnp.concatenate([hot, hot], axis=0))
        if k == 2:
            here = jnp.pad(d_head_ref[...], ((0, 128 - OUT), (0, 0))).T
            grad = jnp.concatenate([grad[:, :256], grad[:, 256:] + here], axis=1)
        give(2 + k, grad)
    d_time = split_low((d_time[:8] + d_time[8:]) * silu_slope(pre))
    grad = dot_tn(d_time, jnp.concatenate([feat_ref[...], feat_ref[...]], axis=0))
    here = jnp.pad(d_patch_ref[...], ((0, 128 - PATCH_IN), (0, 0))).T
    give(0, jnp.concatenate([grad[:, :128] + here, grad[:, 128:]], axis=1))
    for k in range(7, SMALL):
        give(k, jnp.zeros((D, D), jnp.float32))


def condition_back(feat, hot, slot_full, ada_full, pre, cond, d_mod, d_fmod, d_patch, d_head):
    vmem = pl.BlockSpec(memory_space=pltpu.VMEM)
    lat_count = d_fmod.shape[0]
    args = (feat, hot, *slot_full, *ada_full, pre, cond, d_mod, d_fmod, d_patch, d_head)
    kept = (*slot_full, *ada_full)
    return pl.pallas_call(
        functools.partial(condition_back_kernel, len(slot_full), lat_count),
        out_shape=[jax.ShapeDtypeStruct(w.shape, BF) for w in kept],
        in_specs=[vmem] * len(args),
        out_specs=[vmem] * len(kept),
        scratch_shapes=[pltpu.VMEM((2, 8, D), jnp.float32)],
        compiler_params=pltpu.CompilerParams(vmem_limit_bytes=LIMIT),
        name="condition_back",
    )(*args)


def adam_kernel(slots, layers, count_rms, *refs):
    stats_ref, both_ref = refs[:2]
    grads = refs[2 : 2 + SPLIT + 3 * layers]
    states = refs[2 + SPLIT + 3 * layers :][:21]
    outs = refs[2 + SPLIT + 3 * layers + 21 :]
    news, (loss_ref, norm_ref, rms_ref) = outs[:21], outs[21:]
    totals = jnp.sum(stats_ref[...], axis=1, keepdims=True)
    norm = jnp.sqrt(totals[0:1])
    factor = jnp.minimum(1.0, 0.01 / (norm + 1e-06))
    loss_ref[...] = totals[1:2]
    norm_ref[...] = norm
    rms_ref[...] = jnp.sqrt(totals[2 : 2 + layers] / count_rms)
    correct = 1.0 - 0.5**STEP

    def update(name, where, grad):
        weight, first, second = (ref[where] for ref in states[3 * name : 3 * name + 3])
        clipped = grad * factor
        first_new = 0.5 * first + 0.5 * clipped
        second_new = 0.5 * second + 0.5 * clipped * clipped
        root = jnp.sqrt(second_new * (1.0 / correct)) + 1e-08
        new = weight - 0.02 * (first_new * (1.0 / correct) / root + 0.01 * weight)
        news[3 * name][where] = new
        news[3 * name + 1][where] = first_new
        news[3 * name + 2][where] = second_new

    def small(k):
        return both_ref[k // slots, k % slots]

    rows = states[0].shape[0]
    early = PATCH_IN + FREQ
    every = slice(0, rows)
    update(0, (every, slice(0, early)), small(0)[:rows, :early])
    update(0, (every, slice(early, early + D)), small(1)[:rows])
    update(1, (every, slice(0, D)), small(2)[:rows])
    update(1, (every, slice(D, 2 * D)), small(3)[:rows])
    update(1, (every, slice(2 * D, CLASSES + 1)), small(4)[:rows, : CLASSES + 1 - 2 * D])
    update(6, (every, slice(0, D)), small(5)[:rows])
    update(6, (every, slice(D, 2 * D)), small(6)[:rows])
    update(6, (every, slice(2 * D, 2 * D + OUT)), small(4)[:rows, 256 : 256 + OUT])
    part = -(-states[15].shape[0] // SPLIT)
    for p in range(SPLIT):
        update(5, (slice(p * part, (p + 1) * part), slice(0, D)), grads[p][:part])
    for l in range(layers):
        for k in range(3):
            update(2 + k, (l, slice(0, states[6].shape[1]), slice(0, D)), grads[SPLIT + 3 * l + k][: states[6].shape[1]])


def adam_all(slots, layers, count_rms, stats, both, grads, states):
    vmem = pl.BlockSpec(memory_space=pltpu.VMEM)
    args = (stats, both, *grads, *states)
    return pl.pallas_call(
        functools.partial(adam_kernel, slots, layers, count_rms),
        out_shape=[jax.ShapeDtypeStruct(s.shape, jnp.float32) for s in states]
        + [jax.ShapeDtypeStruct((n, 1), jnp.float32) for n in (1, 1, layers)],
        in_specs=[vmem] * len(args),
        out_specs=[vmem] * 24,
        compiler_params=pltpu.CompilerParams(vmem_limit_bytes=LIMIT),
        name="adam",
    )(*args)


def fused_adam_kernel(layers, count_rms, *refs):
    stats_ref, both_ref, early_ref, late_ref, class_ref, ada_ref, patch_ref = refs[:7]
    grads = refs[7 : 7 + 3 * layers]
    states = refs[7 + 3 * layers :][:21]
    outs = refs[7 + 3 * layers + 21 :]
    news, (loss_ref, norm_ref, rms_ref) = outs[:21], outs[21:]
    totals = jnp.sum(stats_ref[...], axis=1, keepdims=True)
    norm = jnp.sqrt(totals[0:1])
    factor = jnp.minimum(1.0, 0.01 / (norm + 1e-06))
    loss_ref[...] = totals[1:2]
    norm_ref[...] = norm
    rms = jnp.sqrt(totals / count_rms)
    rms_ref[...] = jnp.concatenate([rms[2 + l : 3 + l] for l in range(layers)], axis=1)
    correct = 1.0 - 0.5**STEP

    def update(name, where, grad):
        weight, first, second = (ref[where] for ref in states[3 * name : 3 * name + 3])
        clipped = grad * factor
        first_new = 0.5 * first + 0.5 * clipped
        second_new = 0.5 * second + 0.5 * clipped * clipped
        root = jnp.sqrt(second_new * (1.0 / correct)) + 1e-08
        new = weight - 0.02 * (first_new * (1.0 / correct) / root + 0.01 * weight)
        news[3 * name][where] = new
        news[3 * name + 1][where] = first_new
        news[3 * name + 2][where] = second_new

    rows = states[0].shape[0]
    early = PATCH_IN + FREQ
    every = slice(0, rows)
    patch = patch_ref[...].T[:rows, :PATCH_IN]
    update(0, (every, slice(0, PATCH_IN)), patch)
    update(0, (every, slice(PATCH_IN, early)), early_ref[:, PATCH_IN:early])
    update(0, (every, slice(early, early + D)), late_ref[...])
    update(1, (every, slice(0, CLASSES + 1)), class_ref[:, : CLASSES + 1])
    update(6, (every, slice(0, D)), both_ref[1])
    update(6, (every, slice(D, 2 * D)), both_ref[2])
    update(6, (every, slice(2 * D, 2 * D + OUT)), both_ref[0][:, :OUT])
    update(5, (slice(0, states[15].shape[0]), slice(0, D)), ada_ref[...])
    for l in range(layers):
        for k in range(3):
            update(2 + k, (l, slice(0, states[6].shape[1]), slice(0, D)), grads[3 * l + k][: states[6].shape[1]])


def fused_adam(layers, count_rms, small, grads, states):
    vmem = pl.BlockSpec(memory_space=pltpu.VMEM)
    args = (*small, *grads, *states)
    return pl.pallas_call(
        functools.partial(fused_adam_kernel, layers, count_rms),
        out_shape=[jax.ShapeDtypeStruct(s.shape, jnp.float32) for s in states]
        + [jax.ShapeDtypeStruct((1, n), jnp.float32) for n in (1, 1, layers)],
        in_specs=[vmem] * len(args),
        out_specs=[vmem] * 24,
        compiler_params=pltpu.CompilerParams(vmem_limit_bytes=LIMIT),
        name="adam_update",
    )(*args)


def modulation_pieces(layers, ada_rows, part_rows, part_pad, count):
    pieces = []
    for j in range(count):
        for l in range(layers):
            low = l * ada_rows
            while low < (l + 1) * ada_rows:
                p, r = divmod(low, part_rows)
                length = min((l + 1) * ada_rows - low, part_rows - r)
                pieces.append((l, j * ada_rows + low - l * ada_rows, p, j * part_pad + r, length))
                low += length
    return pieces


def class_of(labels_ref, drops_ref, b):
    return jnp.where(drops_ref[b] == 1, CLASSES, labels_ref[b])


def embed_inputs(lat_count, times_ref, labels_ref, drops_ref, freq_ref, feat_s, hot_s, fact_s):
    feat_s[...] = jnp.zeros_like(feat_s)
    hot_s[...] = jnp.zeros_like(hot_s)
    fact_s[...] = jnp.zeros_like(fact_s)
    column = lax.broadcasted_iota(jnp.int32, (1, 3 * D), 1)
    half = FREQ // 2
    for b in range(lat_count):
        angles = times_ref[b].astype(jnp.float32) * freq_ref[...]
        feat_s[b : b + 1, PATCH_IN : PATCH_IN + half] = jnp.cos(angles)
        feat_s[b : b + 1, PATCH_IN + half : PATCH_IN + FREQ] = jnp.sin(angles)
        label = class_of(labels_ref, drops_ref, b)
        hot_s[b : b + 1, :] = jnp.where(column == label, 1.0, 0.0)
        low = lax.rem(label, 32)
        high = (label - low) // 32
        fact_s[12 + b : 13 + b, :128] = jnp.full((1, 128), low, jnp.int32).astype(jnp.float32)
        fact_s[12 + b : 13 + b, 128:256] = jnp.full((1, 128), high, jnp.int32).astype(jnp.float32)
    fact_s[4 : 4 + lat_count, :] = feat_s[:lat_count, :]


def embed_condition(lat_count, feat_s, hot_s, fact_s, slot_refs, pre_ref, cond_ref, fmod_ref):
    pre = dot_nt(feat_s[...].astype(BF), block_of(slot_refs, 0))
    pre_ref[...] = pre
    time_act = silu(pre).astype(BF)
    cond = dot_nt(time_act, block_of(slot_refs, 1))
    for k in range(3):
        cond = cond + dot_nt(hot_s[:, k * D : (k + 1) * D].astype(BF), block_of(slot_refs, 2 + k))
    cond_ref[...] = cond
    act = silu(cond).astype(BF)
    fact_s[8 : 8 + lat_count, :] = act.astype(jnp.float32)[:lat_count]
    fact_s[:lat_count, :] = time_act.astype(jnp.float32)[:lat_count]
    for k in range(2):
        fmod_ref[:, k * D : (k + 1) * D] = dot_nn(act, block_of(slot_refs, 5 + k))


def mod_rows(mod_ref, index, n, nb, part):
    rows = [mod_ref[(*index, pl.ds(n * nb + b, 1), slice(part * D, (part + 1) * D))] for b in range(nb)]
    return jnp.stack(rows, axis=0)


def attend_forward(nb, tokens, stream, mod, attn_w, out_w, qkv_ref, probs_ref, mixed_ref, branch_ref):
    rows = nb * tokens
    hat, _ = norm_rows(stream)
    attn_in = (hat * (1.0 + mod(1)) + mod(0)).astype(BF).reshape(rows, D)
    qkv_ref[...] = dot_nt(attn_in, attn_w[...]).astype(BF)
    masks = half_masks()
    for b in range(nb):
        here = slice(b * tokens, (b + 1) * tokens)
        for pair in range(HEADS // 2):
            col = pair * 2 * HEAD_DIM
            queries = qkv_ref[here, col : col + 2 * HEAD_DIM] * jnp.asarray(HEAD_DIM**-0.5, BF)
            keys = stack_heads(qkv_ref[here, D + col : D + col + 2 * HEAD_DIM], masks)
            values = stack_heads(qkv_ref[here, 2 * D + col : 2 * D + col + 2 * HEAD_DIM], masks)
            scores = dot_nt(queries, keys)
            halves = []
            for side in range(2):
                part = scores[:, side * tokens : (side + 1) * tokens]
                grown = jnp.exp(part - jnp.max(part, axis=-1, keepdims=True))
                halves.append((grown * (1.0 / jnp.sum(grown, axis=-1, keepdims=True))).astype(BF))
            probs = jnp.concatenate(halves, axis=1)
            probs_ref[here, pair * 2 * tokens : (pair + 1) * 2 * tokens] = probs
            mixed_ref[here, col : col + 2 * HEAD_DIM] = dot_nn(probs, values).astype(BF)
    branch = dot_nt(mixed_ref[...], out_w[...])
    branch_ref[...] = branch.astype(BF)
    return stream + mod(2) * branch.reshape(nb, tokens, D)


def feed_forward(nb, tokens, middle, mod, in_w, out_w, mlp_ref, act_ref, slope_ref):
    rows = nb * tokens
    hat, _ = norm_rows(middle)
    mlp_in = (hat * (1.0 + mod(4)) + mod(3)).astype(BF).reshape(rows, D)
    hidden = dot_nt(mlp_in, in_w[...])
    squared = hidden * hidden
    bent = jnp.tanh(hidden * (GELU_A + (GELU_A * GELU_B) * squared))
    half = 0.5 * hidden
    act = (half + half * bent).astype(BF)
    act_ref[...] = act
    slope_ref[...] = (
        0.5
        + 0.5 * bent
        + half * (1.0 - bent * bent) * (GELU_A + (3.0 * GELU_A * GELU_B) * squared)
    ).astype(BF)
    mlp = dot_nn(act, out_w[...])
    mlp_ref[...] = mlp.astype(BF)
    return middle + mod(5) * mlp.reshape(nb, tokens, D)


def fixed_tables(tokens):
    half, quarter = FREQ // 2, D // 4
    freq = np.exp(np.float32(-math.log(10000.0)) * np.arange(half, dtype=np.float32) / np.float32(half))
    omegas = np.exp(np.float32(-math.log(10000.0)) * np.arange(quarter, dtype=np.float32) / np.float32(quarter))
    token = np.arange(tokens)
    row = (token // GRID).astype(np.float32)[:, None] * omegas
    col = (token % GRID).astype(np.float32)[:, None] * omegas
    table = np.concatenate([np.sin(row), np.cos(row), np.sin(col), np.cos(col)], axis=-1)
    return jnp.asarray(freq[None], jnp.float32), jnp.asarray(table, jnp.float32)


PROLOGUE = [(0, 1), (0, 2), (1, 1), (0, 3), (2, 0), (1, 2), (0, 4), 'cond', (2, 1), (1, 3), (3, 0), (1, 4), 'mods', (2, 2)]
LATER = {1: [(3, 1), (4, 0)], 3: [(2, 3)], 4: [(2, 4), (3, 2)], 6: [(4, 1), (5, 0)], 7: [(3, 3)], 8: [(3, 4), 'mods', (5, 1)], 9: [(4, 2)], 10: [(5, 2)], 11: [(4, 3)], 12: [(4, 4), (5, 3)], 14: [(5, 4), 'hand']}


def fused_forward_kernel(places, slots, layers, nb, tokens, lat_count, sizes, *refs):
    small_rows, ada_rows, part_rows, part_pad, wide_rows = sizes
    chunks = slots + SPLIT + 3 * layers
    entry_ref, table_ref, final_ref, ada_ref, attn_ref, in_ref, out_ref = refs[:7]
    times_ref, labels_ref, drops_ref, freq_ref, clean_ref, noise_ref, pos_ref = refs[7:14]
    refs = refs[14:]
    given = refs[: chunks + 1]
    (
        mods_ref,
        fmod_ref,
        pre_ref,
        cond_ref,
        noisy_ref,
        start_ref,
        result_ref,
        qkv_ref,
        probs_ref,
        mixed_ref,
        branch_ref,
        middle_ref,
        mlp_ref,
        act_ref,
        slope_ref,
        square_ref,
    ) = refs[chunks + 1 : chunks + 17]
    refs = refs[chunks + 17 :]
    fulls = refs[: chunks + 1]
    (
        small,
        packed_ada,
        packed,
        stream_s,
        middle_s,
        feat_s,
        hot_s,
        fact_s,
        fact_bf,
        send_sems,
        recv_sems,
        own_sems,
        give_sems,
    ) = refs[chunks + 1 :]
    l, h, n = (pl.program_id(axis) for axis in range(3))
    mine = places.mine()
    first = lax.axis_index("tp") * slots
    order = [*range(slots)]
    for ll in range(layers):
        at = slots + SPLIT + 3 * ll
        order += [at, slots + ll, at + 1, at + 2]
    sources = [small.at[first + s] for s in range(slots)] + [packed_ada.at[p] for p in range(SPLIT)]
    sources += [packed.at[m] for m in range(3 * layers)]
    traffic = Traffic(places, mine, send_sems, recv_sems, own_sems)
    jobs = [gather_job(traffic, at % 2 == 1, sources[m], fulls[m]) for at, m in enumerate(order)]
    pairs = [jobs[at : at + 2] for at in range(0, chunks, 2)]
    pairs.append([gather_job(traffic, False, fact_bf, fulls[chunks])])
    handed = [pltpu.make_async_copy(fulls[m], given[m], give_sems.at[m]) for m in range(chunks + 1)]

    def flat(m, rows):
        return fulls[m].reshape(places.count * rows, D)

    def run(*names):
        for pair, k in names:
            for job in pairs[pair]:
                job[k]()

    def at_step(layer, half, step):
        return pl.when((l == layer) & (h == half) & (n == step))

    def set_mods(layer):
        act = silu(cond_ref[...]).astype(BF)
        low, high = layer * ada_rows, (layer + 1) * ada_rows
        parts = range(low // part_rows, -(-high // part_rows))
        raw = {p: dot_nt(act, flat(slots + p, part_pad)[...]) for p in parts}
        for ll, col, p, at, length in modulation_pieces(layers, ada_rows, part_rows, part_pad, places.count):
            if ll == layer:
                mods_ref[layer, :, col : col + length] = raw[p][:, at : at + length]

    slot_refs = [f.reshape(-1, lax.axis_size("tp"), small_rows, D) for f in fulls[:slots]]

    def pack_blocks():
        for ll in range(layers):
            for k, source in enumerate((attn_ref, in_ref, out_ref)):
                if ll or k:
                    packed[3 * ll + k] = source[ll].astype(BF)

    @at_step(0, 0, 0)
    def _():
        small[...] = jnp.zeros_like(small)
        for k, at, source, low, high in small_blocks(entry_ref, table_ref, final_ref):
            small[k, : source.shape[0], at : at + high - low] = source[:, low:high].astype(BF)
        places.barrier(mine)
        run((0, 0))
        packed_ada[...] = jnp.zeros_like(packed_ada)
        for p in range(SPLIT):
            packed_ada[p, :part_rows, :] = ada_ref[p * part_rows : (p + 1) * part_rows, :].astype(BF)
        packed[0] = attn_ref[0].astype(BF)
        run((1, 0))
        pack_blocks()
        embed_inputs(lat_count, times_ref, labels_ref, drops_ref, freq_ref, feat_s, hot_s, fact_s)
        for entry in PROLOGUE:
            if entry == "cond":
                embed_condition(lat_count, feat_s, hot_s, fact_s, slot_refs, pre_ref, cond_ref, fmod_ref)
                fact_bf[...] = fact_s[...].astype(BF)
            elif entry == "mods":
                set_mods(0)
            else:
                run(entry)

    steps = lat_count // nb
    for number, names in sorted(LATER.items()):
        number = number * steps // 4
        layer_at, rest = divmod(number, 2 * steps)

        @at_step(layer_at, rest // steps, rest % steps)
        def _(names=names):
            for entry in names:
                if entry == "mods":
                    for layer in range(1, layers):
                        set_mods(layer)
                elif entry == "hand":
                    for copy in handed:
                        copy.start()
                else:
                    run(entry)

    rows = nb * tokens
    here = pl.ds(pl.multiple_of(n * rows, rows), rows)

    def weight(layer, k):
        return flat(slots + SPLIT + 3 * layer + k, wide_rows)

    for layer in range(layers):
        mod = lambda part, layer=layer: mod_rows(mods_ref, (layer,), n, nb, part)

        @pl.when((l == layer) & (h == 0))
        def _(layer=layer, mod=mod):
            if layer == 0:
                patch = block_of(slot_refs, 0)[:, :PATCH_IN]
                for b in range(nb):
                    when = jnp.full((1, tokens), times_ref[n * nb + b], jnp.int32).astype(jnp.float32)
                    phase = (when / NOISE_STEPS + 0.008) / 1.008 * (math.pi / 2)
                    noisy_ref[b] = (jnp.cos(phase) * clean_ref[b] + jnp.sin(phase) * noise_ref[b]).astype(BF)
                parts = [
                    lax.dot_general(
                        noisy_ref[b], patch, (((0,), (1,)), ((), ())), preferred_element_type=jnp.float32
                    )
                    + pos_ref[...]
                    for b in range(nb)
                ]
                stream = parts[0] if nb == 1 else jnp.concatenate(parts, axis=0)
                start_ref[...] = stream
            else:
                stream = stream_s[here, :]
            stream = stream.reshape(nb, tokens, D)
            middle = attend_forward(
                nb,
                tokens,
                stream,
                mod,
                weight(layer, 0).at[: 3 * D],
                weight(layer, 0).at[3 * D :],
                qkv_ref.at[0],
                probs_ref.at[0],
                mixed_ref.at[0],
                branch_ref.at[0],
            )
            middle_ref[0] = middle.reshape(rows, D)
            middle_s[here, :] = middle.reshape(rows, D)

        @pl.when((l == layer) & (h == 1))
        def _(layer=layer, mod=mod):
            middle = middle_s[here, :].reshape(nb, tokens, D)
            result = feed_forward(
                nb,
                tokens,
                middle,
                mod,
                weight(layer, 1),
                weight(layer, 2),
                mlp_ref.at[0],
                act_ref.at[0],
                slope_ref.at[0],
            )
            result_ref[0] = result.reshape(rows, D)
            if layer < layers - 1:
                stream_s[here, :] = result.reshape(rows, D)
            square_ref[0, 0] = jnp.sum((result * result).reshape(rows // 8, 8, D), axis=0)

    @at_step(layers - 1, 1, lat_count // nb - 1)
    def _():
        for copy in handed:
            copy.wait()
        traffic.finish()


def fused_forward(places, slots, nb, weights_in, ids, clean_t, noise_t):
    entry_t, table_t, final, ada_t, attn_t, in_t, out_w = weights_in
    layers, wide_rows = attn_t.shape[:2]
    lat_count, _, tokens = clean_t.shape
    small_rows, part_rows, ada_rows = final.shape[0], ada_t.shape[0] // SPLIT, ada_t.shape[0] // layers
    part_pad = pad16(part_rows)
    sizes = [small_rows] * slots + [part_pad] * SPLIT + [wide_rows] * (3 * layers)
    chunks = len(sizes)
    steps = lat_count // nb
    rows, total = nb * tokens, lat_count * tokens
    full_shapes = [(*places.dims, r, D) for r in (*sizes, 16)]

    def const(array):
        return pl.BlockSpec(array.shape, lambda l, h, n: (0,) * array.ndim)

    def const_shape(shape):
        return pl.BlockSpec(shape, lambda l, h, n: (0,) * len(shape))

    def early(l, h, n):
        return jnp.where(h == 0, n, steps - 1)

    def half_one(cols):
        return pl.BlockSpec((1, rows, cols), lambda l, h, n: (l, early(l, h, n), 0))

    def half_two(cols):
        def index(l, h, n):
            before = jnp.where(l == 0, 0, steps - 1)
            return (jnp.where(h == 0, jnp.maximum(l - 1, 0), l), jnp.where(h == 0, before, n), 0)

        return pl.BlockSpec((1, rows, cols), index)

    def square_index(l, h, n):
        before = jnp.where(l == 0, 0, steps - 1)
        return (jnp.where(h == 0, jnp.maximum(l - 1, 0), l), jnp.where(h == 0, before, n), 0, 0)

    out_shape = [jax.ShapeDtypeStruct(s, BF) for s in full_shapes]
    out_specs = [pl.BlockSpec(memory_space=pl.ANY)] * (chunks + 1)

    def add(shape, kind, spec):
        out_shape.append(jax.ShapeDtypeStruct(shape, kind))
        out_specs.append(spec)

    for shape in ((layers, 8, 6 * D), (8, 2 * D), (8, D), (8, D)):
        add(shape, jnp.float32, const_shape(shape))
    def opening(l, h, n):
        return jnp.where((l == 0) & (h == 0), n, steps - 1)

    latents = pl.BlockSpec((nb, PATCH_IN, tokens), lambda l, h, n: (opening(l, h, n), 0, 0))
    add((lat_count, PATCH_IN, tokens), BF, latents)
    add((total, D), jnp.float32, pl.BlockSpec((rows, D), lambda l, h, n: (opening(l, h, n), 0)))
    add((layers, total, D), jnp.float32, half_two(D))
    for cols, kind in ((3 * D, BF), (HEADS * tokens, BF), (D, BF), (D, BF), (D, jnp.float32)):
        add((layers, total, cols), kind, half_one(cols))
    for cols in (D, 4 * D, 4 * D):
        add((layers, total, cols), BF, half_two(cols))
    add((layers, steps, 8, D), jnp.float32, pl.BlockSpec((1, 1, 8, D), square_index))
    freq, pos = fixed_tables(tokens)
    args = (*weights_in, *ids, freq, clean_t, noise_t, pos)
    in_specs = [const(a) for a in weights_in]
    in_specs += [pl.BlockSpec(memory_space=pltpu.SMEM)] * 3 + [const(freq), latents, latents, const(pos)]
    count = (chunks + 1) * copies_per_part(places)
    return pl.pallas_call(
        functools.partial(
            fused_forward_kernel,
            places,
            slots,
            layers,
            nb,
            tokens,
            lat_count,
            (small_rows, ada_rows, part_rows, part_pad, wide_rows),
        ),
        grid=(layers, 2, steps),
        out_shape=out_shape,
        in_specs=in_specs,
        out_specs=out_specs,
        scratch_shapes=[pltpu.VMEM(s, BF) for s in full_shapes]
        + [
            pltpu.VMEM((slots * lax.axis_size("tp"), small_rows, D), BF),
            pltpu.VMEM((SPLIT, part_pad, D), BF),
            pltpu.VMEM((3 * layers, wide_rows, D), BF),
            pltpu.VMEM((total, D), jnp.float32),
            pltpu.VMEM((total, D), jnp.float32),
            pltpu.VMEM((8, D), jnp.float32),
            pltpu.VMEM((8, 3 * D), jnp.float32),
            pltpu.VMEM((16, D), jnp.float32),
            pltpu.VMEM((16, D), BF),
            pltpu.SemaphoreType.DMA((count,)),
            pltpu.SemaphoreType.DMA((count,)),
            pltpu.SemaphoreType.DMA((chunks + 1,)),
            pltpu.SemaphoreType.DMA((chunks + 1,)),
        ],
        compiler_params=pltpu.CompilerParams(
            collective_id=3, has_side_effects=True, vmem_limit_bytes=LIMIT
        ),
        name="gather_and_forward",
    )(*args)


LIMIT_B = 62 * 1024 * 1024

LATER_BACK = {5: [(0, 1)], 8: [(0, 2)], 9: [(1, 1)], 10: [(0, 3), (7, 1)], 11: [(1, 2)], 12: [(7, 2)], 13: [(1, 3), (2, 1), (0, 4)], 14: [(7, 3)], 15: [(2, 2)]}
SHARES = {}
TAIL_ONE = [(3, 1), (2, 3), (6, 1), (4, 1)]
TAIL_TWO = [(5, 1), (7, 4), (1, 4), 0, (3, 2), (6, 2), (4, 2), 1, (3, 3), (6, 3), (5, 2), (4, 3), (2, 4), 2, (5, 3), (6, 4), 'ada', (5, 4), 'small', (4, 4), (3, 4)]


def exchange_job(traffic, bufs):
    places, mine = traffic.places, traffic.mine
    depth = len(places.dims)
    stages = []
    for k, digit in enumerate(reversed(range(depth))):
        copies = []
        for shift in range(1, places.dims[digit]):
            there = tuple(traffic.ahead(digit, shift) if d == digit else slice(None) for d in range(depth))
            here = tuple(mine[d] if d == digit else slice(None) for d in range(depth))
            copies.append(traffic.remote(bufs[k].at[there], bufs[k + 1].at[here], digit, shift))
        stages.append((copies, here))

    def action(k):
        if k > 0:
            for copy in stages[k - 1][0]:
                copy.wait_recv()
        if k < depth:
            copies, here = stages[k]
            for copy in copies:
                copy.start()
            bufs[k + 1][here] = bufs[k][here]

    return [functools.partial(action, k) for k in range(depth + 1)]


def attend_backward(nb, tokens, qkv_ref, probs_ref, d_mix, d_qkv_s):
    masks = half_masks()
    lane = lax.broadcasted_iota(jnp.int32, (tokens, 2 * HEAD_DIM), 1)
    low_side = lane < HEAD_DIM
    root = HEAD_DIM**-0.5
    for b in range(nb):
        here = slice(b * tokens, (b + 1) * tokens)
        for pair in range(HEADS // 2):
            col = pair * 2 * HEAD_DIM
            queries = qkv_ref[here, col : col + 2 * HEAD_DIM]
            keys = stack_heads(qkv_ref[here, D + col : D + col + 2 * HEAD_DIM], masks)
            values = stack_heads(qkv_ref[here, 2 * D + col : 2 * D + col + 2 * HEAD_DIM], masks)
            d_out = d_mix[here, col : col + 2 * HEAD_DIM]
            probs_bf = probs_ref[here, pair * 2 * tokens : (pair + 1) * 2 * tokens]
            d_probs = dot_nt(d_out, values)
            halves = []
            for side in range(2):
                cut = slice(side * tokens, (side + 1) * tokens)
                probs = probs_bf[:, cut].astype(jnp.float32)
                part = d_probs[:, cut]
                halves.append((probs * (part - jnp.sum(probs * part, axis=-1, keepdims=True))).astype(BF))
            d_scores = jnp.concatenate(halves, axis=1)
            d_queries = dot_nn(d_scores, keys) * root
            d_keys = dot_tn(d_scores, queries)
            d_keys = jnp.where(low_side, d_keys[:tokens], d_keys[tokens:]) * root
            d_values = dot_tn(probs_bf, d_out)
            d_values = jnp.where(low_side, d_values[:tokens], d_values[tokens:])
            d_qkv_s[here, col : col + 2 * HEAD_DIM] = d_queries.astype(BF)
            d_qkv_s[here, D + col : D + col + 2 * HEAD_DIM] = d_keys.astype(BF)
            d_qkv_s[here, 2 * D + col : 2 * D + col + 2 * HEAD_DIM] = d_values.astype(BF)


def lane_sums(rows):
    total = jnp.sum(rows, axis=0, keepdims=True)
    return sum(total[:, at : at + 128] for at in range(0, total.shape[1], 128))


def fused_backward_kernel(places, slots, layers, nb, tokens, lat_count, count_all, sizes, *refs):
    small_rows, ada_rows, part_rows, part_pad, wide_rows = sizes
    chunks = slots + SPLIT + 3 * layers
    steps = lat_count // nb
    depth = len(places.dims)
    rows = nb * tokens
    given = refs[: chunks + 1]
    refs = refs[1:]
    mods_ref, fmod_ref, pre_ref, cond_ref, square_ref = refs[chunks : chunks + 5]
    (
        clean_ref,
        noise_ref,
        noisy_ref,
        start_ref,
        result_ref,
        qkv_ref,
        probs_ref,
        mixed_ref,
        branch_ref,
        middle_ref,
        mlp_ref,
        act_ref,
        slope_ref,
    ) = refs[chunks + 5 : chunks + 18]
    refs = refs[chunks + 18 :]
    count = 3 * layers + 2
    outs = refs[: count - 1]
    both_ref, early_ref, late_ref, class_ref, ada_grad_ref, stats_ref = refs[count - 1 : count + 5]
    refs = refs[count + 5 :]
    fulls = refs[: chunks + 1]
    refs = refs[chunks + 1 :]
    accs = refs[:count]
    lands = refs[count : (1 + depth) * count]
    (
        *swaps,
        wide_s,
        small_s,
        patch_s,
        small_out,
        mine_s,
        all_s,
        signal_s,
        code_s,
        stage_attn,
        stage_in,
        stage_out,
        acc_one,
        acc_two,
        d_stream_s,
        d_qkv_s,
        d_mods_s,
        d_raw_s,
        d_fmod_s,
        d_patch_s,
        d_head_s,
        loss_s,
        sum_s,
        stats_s,
        both_s,
        stats_land,
        send_sems,
        recv_sems,
        own_sems,
        take_sems,
        stats_send,
        stats_recv,
        both_send,
        both_recv,
    ) = refs[(1 + depth) * count :]
    turn, h, n = (pl.program_id(axis) for axis in range(3))
    mine = places.mine()
    lead = slots + SPLIT

    def flat(ref, count):
        return ref.reshape(places.count * count, D)

    takes = [pltpu.make_async_copy(given[m], fulls[m], take_sems.at[m]) for m in range(chunks + 1)]
    slot_refs = [f.reshape(-1, lax.axis_size("tp"), small_rows, D) for f in fulls[:slots]]
    ada_refs = [flat(f, part_pad) for f in fulls[slots:lead]]
    staged = {0: stage_attn, 1: stage_in, 2: stage_out}
    order = [lead + 4, lead + 5, lead + 3, lead + 1, lead + 2, lead]
    sources = [staged[(m - lead) % 3] for m in order] + [patch_s]
    targets = [outs[m - lead] for m in order] + [outs[count - 2]]
    sources.insert(3, small_s)
    targets.insert(3, small_out)
    traffic = Traffic(places, mine, send_sems, recv_sems, own_sems)
    jobs = []
    first_copies = []
    for at in range(count):
        used = traffic.used
        jobs.append(
            reduce_job(
                traffic, at % 2 == 1, sources[at], accs[at], lands[at * depth : (at + 1) * depth], targets[at]
            )
        )
        digit = places.order(at % 2 == 1)[-1]
        first_copies.append(traffic.copies[used : used + places.dims[digit] - 1])
    factors = len(jobs)
    jobs.append(gather_job(traffic, False, mine_s, all_s))
    for l in range(layers):
        jobs.append(exchange_job(traffic, swaps[l * (depth + 1) : (l + 1) * (depth + 1)]))
    inner = [d for d in reversed(range(depth)) if places.digits[d][0] == "tp"]

    def both_copies(stage):
        digit = inner[stage]
        _, stride, size = places.digits[digit]
        where = both_s.at[pl.ds(lax.axis_index("tp") // stride * stride, stride)]
        return [
            pltpu.make_async_remote_copy(
                src_ref=where,
                dst_ref=where,
                send_sem=both_send.at[stage, shift - 1],
                recv_sem=both_recv.at[stage, shift - 1],
                device_id=places.other(mine, digit, shift)[0],
                device_id_type=MESH,
            )
            for shift in range(1, size)
        ]

    exchange = [both_copies(stage) for stage in range(len(inner))]

    def share(stage):
        if stage == 0:
            both_s[lax.axis_index("tp")] = small_out[...]
        else:
            for copy in exchange[stage - 1]:
                copy.wait()
        if stage < len(exchange):
            for copy in exchange[stage]:
                copy.start()

    def run(*names):
        for job, k in names:
            jobs[job][k]()

    def at_step(number):
        layer_turn, rest = divmod(number, 2 * steps)
        half, step = divmod(rest, steps)
        return pl.when((turn == layer_turn) & (h == half) & (n == step))

    def both(pair, k):
        return [(job, k) for job in (2 * pair, 2 * pair + 1)]

    def extra(name, k):
        return [({3: 6, 4: 7}.get(name, name + 3), k)]

    def swap_job(layer):
        return factors + 1 + layer

    here = pl.ds(pl.multiple_of(n * rows, rows), rows)

    def mod_of(layer):
        return lambda part: mod_rows(mods_ref, (layer,), n, nb, part)

    def put_mod(layer, part, value):
        for b in range(nb):
            d_mods_s[layer, pl.ds(n * nb + b, 1), part * D : (part + 1) * D] = value[b]

    @at_step(0)
    def _():
        for m in [*range(slots), *range(chunks - 1, slots - 1, -1), chunks]:
            takes[m].start()
        d_mods_s[...] = jnp.zeros_like(d_mods_s)
        d_raw_s[...] = jnp.zeros_like(d_raw_s)
        d_fmod_s[...] = jnp.zeros_like(d_fmod_s)
        d_patch_s[...] = jnp.zeros_like(d_patch_s)
        d_head_s[...] = jnp.zeros_like(d_head_s)
        loss_s[...] = jnp.zeros_like(loss_s)
        sum_s[...] = jnp.zeros_like(sum_s)
        mine_s[...] = jnp.zeros_like(mine_s)
        wide_s[...] = jnp.zeros_like(wide_s)
        signal_s[...] = jnp.zeros_like(signal_s)
        small_s[...] = jnp.zeros_like(small_s)
        patch_s[...] = jnp.zeros_like(patch_s)
        places.barrier_all()
        for m in (*range(slots), lead + 5, lead + 4):
            takes[m].wait()

    hooks = {
        at * steps // 4: [job for name, k in names for job in (both(name, k) if name < 3 else extra(name, k))]
        for at, names in LATER_BACK.items()
    }
    shares = {at * steps // 4: stage for at, stage in SHARES.items()}
    early_ada = [slots + p for p in range(SPLIT) if p * part_rows < (layers - 1) * ada_rows]
    loads = {steps: [lead + 3], 2 * steps: [lead + 2, lead + 1], 3 * steps: [lead, chunks, *early_ada]}
    for number in sorted(set(hooks) | set(loads)):

        @at_step(number)
        def _(number=number):
            for m in loads.get(number, []):
                takes[m].wait()
            run(*hooks.get(number, []))
            if number in shares:
                share(shares[number])

    def raw_part(p):
        wide = places.count * part_pad
        return split_low(d_raw_s[:, p * wide : (p + 1) * wide])

    def send_mods(layer):
        first = swaps[layer * (depth + 1)].reshape(places.count, 8, 128)
        for j in range(places.count):
            first[j] = d_mods_s[layer, :, j * ada_rows : j * ada_rows + 128]
        run((swap_job(layer), 0))

    def ada_grads(layer):
        arrived = swaps[layer * (depth + 1) + depth].reshape(places.count, 8, 128)
        wide_s[:, 8:, :] = arrived[...]
        signal = wide_s.reshape(places.count * 16, 128)[...]
        high = signal.astype(BF)
        low = (signal - high.astype(jnp.float32)).astype(BF)
        fact = fulls[chunks].reshape(places.count * 16, D)[...]
        grad = dot_tn(high, fact) + dot_tn(low, fact)
        ada_grad_ref[layer * ada_rows : (layer + 1) * ada_rows, :] = grad[:ada_rows]

    def spread(layer):
        wide = places.count * part_pad
        for l, col, p, at, length in modulation_pieces(layers, ada_rows, part_rows, part_pad, places.count):
            if l == layer:
                d_raw_s[:, p * wide + at : p * wide + at + length] = d_mods_s[layer, :, col : col + length]

    def send_small():
        cond_act = silu(cond_ref[...]).astype(BF)
        cond_two = jnp.concatenate([cond_act, cond_act], axis=0)
        view = small_s.reshape(-1, lax.axis_size("tp"), small_rows, D)

        def give(k, grad):
            view[:, k] = grad.astype(BF).reshape(view.shape[0], small_rows, D)

        head = jnp.pad(d_head_s[...], ((0, 128 - OUT), (0, 0))).T
        give(0, jnp.pad(head, ((0, 0), (0, D - 128))))
        for k in range(2):
            give(1 + k, dot_tn(cond_two, split_low(d_fmod_s[:, k * D : (k + 1) * D])))

    def expand(entry):
        name, k = entry
        return both(name, k) if name < 3 else extra(name, k)

    def finish_all():
        run((6, 0))
        cond = cond_ref[...]
        pre = pre_ref[...]
        spread(0)
        d_cond = sum_s[...]
        for p in range(SPLIT):
            if p * part_rows < (layers - 1) * ada_rows:
                d_cond = d_cond + dot_nn(raw_part(p), ada_refs[p][...])
        for k in range(2):
            d_fmod = split_low(d_fmod_s[:, k * D : (k + 1) * D])
            d_cond = d_cond + dot_nt(d_fmod, block_of(slot_refs, 5 + k))
        d_pre = (d_cond[:8] + d_cond[8:]) * silu_slope(cond)
        d_time = dot_nn(split_low(d_pre), block_of(slot_refs, 1))
        d_time = (d_time[:8] + d_time[8:]) * silu_slope(pre)
        mine_s[:lat_count, :] = d_pre[:lat_count]
        mine_s[4 : 4 + lat_count, :] = d_time[:lat_count]
        run((factors, 0))
        send_mods(0)
        patch = jnp.pad(d_patch_s[...], ((0, 0), (0, 128)))
        view = patch_s.reshape(-1, lax.axis_size("tp"), PATCH_IN, 128)
        for i in range(view.shape[0]):
            here_cols = patch[:, i * small_rows : i * small_rows + 128].astype(BF)
            for t in range(view.shape[1]):
                view[i, t] = here_cols
        run((7, 0))
        for entry in TAIL_ONE:
            run(*expand(entry))
        for entry in TAIL_TWO:
            if entry == "small":
                small_grads()
            elif entry == "ada":
                for layer in range(layers):
                    ada_grads(layer)
            elif isinstance(entry, int):
                share(entry)
            else:
                run(*expand(entry))
        copies_of_tp = 1.0 / lax.axis_size("tp")
        grad = sum(lane_sums(out[...] * out[...]) for out in (*outs[:-1], small_out, ada_grad_ref))
        lane = lax.broadcasted_iota(jnp.int32, (PATCH_IN, 128), 1)
        patch = jnp.where(lane < small_rows, outs[-1][...], 0.0)
        alike = sum(lane_sums(g * g) for g in (patch, early_ref[...], late_ref[...], class_ref[...]))
        grad = grad + alike * copies_of_tp
        squares = [lane_sums(jnp.sum(square_ref[l], axis=0)) for l in range(layers)]
        stats_s[...] = jnp.concatenate(
            [grad, lane_sums(loss_s[...]), *squares, jnp.zeros((6 - layers, 128), jnp.float32)], axis=0
        )
        me = places.index()
        stats_land[me] = stats_s[...]
        copies = []
        for shift in range(1, places.count):
            copies.append(
                pltpu.make_async_remote_copy(
                    src_ref=stats_s,
                    dst_ref=stats_land.at[me],
                    send_sem=stats_send.at[shift - 1],
                    recv_sem=stats_recv.at[shift - 1],
                    device_id=places.device(lax.rem(me + shift, places.count)),
                    device_id_type=MESH,
                )
            )
            copies[-1].start()
        for copy in copies:
            copy.wait()
        stats_s[...] = jnp.sum(stats_land[...], axis=0)
        stats_ref[...] = stats_s[...]
        both_ref[...] = both_s[...]
        waited = {id(copy) for group in first_copies[:3] for copy in group}
        for copy in traffic.copies:
            if id(copy) not in waited:
                copy.wait_send()

    def small_grads():
        total = places.count * 16
        fact = fulls[chunks].reshape(total, D)[...]
        signal_s[:, :8, :] = all_s.reshape(places.count, 8, D)[...]
        signal = signal_s.reshape(total, D)[...]
        row = lax.broadcasted_iota(jnp.int32, (D, small_rows), 0)
        column = lax.broadcasted_iota(jnp.int32, (D, small_rows), 1)
        pick = jnp.where(row == column + lax.axis_index("dp") * small_rows, 1.0, 0.0).astype(BF)
        high = signal.astype(BF)
        low = (signal - high.astype(jnp.float32)).astype(BF)
        picked = [dot_nn(part, pick).astype(BF) for part in (high, low)]
        kind = lax.rem(lax.broadcasted_iota(jnp.int32, (total, 1), 0), 16) // 4

        def rows_of(which):
            mask = jnp.where(kind == which, 1.0, 0.0).astype(BF)
            return [part * mask for part in picked]

        late_ref[...] = sum(dot_tn(part, fact) for part in rows_of(0))
        early_ref[...] = sum(dot_tn(part, fact) for part in rows_of(1))
        code_s[...] = (fact[:, :128].astype(jnp.float32) + 32.0 * fact[:, 128:256].astype(jnp.float32)).reshape(
            places.count, 16, 128
        )
        code_s[:, :4, :] = code_s[:, 12:, :]
        label = code_s.reshape(total, 128)[:, 0:1]
        wide = lax.broadcasted_iota(jnp.int32, (total, 3 * D), 1).astype(jnp.float32)
        hot = jnp.where(wide == label, 1.0, 0.0).astype(BF)
        class_ref[...] = sum(dot_tn(part, hot) for part in rows_of(0))

    for layer in range(layers):
        mod = mod_of(layer)
        is_turn = turn == layers - 1 - layer
        attn_w, in_w, out_w = (flat(fulls[lead + 3 * layer + k], wide_rows) for k in range(3))

        @pl.when(is_turn & (h == 0))
        def _(layer=layer, mod=mod, in_w=in_w, out_w=out_w):
            @pl.when(n == 0)
            def _():
                acc_one[...] = jnp.zeros_like(acc_one)
                acc_two[...] = jnp.zeros_like(acc_two)

            if layer == layers - 1:
                head = block_of(slot_refs, 4)[:, 256 : 256 + OUT]
                fmod = lambda part: mod_rows(fmod_ref, (), n, nb, part)
                hat, rstd = norm_rows(result_ref[0].reshape(nb, tokens, D))
                final_in = (hat * (1.0 + fmod(1)) + fmod(0)).astype(BF)
                d_parts = []
                for b in range(nb):
                    predicted = lax.dot_general(
                        head, final_in[b], (((0,), (1,)), ((), ())), preferred_element_type=jnp.float32
                    )
                    errors = predicted - jnp.concatenate([noise_ref[b], clean_ref[b]], axis=0)
                    loss_s[...] += jnp.sum((errors * errors).reshape(OUT // 8, 8, tokens), axis=0)
                    d_pred = (errors * (2.0 / count_all)).astype(BF)
                    d_head_s[...] += dot_nn(d_pred, final_in[b])
                    d_parts.append(
                        lax.dot_general(
                            d_pred, head, (((0,), (1,)), ((), ())), preferred_element_type=jnp.float32
                        )
                    )
                d_stream, d_shift, d_scale = norm_back(jnp.stack(d_parts, axis=0), hat, rstd, fmod(1))
                for b in range(nb):
                    d_fmod_s[pl.ds(n * nb + b, 1), :D] = d_shift[b]
                    d_fmod_s[pl.ds(n * nb + b, 1), D:] = d_scale[b]
            else:
                d_stream = d_stream_s[here, :].reshape(nb, tokens, D)
            mlp = mlp_ref[0].astype(jnp.float32).reshape(nb, tokens, D)
            put_mod(layer, 5, jnp.sum(d_stream * mlp, axis=1, keepdims=True))
            d_mlp = (d_stream * mod(5)).astype(BF).reshape(rows, D)
            d_hidden = (dot_nt(d_mlp, out_w[...]) * slope_ref[0].astype(jnp.float32)).astype(BF)
            acc_two[...] += dot_tn(act_ref[0], d_mlp)
            hat, rstd = norm_rows(middle_ref[0].reshape(nb, tokens, D))
            mlp_in = (hat * (1.0 + mod(4)) + mod(3)).astype(BF).reshape(rows, D)
            acc_one[...] += dot_tn(d_hidden, mlp_in)
            d_input = dot_nn(d_hidden, in_w[...]).reshape(nb, tokens, D)
            d_middle, d_shift, d_scale = norm_back(d_input, hat, rstd, mod(4))
            put_mod(layer, 3, d_shift)
            put_mod(layer, 4, d_scale)
            d_stream_s[here, :] = (d_middle + d_stream).reshape(rows, D)

            @pl.when(n == steps - 1)
            def _():
                pair = 0 if layer == layers - 1 else 2
                if pair:
                    for copy in first_copies[0] + first_copies[1]:
                        copy.wait_send()
                flat(stage_in, wide_rows)[...] = acc_one[...].astype(BF)
                flat(stage_out, wide_rows)[...] = acc_two[...].astype(BF)
                run(*both(pair, 0))
                if layer == layers - 1:
                    send_small()

        @pl.when(is_turn & (h == 1))
        def _(layer=layer, mod=mod, attn_w=attn_w):
            @pl.when(n == 0)
            def _():
                acc_one[...] = jnp.zeros_like(acc_one)

            d_middle = d_stream_s[here, :].reshape(nb, tokens, D)
            branch = branch_ref[0].astype(jnp.float32).reshape(nb, tokens, D)
            put_mod(layer, 2, jnp.sum(d_middle * branch, axis=1, keepdims=True))
            d_proj = (d_middle * mod(2)).astype(BF).reshape(rows, D)
            acc_one[3 * D :, :] += dot_tn(d_proj, mixed_ref[0])
            d_mix = dot_nn(d_proj, attn_w[3 * D :, :]).astype(BF)
            attend_backward(nb, tokens, qkv_ref.at[0], probs_ref.at[0], d_mix, d_qkv_s)
            d_qkv = d_qkv_s[...]
            stream = start_ref[...] if layer == 0 else result_ref[0]
            hat, rstd = norm_rows(stream.reshape(nb, tokens, D))
            attn_in = (hat * (1.0 + mod(1)) + mod(0)).astype(BF).reshape(rows, D)
            acc_one[: 3 * D, :] += dot_tn(d_qkv, attn_in)
            d_attn_in = dot_nn(d_qkv, attn_w[: 3 * D, :]).reshape(nb, tokens, D)
            d_before, d_shift, d_scale = norm_back(d_attn_in, hat, rstd, mod(1))
            put_mod(layer, 0, d_shift)
            put_mod(layer, 1, d_scale)
            d_prev = d_middle + d_before
            if layer == 0:
                for b in range(nb):
                    d_patch_s[...] += lax.dot_general(
                        noisy_ref[b].astype(jnp.float32),
                        d_prev[b],
                        (((1,), (0,)), ((), ())),
                        precision=highest,
                    )
            else:
                d_stream_s[here, :] = d_prev.reshape(rows, D)

            @pl.when(n == steps - 1)
            def _():
                if layer == 0:
                    for copy in first_copies[2]:
                        copy.wait_send()
                flat(stage_attn, wide_rows)[...] = acc_one[...].astype(BF)
                if layer > 0:
                    run(*both(1, 0))
                    spread(layer)
                    for p in range(SPLIT):
                        if p * part_rows >= layer * ada_rows:
                            takes[slots + p].wait()
                            sum_s[...] += dot_nn(raw_part(p), ada_refs[p][...])
                    send_mods(layer)
                else:
                    finish_all()


def fused_backward(places, slots, nb, count_all, given, mods, fmod, pre, cond, square, streams):
    clean_t, noise_t, noisy, start, result, *kept = streams
    layers = mods.shape[0]
    lat_count, _, tokens = noisy.shape
    total, rows, steps = lat_count * tokens, nb * tokens, lat_count // nb
    chunks = len(given) - 1
    jobs = chunks - slots - SPLIT + 2
    dims = places.dims
    depth, widest = len(dims), max(dims)
    block = given[0].shape[-2:]
    last = steps - 1

    def const_shape(shape):
        return pl.BlockSpec(shape, lambda t, h, n: (0,) * len(shape))

    def only(turn, half, before, after):
        def pick(t, h, n):
            at, phase = 2 * t + h, 2 * turn + half
            return jnp.where(at == phase, n, jnp.where(at < phase, before, after))

        return pick

    def spec(block_shape, pick):
        return pl.BlockSpec(block_shape, lambda t, h, n: (pick(t, h, n),) + (0,) * (len(block_shape) - 1))

    def result_index(t, h, n):
        head = (t == 0) & (h == 0)
        body_step = (t == 0) & (h == 1)
        return (jnp.where(head, 1, 0), jnp.where(head | body_step, n, last), 0)

    def mlp_spec(cols):
        return pl.BlockSpec(
            (1, rows, cols), lambda t, h, n: (layers - 1 - t, jnp.where(h == 0, n, last), 0)
        )

    def attn_spec(cols):
        return pl.BlockSpec((1, rows, cols), lambda t, h, n: (layers - 1 - t, jnp.where(h == 1, n, 0), 0))

    consts = (mods, fmod, pre, cond, square)
    in_specs = [pl.BlockSpec(memory_space=pl.ANY)] * (chunks + 1) + [const_shape(a.shape) for a in consts]
    in_specs += [spec((nb, PATCH_IN, tokens), only(0, 0, 0, last))] * 2
    in_specs += [
        spec((nb, PATCH_IN, tokens), only(1, 1, 0, last)),
        spec((rows, D), only(1, 1, 0, last)),
        pl.BlockSpec((1, rows, D), result_index),
    ]
    in_specs += [attn_spec(a.shape[2]) for a in kept[:4]] + [mlp_spec(a.shape[2]) for a in kept[4:]]
    patch_block = (PATCH_IN, 128)
    shared = (lax.axis_size("tp"), *block)
    out_shape = [jax.ShapeDtypeStruct(block, jnp.float32)] * (jobs - 2)
    out_shape += [
        jax.ShapeDtypeStruct(s, jnp.float32)
        for s in (patch_block, shared, block, block, (block[0], 3 * D), (layers * mods.shape[2] // places.count, D), (8, 128))
    ]
    full = (*dims, *block)
    blocks = [block] * (jobs - 1) + [patch_block]
    accs, lands = [], []
    for at in range(jobs):
        accs.append(pltpu.VMEM(dims[:-1] + blocks[at], BF))
        lands += [pltpu.VMEM(shape, BF) for shape in land_shapes(places, at % 2 == 1, blocks[at])]
    f32 = jnp.float32
    scratch = [pltpu.VMEM(g.shape, BF) for g in given[:-1]] + [pltpu.VMEM((*dims, 16, D), BF)] + accs + lands
    scratch += [pltpu.VMEM((*dims, 8, 128), f32)] * (layers * (depth + 1))
    scratch += [
        pltpu.VMEM((places.count, 16, 128), f32),
        pltpu.VMEM(full, BF),
        pltpu.VMEM((*dims, *patch_block), BF),
        pltpu.VMEM(block, f32),
        pltpu.VMEM((8, D), f32),
        pltpu.VMEM((*dims, 8, D), f32),
        pltpu.VMEM((places.count, 16, D), f32),
        pltpu.VMEM((places.count, 16, 128), f32),
    ]
    scratch += [pltpu.VMEM(full, BF)] * 3
    scratch += [
        pltpu.VMEM(shape, kind)
        for shape, kind in (
            ((4 * D, D), f32),
            ((4 * D, D), f32),
            ((total, D), f32),
            ((rows, 3 * D), BF),
            ((*mods.shape[:2], mods.shape[2] + 128), f32),
            ((8, SPLIT * places.count * given[slots].shape[-2]), f32),
            ((8, 2 * D), f32),
            ((PATCH_IN, D), f32),
            ((OUT, D), f32),
            ((8, tokens), f32),
            ((16, D), f32),
            ((8, 128), f32),
            (shared, f32),
            ((places.count, 8, 128), f32),
        )
    ]
    dma = pltpu.SemaphoreType.DMA
    count = (jobs + 1 + layers) * copies_per_part(places)
    scratch += [dma((count,)), dma((count,)), dma((jobs + 1,)), dma((chunks + 1,))]
    scratch += [dma((places.count - 1,))] * 2 + [dma((depth, widest - 1))] * 2
    ada_rows = mods.shape[2] // places.count
    sizes = (block[0], ada_rows, layers * ada_rows // SPLIT, given[slots].shape[-2], block[0])
    return pl.pallas_call(
        functools.partial(
            fused_backward_kernel, places, slots, layers, nb, tokens, lat_count, count_all, sizes
        ),
        grid=(layers, 2, steps),
        out_shape=out_shape,
        in_specs=in_specs,
        out_specs=[const_shape(s.shape) for s in out_shape],
        scratch_shapes=scratch,
        compiler_params=pltpu.CompilerParams(
            collective_id=4, has_side_effects=True, vmem_limit_bytes=LIMIT_B
        ),
        name="backward_and_reduce",
    )(*given, *consts, *streams)


def position_table(grid_side, columns):
    quarter = columns // 4
    omegas = jnp.exp(-math.log(10000.0) * jnp.arange(quarter, dtype=jnp.float32) / quarter)
    positions = jnp.arange(grid_side * grid_side, dtype=jnp.int32)
    row_pos = (positions // grid_side).astype(jnp.float32)[:, None] * omegas
    col_pos = (positions % grid_side).astype(jnp.float32)[:, None] * omegas
    return jnp.concatenate(
        [jnp.sin(row_pos), jnp.cos(row_pos), jnp.sin(col_pos), jnp.cos(col_pos)], axis=-1
    )


def time_table(step_ids, columns):
    half_cols = columns // 2
    frequency = jnp.exp(-math.log(10000.0) * jnp.arange(half_cols, dtype=jnp.float32) / half_cols)
    angles = step_ids.astype(jnp.float32)[:, None] * frequency
    return jnp.concatenate([jnp.cos(angles), jnp.sin(angles)], axis=-1)


def noise_scales(step_ids):
    phases = (step_ids.astype(jnp.float32) / NOISE_STEPS + 0.008) / 1.008 * (math.pi / 2)
    return (jnp.cos(phases), jnp.sin(phases))


def swap(array):
    return jnp.swapaxes(array, -1, -2)


def pad_rows(part):
    extra = -part.shape[-2] % 16
    if extra == 0:
        return part
    return jnp.pad(part, [(0, 0)] * (part.ndim - 2) + [(0, extra), (0, 0)])


def body(
    clean_latents,
    noise_field,
    timesteps,
    labels,
    drop_flags,
    entry_weight,
    class_table,
    attn_weight,
    ffn_in_weight,
    ffn_out_weight,
    ada_weight,
    final_weight,
    entry_first,
    entry_second,
    class_first,
    class_second,
    attn_first,
    attn_second,
    ffn_in_first,
    ffn_in_second,
    ffn_out_first,
    ffn_out_second,
    ada_first,
    ada_second,
    final_first,
    final_second,
):
    lat_count = clean_latents.shape[0]
    tokens = clean_latents.shape[1]
    layers = attn_weight.shape[0]
    both = ("dp", "tp")
    devices = lax.axis_size("dp") * lax.axis_size("tp")
    count_all = float(lat_count * devices * tokens * OUT)
    count_rms = float(lat_count * devices * tokens * D)
    nb = 1
    clean_t, noise_t = swap(clean_latents), swap(noise_field)
    n_dp, n_tp = lax.axis_size("dp"), lax.axis_size("tp")
    places = Places(n_dp, n_tp)
    slots = -(-SMALL // n_tp)
    dp_rows = final_weight.shape[0]
    wide_rows = attn_weight.shape[2]
    ada_rows = ada_weight.shape[2]
    part_rows = -(-layers * ada_rows // SPLIT)

    def flat_ada(array):
        return swap(array).reshape(layers * ada_rows, D)

    weights_in = (
        swap(entry_weight),
        swap(class_table),
        final_weight,
        flat_ada(ada_weight),
        swap(attn_weight),
        swap(ffn_in_weight),
        ffn_out_weight,
    )
    def whole_rows(block, rows):
        return block[:, :rows].reshape(-1, D)

    def to_slot(block):
        if dp_rows % 16 == 0:
            return block.reshape(n_dp, n_tp, dp_rows, D)
        block = block.reshape(n_dp, n_tp, -1, D)[:, :, :dp_rows]
        return block.swapaxes(0, 1).reshape(1, n_tp, n_dp * dp_rows, D)

    def from_slot(block):
        if dp_rows % 16 == 0:
            return block.reshape(places.count, dp_rows, D)
        block = block.reshape(n_tp, n_dp, dp_rows, D).swapaxes(0, 1)
        return pad_rows(block.reshape(places.count, dp_rows, D))

    fused = dp_rows == wide_rows and dp_rows % 16 == 0 and part_rows == ada_rows and len(places.dims) >= 4 and layers == 2
    fused = fused and n_tp >= 3 and lat_count == 4
    if fused:
        outs = fused_forward(
            places, slots, NB_FORWARD, weights_in, (timesteps, labels, drop_flags), clean_t, noise_t
        )
        chunks = slots + SPLIT + 3 * layers
        mods, fmod, pre, cond, noisy, start, result, *kept, square = outs[chunks + 1 :]
        streams = (clean_t, noise_t, noisy, start, result, *kept)
        *summed, patch, both, early, late, classes, ada_grad, stats = fused_backward(
            places, slots, nb, count_all, outs[: chunks + 1], mods, fmod, pre, cond, square, streams
        )
    else:
        cos_part, sin_part = noise_scales(timesteps)
        noisy = (cos_part[:, None, None] * clean_t + sin_part[:, None, None] * noise_t).astype(BF)
        time_feat = time_table(timesteps, FREQ).astype(BF)
        feat = jnp.pad(time_feat, ((0, 8 - lat_count), (PATCH_IN, D - PATCH_IN - FREQ)))
        classes_used = jnp.where(drop_flags == 1, CLASSES, labels)
        classes_used = jnp.pad(classes_used, (0, 8 - lat_count), constant_values=3 * D)
        class_hot = (classes_used[:, None] == jnp.arange(3 * D, dtype=jnp.int32)[None, :]).astype(BF)
        pos = position_table(GRID, D)
        gathered = gather_all(places, slots, *weights_in)
        slot_full = [to_slot(g) for g in gathered[:slots]]
        ada_full = [whole_rows(g, part_rows) for g in gathered[slots : slots + SPLIT]]
        block_full = [whole_rows(g, wide_rows) for g in gathered[slots + SPLIT :]]
        weights = [tuple(block_full[3 * l : 3 * l + 3]) for l in range(layers)]

        raw, fmod, pre, cond, patch_t, head = condition(feat, class_hot, slot_full, ada_full, lat_count)
        mods = raw[:lat_count].reshape(lat_count, SPLIT, places.count, part_rows).swapaxes(1, 2)
        mods = mods.reshape(lat_count, places.count, layers, ada_rows).transpose(2, 0, 1, 3)
        mods = mods.reshape(layers, lat_count, 6, D)
        mods = jnp.pad(mods, ((0, 0), (0, 0), (0, 2), (0, 0)))
        mods = [mods[l] for l in range(layers)]
        saved = []
        squares = []
        stream = None
        for l in range(layers):
            if l == 0:
                outs = forward_layer(True, (noisy, patch_t, pos), mods[l], weights[l], nb, tokens)
                stream, outs = outs[0], outs[1:]
            else:
                outs = forward_layer(False, (stream,), mods[l], weights[l], nb, tokens)
            saved.append((stream, *outs[1:9]))
            stream = outs[0]
            squares.append(outs[9])
        layer_grads = [None] * layers
        d_mods = [None] * layers
        d_stream = None
        for l in reversed(range(layers)):
            last, first = l == layers - 1, l == 0
            entry_args = (stream, fmod, head, clean_t, noise_t) if last else (d_stream,)
            if first:
                entry_args = (*entry_args, noisy)
            outs = list(backward_layer(first, last, entry_args, mods[l], weights[l], saved[l], nb, tokens, count_all))
            if last:
                loss_part, d_head_t, d_fmod = outs[:3]
                outs = outs[3:]
            if first:
                d_patch = outs[0]
            else:
                d_stream = outs[0]
            layer_grads[l] = outs[1:4]
            d_mods[l] = outs[4]
        d_raw = jnp.stack([d[:, :6] for d in d_mods]).reshape(layers, lat_count, places.count, ada_rows)
        d_raw = d_raw.transpose(1, 2, 0, 3).reshape(lat_count, places.count, SPLIT, part_rows)
        d_raw = d_raw.swapaxes(1, 2).reshape(lat_count, -1)
        d_raw = jnp.pad(d_raw, ((0, 8 - lat_count), (0, 0)))
        small_grads = condition_back(
            feat, class_hot, slot_full, ada_full, pre, cond, d_raw, d_fmod, d_patch, d_head_t
        )
        grads = [from_slot(g) for g in small_grads[:slots]]
        grads += [pad_rows(g.reshape(places.count, part_rows, D)) for g in small_grads[slots:]]
        for l in reversed(range(layers)):
            for k in range(3):
                grads.append(pad_rows(layer_grads[l][k].reshape(places.count, wide_rows, D)))
        *summed, both, stats = reduce_all(places, slots, grads, loss_part, squares)
        wide = summed[slots + SPLIT :]
        wide = [wide[3 * (layers - 1 - l) + k] for l in range(layers) for k in range(3)]
    states = []
    for shape_it, triple in (
        (swap, (entry_weight, entry_first, entry_second)),
        (swap, (class_table, class_first, class_second)),
        (swap, (attn_weight, attn_first, attn_second)),
        (swap, (ffn_in_weight, ffn_in_first, ffn_in_second)),
        (lambda a: a, (ffn_out_weight, ffn_out_first, ffn_out_second)),
        (flat_ada, (ada_weight, ada_first, ada_second)),
        (lambda a: a, (final_weight, final_first, final_second)),
    ):
        states.extend(shape_it(a) for a in triple)
    if fused:
        out = fused_adam(layers, count_rms, (stats, both, early, late, classes, ada_grad, patch), summed, states)
    else:
        out = adam_all(slots, layers, count_rms, stats, both, [*summed[slots : slots + SPLIT], *wide], states)
    news = []
    for at in range(21):
        value = out[at]
        if at // 3 == 5:
            value = value.reshape(layers, ada_rows, D)
        news.append(value if at // 3 in (4, 6) else swap(value))
    return (*news, out[21].reshape(()), out[22].reshape(()), out[23].reshape(layers))


def solution(mesh):
    lead = P(("dp", "tp"), None, None)
    ids = P(("dp", "tp"))
    wide = P(None, "dp")
    cols = P(None, None, ("dp", "tp"))
    rows = P(None, ("dp", "tp"), None)
    top = P("dp", None)
    return jax.shard_map(
        body,
        mesh=mesh,
        in_specs=(
            lead,
            lead,
            ids,
            ids,
            ids,
            wide,
            wide,
            cols,
            cols,
            rows,
            cols,
            top,
            wide,
            wide,
            wide,
            wide,
            cols,
            cols,
            cols,
            cols,
            rows,
            rows,
            cols,
            cols,
            top,
            top,
        ),
        out_specs=(wide,) * 6 + (cols,) * 6 + (rows,) * 3 + (cols,) * 3 + (top,) * 3 + (P(), P(), P()),
        check_vma=False,
    )
```

```python
import functools
import math

import jax
import jax.numpy as jnp
import numpy as np
from jax import lax
from jax.experimental import pallas as pl
from jax.experimental.pallas import tpu as pltpu
from jax.sharding import PartitionSpec as P

D = 384
HEADS = 6
HEAD_DIM = 64
CLASSES = 1000
GRID = 16
PATCH_IN = 16
OUT = 32
FREQ = 256
NOISE_STEPS = 1000
STEP = 10
BF = jnp.bfloat16
NB_FORWARD = 1


highest = lax.Precision.HIGHEST


def dot_nn(a, b):
    return lax.dot_general(a, b, (((1,), (0,)), ((), ())), preferred_element_type=jnp.float32)


def dot_nt(a, b):
    return lax.dot_general(a, b, (((1,), (1,)), ((), ())), preferred_element_type=jnp.float32)


def dot_tn(a, b):
    return lax.dot_general(a, b, (((0,), (0,)), ((), ())), preferred_element_type=jnp.float32)


def norm_rows(rows):
    center = rows - jnp.mean(rows, axis=-1, keepdims=True)
    rstd = lax.rsqrt(jnp.mean(center * center, axis=-1, keepdims=True) + 1e-06)
    return center * rstd, rstd


def norm_back(d_out, hat, rstd, scale):
    d_shift = jnp.sum(d_out, axis=1, keepdims=True)
    d_scale = jnp.sum(d_out * hat, axis=1, keepdims=True)
    d_hat = d_out * (1.0 + scale)
    m_one = jnp.mean(d_hat, axis=-1, keepdims=True)
    m_two = jnp.mean(d_hat * hat, axis=-1, keepdims=True)
    return rstd * (d_hat - m_one - hat * m_two), d_shift, d_scale


def half_masks():
    lane = lax.broadcasted_iota(jnp.int32, (1, 2 * HEAD_DIM), 1)
    low = jnp.where(lane < HEAD_DIM, 1.0, 0.0)
    return low.astype(BF), (1.0 - low).astype(BF)


def stack_heads(pair, masks):
    return jnp.concatenate([pair * masks[0], pair * masks[1]], axis=0)


GELU_A = math.sqrt(2.0 / math.pi)
GELU_B = 0.044715


def forward_kernel(first, nb, tokens, *refs):
    if first:
        noisy_ref, patch_ref, pos_ref = refs[:3]
        refs = refs[3:]
    else:
        stream_ref = refs[0]
        refs = refs[1:]
    mod_ref, attn_ref, in_ref, out_ref = refs[:4]
    refs = refs[4:]
    if first:
        start_ref = refs[0]
        refs = refs[1:]
    (
        result_ref,
        qkv_ref,
        probs_ref,
        mixed_ref,
        branch_ref,
        middle_ref,
        mlp_ref,
        act_ref,
        slope_ref,
        square_ref,
    ) = refs
    rows = nb * tokens
    if first:
        parts = [
            lax.dot_general(
                noisy_ref[n], patch_ref[...], (((0,), (1,)), ((), ())), preferred_element_type=jnp.float32
            )
            + pos_ref[...]
            for n in range(nb)
        ]
        stream = parts[0] if nb == 1 else jnp.concatenate(parts, axis=0)
        start_ref[...] = stream
    else:
        stream = stream_ref[...]
    mod = mod_ref[...]
    stream = stream.reshape(nb, tokens, D)
    hat, _ = norm_rows(stream)
    attn_in = (hat * (1.0 + mod[:, 1:2]) + mod[:, 0:1]).astype(BF).reshape(rows, D)
    qkv_ref[...] = dot_nt(attn_in, attn_ref[: 3 * D, :]).astype(BF)
    masks = half_masks()
    for n in range(nb):
        here = slice(n * tokens, (n + 1) * tokens)
        for pair in range(HEADS // 2):
            col = pair * 2 * HEAD_DIM
            queries = qkv_ref[here, col : col + 2 * HEAD_DIM] * jnp.asarray(HEAD_DIM**-0.5, BF)
            keys = stack_heads(qkv_ref[here, D + col : D + col + 2 * HEAD_DIM], masks)
            values = stack_heads(qkv_ref[here, 2 * D + col : 2 * D + col + 2 * HEAD_DIM], masks)
            scores = dot_nt(queries, keys)
            halves = []
            for side in range(2):
                part = scores[:, side * tokens : (side + 1) * tokens]
                grown = jnp.exp(part - jnp.max(part, axis=-1, keepdims=True))
                halves.append((grown * (1.0 / jnp.sum(grown, axis=-1, keepdims=True))).astype(BF))
            probs = jnp.concatenate(halves, axis=1)
            probs_ref[here, pair * 2 * tokens : (pair + 1) * 2 * tokens] = probs
            mixed_ref[here, col : col + 2 * HEAD_DIM] = dot_nn(probs, values).astype(BF)
    branch = dot_nt(mixed_ref[...], attn_ref[3 * D :, :])
    branch_ref[...] = branch.astype(BF)
    middle = stream + mod[:, 2:3] * branch.reshape(nb, tokens, D)
    middle_ref[...] = middle.reshape(rows, D)
    hat, _ = norm_rows(middle)
    mlp_in = (hat * (1.0 + mod[:, 4:5]) + mod[:, 3:4]).astype(BF).reshape(rows, D)
    hidden = dot_nt(mlp_in, in_ref[...])
    squared = hidden * hidden
    bent = jnp.tanh(hidden * (GELU_A + (GELU_A * GELU_B) * squared))
    half = 0.5 * hidden
    act = (half + half * bent).astype(BF)
    act_ref[...] = act
    slope_ref[...] = (
        0.5
        + 0.5 * bent
        + half * (1.0 - bent * bent) * (GELU_A + (3.0 * GELU_A * GELU_B) * squared)
    ).astype(BF)
    mlp = dot_nn(act, out_ref[...])
    mlp_ref[...] = mlp.astype(BF)
    result = middle + mod[:, 5:6] * mlp.reshape(nb, tokens, D)
    result_ref[...] = result.reshape(rows, D)
    square_ref[0] = jnp.sum((result * result).reshape(rows // 8, 8, D), axis=0)


def backward_kernel(first, last, nb, tokens, steps, count_all, *refs):
    if last:
        final_ref, fmod_ref, head_ref, clean_ref, noise_ref = refs[:5]
        refs = refs[5:]
    else:
        d_stream_ref = refs[0]
        refs = refs[1:]
    if first:
        noisy_ref = refs[0]
        refs = refs[1:]
    (
        mod_ref,
        attn_ref,
        in_ref,
        out_ref,
        stream_ref,
        qkv_ref,
        probs_ref,
        mixed_ref,
        branch_ref,
        middle_ref,
        mlp_ref,
        act_ref,
        slope_ref,
    ) = refs[:13]
    refs = refs[13:]
    if last:
        loss_ref, dhead_ref, dfmod_ref = refs[:3]
        refs = refs[3:]
    if first:
        dpatch_ref = refs[0]
    else:
        d_prev_ref = refs[0]
    gattn_ref, gin_ref, gout_ref, dmod_ref, acc_attn, acc_in, acc_out, d_qkv_s = refs[1:]
    rows = nb * tokens
    step = pl.program_id(0)

    @pl.when(step == 0)
    def _():
        acc_attn[...] = jnp.zeros_like(acc_attn)
        acc_in[...] = jnp.zeros_like(acc_in)
        acc_out[...] = jnp.zeros_like(acc_out)
        if last:
            dhead_ref[...] = jnp.zeros_like(dhead_ref)
        if first:
            dpatch_ref[...] = jnp.zeros_like(dpatch_ref)

    mod = mod_ref[...]
    if last:
        fmod = fmod_ref[...]
        hat, rstd = norm_rows(final_ref[...].reshape(nb, tokens, D))
        final_in = (hat * (1.0 + fmod[:, 1:2]) + fmod[:, 0:1]).astype(BF)
        d_parts = []
        loss = jnp.zeros((8, tokens), jnp.float32)
        for n in range(nb):
            predicted = lax.dot_general(
                head_ref[...], final_in[n], (((0,), (1,)), ((), ())), preferred_element_type=jnp.float32
            )
            errors = predicted - jnp.concatenate([noise_ref[n], clean_ref[n]], axis=0)
            loss = loss + jnp.sum((errors * errors).reshape(OUT // 8, 8, tokens), axis=0)
            d_pred = (errors * (2.0 / count_all)).astype(BF)
            dhead_ref[...] += dot_nn(d_pred, final_in[n])
            d_parts.append(
                lax.dot_general(
                    d_pred, head_ref[...], (((0,), (1,)), ((), ())), preferred_element_type=jnp.float32
                )
            )
        loss_ref[0] = loss
        d_final = jnp.stack(d_parts, axis=0)
        d_stream, d_shift, d_scale = norm_back(d_final, hat, rstd, fmod[:, 1:2])
        dfmod_ref[:, 0:1] = d_shift
        dfmod_ref[:, 1:2] = d_scale
    else:
        d_stream = d_stream_ref[...].reshape(nb, tokens, D)
    dmod_ref[:, 5:6] = jnp.sum(d_stream * mlp_ref[...].astype(jnp.float32).reshape(nb, tokens, D), axis=1, keepdims=True)
    d_mlp = (d_stream * mod[:, 5:6]).astype(BF).reshape(rows, D)
    d_hidden = (dot_nt(d_mlp, out_ref[...]) * slope_ref[...].astype(jnp.float32)).astype(BF)
    acc_out[...] += dot_tn(act_ref[...], d_mlp)
    hat, rstd = norm_rows(middle_ref[...].reshape(nb, tokens, D))
    mlp_in = (hat * (1.0 + mod[:, 4:5]) + mod[:, 3:4]).astype(BF).reshape(rows, D)
    acc_in[...] += dot_tn(d_hidden, mlp_in)
    d_input = dot_nn(d_hidden, in_ref[...]).reshape(nb, tokens, D)
    d_middle, d_shift, d_scale = norm_back(d_input, hat, rstd, mod[:, 4:5])
    dmod_ref[:, 3:4] = d_shift
    dmod_ref[:, 4:5] = d_scale
    d_middle = d_middle + d_stream
    dmod_ref[:, 2:3] = jnp.sum(
        d_middle * branch_ref[...].astype(jnp.float32).reshape(nb, tokens, D), axis=1, keepdims=True
    )
    d_proj = (d_middle * mod[:, 2:3]).astype(BF).reshape(rows, D)
    acc_attn[3 * D :, :] += dot_tn(d_proj, mixed_ref[...])
    d_mix = dot_nn(d_proj, attn_ref[3 * D :, :]).astype(BF)
    masks = half_masks()
    lane = lax.broadcasted_iota(jnp.int32, (tokens, 2 * HEAD_DIM), 1)
    low_side = lane < HEAD_DIM
    root = HEAD_DIM**-0.5
    for n in range(nb):
        here = slice(n * tokens, (n + 1) * tokens)
        for pair in range(HEADS // 2):
            col = pair * 2 * HEAD_DIM
            queries = qkv_ref[here, col : col + 2 * HEAD_DIM]
            keys = stack_heads(qkv_ref[here, D + col : D + col + 2 * HEAD_DIM], masks)
            values = stack_heads(qkv_ref[here, 2 * D + col : 2 * D + col + 2 * HEAD_DIM], masks)
            d_out = d_mix[here, col : col + 2 * HEAD_DIM]
            probs_bf = probs_ref[here, pair * 2 * tokens : (pair + 1) * 2 * tokens]
            d_probs = dot_nt(d_out, values)
            halves = []
            for side in range(2):
                cut = slice(side * tokens, (side + 1) * tokens)
                probs = probs_bf[:, cut].astype(jnp.float32)
                part = d_probs[:, cut]
                halves.append((probs * (part - jnp.sum(probs * part, axis=-1, keepdims=True))).astype(BF))
            d_scores = jnp.concatenate(halves, axis=1)
            d_queries = dot_nn(d_scores, keys) * root
            d_keys = dot_tn(d_scores, queries)
            d_keys = jnp.where(low_side, d_keys[:tokens], d_keys[tokens:]) * root
            d_values = dot_tn(probs_bf, d_out)
            d_values = jnp.where(low_side, d_values[:tokens], d_values[tokens:])
            d_qkv_s[here, col : col + 2 * HEAD_DIM] = d_queries.astype(BF)
            d_qkv_s[here, D + col : D + col + 2 * HEAD_DIM] = d_keys.astype(BF)
            d_qkv_s[here, 2 * D + col : 2 * D + col + 2 * HEAD_DIM] = d_values.astype(BF)
    d_qkv = d_qkv_s[...]
    hat, rstd = norm_rows(stream_ref[...].reshape(nb, tokens, D))
    attn_in = (hat * (1.0 + mod[:, 1:2]) + mod[:, 0:1]).astype(BF).reshape(rows, D)
    acc_attn[: 3 * D, :] += dot_tn(d_qkv, attn_in)
    d_attn_in = dot_nn(d_qkv, attn_ref[: 3 * D, :]).reshape(nb, tokens, D)
    d_before, d_shift, d_scale = norm_back(d_attn_in, hat, rstd, mod[:, 1:2])
    dmod_ref[:, 0:1] = d_shift
    dmod_ref[:, 1:2] = d_scale
    d_prev = d_middle + d_before
    if first:
        for n in range(nb):
            dpatch_ref[...] += lax.dot_general(
                noisy_ref[n].astype(jnp.float32), d_prev[n], (((1,), (0,)), ((), ())), precision=highest
            )
    else:
        d_prev_ref[...] = d_prev.reshape(rows, D)

    @pl.when(step == steps - 1)
    def _():
        gattn_ref[...] = acc_attn[...].astype(BF)
        gin_ref[...] = acc_in[...].astype(BF)
        gout_ref[...] = acc_out[...].astype(BF)


def whole_spec(array):
    return pl.BlockSpec(array.shape, lambda i: (0,) * array.ndim)


def lead_spec(block, ndim):
    return pl.BlockSpec(block, lambda i: (i,) + (0,) * (ndim - 1))


LIMIT = 56 * 1024 * 1024


def forward_layer(first, entry_args, mod, weights, nb, tokens):
    lat_count = mod.shape[0]
    rows = nb * tokens
    steps = lat_count // nb
    total = lat_count * tokens
    kinds = [(D, jnp.float32)] if first else []
    kinds += [
        (D, jnp.float32),
        (3 * D, BF),
        (HEADS * tokens, BF),
        (D, BF),
        (D, BF),
        (D, jnp.float32),
        (D, BF),
        (4 * D, BF),
        (4 * D, BF),
    ]
    out_shape = [jax.ShapeDtypeStruct((total, cols), kind) for cols, kind in kinds]
    out_specs = [lead_spec((rows, cols), 2) for cols, _ in kinds]
    out_shape.append(jax.ShapeDtypeStruct((steps, 8, D), jnp.float32))
    out_specs.append(lead_spec((1, 8, D), 3))
    if first:
        noisy, patch, pos = entry_args
        in_specs = [lead_spec((nb, PATCH_IN, tokens), 3), whole_spec(patch), whole_spec(pos)]
    else:
        in_specs = [lead_spec((rows, D), 2)]
    in_specs += [lead_spec((nb, 8, D), 3)] + [whole_spec(w) for w in weights]
    return pl.pallas_call(
        functools.partial(forward_kernel, first, nb, tokens),
        grid=(steps,),
        out_shape=out_shape,
        in_specs=in_specs,
        out_specs=out_specs,
        compiler_params=pltpu.CompilerParams(vmem_limit_bytes=LIMIT),
        name="block_forward",
    )(*entry_args, mod, *weights)


def backward_layer(first, last, entry_args, mod, weights, saved, nb, tokens, count_all):
    lat_count = mod.shape[0]
    rows = nb * tokens
    steps = lat_count // nb
    total = lat_count * tokens
    in_specs = []
    args = list(entry_args)
    if last:
        in_specs += [
            lead_spec((rows, D), 2),
            lead_spec((nb, 8, D), 3),
            whole_spec(args[2]),
            lead_spec((nb, PATCH_IN, tokens), 3),
            lead_spec((nb, PATCH_IN, tokens), 3),
        ]
    else:
        in_specs += [lead_spec((rows, D), 2)]
    if first:
        in_specs += [lead_spec((nb, PATCH_IN, tokens), 3)]
    in_specs += [lead_spec((nb, 8, D), 3)] + [whole_spec(w) for w in weights]
    in_specs += [lead_spec((rows, s.shape[1]), 2) for s in saved]
    out_shape = []
    out_specs = []

    def add(shape, kind, spec):
        out_shape.append(jax.ShapeDtypeStruct(shape, kind))
        out_specs.append(spec)

    def whole(shape):
        return pl.BlockSpec(shape, lambda i: (0,) * len(shape))

    if last:
        add((steps, 8, tokens), jnp.float32, lead_spec((1, 8, tokens), 3))
        add((OUT, D), jnp.float32, whole((OUT, D)))
        add((lat_count, 8, D), jnp.float32, lead_spec((nb, 8, D), 3))
    if first:
        add((PATCH_IN, D), jnp.float32, whole((PATCH_IN, D)))
    else:
        add((total, D), jnp.float32, lead_spec((rows, D), 2))
    for _ in range(3):
        add((4 * D, D), BF, whole((4 * D, D)))
    add((lat_count, 8, D), jnp.float32, lead_spec((nb, 8, D), 3))
    return pl.pallas_call(
        functools.partial(backward_kernel, first, last, nb, tokens, steps, count_all),
        grid=(steps,),
        out_shape=out_shape,
        in_specs=in_specs,
        out_specs=out_specs,
        scratch_shapes=[pltpu.VMEM((4 * D, D), jnp.float32)] * 3 + [pltpu.VMEM((rows, 3 * D), BF)],
        compiler_params=pltpu.CompilerParams(vmem_limit_bytes=LIMIT),
        name="block_backward",
    )(*args, mod, *weights, *saved)


MESH = pl.DeviceIdType.MESH


class Places:
    def __init__(self, n_dp, n_tp):
        self.digits = []
        for axis, count, top in (("dp", n_dp, 4), ("tp", n_tp, 2)):
            sizes = []
            rest = count
            while rest > 1:
                size = next((s for s in (top, 2, 3, 5, 7) if rest % s == 0), rest)
                sizes.append(size)
                rest //= size
            stride = count
            for size in sizes:
                stride //= size
                self.digits.append((axis, stride, size))
        self.dims = tuple(size for _, _, size in self.digits)
        self.count = n_dp * n_tp
        self.n_tp = n_tp

    def order(self, odd):
        names = list(range(len(self.digits)))
        if odd and len(names) >= 4:
            names[-3], names[-2] = names[-2], names[-3]
        return names

    def mine(self):
        return [lax.rem(lax.axis_index(axis) // stride, size) for axis, stride, size in self.digits]

    def other(self, mine, digit, shift):
        axis, stride, size = self.digits[digit]
        value = lax.rem(mine[digit] + shift, size)
        return {axis: lax.axis_index(axis) + (value - mine[digit]) * stride}, value

    def index(self):
        return lax.axis_index("dp") * self.n_tp + lax.axis_index("tp")

    def device(self, index):
        return (index // self.n_tp, lax.rem(index, self.n_tp))

    def barrier_all(self):
        barrier = pltpu.get_barrier_semaphore()
        me = self.index()
        for shift in range(1, self.count):
            target = self.device(lax.rem(me + shift, self.count))
            pl.semaphore_signal(barrier, inc=1, device_id=target, device_id_type=MESH)
        pl.semaphore_wait(barrier, self.count - 1)

    def barrier(self, mine):
        barrier = pltpu.get_barrier_semaphore()
        count = 0
        for digit, size in enumerate(self.dims):
            for shift in range(1, size):
                target, _ = self.other(mine, digit, shift)
                pl.semaphore_signal(barrier, inc=1, device_id=target, device_id_type=MESH)
                count += 1
        pl.semaphore_wait(barrier, count)


SMALL = 8
SPLIT = 2


def small_blocks(entry_t, table_t, final):
    early = PATCH_IN + FREQ
    return [
        (0, 0, entry_t, 0, early),
        (1, 0, entry_t, early, early + D),
        (2, 0, table_t, 0, D),
        (3, 0, table_t, D, 2 * D),
        (4, 0, table_t, 2 * D, CLASSES + 1),
        (4, 256, final, 2 * D, 2 * D + OUT),
        (5, 0, final, 0, D),
        (6, 0, final, D, 2 * D),
    ]


class Traffic:
    def __init__(self, places, mine, sends, recvs, locals_):
        self.places, self.mine = places, mine
        self.sends, self.recvs, self.locals = sends, recvs, locals_
        self.used = self.used_local = 0
        self.copies = []

    def remote(self, source, target_ref, digit, shift):
        target, _ = self.places.other(self.mine, digit, shift)
        at = self.used
        self.used += 1
        copy = pltpu.make_async_remote_copy(
            src_ref=source,
            dst_ref=target_ref,
            send_sem=self.sends.at[at],
            recv_sem=self.recvs.at[at],
            device_id=target,
            device_id_type=MESH,
        )
        self.copies.append(copy)
        return copy

    def local(self, source, target_ref):
        at = self.used_local
        self.used_local += 1
        return pltpu.make_async_copy(source, target_ref, self.locals.at[at])

    def ahead(self, digit, shift):
        return lax.rem(self.mine[digit] + shift, self.places.dims[digit])

    def finish(self):
        for copy in self.copies:
            copy.wait_send()


def copies_per_part(places):
    dims = places.dims
    return sum(dims) - len(dims) + max(dims) * max(dims)


def gather_job(traffic, odd, source, out):
    places, mine = traffic.places, traffic.mine
    order = places.order(odd)
    depth = len(order)
    split = depth - 2 if depth >= 4 else -1
    own = traffic.local(source, out.at[tuple(mine)])
    waits = [[] for _ in range(depth + 1)]
    starts = [[] for _ in range(depth + 1)]

    def region(done, fixed):
        return tuple(fixed.get(d, slice(None) if d in done else mine[d]) for d in range(depth))

    for stage, digit in enumerate(order):
        done = order[:stage]
        for shift in range(1, places.dims[digit]):
            pieces = [(stage, {})]
            if stage == split:
                before = order[stage - 1]
                pieces = [(stage - 1, {before: mine[before]})]
                pieces += [(stage, {before: traffic.ahead(before, k)}) for k in range(1, places.dims[before])]
            for when, fixed in pieces:
                where = region(done, fixed)
                copy = traffic.remote(source if stage == 0 else out.at[where], out.at[where], digit, shift)
                starts[when].append(copy)
                waits[stage + 1].append(copy)

    def action(k):
        if k == 0:
            own.start()
        if k == 1:
            own.wait()
        for copy in waits[k]:
            copy.wait_recv()
        for copy in starts[k]:
            copy.start()

    return [functools.partial(action, k) for k in range(depth + 1)]


def land_shapes(places, odd, block):
    route = places.order(odd)[::-1]
    depth = len(route)
    shapes = []
    for stage, digit in enumerate(route):
        left = [d for d in range(depth) if d not in route[: stage + 1]]
        shapes.append((places.dims[digit] - 1, *(places.dims[d] for d in left), *block))
    return shapes


def reduce_job(traffic, odd, source, acc, lands, out):
    places, mine = traffic.places, traffic.mine
    route = places.order(odd)[::-1]
    depth = len(route)
    split = 1 if depth >= 4 else -1
    waits = [[] for _ in range(depth + 1)]
    starts = [[] for _ in range(depth + 1)]
    adds = [[] for _ in range(depth + 1)]
    own = traffic.local(
        source.at[tuple(mine[d] if d == route[0] else slice(None) for d in range(depth))], acc
    )

    def left_of(stage):
        return [d for d in range(depth) if d not in route[: stage + 1]]

    def in_acc(values):
        return tuple(values.get(d, mine[d]) for d in range(depth) if d != route[0])

    for stage, digit in enumerate(route):
        gone = route[:stage]
        left = left_of(stage)
        pieces = [(stage + 1, {})]
        if stage == split:
            after = route[stage + 1]
            pieces = [(stage + 1, {after: traffic.ahead(after, k)}) for k in range(1, places.dims[after])]
            pieces += [(stage + 2, {after: mine[after]})]
        for when, fixed in pieces:
            for shift in range(1, places.dims[digit]):
                values = {d: slice(None) for d in left} | fixed | {digit: traffic.ahead(digit, shift)}
                if stage == 0:
                    sent = source.at[tuple(values[d] for d in range(depth))]
                else:
                    sent = acc.at[in_acc(values)]
                target = lands[stage].at[(shift - 1, *(values[d] for d in left))]
                copy = traffic.remote(sent, target, digit, shift)
                starts[stage].append(copy)
                waits[when].append(copy)
            adds[when].append((stage, fixed))

    def add(group):
        stage, fixed = group[-1]
        free = [d for d in left_of(stage) if d not in fixed]
        count = math.prod(places.dims[d] for d in free)
        last = stage == depth - 1

        def one(flat, carry):
            values = dict(fixed)
            rest = flat
            for d in reversed(free):
                values[d] = lax.rem(rest, places.dims[d])
                rest = rest // places.dims[d]
            total = acc[in_acc(values)].astype(jnp.float32)
            for near, _ in group:
                for shift in range(places.dims[route[near]] - 1):
                    index = (shift, *(values.get(d, mine[d]) for d in left_of(near)))
                    total = total + lands[near][index].astype(jnp.float32)
            if last:
                out[...] = total
            else:
                acc[in_acc(values)] = total.astype(BF)
            return carry

        lax.fori_loop(0, count, one, 0)

    def action(k):
        if k == 0:
            own.start()
        if k == 1:
            own.wait()
        for copy in waits[k]:
            copy.wait_recv()
        if k == split + 2:
            add(adds[k])
        else:
            for entry in adds[k]:
                add([entry])
        if k < depth:
            for copy in starts[k]:
                copy.start()

    return [functools.partial(action, k) for k in range(depth + 1)]


def in_waves(jobs):
    pairs = [jobs[at : at + 2] for at in range(0, len(jobs), 2)]
    depth = len(jobs[0])
    sequence = []
    for tick in range(len(pairs) + depth - 1):
        for k in range(depth):
            if 0 <= tick - k < len(pairs):
                sequence.extend(job[k] for job in pairs[tick - k])
    return sequence


def gather_kernel(places, slots, layers, *refs):
    entry_ref, table_ref, final_ref, ada_ref, attn_ref, in_ref, out_ref = refs[:7]
    chunks = slots + SPLIT + 3 * layers
    outs = refs[7 : 7 + chunks]
    small, packed, send_sems, recv_sems, own_sems = refs[7 + chunks :]
    mine = places.mine()
    small[...] = jnp.zeros_like(small)
    for k, at, source, low, high in small_blocks(entry_ref, table_ref, final_ref):
        small[k, : source.shape[0], at : at + high - low] = source[:, low:high].astype(BF)
    part = -(-ada_ref.shape[0] // SPLIT)
    for p in range(SPLIT):
        packed[p, :part, :] = ada_ref[p * part : (p + 1) * part, :].astype(BF)
    for l in range(layers):
        for k, source in enumerate((attn_ref, in_ref, out_ref)):
            packed[SPLIT + 3 * l + k, : source.shape[1], :] = source[l].astype(BF)
    first = lax.axis_index("tp") * slots
    ins = [small.at[first + s] for s in range(slots)]
    ins += [packed.at[m, : outs[slots + m].shape[-2]] for m in range(SPLIT + 3 * layers)]
    places.barrier(mine)
    traffic = Traffic(places, mine, send_sems, recv_sems, own_sems)
    jobs = [gather_job(traffic, m % 2 == 1, ins[m], outs[m]) for m in range(chunks)]
    for action in in_waves(jobs):
        action()
    traffic.finish()


def pad16(rows):
    return rows + -rows % 16


def gather_all(places, slots, entry_t, table_t, final, ada_t, attn_t, in_t, out_w):
    layers = attn_t.shape[0]
    small_rows, ada_rows = pad16(final.shape[0]), pad16(-(-ada_t.shape[0] // SPLIT))
    wide_rows = pad16(attn_t.shape[1])
    sizes = [small_rows] * slots + [ada_rows] * SPLIT + [wide_rows] * (3 * layers)
    chunks = len(sizes)
    vmem = pl.BlockSpec(memory_space=pltpu.VMEM)
    packed_rows = max(ada_rows, wide_rows)
    outs = pl.pallas_call(
        functools.partial(gather_kernel, places, slots, layers),
        out_shape=[jax.ShapeDtypeStruct((*places.dims, rows, D), BF) for rows in sizes],
        in_specs=[vmem] * 7,
        out_specs=[pl.BlockSpec(memory_space=pl.ANY)] * chunks,
        scratch_shapes=[
            pltpu.VMEM((slots * lax.axis_size("tp"), small_rows, D), BF),
            pltpu.VMEM((SPLIT + 3 * layers, packed_rows, D), BF),
            pltpu.SemaphoreType.DMA((chunks * copies_per_part(places),)),
            pltpu.SemaphoreType.DMA((chunks * copies_per_part(places),)),
            pltpu.SemaphoreType.DMA((chunks,)),
        ],
        compiler_params=pltpu.CompilerParams(collective_id=1, has_side_effects=True, vmem_limit_bytes=LIMIT),
        name="gather_weights",
    )(entry_t, table_t, final, ada_t, attn_t, in_t, out_w)
    return [o.reshape((places.count,) + o.shape[-2:]) for o in outs]


def reduce_kernel(places, chunks, slots, layers, *refs):
    ins = refs[:chunks]
    loss_ref = refs[chunks]
    square_refs = refs[chunks + 1 : chunks + 1 + layers]
    refs = refs[chunks + 1 + layers :]
    outs, both_ref, stats_ref = refs[:chunks], refs[chunks], refs[chunks + 1]
    refs = refs[chunks + 2 :]
    stats_land, stats_send, stats_recv, both_send, both_recv = refs[-5:]
    refs = refs[:-5]
    depth = len(places.dims)
    accs = refs[:chunks]
    lands = refs[chunks : chunks * (1 + depth)]
    send_sems, recv_sems, own_sems = refs[chunks * (1 + depth) :]
    mine = places.mine()
    places.barrier(mine)
    traffic = Traffic(places, mine, send_sems, recv_sems, own_sems)
    jobs = [
        reduce_job(traffic, m % 2 == 1, ins[m], accs[m], lands[m * depth : (m + 1) * depth], outs[m])
        for m in range(chunks)
    ]
    for action in in_waves(jobs):
        action()
    traffic.finish()

    def lane_sums(rows):
        total = jnp.sum(rows, axis=0, keepdims=True)
        return sum(total[:, at : at + 128] for at in range(0, total.shape[1], 128))

    grad = sum(lane_sums(out[...] * out[...]) for out in outs)
    loss = lane_sums(jnp.sum(loss_ref[...], axis=0))
    squares = [lane_sums(jnp.sum(ref[...], axis=0)) for ref in square_refs]
    stats_ref[...] = jnp.concatenate([grad, loss, *squares, jnp.zeros((6 - layers, 128), jnp.float32)], axis=0)
    for s in range(slots):
        both_ref[(lax.axis_index("tp"), s)] = outs[s][...]
    inner = [d for d in range(depth) if places.digits[d][0] == "tp"]
    for stage, digit in enumerate(reversed(range(depth))):
        size = places.dims[digit]
        axis, stride, _ = places.digits[digit]
        stats_land[stage, mine[digit]] = stats_ref[...]
        copies = []
        for shift in range(1, size):
            target, _ = places.other(mine, digit, shift)
            copies.append(
                pltpu.make_async_remote_copy(
                    src_ref=stats_ref,
                    dst_ref=stats_land.at[stage, mine[digit]],
                    send_sem=stats_send.at[stage, shift - 1],
                    recv_sem=stats_recv.at[stage, shift - 1],
                    device_id=target,
                    device_id_type=MESH,
                )
            )
            if digit in inner:
                held = stride
                start = lax.axis_index("tp") // stride * stride
                where = both_ref.at[pl.ds(start, held)]
                copies.append(
                    pltpu.make_async_remote_copy(
                        src_ref=where,
                        dst_ref=where,
                        send_sem=both_send.at[stage, shift - 1],
                        recv_sem=both_recv.at[stage, shift - 1],
                        device_id=target,
                        device_id_type=MESH,
                    )
                )
        for copy in copies:
            copy.start()
        for copy in copies:
            copy.wait()
        total = stats_land[stage, 0]
        for value in range(1, size):
            total = total + stats_land[stage, value]
        stats_ref[...] = total


def reduce_all(places, slots, parts, loss, squares):
    layers = len(squares)
    vmem = pl.BlockSpec(memory_space=pltpu.VMEM)
    chunks = len(parts)
    dims = places.dims
    depth, widest = len(dims), max(dims)
    blocks = [p.shape[1:] for p in parts]
    lands = []
    for m in range(chunks):
        lands += [pltpu.VMEM(shape, BF) for shape in land_shapes(places, m % 2 == 1, blocks[m])]
    return pl.pallas_call(
        functools.partial(reduce_kernel, places, chunks, slots, layers),
        out_shape=[jax.ShapeDtypeStruct(block, jnp.float32) for block in blocks]
        + [
            jax.ShapeDtypeStruct((lax.axis_size("tp"), slots, *blocks[0]), jnp.float32),
            jax.ShapeDtypeStruct((8, 128), jnp.float32),
        ],
        in_specs=[pl.BlockSpec(memory_space=pl.ANY)] * chunks + [vmem] * (1 + layers),
        out_specs=[vmem] * (chunks + 2),
        scratch_shapes=[pltpu.VMEM(dims[:-1] + block, BF) for block in blocks]
        + lands
        + [
            pltpu.SemaphoreType.DMA((chunks * copies_per_part(places),)),
            pltpu.SemaphoreType.DMA((chunks * copies_per_part(places),)),
            pltpu.SemaphoreType.DMA((chunks,)),
            pltpu.VMEM((depth, widest, 8, 128), jnp.float32),
            pltpu.SemaphoreType.DMA((depth, widest - 1)),
            pltpu.SemaphoreType.DMA((depth, widest - 1)),
            pltpu.SemaphoreType.DMA((depth, widest - 1)),
            pltpu.SemaphoreType.DMA((depth, widest - 1)),
        ],
        compiler_params=pltpu.CompilerParams(collective_id=2, has_side_effects=True, vmem_limit_bytes=LIMIT),
        name="reduce_gradients",
    )(*[p.reshape(dims + p.shape[1:]) for p in parts], loss, *squares)


def silu(values):
    return values * (1.0 / (1.0 + jnp.exp(-values)))


def silu_slope(values):
    gate = 1.0 / (1.0 + jnp.exp(-values))
    return gate * (1.0 + values * (1.0 - gate))


def split_low(values):
    high = values.astype(BF)
    return jnp.concatenate([high, (values - high.astype(jnp.float32)).astype(BF)], axis=0)


def block_of(refs, k):
    slots = len(refs)
    part = refs[k % slots][:, k // slots]
    return part.reshape(-1, D)


def condition_kernel(slots, lat_count, *refs):
    feat_ref, hot_ref = refs[:2]
    slot_refs = refs[2 : 2 + slots]
    ada_refs = refs[2 + slots : 2 + slots + SPLIT]
    mod_ref, fmod_ref, pre_ref, cond_ref, patch_ref, head_ref = refs[2 + slots + SPLIT :]
    entry = block_of(slot_refs, 0)
    patch_ref[...] = entry[:, :PATCH_IN]
    pre = dot_nt(feat_ref[...], entry)
    pre_ref[...] = pre
    cond = dot_nt(silu(pre).astype(BF), block_of(slot_refs, 1))
    for k in range(3):
        cond = cond + dot_nt(hot_ref[:, k * D : (k + 1) * D], block_of(slot_refs, 2 + k))
    cond_ref[...] = cond
    head_ref[...] = block_of(slot_refs, 4)[:, 256 : 256 + OUT]
    act = silu(cond).astype(BF)
    for p in range(SPLIT):
        wide = ada_refs[p].shape[0]
        mod_ref[:, p * wide : (p + 1) * wide] = dot_nt(act, ada_refs[p][...])
    for k in range(2):
        part = dot_nn(act, block_of(slot_refs, 5 + k))
        for b in range(lat_count):
            fmod_ref[b, k : k + 1, :] = part[b : b + 1, :]


def condition(feat, hot, slot_full, ada_full, lat_count):
    vmem = pl.BlockSpec(memory_space=pltpu.VMEM)
    wide = ada_full[0].shape[0]
    shapes = [
        ((8, SPLIT * wide), jnp.float32),
        ((lat_count, 8, D), jnp.float32),
        ((8, D), jnp.float32),
        ((8, D), jnp.float32),
        ((D, PATCH_IN), BF),
        ((D, OUT), BF),
    ]
    return pl.pallas_call(
        functools.partial(condition_kernel, len(slot_full), lat_count),
        out_shape=[jax.ShapeDtypeStruct(*s) for s in shapes],
        in_specs=[vmem] * (2 + len(slot_full) + SPLIT),
        out_specs=[vmem] * len(shapes),
        compiler_params=pltpu.CompilerParams(vmem_limit_bytes=LIMIT),
        name="condition",
    )(feat, hot, *slot_full, *ada_full)


def condition_back_kernel(slots, lat_count, *refs):
    feat_ref, hot_ref = refs[:2]
    slot_refs = refs[2 : 2 + slots]
    ada_refs = refs[2 + slots : 2 + slots + SPLIT]
    pre_ref, cond_ref, d_mod_ref, d_fmod_ref, d_patch_ref, d_head_ref = refs[2 + slots + SPLIT :][:6]
    outs = refs[2 + slots + SPLIT + 6 :]
    g_slots, g_ada = outs[:slots], outs[slots : slots + SPLIT]
    fmod_s = outs[slots + SPLIT]
    pre, cond = pre_ref[...], cond_ref[...]
    act = silu(cond).astype(BF)
    act_two = jnp.concatenate([act, act], axis=0)
    d_cond = jnp.zeros((16, D), jnp.float32)
    for p in range(SPLIT):
        wide = ada_refs[p].shape[0]
        d_mod = split_low(d_mod_ref[:, p * wide : (p + 1) * wide])
        d_cond = d_cond + dot_nn(d_mod, ada_refs[p][...])
        g_ada[p][...] = dot_tn(d_mod, act_two).astype(BF)

    def give(k, grad):
        ref = g_slots[k % slots]
        ref[:, k // slots] = grad.astype(BF).reshape(ref.shape[0], ref.shape[2], D)

    fmod_s[...] = jnp.zeros_like(fmod_s)
    for k in range(2):
        for b in range(lat_count):
            fmod_s[k, b : b + 1, :] = d_fmod_ref[b, k : k + 1, :]
        d_fmod = split_low(fmod_s[k])
        d_cond = d_cond + dot_nt(d_fmod, block_of(slot_refs, 5 + k))
        give(5 + k, dot_tn(act_two, d_fmod))
    d_pre = split_low((d_cond[:8] + d_cond[8:]) * silu_slope(cond))
    time_act = silu(pre).astype(BF)
    give(1, dot_tn(d_pre, jnp.concatenate([time_act, time_act], axis=0)))
    d_time = dot_nn(d_pre, block_of(slot_refs, 1))
    for k in range(3):
        hot = hot_ref[:, k * D : (k + 1) * D]
        grad = dot_tn(d_pre, jnp.concatenate([hot, hot], axis=0))
        if k == 2:
            here = jnp.pad(d_head_ref[...], ((0, 128 - OUT), (0, 0))).T
            grad = jnp.concatenate([grad[:, :256], grad[:, 256:] + here], axis=1)
        give(2 + k, grad)
    d_time = split_low((d_time[:8] + d_time[8:]) * silu_slope(pre))
    grad = dot_tn(d_time, jnp.concatenate([feat_ref[...], feat_ref[...]], axis=0))
    here = jnp.pad(d_patch_ref[...], ((0, 128 - PATCH_IN), (0, 0))).T
    give(0, jnp.concatenate([grad[:, :128] + here, grad[:, 128:]], axis=1))
    for k in range(7, SMALL):
        give(k, jnp.zeros((D, D), jnp.float32))


def condition_back(feat, hot, slot_full, ada_full, pre, cond, d_mod, d_fmod, d_patch, d_head):
    vmem = pl.BlockSpec(memory_space=pltpu.VMEM)
    lat_count = d_fmod.shape[0]
    args = (feat, hot, *slot_full, *ada_full, pre, cond, d_mod, d_fmod, d_patch, d_head)
    kept = (*slot_full, *ada_full)
    return pl.pallas_call(
        functools.partial(condition_back_kernel, len(slot_full), lat_count),
        out_shape=[jax.ShapeDtypeStruct(w.shape, BF) for w in kept],
        in_specs=[vmem] * len(args),
        out_specs=[vmem] * len(kept),
        scratch_shapes=[pltpu.VMEM((2, 8, D), jnp.float32)],
        compiler_params=pltpu.CompilerParams(vmem_limit_bytes=LIMIT),
        name="condition_back",
    )(*args)


def adam_kernel(slots, layers, count_rms, *refs):
    stats_ref, both_ref = refs[:2]
    grads = refs[2 : 2 + SPLIT + 3 * layers]
    states = refs[2 + SPLIT + 3 * layers :][:21]
    outs = refs[2 + SPLIT + 3 * layers + 21 :]
    news, (loss_ref, norm_ref, rms_ref) = outs[:21], outs[21:]
    totals = jnp.sum(stats_ref[...], axis=1, keepdims=True)
    norm = jnp.sqrt(totals[0:1])
    factor = jnp.minimum(1.0, 0.01 / (norm + 1e-06))
    loss_ref[...] = totals[1:2]
    norm_ref[...] = norm
    rms_ref[...] = jnp.sqrt(totals[2 : 2 + layers] / count_rms)
    correct = 1.0 - 0.5**STEP

    def update(name, where, grad):
        weight, first, second = (ref[where] for ref in states[3 * name : 3 * name + 3])
        clipped = grad * factor
        first_new = 0.5 * first + 0.5 * clipped
        second_new = 0.5 * second + 0.5 * clipped * clipped
        root = jnp.sqrt(second_new * (1.0 / correct)) + 1e-08
        new = weight - 0.02 * (first_new * (1.0 / correct) / root + 0.01 * weight)
        news[3 * name][where] = new
        news[3 * name + 1][where] = first_new
        news[3 * name + 2][where] = second_new

    def small(k):
        return both_ref[k // slots, k % slots]

    rows = states[0].shape[0]
    early = PATCH_IN + FREQ
    every = slice(0, rows)
    update(0, (every, slice(0, early)), small(0)[:rows, :early])
    update(0, (every, slice(early, early + D)), small(1)[:rows])
    update(1, (every, slice(0, D)), small(2)[:rows])
    update(1, (every, slice(D, 2 * D)), small(3)[:rows])
    update(1, (every, slice(2 * D, CLASSES + 1)), small(4)[:rows, : CLASSES + 1 - 2 * D])
    update(6, (every, slice(0, D)), small(5)[:rows])
    update(6, (every, slice(D, 2 * D)), small(6)[:rows])
    update(6, (every, slice(2 * D, 2 * D + OUT)), small(4)[:rows, 256 : 256 + OUT])
    part = -(-states[15].shape[0] // SPLIT)
    for p in range(SPLIT):
        update(5, (slice(p * part, (p + 1) * part), slice(0, D)), grads[p][:part])
    for l in range(layers):
        for k in range(3):
            update(2 + k, (l, slice(0, states[6].shape[1]), slice(0, D)), grads[SPLIT + 3 * l + k][: states[6].shape[1]])


def adam_all(slots, layers, count_rms, stats, both, grads, states):
    vmem = pl.BlockSpec(memory_space=pltpu.VMEM)
    args = (stats, both, *grads, *states)
    return pl.pallas_call(
        functools.partial(adam_kernel, slots, layers, count_rms),
        out_shape=[jax.ShapeDtypeStruct(s.shape, jnp.float32) for s in states]
        + [jax.ShapeDtypeStruct((n, 1), jnp.float32) for n in (1, 1, layers)],
        in_specs=[vmem] * len(args),
        out_specs=[vmem] * 24,
        compiler_params=pltpu.CompilerParams(vmem_limit_bytes=LIMIT),
        name="adam",
    )(*args)


def fused_adam_kernel(layers, count_rms, *refs):
    stats_ref, both_ref, early_ref, late_ref, class_ref, ada_ref, patch_ref = refs[:7]
    grads = refs[7 : 7 + 3 * layers]
    states = refs[7 + 3 * layers :][:21]
    outs = refs[7 + 3 * layers + 21 :]
    news, (loss_ref, norm_ref, rms_ref) = outs[:21], outs[21:]
    totals = jnp.sum(stats_ref[...], axis=1, keepdims=True)
    norm = jnp.sqrt(totals[0:1])
    factor = jnp.minimum(1.0, 0.01 / (norm + 1e-06))
    loss_ref[...] = totals[1:2]
    norm_ref[...] = norm
    rms = jnp.sqrt(totals / count_rms)
    rms_ref[...] = jnp.concatenate([rms[2 + l : 3 + l] for l in range(layers)], axis=1)
    correct = 1.0 - 0.5**STEP

    def update(name, where, grad):
        weight, first, second = (ref[where] for ref in states[3 * name : 3 * name + 3])
        clipped = grad * factor
        first_new = 0.5 * first + 0.5 * clipped
        second_new = 0.5 * second + 0.5 * clipped * clipped
        root = jnp.sqrt(second_new * (1.0 / correct)) + 1e-08
        new = weight - 0.02 * (first_new * (1.0 / correct) / root + 0.01 * weight)
        news[3 * name][where] = new
        news[3 * name + 1][where] = first_new
        news[3 * name + 2][where] = second_new

    rows = states[0].shape[0]
    early = PATCH_IN + FREQ
    every = slice(0, rows)
    patch = patch_ref[...].T[:rows, :PATCH_IN]
    update(0, (every, slice(0, PATCH_IN)), patch)
    update(0, (every, slice(PATCH_IN, early)), early_ref[:, PATCH_IN:early])
    update(0, (every, slice(early, early + D)), late_ref[...])
    update(1, (every, slice(0, CLASSES + 1)), class_ref[:, : CLASSES + 1])
    update(6, (every, slice(0, D)), both_ref[1])
    update(6, (every, slice(D, 2 * D)), both_ref[2])
    update(6, (every, slice(2 * D, 2 * D + OUT)), both_ref[0][:, :OUT])
    update(5, (slice(0, states[15].shape[0]), slice(0, D)), ada_ref[...])
    for l in range(layers):
        for k in range(3):
            update(2 + k, (l, slice(0, states[6].shape[1]), slice(0, D)), grads[3 * l + k][: states[6].shape[1]])


def fused_adam(layers, count_rms, small, grads, states):
    vmem = pl.BlockSpec(memory_space=pltpu.VMEM)
    args = (*small, *grads, *states)
    return pl.pallas_call(
        functools.partial(fused_adam_kernel, layers, count_rms),
        out_shape=[jax.ShapeDtypeStruct(s.shape, jnp.float32) for s in states]
        + [jax.ShapeDtypeStruct((1, n), jnp.float32) for n in (1, 1, layers)],
        in_specs=[vmem] * len(args),
        out_specs=[vmem] * 24,
        compiler_params=pltpu.CompilerParams(vmem_limit_bytes=LIMIT),
        name="adam_update",
    )(*args)


def modulation_pieces(layers, ada_rows, part_rows, part_pad, count):
    pieces = []
    for j in range(count):
        for l in range(layers):
            low = l * ada_rows
            while low < (l + 1) * ada_rows:
                p, r = divmod(low, part_rows)
                length = min((l + 1) * ada_rows - low, part_rows - r)
                pieces.append((l, j * ada_rows + low - l * ada_rows, p, j * part_pad + r, length))
                low += length
    return pieces


def class_of(labels_ref, drops_ref, b):
    return jnp.where(drops_ref[b] == 1, CLASSES, labels_ref[b])


def embed_inputs(lat_count, times_ref, labels_ref, drops_ref, freq_ref, feat_s, hot_s, fact_s):
    feat_s[...] = jnp.zeros_like(feat_s)
    hot_s[...] = jnp.zeros_like(hot_s)
    fact_s[...] = jnp.zeros_like(fact_s)
    column = lax.broadcasted_iota(jnp.int32, (1, 3 * D), 1)
    half = FREQ // 2
    for b in range(lat_count):
        angles = times_ref[b].astype(jnp.float32) * freq_ref[...]
        feat_s[b : b + 1, PATCH_IN : PATCH_IN + half] = jnp.cos(angles)
        feat_s[b : b + 1, PATCH_IN + half : PATCH_IN + FREQ] = jnp.sin(angles)
        label = class_of(labels_ref, drops_ref, b)
        hot_s[b : b + 1, :] = jnp.where(column == label, 1.0, 0.0)
        low = lax.rem(label, 32)
        high = (label - low) // 32
        fact_s[12 + b : 13 + b, :128] = jnp.full((1, 128), low, jnp.int32).astype(jnp.float32)
        fact_s[12 + b : 13 + b, 128:256] = jnp.full((1, 128), high, jnp.int32).astype(jnp.float32)
    fact_s[4 : 4 + lat_count, :] = feat_s[:lat_count, :]


def embed_condition(lat_count, feat_s, hot_s, fact_s, slot_refs, pre_ref, cond_ref, fmod_ref):
    pre = dot_nt(feat_s[...].astype(BF), block_of(slot_refs, 0))
    pre_ref[...] = pre
    time_act = silu(pre).astype(BF)
    cond = dot_nt(time_act, block_of(slot_refs, 1))
    for k in range(3):
        cond = cond + dot_nt(hot_s[:, k * D : (k + 1) * D].astype(BF), block_of(slot_refs, 2 + k))
    cond_ref[...] = cond
    act = silu(cond).astype(BF)
    fact_s[8 : 8 + lat_count, :] = act.astype(jnp.float32)[:lat_count]
    fact_s[:lat_count, :] = time_act.astype(jnp.float32)[:lat_count]
    for k in range(2):
        fmod_ref[:, k * D : (k + 1) * D] = dot_nn(act, block_of(slot_refs, 5 + k))


def mod_rows(mod_ref, index, n, nb, part):
    rows = [mod_ref[(*index, pl.ds(n * nb + b, 1), slice(part * D, (part + 1) * D))] for b in range(nb)]
    return jnp.stack(rows, axis=0)


def attend_forward(nb, tokens, stream, mod, attn_w, out_w, qkv_ref, probs_ref, mixed_ref, branch_ref):
    rows = nb * tokens
    hat, _ = norm_rows(stream)
    attn_in = (hat * (1.0 + mod(1)) + mod(0)).astype(BF).reshape(rows, D)
    qkv_ref[...] = dot_nt(attn_in, attn_w[...]).astype(BF)
    masks = half_masks()
    for b in range(nb):
        here = slice(b * tokens, (b + 1) * tokens)
        for pair in range(HEADS // 2):
            col = pair * 2 * HEAD_DIM
            queries = qkv_ref[here, col : col + 2 * HEAD_DIM] * jnp.asarray(HEAD_DIM**-0.5, BF)
            keys = stack_heads(qkv_ref[here, D + col : D + col + 2 * HEAD_DIM], masks)
            values = stack_heads(qkv_ref[here, 2 * D + col : 2 * D + col + 2 * HEAD_DIM], masks)
            scores = dot_nt(queries, keys)
            halves = []
            for side in range(2):
                part = scores[:, side * tokens : (side + 1) * tokens]
                grown = jnp.exp(part - jnp.max(part, axis=-1, keepdims=True))
                halves.append((grown * (1.0 / jnp.sum(grown, axis=-1, keepdims=True))).astype(BF))
            probs = jnp.concatenate(halves, axis=1)
            probs_ref[here, pair * 2 * tokens : (pair + 1) * 2 * tokens] = probs
            mixed_ref[here, col : col + 2 * HEAD_DIM] = dot_nn(probs, values).astype(BF)
    branch = dot_nt(mixed_ref[...], out_w[...])
    branch_ref[...] = branch.astype(BF)
    return stream + mod(2) * branch.reshape(nb, tokens, D)


def feed_forward(nb, tokens, middle, mod, in_w, out_w, mlp_ref, act_ref, slope_ref):
    rows = nb * tokens
    hat, _ = norm_rows(middle)
    mlp_in = (hat * (1.0 + mod(4)) + mod(3)).astype(BF).reshape(rows, D)
    hidden = dot_nt(mlp_in, in_w[...])
    squared = hidden * hidden
    bent = jnp.tanh(hidden * (GELU_A + (GELU_A * GELU_B) * squared))
    half = 0.5 * hidden
    act = (half + half * bent).astype(BF)
    act_ref[...] = act
    slope_ref[...] = (
        0.5
        + 0.5 * bent
        + half * (1.0 - bent * bent) * (GELU_A + (3.0 * GELU_A * GELU_B) * squared)
    ).astype(BF)
    mlp = dot_nn(act, out_w[...])
    mlp_ref[...] = mlp.astype(BF)
    return middle + mod(5) * mlp.reshape(nb, tokens, D)


def fixed_tables(tokens):
    half, quarter = FREQ // 2, D // 4
    freq = np.exp(np.float32(-math.log(10000.0)) * np.arange(half, dtype=np.float32) / np.float32(half))
    omegas = np.exp(np.float32(-math.log(10000.0)) * np.arange(quarter, dtype=np.float32) / np.float32(quarter))
    token = np.arange(tokens)
    row = (token // GRID).astype(np.float32)[:, None] * omegas
    col = (token % GRID).astype(np.float32)[:, None] * omegas
    table = np.concatenate([np.sin(row), np.cos(row), np.sin(col), np.cos(col)], axis=-1)
    return jnp.asarray(freq[None], jnp.float32), jnp.asarray(table, jnp.float32)


PROLOGUE = [(0, 1), (0, 2), (1, 1), (0, 3), (2, 0), (1, 2), (0, 4), 'cond', (3, 0), (2, 1), (1, 3), (1, 4), 'mods', (2, 2), (3, 1)]
LATER = {1: [(4, 0)], 3: [(2, 3)], 4: [(2, 4), (3, 2)], 6: [(4, 1), (5, 0)], 7: [(3, 3)], 8: [(3, 4), 'mods', (5, 1)], 9: [(4, 2)], 10: [(5, 2)], 11: [(4, 3)], 12: [(4, 4), (5, 3)], 14: [(5, 4), 'hand']}


def fused_forward_kernel(places, slots, layers, nb, tokens, lat_count, sizes, *refs):
    small_rows, ada_rows, part_rows, part_pad, wide_rows = sizes
    chunks = slots + SPLIT + 3 * layers
    entry_ref, table_ref, final_ref, ada_ref, attn_ref, in_ref, out_ref = refs[:7]
    times_ref, labels_ref, drops_ref, freq_ref, clean_ref, noise_ref, pos_ref = refs[7:14]
    refs = refs[14:]
    given = refs[: chunks + 1]
    (
        mods_ref,
        fmod_ref,
        pre_ref,
        cond_ref,
        noisy_ref,
        start_ref,
        result_ref,
        qkv_ref,
        probs_ref,
        mixed_ref,
        branch_ref,
        middle_ref,
        mlp_ref,
        act_ref,
        slope_ref,
        square_ref,
    ) = refs[chunks + 1 : chunks + 17]
    refs = refs[chunks + 17 :]
    fulls = refs[: chunks + 1]
    (
        small,
        packed_ada,
        packed,
        stream_s,
        middle_s,
        feat_s,
        hot_s,
        fact_s,
        fact_bf,
        send_sems,
        recv_sems,
        own_sems,
        give_sems,
    ) = refs[chunks + 1 :]
    l, h, n = (pl.program_id(axis) for axis in range(3))
    mine = places.mine()
    first = lax.axis_index("tp") * slots
    order = [*range(slots)]
    for ll in range(layers):
        at = slots + SPLIT + 3 * ll
        order += [at, slots + ll, at + 1, at + 2]
    sources = [small.at[first + s] for s in range(slots)] + [packed_ada.at[p] for p in range(SPLIT)]
    sources += [packed.at[m] for m in range(3 * layers)]
    traffic = Traffic(places, mine, send_sems, recv_sems, own_sems)
    jobs = [gather_job(traffic, at % 2 == 1, sources[m], fulls[m]) for at, m in enumerate(order)]
    pairs = [jobs[at : at + 2] for at in range(0, chunks, 2)]
    pairs.append([gather_job(traffic, False, fact_bf, fulls[chunks])])
    handed = [pltpu.make_async_copy(fulls[m], given[m], give_sems.at[m]) for m in range(chunks + 1)]

    def flat(m, rows):
        return fulls[m].reshape(places.count * rows, D)

    def run(*names):
        for pair, k in names:
            for job in pairs[pair]:
                job[k]()

    def at_step(layer, half, step):
        return pl.when((l == layer) & (h == half) & (n == step))

    def set_mods(layer):
        act = silu(cond_ref[...]).astype(BF)
        low, high = layer * ada_rows, (layer + 1) * ada_rows
        parts = range(low // part_rows, -(-high // part_rows))
        raw = {p: dot_nt(act, flat(slots + p, part_pad)[...]) for p in parts}
        for ll, col, p, at, length in modulation_pieces(layers, ada_rows, part_rows, part_pad, places.count):
            if ll == layer:
                mods_ref[layer, :, col : col + length] = raw[p][:, at : at + length]

    slot_refs = [f.reshape(-1, lax.axis_size("tp"), small_rows, D) for f in fulls[:slots]]

    def pack_blocks():
        for ll in range(layers):
            for k, source in enumerate((attn_ref, in_ref, out_ref)):
                if ll or k:
                    packed[3 * ll + k] = source[ll].astype(BF)

    @at_step(0, 0, 0)
    def _():
        small[...] = jnp.zeros_like(small)
        for k, at, source, low, high in small_blocks(entry_ref, table_ref, final_ref):
            small[k, : source.shape[0], at : at + high - low] = source[:, low:high].astype(BF)
        places.barrier(mine)
        run((0, 0))
        packed_ada[...] = jnp.zeros_like(packed_ada)
        for p in range(SPLIT):
            packed_ada[p, :part_rows, :] = ada_ref[p * part_rows : (p + 1) * part_rows, :].astype(BF)
        packed[0] = attn_ref[0].astype(BF)
        run((1, 0))
        pack_blocks()
        embed_inputs(lat_count, times_ref, labels_ref, drops_ref, freq_ref, feat_s, hot_s, fact_s)
        for entry in PROLOGUE:
            if entry == "cond":
                embed_condition(lat_count, feat_s, hot_s, fact_s, slot_refs, pre_ref, cond_ref, fmod_ref)
                fact_bf[...] = fact_s[...].astype(BF)
            elif entry == "mods":
                set_mods(0)
            else:
                run(entry)

    steps = lat_count // nb
    for number, names in sorted(LATER.items()):
        number = number * steps // 4
        layer_at, rest = divmod(number, 2 * steps)

        @at_step(layer_at, rest // steps, rest % steps)
        def _(names=names):
            for entry in names:
                if entry == "mods":
                    for layer in range(1, layers):
                        set_mods(layer)
                elif entry == "hand":
                    for copy in handed:
                        copy.start()
                else:
                    run(entry)

    rows = nb * tokens
    here = pl.ds(pl.multiple_of(n * rows, rows), rows)

    def weight(layer, k):
        return flat(slots + SPLIT + 3 * layer + k, wide_rows)

    for layer in range(layers):
        mod = lambda part, layer=layer: mod_rows(mods_ref, (layer,), n, nb, part)

        @pl.when((l == layer) & (h == 0))
        def _(layer=layer, mod=mod):
            if layer == 0:
                patch = block_of(slot_refs, 0)[:, :PATCH_IN]
                for b in range(nb):
                    when = jnp.full((1, tokens), times_ref[n * nb + b], jnp.int32).astype(jnp.float32)
                    phase = (when / NOISE_STEPS + 0.008) / 1.008 * (math.pi / 2)
                    noisy_ref[b] = (jnp.cos(phase) * clean_ref[b] + jnp.sin(phase) * noise_ref[b]).astype(BF)
                parts = [
                    lax.dot_general(
                        noisy_ref[b], patch, (((0,), (1,)), ((), ())), preferred_element_type=jnp.float32
                    )
                    + pos_ref[...]
                    for b in range(nb)
                ]
                stream = parts[0] if nb == 1 else jnp.concatenate(parts, axis=0)
                start_ref[...] = stream
            else:
                stream = stream_s[here, :]
            stream = stream.reshape(nb, tokens, D)
            middle = attend_forward(
                nb,
                tokens,
                stream,
                mod,
                weight(layer, 0).at[: 3 * D],
                weight(layer, 0).at[3 * D :],
                qkv_ref.at[0],
                probs_ref.at[0],
                mixed_ref.at[0],
                branch_ref.at[0],
            )
            middle_ref[0] = middle.reshape(rows, D)
            middle_s[here, :] = middle.reshape(rows, D)

        @pl.when((l == layer) & (h == 1))
        def _(layer=layer, mod=mod):
            middle = middle_s[here, :].reshape(nb, tokens, D)
            result = feed_forward(
                nb,
                tokens,
                middle,
                mod,
                weight(layer, 1),
                weight(layer, 2),
                mlp_ref.at[0],
                act_ref.at[0],
                slope_ref.at[0],
            )
            result_ref[0] = result.reshape(rows, D)
            if layer < layers - 1:
                stream_s[here, :] = result.reshape(rows, D)
            square_ref[0, 0] = jnp.sum((result * result).reshape(rows // 8, 8, D), axis=0)

    @at_step(layers - 1, 1, lat_count // nb - 1)
    def _():
        for copy in handed:
            copy.wait()
        traffic.finish()


def fused_forward(places, slots, nb, weights_in, ids, clean_t, noise_t):
    entry_t, table_t, final, ada_t, attn_t, in_t, out_w = weights_in
    layers, wide_rows = attn_t.shape[:2]
    lat_count, _, tokens = clean_t.shape
    small_rows, part_rows, ada_rows = final.shape[0], ada_t.shape[0] // SPLIT, ada_t.shape[0] // layers
    part_pad = pad16(part_rows)
    sizes = [small_rows] * slots + [part_pad] * SPLIT + [wide_rows] * (3 * layers)
    chunks = len(sizes)
    steps = lat_count // nb
    rows, total = nb * tokens, lat_count * tokens
    full_shapes = [(*places.dims, r, D) for r in (*sizes, 16)]

    def const(array):
        return pl.BlockSpec(array.shape, lambda l, h, n: (0,) * array.ndim)

    def const_shape(shape):
        return pl.BlockSpec(shape, lambda l, h, n: (0,) * len(shape))

    def early(l, h, n):
        return jnp.where(h == 0, n, steps - 1)

    def half_one(cols):
        return pl.BlockSpec((1, rows, cols), lambda l, h, n: (l, early(l, h, n), 0))

    def half_two(cols):
        def index(l, h, n):
            before = jnp.where(l == 0, 0, steps - 1)
            return (jnp.where(h == 0, jnp.maximum(l - 1, 0), l), jnp.where(h == 0, before, n), 0)

        return pl.BlockSpec((1, rows, cols), index)

    def square_index(l, h, n):
        before = jnp.where(l == 0, 0, steps - 1)
        return (jnp.where(h == 0, jnp.maximum(l - 1, 0), l), jnp.where(h == 0, before, n), 0, 0)

    out_shape = [jax.ShapeDtypeStruct(s, BF) for s in full_shapes]
    out_specs = [pl.BlockSpec(memory_space=pl.ANY)] * (chunks + 1)

    def add(shape, kind, spec):
        out_shape.append(jax.ShapeDtypeStruct(shape, kind))
        out_specs.append(spec)

    for shape in ((layers, 8, 6 * D), (8, 2 * D), (8, D), (8, D)):
        add(shape, jnp.float32, const_shape(shape))
    def opening(l, h, n):
        return jnp.where((l == 0) & (h == 0), n, steps - 1)

    latents = pl.BlockSpec((nb, PATCH_IN, tokens), lambda l, h, n: (opening(l, h, n), 0, 0))
    add((lat_count, PATCH_IN, tokens), BF, latents)
    add((total, D), jnp.float32, pl.BlockSpec((rows, D), lambda l, h, n: (opening(l, h, n), 0)))
    add((layers, total, D), jnp.float32, half_two(D))
    for cols, kind in ((3 * D, BF), (HEADS * tokens, BF), (D, BF), (D, BF), (D, jnp.float32)):
        add((layers, total, cols), kind, half_one(cols))
    for cols in (D, 4 * D, 4 * D):
        add((layers, total, cols), BF, half_two(cols))
    add((layers, steps, 8, D), jnp.float32, pl.BlockSpec((1, 1, 8, D), square_index))
    freq, pos = fixed_tables(tokens)
    args = (*weights_in, *ids, freq, clean_t, noise_t, pos)
    in_specs = [const(a) for a in weights_in]
    in_specs += [pl.BlockSpec(memory_space=pltpu.SMEM)] * 3 + [const(freq), latents, latents, const(pos)]
    count = (chunks + 1) * copies_per_part(places)
    return pl.pallas_call(
        functools.partial(
            fused_forward_kernel,
            places,
            slots,
            layers,
            nb,
            tokens,
            lat_count,
            (small_rows, ada_rows, part_rows, part_pad, wide_rows),
        ),
        grid=(layers, 2, steps),
        out_shape=out_shape,
        in_specs=in_specs,
        out_specs=out_specs,
        scratch_shapes=[pltpu.VMEM(s, BF) for s in full_shapes]
        + [
            pltpu.VMEM((slots * lax.axis_size("tp"), small_rows, D), BF),
            pltpu.VMEM((SPLIT, part_pad, D), BF),
            pltpu.VMEM((3 * layers, wide_rows, D), BF),
            pltpu.VMEM((total, D), jnp.float32),
            pltpu.VMEM((total, D), jnp.float32),
            pltpu.VMEM((8, D), jnp.float32),
            pltpu.VMEM((8, 3 * D), jnp.float32),
            pltpu.VMEM((16, D), jnp.float32),
            pltpu.VMEM((16, D), BF),
            pltpu.SemaphoreType.DMA((count,)),
            pltpu.SemaphoreType.DMA((count,)),
            pltpu.SemaphoreType.DMA((chunks + 1,)),
            pltpu.SemaphoreType.DMA((chunks + 1,)),
        ],
        compiler_params=pltpu.CompilerParams(
            collective_id=3, has_side_effects=True, vmem_limit_bytes=LIMIT
        ),
        name="gather_and_forward",
    )(*args)


LIMIT_B = 62 * 1024 * 1024

LATER_BACK = {5: [(0, 1)], 8: [(0, 2)], 9: [(1, 1)], 10: [(0, 3), (7, 1)], 11: [(1, 2)], 12: [(7, 2)], 13: [(1, 3), (2, 1), (0, 4)], 14: [(7, 3)], 15: [(2, 2)]}
SHARES = {}
TAIL_ONE = [(2, 3), (3, 1), (6, 1), (4, 1)]
TAIL_TWO = [(5, 1), (7, 4), (1, 4), 0, (3, 2), (6, 2), (4, 2), 1, (3, 3), (6, 3), (5, 2), (4, 3), (2, 4), 2, (5, 3), (6, 4), 'ada', (5, 4), 'small', (4, 4), (3, 4)]


def exchange_job(traffic, bufs):
    places, mine = traffic.places, traffic.mine
    depth = len(places.dims)
    stages = []
    for k, digit in enumerate(reversed(range(depth))):
        copies = []
        for shift in range(1, places.dims[digit]):
            there = tuple(traffic.ahead(digit, shift) if d == digit else slice(None) for d in range(depth))
            here = tuple(mine[d] if d == digit else slice(None) for d in range(depth))
            copies.append(traffic.remote(bufs[k].at[there], bufs[k + 1].at[here], digit, shift))
        stages.append((copies, here))

    def action(k):
        if k > 0:
            for copy in stages[k - 1][0]:
                copy.wait_recv()
        if k < depth:
            copies, here = stages[k]
            for copy in copies:
                copy.start()
            bufs[k + 1][here] = bufs[k][here]

    return [functools.partial(action, k) for k in range(depth + 1)]


def attend_backward(nb, tokens, qkv_ref, probs_ref, d_mix, d_qkv_s):
    masks = half_masks()
    lane = lax.broadcasted_iota(jnp.int32, (tokens, 2 * HEAD_DIM), 1)
    low_side = lane < HEAD_DIM
    root = HEAD_DIM**-0.5
    for b in range(nb):
        here = slice(b * tokens, (b + 1) * tokens)
        for pair in range(HEADS // 2):
            col = pair * 2 * HEAD_DIM
            queries = qkv_ref[here, col : col + 2 * HEAD_DIM]
            keys = stack_heads(qkv_ref[here, D + col : D + col + 2 * HEAD_DIM], masks)
            values = stack_heads(qkv_ref[here, 2 * D + col : 2 * D + col + 2 * HEAD_DIM], masks)
            d_out = d_mix[here, col : col + 2 * HEAD_DIM]
            probs_bf = probs_ref[here, pair * 2 * tokens : (pair + 1) * 2 * tokens]
            d_probs = dot_nt(d_out, values)
            halves = []
            for side in range(2):
                cut = slice(side * tokens, (side + 1) * tokens)
                probs = probs_bf[:, cut].astype(jnp.float32)
                part = d_probs[:, cut]
                halves.append((probs * (part - jnp.sum(probs * part, axis=-1, keepdims=True))).astype(BF))
            d_scores = jnp.concatenate(halves, axis=1)
            d_queries = dot_nn(d_scores, keys) * root
            d_keys = dot_tn(d_scores, queries)
            d_keys = jnp.where(low_side, d_keys[:tokens], d_keys[tokens:]) * root
            d_values = dot_tn(probs_bf, d_out)
            d_values = jnp.where(low_side, d_values[:tokens], d_values[tokens:])
            d_qkv_s[here, col : col + 2 * HEAD_DIM] = d_queries.astype(BF)
            d_qkv_s[here, D + col : D + col + 2 * HEAD_DIM] = d_keys.astype(BF)
            d_qkv_s[here, 2 * D + col : 2 * D + col + 2 * HEAD_DIM] = d_values.astype(BF)


def lane_sums(rows):
    total = jnp.sum(rows, axis=0, keepdims=True)
    return sum(total[:, at : at + 128] for at in range(0, total.shape[1], 128))


def fused_backward_kernel(places, slots, layers, nb, tokens, lat_count, count_all, sizes, *refs):
    small_rows, ada_rows, part_rows, part_pad, wide_rows = sizes
    chunks = slots + SPLIT + 3 * layers
    steps = lat_count // nb
    depth = len(places.dims)
    rows = nb * tokens
    given = refs[: chunks + 1]
    refs = refs[1:]
    mods_ref, fmod_ref, pre_ref, cond_ref, square_ref = refs[chunks : chunks + 5]
    (
        clean_ref,
        noise_ref,
        noisy_ref,
        start_ref,
        result_ref,
        qkv_ref,
        probs_ref,
        mixed_ref,
        branch_ref,
        middle_ref,
        mlp_ref,
        act_ref,
        slope_ref,
    ) = refs[chunks + 5 : chunks + 18]
    refs = refs[chunks + 18 :]
    count = 3 * layers + 2
    outs = refs[: count - 1]
    both_ref, early_ref, late_ref, class_ref, ada_grad_ref, stats_ref = refs[count - 1 : count + 5]
    refs = refs[count + 5 :]
    fulls = refs[: chunks + 1]
    refs = refs[chunks + 1 :]
    accs = refs[:count]
    lands = refs[count : (1 + depth) * count]
    (
        *swaps,
        wide_s,
        small_s,
        patch_s,
        small_out,
        mine_s,
        all_s,
        signal_s,
        code_s,
        stage_attn,
        stage_in,
        stage_out,
        acc_one,
        acc_two,
        d_stream_s,
        d_qkv_s,
        d_mods_s,
        d_raw_s,
        d_fmod_s,
        d_patch_s,
        d_head_s,
        loss_s,
        sum_s,
        stats_s,
        both_s,
        stats_land,
        send_sems,
        recv_sems,
        own_sems,
        take_sems,
        stats_send,
        stats_recv,
        both_send,
        both_recv,
    ) = refs[(1 + depth) * count :]
    turn, h, n = (pl.program_id(axis) for axis in range(3))
    mine = places.mine()
    lead = slots + SPLIT

    def flat(ref, count):
        return ref.reshape(places.count * count, D)

    takes = [pltpu.make_async_copy(given[m], fulls[m], take_sems.at[m]) for m in range(chunks + 1)]
    slot_refs = [f.reshape(-1, lax.axis_size("tp"), small_rows, D) for f in fulls[:slots]]
    ada_refs = [flat(f, part_pad) for f in fulls[slots:lead]]
    staged = {0: stage_attn, 1: stage_in, 2: stage_out}
    order = [lead + 4, lead + 5, lead + 3, lead + 1, lead + 2, lead]
    sources = [staged[(m - lead) % 3] for m in order] + [patch_s]
    targets = [outs[m - lead] for m in order] + [outs[count - 2]]
    sources.insert(3, small_s)
    targets.insert(3, small_out)
    traffic = Traffic(places, mine, send_sems, recv_sems, own_sems)
    jobs = []
    first_copies = []
    for at in range(count):
        used = traffic.used
        jobs.append(
            reduce_job(
                traffic, at % 2 == 1, sources[at], accs[at], lands[at * depth : (at + 1) * depth], targets[at]
            )
        )
        digit = places.order(at % 2 == 1)[-1]
        first_copies.append(traffic.copies[used : used + places.dims[digit] - 1])
    factors = len(jobs)
    jobs.append(gather_job(traffic, False, mine_s, all_s))
    for l in range(layers):
        jobs.append(exchange_job(traffic, swaps[l * (depth + 1) : (l + 1) * (depth + 1)]))
    inner = [d for d in reversed(range(depth)) if places.digits[d][0] == "tp"]

    def both_copies(stage):
        digit = inner[stage]
        _, stride, size = places.digits[digit]
        where = both_s.at[pl.ds(lax.axis_index("tp") // stride * stride, stride)]
        return [
            pltpu.make_async_remote_copy(
                src_ref=where,
                dst_ref=where,
                send_sem=both_send.at[stage, shift - 1],
                recv_sem=both_recv.at[stage, shift - 1],
                device_id=places.other(mine, digit, shift)[0],
                device_id_type=MESH,
            )
            for shift in range(1, size)
        ]

    exchange = [both_copies(stage) for stage in range(len(inner))]

    def share(stage):
        if stage == 0:
            both_s[lax.axis_index("tp")] = small_out[...]
        else:
            for copy in exchange[stage - 1]:
                copy.wait()
        if stage < len(exchange):
            for copy in exchange[stage]:
                copy.start()

    def run(*names):
        for job, k in names:
            jobs[job][k]()

    def at_step(number):
        layer_turn, rest = divmod(number, 2 * steps)
        half, step = divmod(rest, steps)
        return pl.when((turn == layer_turn) & (h == half) & (n == step))

    def both(pair, k):
        return [(job, k) for job in (2 * pair, 2 * pair + 1)]

    def extra(name, k):
        return [({3: 6, 4: 7}.get(name, name + 3), k)]

    def swap_job(layer):
        return factors + 1 + layer

    here = pl.ds(pl.multiple_of(n * rows, rows), rows)

    def mod_of(layer):
        return lambda part: mod_rows(mods_ref, (layer,), n, nb, part)

    def put_mod(layer, part, value):
        for b in range(nb):
            d_mods_s[layer, pl.ds(n * nb + b, 1), part * D : (part + 1) * D] = value[b]

    @at_step(0)
    def _():
        for m in [*range(slots), *range(chunks - 1, slots - 1, -1), chunks]:
            takes[m].start()
        d_mods_s[...] = jnp.zeros_like(d_mods_s)
        d_raw_s[...] = jnp.zeros_like(d_raw_s)
        d_fmod_s[...] = jnp.zeros_like(d_fmod_s)
        d_patch_s[...] = jnp.zeros_like(d_patch_s)
        d_head_s[...] = jnp.zeros_like(d_head_s)
        loss_s[...] = jnp.zeros_like(loss_s)
        sum_s[...] = jnp.zeros_like(sum_s)
        mine_s[...] = jnp.zeros_like(mine_s)
        wide_s[...] = jnp.zeros_like(wide_s)
        signal_s[...] = jnp.zeros_like(signal_s)
        small_s[...] = jnp.zeros_like(small_s)
        patch_s[...] = jnp.zeros_like(patch_s)
        places.barrier_all()
        for m in (*range(slots), lead + 5, lead + 4):
            takes[m].wait()

    hooks = {
        at * steps // 4: [job for name, k in names for job in (both(name, k) if name < 3 else extra(name, k))]
        for at, names in LATER_BACK.items()
    }
    shares = {at * steps // 4: stage for at, stage in SHARES.items()}
    early_ada = [slots + p for p in range(SPLIT) if p * part_rows < (layers - 1) * ada_rows]
    loads = {steps: [lead + 3], 2 * steps: [lead + 2, lead + 1], 3 * steps: [lead, chunks, *early_ada]}
    for number in sorted(set(hooks) | set(loads)):

        @at_step(number)
        def _(number=number):
            for m in loads.get(number, []):
                takes[m].wait()
            run(*hooks.get(number, []))
            if number in shares:
                share(shares[number])

    def raw_part(p):
        wide = places.count * part_pad
        return split_low(d_raw_s[:, p * wide : (p + 1) * wide])

    def send_mods(layer):
        first = swaps[layer * (depth + 1)].reshape(places.count, 8, 128)
        for j in range(places.count):
            first[j] = d_mods_s[layer, :, j * ada_rows : j * ada_rows + 128]
        run((swap_job(layer), 0))

    def ada_grads(layer):
        arrived = swaps[layer * (depth + 1) + depth].reshape(places.count, 8, 128)
        wide_s[:, 8:, :] = arrived[...]
        signal = wide_s.reshape(places.count * 16, 128)[...]
        high = signal.astype(BF)
        low = (signal - high.astype(jnp.float32)).astype(BF)
        fact = fulls[chunks].reshape(places.count * 16, D)[...]
        grad = dot_tn(high, fact) + dot_tn(low, fact)
        ada_grad_ref[layer * ada_rows : (layer + 1) * ada_rows, :] = grad[:ada_rows]

    def spread(layer):
        wide = places.count * part_pad
        for l, col, p, at, length in modulation_pieces(layers, ada_rows, part_rows, part_pad, places.count):
            if l == layer:
                d_raw_s[:, p * wide + at : p * wide + at + length] = d_mods_s[layer, :, col : col + length]

    def send_small():
        cond_act = silu(cond_ref[...]).astype(BF)
        cond_two = jnp.concatenate([cond_act, cond_act], axis=0)
        view = small_s.reshape(-1, lax.axis_size("tp"), small_rows, D)

        def give(k, grad):
            view[:, k] = grad.astype(BF).reshape(view.shape[0], small_rows, D)

        head = jnp.pad(d_head_s[...], ((0, 128 - OUT), (0, 0))).T
        give(0, jnp.pad(head, ((0, 0), (0, D - 128))))
        for k in range(2):
            give(1 + k, dot_tn(cond_two, split_low(d_fmod_s[:, k * D : (k + 1) * D])))

    def expand(entry):
        name, k = entry
        return both(name, k) if name < 3 else extra(name, k)

    def finish_all():
        run((6, 0))
        cond = cond_ref[...]
        pre = pre_ref[...]
        spread(0)
        d_cond = sum_s[...]
        for p in range(SPLIT):
            if p * part_rows < (layers - 1) * ada_rows:
                d_cond = d_cond + dot_nn(raw_part(p), ada_refs[p][...])
        for k in range(2):
            d_fmod = split_low(d_fmod_s[:, k * D : (k + 1) * D])
            d_cond = d_cond + dot_nt(d_fmod, block_of(slot_refs, 5 + k))
        d_pre = (d_cond[:8] + d_cond[8:]) * silu_slope(cond)
        d_time = dot_nn(split_low(d_pre), block_of(slot_refs, 1))
        d_time = (d_time[:8] + d_time[8:]) * silu_slope(pre)
        mine_s[:lat_count, :] = d_pre[:lat_count]
        mine_s[4 : 4 + lat_count, :] = d_time[:lat_count]
        run((factors, 0))
        send_mods(0)
        patch = jnp.pad(d_patch_s[...], ((0, 0), (0, 128)))
        view = patch_s.reshape(-1, lax.axis_size("tp"), PATCH_IN, 128)
        for i in range(view.shape[0]):
            here_cols = patch[:, i * small_rows : i * small_rows + 128].astype(BF)
            for t in range(view.shape[1]):
                view[i, t] = here_cols
        run((7, 0))
        for entry in TAIL_ONE:
            run(*expand(entry))
        for entry in TAIL_TWO:
            if entry == "small":
                small_grads()
            elif entry == "ada":
                for layer in range(layers):
                    ada_grads(layer)
            elif isinstance(entry, int):
                share(entry)
            else:
                run(*expand(entry))
        copies_of_tp = 1.0 / lax.axis_size("tp")
        grad = sum(lane_sums(out[...] * out[...]) for out in (*outs[:-1], small_out, ada_grad_ref))
        lane = lax.broadcasted_iota(jnp.int32, (PATCH_IN, 128), 1)
        patch = jnp.where(lane < small_rows, outs[-1][...], 0.0)
        alike = sum(lane_sums(g * g) for g in (patch, early_ref[...], late_ref[...], class_ref[...]))
        grad = grad + alike * copies_of_tp
        squares = [lane_sums(jnp.sum(square_ref[l], axis=0)) for l in range(layers)]
        stats_s[...] = jnp.concatenate(
            [grad, lane_sums(loss_s[...]), *squares, jnp.zeros((6 - layers, 128), jnp.float32)], axis=0
        )
        me = places.index()
        stats_land[me] = stats_s[...]
        copies = []
        for shift in range(1, places.count):
            copies.append(
                pltpu.make_async_remote_copy(
                    src_ref=stats_s,
                    dst_ref=stats_land.at[me],
                    send_sem=stats_send.at[shift - 1],
                    recv_sem=stats_recv.at[shift - 1],
                    device_id=places.device(lax.rem(me + shift, places.count)),
                    device_id_type=MESH,
                )
            )
            copies[-1].start()
        for copy in copies:
            copy.wait()
        stats_s[...] = jnp.sum(stats_land[...], axis=0)
        stats_ref[...] = stats_s[...]
        both_ref[...] = both_s[...]
        waited = {id(copy) for group in first_copies[:3] for copy in group}
        for copy in traffic.copies:
            if id(copy) not in waited:
                copy.wait_send()

    def small_grads():
        total = places.count * 16
        fact = fulls[chunks].reshape(total, D)[...]
        signal_s[:, :8, :] = all_s.reshape(places.count, 8, D)[...]
        signal = signal_s.reshape(total, D)[...]
        row = lax.broadcasted_iota(jnp.int32, (D, small_rows), 0)
        column = lax.broadcasted_iota(jnp.int32, (D, small_rows), 1)
        pick = jnp.where(row == column + lax.axis_index("dp") * small_rows, 1.0, 0.0).astype(BF)
        high = signal.astype(BF)
        low = (signal - high.astype(jnp.float32)).astype(BF)
        picked = [dot_nn(part, pick).astype(BF) for part in (high, low)]
        kind = lax.rem(lax.broadcasted_iota(jnp.int32, (total, 1), 0), 16) // 4

        def rows_of(which):
            mask = jnp.where(kind == which, 1.0, 0.0).astype(BF)
            return [part * mask for part in picked]

        late_ref[...] = sum(dot_tn(part, fact) for part in rows_of(0))
        early_ref[...] = sum(dot_tn(part, fact) for part in rows_of(1))
        code_s[...] = (fact[:, :128].astype(jnp.float32) + 32.0 * fact[:, 128:256].astype(jnp.float32)).reshape(
            places.count, 16, 128
        )
        code_s[:, :4, :] = code_s[:, 12:, :]
        label = code_s.reshape(total, 128)[:, 0:1]
        wide = lax.broadcasted_iota(jnp.int32, (total, 3 * D), 1).astype(jnp.float32)
        hot = jnp.where(wide == label, 1.0, 0.0).astype(BF)
        class_ref[...] = sum(dot_tn(part, hot) for part in rows_of(0))

    for layer in range(layers):
        mod = mod_of(layer)
        is_turn = turn == layers - 1 - layer
        attn_w, in_w, out_w = (flat(fulls[lead + 3 * layer + k], wide_rows) for k in range(3))

        @pl.when(is_turn & (h == 0))
        def _(layer=layer, mod=mod, in_w=in_w, out_w=out_w):
            @pl.when(n == 0)
            def _():
                acc_one[...] = jnp.zeros_like(acc_one)
                acc_two[...] = jnp.zeros_like(acc_two)

            if layer == layers - 1:
                head = block_of(slot_refs, 4)[:, 256 : 256 + OUT]
                fmod = lambda part: mod_rows(fmod_ref, (), n, nb, part)
                hat, rstd = norm_rows(result_ref[0].reshape(nb, tokens, D))
                final_in = (hat * (1.0 + fmod(1)) + fmod(0)).astype(BF)
                d_parts = []
                for b in range(nb):
                    predicted = lax.dot_general(
                        head, final_in[b], (((0,), (1,)), ((), ())), preferred_element_type=jnp.float32
                    )
                    errors = predicted - jnp.concatenate([noise_ref[b], clean_ref[b]], axis=0)
                    loss_s[...] += jnp.sum((errors * errors).reshape(OUT // 8, 8, tokens), axis=0)
                    d_pred = (errors * (2.0 / count_all)).astype(BF)
                    d_head_s[...] += dot_nn(d_pred, final_in[b])
                    d_parts.append(
                        lax.dot_general(
                            d_pred, head, (((0,), (1,)), ((), ())), preferred_element_type=jnp.float32
                        )
                    )
                d_stream, d_shift, d_scale = norm_back(jnp.stack(d_parts, axis=0), hat, rstd, fmod(1))
                for b in range(nb):
                    d_fmod_s[pl.ds(n * nb + b, 1), :D] = d_shift[b]
                    d_fmod_s[pl.ds(n * nb + b, 1), D:] = d_scale[b]
            else:
                d_stream = d_stream_s[here, :].reshape(nb, tokens, D)
            mlp = mlp_ref[0].astype(jnp.float32).reshape(nb, tokens, D)
            put_mod(layer, 5, jnp.sum(d_stream * mlp, axis=1, keepdims=True))
            d_mlp = (d_stream * mod(5)).astype(BF).reshape(rows, D)
            d_hidden = (dot_nt(d_mlp, out_w[...]) * slope_ref[0].astype(jnp.float32)).astype(BF)
            acc_two[...] += dot_tn(act_ref[0], d_mlp)
            hat, rstd = norm_rows(middle_ref[0].reshape(nb, tokens, D))
            mlp_in = (hat * (1.0 + mod(4)) + mod(3)).astype(BF).reshape(rows, D)
            acc_one[...] += dot_tn(d_hidden, mlp_in)
            d_input = dot_nn(d_hidden, in_w[...]).reshape(nb, tokens, D)
            d_middle, d_shift, d_scale = norm_back(d_input, hat, rstd, mod(4))
            put_mod(layer, 3, d_shift)
            put_mod(layer, 4, d_scale)
            d_stream_s[here, :] = (d_middle + d_stream).reshape(rows, D)

            @pl.when(n == steps - 1)
            def _():
                pair = 0 if layer == layers - 1 else 2
                if pair:
                    for copy in first_copies[0] + first_copies[1]:
                        copy.wait_send()
                flat(stage_in, wide_rows)[...] = acc_one[...].astype(BF)
                flat(stage_out, wide_rows)[...] = acc_two[...].astype(BF)
                run(*both(pair, 0))
                if layer == layers - 1:
                    send_small()

        @pl.when(is_turn & (h == 1))
        def _(layer=layer, mod=mod, attn_w=attn_w):
            @pl.when(n == 0)
            def _():
                acc_one[...] = jnp.zeros_like(acc_one)

            d_middle = d_stream_s[here, :].reshape(nb, tokens, D)
            branch = branch_ref[0].astype(jnp.float32).reshape(nb, tokens, D)
            put_mod(layer, 2, jnp.sum(d_middle * branch, axis=1, keepdims=True))
            d_proj = (d_middle * mod(2)).astype(BF).reshape(rows, D)
            acc_one[3 * D :, :] += dot_tn(d_proj, mixed_ref[0])
            d_mix = dot_nn(d_proj, attn_w[3 * D :, :]).astype(BF)
            attend_backward(nb, tokens, qkv_ref.at[0], probs_ref.at[0], d_mix, d_qkv_s)
            d_qkv = d_qkv_s[...]
            stream = start_ref[...] if layer == 0 else result_ref[0]
            hat, rstd = norm_rows(stream.reshape(nb, tokens, D))
            attn_in = (hat * (1.0 + mod(1)) + mod(0)).astype(BF).reshape(rows, D)
            acc_one[: 3 * D, :] += dot_tn(d_qkv, attn_in)
            d_attn_in = dot_nn(d_qkv, attn_w[: 3 * D, :]).reshape(nb, tokens, D)
            d_before, d_shift, d_scale = norm_back(d_attn_in, hat, rstd, mod(1))
            put_mod(layer, 0, d_shift)
            put_mod(layer, 1, d_scale)
            d_prev = d_middle + d_before
            if layer == 0:
                for b in range(nb):
                    d_patch_s[...] += lax.dot_general(
                        noisy_ref[b].astype(jnp.float32),
                        d_prev[b],
                        (((1,), (0,)), ((), ())),
                        precision=highest,
                    )
            else:
                d_stream_s[here, :] = d_prev.reshape(rows, D)

            @pl.when(n == steps - 1)
            def _():
                if layer == 0:
                    for copy in first_copies[2]:
                        copy.wait_send()
                flat(stage_attn, wide_rows)[...] = acc_one[...].astype(BF)
                if layer > 0:
                    run(*both(1, 0))
                    spread(layer)
                    for p in range(SPLIT):
                        if p * part_rows >= layer * ada_rows:
                            takes[slots + p].wait()
                            sum_s[...] += dot_nn(raw_part(p), ada_refs[p][...])
                    send_mods(layer)
                else:
                    finish_all()


def fused_backward(places, slots, nb, count_all, given, mods, fmod, pre, cond, square, streams):
    clean_t, noise_t, noisy, start, result, *kept = streams
    layers = mods.shape[0]
    lat_count, _, tokens = noisy.shape
    total, rows, steps = lat_count * tokens, nb * tokens, lat_count // nb
    chunks = len(given) - 1
    jobs = chunks - slots - SPLIT + 2
    dims = places.dims
    depth, widest = len(dims), max(dims)
    block = given[0].shape[-2:]
    last = steps - 1

    def const_shape(shape):
        return pl.BlockSpec(shape, lambda t, h, n: (0,) * len(shape))

    def only(turn, half, before, after):
        def pick(t, h, n):
            at, phase = 2 * t + h, 2 * turn + half
            return jnp.where(at == phase, n, jnp.where(at < phase, before, after))

        return pick

    def spec(block_shape, pick):
        return pl.BlockSpec(block_shape, lambda t, h, n: (pick(t, h, n),) + (0,) * (len(block_shape) - 1))

    def result_index(t, h, n):
        head = (t == 0) & (h == 0)
        body_step = (t == 0) & (h == 1)
        return (jnp.where(head, 1, 0), jnp.where(head | body_step, n, last), 0)

    def mlp_spec(cols):
        return pl.BlockSpec(
            (1, rows, cols), lambda t, h, n: (layers - 1 - t, jnp.where(h == 0, n, last), 0)
        )

    def attn_spec(cols):
        return pl.BlockSpec((1, rows, cols), lambda t, h, n: (layers - 1 - t, jnp.where(h == 1, n, 0), 0))

    consts = (mods, fmod, pre, cond, square)
    in_specs = [pl.BlockSpec(memory_space=pl.ANY)] * (chunks + 1) + [const_shape(a.shape) for a in consts]
    in_specs += [spec((nb, PATCH_IN, tokens), only(0, 0, 0, last))] * 2
    in_specs += [
        spec((nb, PATCH_IN, tokens), only(1, 1, 0, last)),
        spec((rows, D), only(1, 1, 0, last)),
        pl.BlockSpec((1, rows, D), result_index),
    ]
    in_specs += [attn_spec(a.shape[2]) for a in kept[:4]] + [mlp_spec(a.shape[2]) for a in kept[4:]]
    patch_block = (PATCH_IN, 128)
    shared = (lax.axis_size("tp"), *block)
    out_shape = [jax.ShapeDtypeStruct(block, jnp.float32)] * (jobs - 2)
    out_shape += [
        jax.ShapeDtypeStruct(s, jnp.float32)
        for s in (patch_block, shared, block, block, (block[0], 3 * D), (layers * mods.shape[2] // places.count, D), (8, 128))
    ]
    full = (*dims, *block)
    blocks = [block] * (jobs - 1) + [patch_block]
    accs, lands = [], []
    for at in range(jobs):
        accs.append(pltpu.VMEM(dims[:-1] + blocks[at], BF))
        lands += [pltpu.VMEM(shape, BF) for shape in land_shapes(places, at % 2 == 1, blocks[at])]
    f32 = jnp.float32
    scratch = [pltpu.VMEM(g.shape, BF) for g in given[:-1]] + [pltpu.VMEM((*dims, 16, D), BF)] + accs + lands
    scratch += [pltpu.VMEM((*dims, 8, 128), f32)] * (layers * (depth + 1))
    scratch += [
        pltpu.VMEM((places.count, 16, 128), f32),
        pltpu.VMEM(full, BF),
        pltpu.VMEM((*dims, *patch_block), BF),
        pltpu.VMEM(block, f32),
        pltpu.VMEM((8, D), f32),
        pltpu.VMEM((*dims, 8, D), f32),
        pltpu.VMEM((places.count, 16, D), f32),
        pltpu.VMEM((places.count, 16, 128), f32),
    ]
    scratch += [pltpu.VMEM(full, BF)] * 3
    scratch += [
        pltpu.VMEM(shape, kind)
        for shape, kind in (
            ((4 * D, D), f32),
            ((4 * D, D), f32),
            ((total, D), f32),
            ((rows, 3 * D), BF),
            ((*mods.shape[:2], mods.shape[2] + 128), f32),
            ((8, SPLIT * places.count * given[slots].shape[-2]), f32),
            ((8, 2 * D), f32),
            ((PATCH_IN, D), f32),
            ((OUT, D), f32),
            ((8, tokens), f32),
            ((16, D), f32),
            ((8, 128), f32),
            (shared, f32),
            ((places.count, 8, 128), f32),
        )
    ]
    dma = pltpu.SemaphoreType.DMA
    count = (jobs + 1 + layers) * copies_per_part(places)
    scratch += [dma((count,)), dma((count,)), dma((jobs + 1,)), dma((chunks + 1,))]
    scratch += [dma((places.count - 1,))] * 2 + [dma((depth, widest - 1))] * 2
    ada_rows = mods.shape[2] // places.count
    sizes = (block[0], ada_rows, layers * ada_rows // SPLIT, given[slots].shape[-2], block[0])
    return pl.pallas_call(
        functools.partial(
            fused_backward_kernel, places, slots, layers, nb, tokens, lat_count, count_all, sizes
        ),
        grid=(layers, 2, steps),
        out_shape=out_shape,
        in_specs=in_specs,
        out_specs=[const_shape(s.shape) for s in out_shape],
        scratch_shapes=scratch,
        compiler_params=pltpu.CompilerParams(
            collective_id=4, has_side_effects=True, vmem_limit_bytes=LIMIT_B
        ),
        name="backward_and_reduce",
    )(*given, *consts, *streams)


def position_table(grid_side, columns):
    quarter = columns // 4
    omegas = jnp.exp(-math.log(10000.0) * jnp.arange(quarter, dtype=jnp.float32) / quarter)
    positions = jnp.arange(grid_side * grid_side, dtype=jnp.int32)
    row_pos = (positions // grid_side).astype(jnp.float32)[:, None] * omegas
    col_pos = (positions % grid_side).astype(jnp.float32)[:, None] * omegas
    return jnp.concatenate(
        [jnp.sin(row_pos), jnp.cos(row_pos), jnp.sin(col_pos), jnp.cos(col_pos)], axis=-1
    )


def time_table(step_ids, columns):
    half_cols = columns // 2
    frequency = jnp.exp(-math.log(10000.0) * jnp.arange(half_cols, dtype=jnp.float32) / half_cols)
    angles = step_ids.astype(jnp.float32)[:, None] * frequency
    return jnp.concatenate([jnp.cos(angles), jnp.sin(angles)], axis=-1)


def noise_scales(step_ids):
    phases = (step_ids.astype(jnp.float32) / NOISE_STEPS + 0.008) / 1.008 * (math.pi / 2)
    return (jnp.cos(phases), jnp.sin(phases))


def swap(array):
    return jnp.swapaxes(array, -1, -2)


def pad_rows(part):
    extra = -part.shape[-2] % 16
    if extra == 0:
        return part
    return jnp.pad(part, [(0, 0)] * (part.ndim - 2) + [(0, extra), (0, 0)])


def body(
    clean_latents,
    noise_field,
    timesteps,
    labels,
    drop_flags,
    entry_weight,
    class_table,
    attn_weight,
    ffn_in_weight,
    ffn_out_weight,
    ada_weight,
    final_weight,
    entry_first,
    entry_second,
    class_first,
    class_second,
    attn_first,
    attn_second,
    ffn_in_first,
    ffn_in_second,
    ffn_out_first,
    ffn_out_second,
    ada_first,
    ada_second,
    final_first,
    final_second,
):
    lat_count = clean_latents.shape[0]
    tokens = clean_latents.shape[1]
    layers = attn_weight.shape[0]
    both = ("dp", "tp")
    devices = lax.axis_size("dp") * lax.axis_size("tp")
    count_all = float(lat_count * devices * tokens * OUT)
    count_rms = float(lat_count * devices * tokens * D)
    nb = 1
    clean_t, noise_t = swap(clean_latents), swap(noise_field)
    n_dp, n_tp = lax.axis_size("dp"), lax.axis_size("tp")
    places = Places(n_dp, n_tp)
    slots = -(-SMALL // n_tp)
    dp_rows = final_weight.shape[0]
    wide_rows = attn_weight.shape[2]
    ada_rows = ada_weight.shape[2]
    part_rows = -(-layers * ada_rows // SPLIT)

    def flat_ada(array):
        return swap(array).reshape(layers * ada_rows, D)

    weights_in = (
        swap(entry_weight),
        swap(class_table),
        final_weight,
        flat_ada(ada_weight),
        swap(attn_weight),
        swap(ffn_in_weight),
        ffn_out_weight,
    )
    def whole_rows(block, rows):
        return block[:, :rows].reshape(-1, D)

    def to_slot(block):
        if dp_rows % 16 == 0:
            return block.reshape(n_dp, n_tp, dp_rows, D)
        block = block.reshape(n_dp, n_tp, -1, D)[:, :, :dp_rows]
        return block.swapaxes(0, 1).reshape(1, n_tp, n_dp * dp_rows, D)

    def from_slot(block):
        if dp_rows % 16 == 0:
            return block.reshape(places.count, dp_rows, D)
        block = block.reshape(n_tp, n_dp, dp_rows, D).swapaxes(0, 1)
        return pad_rows(block.reshape(places.count, dp_rows, D))

    fused = dp_rows == wide_rows and dp_rows % 16 == 0 and part_rows == ada_rows and len(places.dims) >= 4 and layers == 2
    fused = fused and n_tp >= 3 and lat_count == 4
    if fused:
        outs = fused_forward(
            places, slots, NB_FORWARD, weights_in, (timesteps, labels, drop_flags), clean_t, noise_t
        )
        chunks = slots + SPLIT + 3 * layers
        mods, fmod, pre, cond, noisy, start, result, *kept, square = outs[chunks + 1 :]
        streams = (clean_t, noise_t, noisy, start, result, *kept)
        *summed, patch, both, early, late, classes, ada_grad, stats = fused_backward(
            places, slots, nb, count_all, outs[: chunks + 1], mods, fmod, pre, cond, square, streams
        )
    else:
        cos_part, sin_part = noise_scales(timesteps)
        noisy = (cos_part[:, None, None] * clean_t + sin_part[:, None, None] * noise_t).astype(BF)
        time_feat = time_table(timesteps, FREQ).astype(BF)
        feat = jnp.pad(time_feat, ((0, 8 - lat_count), (PATCH_IN, D - PATCH_IN - FREQ)))
        classes_used = jnp.where(drop_flags == 1, CLASSES, labels)
        classes_used = jnp.pad(classes_used, (0, 8 - lat_count), constant_values=3 * D)
        class_hot = (classes_used[:, None] == jnp.arange(3 * D, dtype=jnp.int32)[None, :]).astype(BF)
        pos = position_table(GRID, D)
        gathered = gather_all(places, slots, *weights_in)
        slot_full = [to_slot(g) for g in gathered[:slots]]
        ada_full = [whole_rows(g, part_rows) for g in gathered[slots : slots + SPLIT]]
        block_full = [whole_rows(g, wide_rows) for g in gathered[slots + SPLIT :]]
        weights = [tuple(block_full[3 * l : 3 * l + 3]) for l in range(layers)]

        raw, fmod, pre, cond, patch_t, head = condition(feat, class_hot, slot_full, ada_full, lat_count)
        mods = raw[:lat_count].reshape(lat_count, SPLIT, places.count, part_rows).swapaxes(1, 2)
        mods = mods.reshape(lat_count, places.count, layers, ada_rows).transpose(2, 0, 1, 3)
        mods = mods.reshape(layers, lat_count, 6, D)
        mods = jnp.pad(mods, ((0, 0), (0, 0), (0, 2), (0, 0)))
        mods = [mods[l] for l in range(layers)]
        saved = []
        squares = []
        stream = None
        for l in range(layers):
            if l == 0:
                outs = forward_layer(True, (noisy, patch_t, pos), mods[l], weights[l], nb, tokens)
                stream, outs = outs[0], outs[1:]
            else:
                outs = forward_layer(False, (stream,), mods[l], weights[l], nb, tokens)
            saved.append((stream, *outs[1:9]))
            stream = outs[0]
            squares.append(outs[9])
        layer_grads = [None] * layers
        d_mods = [None] * layers
        d_stream = None
        for l in reversed(range(layers)):
            last, first = l == layers - 1, l == 0
            entry_args = (stream, fmod, head, clean_t, noise_t) if last else (d_stream,)
            if first:
                entry_args = (*entry_args, noisy)
            outs = list(backward_layer(first, last, entry_args, mods[l], weights[l], saved[l], nb, tokens, count_all))
            if last:
                loss_part, d_head_t, d_fmod = outs[:3]
                outs = outs[3:]
            if first:
                d_patch = outs[0]
            else:
                d_stream = outs[0]
            layer_grads[l] = outs[1:4]
            d_mods[l] = outs[4]
        d_raw = jnp.stack([d[:, :6] for d in d_mods]).reshape(layers, lat_count, places.count, ada_rows)
        d_raw = d_raw.transpose(1, 2, 0, 3).reshape(lat_count, places.count, SPLIT, part_rows)
        d_raw = d_raw.swapaxes(1, 2).reshape(lat_count, -1)
        d_raw = jnp.pad(d_raw, ((0, 8 - lat_count), (0, 0)))
        small_grads = condition_back(
            feat, class_hot, slot_full, ada_full, pre, cond, d_raw, d_fmod, d_patch, d_head_t
        )
        grads = [from_slot(g) for g in small_grads[:slots]]
        grads += [pad_rows(g.reshape(places.count, part_rows, D)) for g in small_grads[slots:]]
        for l in reversed(range(layers)):
            for k in range(3):
                grads.append(pad_rows(layer_grads[l][k].reshape(places.count, wide_rows, D)))
        *summed, both, stats = reduce_all(places, slots, grads, loss_part, squares)
        wide = summed[slots + SPLIT :]
        wide = [wide[3 * (layers - 1 - l) + k] for l in range(layers) for k in range(3)]
    states = []
    for shape_it, triple in (
        (swap, (entry_weight, entry_first, entry_second)),
        (swap, (class_table, class_first, class_second)),
        (swap, (attn_weight, attn_first, attn_second)),
        (swap, (ffn_in_weight, ffn_in_first, ffn_in_second)),
        (lambda a: a, (ffn_out_weight, ffn_out_first, ffn_out_second)),
        (flat_ada, (ada_weight, ada_first, ada_second)),
        (lambda a: a, (final_weight, final_first, final_second)),
    ):
        states.extend(shape_it(a) for a in triple)
    if fused:
        out = fused_adam(layers, count_rms, (stats, both, early, late, classes, ada_grad, patch), summed, states)
    else:
        out = adam_all(slots, layers, count_rms, stats, both, [*summed[slots : slots + SPLIT], *wide], states)
    news = []
    for at in range(21):
        value = out[at]
        if at // 3 == 5:
            value = value.reshape(layers, ada_rows, D)
        news.append(value if at // 3 in (4, 6) else swap(value))
    return (*news, out[21].reshape(()), out[22].reshape(()), out[23].reshape(layers))


def solution(mesh):
    lead = P(("dp", "tp"), None, None)
    ids = P(("dp", "tp"))
    wide = P(None, "dp")
    cols = P(None, None, ("dp", "tp"))
    rows = P(None, ("dp", "tp"), None)
    top = P("dp", None)
    return jax.shard_map(
        body,
        mesh=mesh,
        in_specs=(
            lead,
            lead,
            ids,
            ids,
            ids,
            wide,
            wide,
            cols,
            cols,
            rows,
            cols,
            top,
            wide,
            wide,
            wide,
            wide,
            cols,
            cols,
            cols,
            cols,
            rows,
            rows,
            cols,
            cols,
            top,
            top,
        ),
        out_specs=(wide,) * 6 + (cols,) * 6 + (rows,) * 3 + (cols,) * 3 + (top,) * 3 + (P(), P(), P()),
        check_vma=False,
    )
```
